32 devices in a mesh: groups: 2 (over x), blk: 16 (over z, y, core).
Axes of the slice: x: 2, y: 2, z: 4, core: 2. Of those that a mesh axis runs over, the one named last changes fastest.
Arguments:
- trans_east: float32 [1024, 16, 128], P(('groups', 'blk')), parts along dimension 0, may hold values from 2 to 20
- trans_north: float32 [1024, 16, 128], P(('groups', 'blk')), parts along dimension 0, may hold values from 0.05 to 3
- trans_up: float32 [1024, 16, 128], P(('groups', 'blk')), parts along dimension 0, may hold values from 0.05 to 3
- storage: float32 [1024, 16, 128], P(('groups', 'blk')), parts along dimension 0, may hold values from 0.2 to 4
- support_reach: int32 [64, 8, 4], P(('groups', 'blk')), parts along dimension 0, may hold values from 1 to 16, as said below
Outputs:
- basis_out: float32 [64, 8, 48, 16, 128], P(('groups', 'blk')), parts along dimension 0
The draws below stay inside these ranges and needn't reach their ends.
There are 2 independent parts, one for each index of `groups`. The reference program is written for one: setup_inputs(seed, part) draws one part's arguments, and reference() takes and returns one part's arrays. A program takes and returns all parts, laid end to end along the dimension named above; each array names one. Nothing has to cross between parts.
Inputs may be any that keep to these rules, and one draw needn't show every extreme that they name: `support_reach`: at least one coarse block reaches the full 16 cells in all four directions.
All inputs are finite; a program needn't handle non-finite values.
Results may differ from the reference program's by a relative error of at most 0.0003.
Values sent between devices are 32-bit elements; how exact they have to be, the bound alone decides.
No kernel may reach another device: no remote copies, remote signals or barrier semaphores. Data moves between devices by JAX's collectives and lax.ppermute only.
A program may use at most 128 MiB of HBM per device.

```python
import math
import jax
import jax.numpy as jnp
from jax import lax

BS = 16
CZ = 8
ITERS = 2
NCX = 32
NX = 512
NY = 16
NZ = 128


def draw_support_reach(key, part):
    key = jax.random.fold_in(key, 7)
    key_vals, key_pick, key_row, key_col = jax.random.split(key, 4)
    values = jax.random.randint(key_vals, (NCX, CZ, 4), 1, BS + 1)
    picks = jax.random.randint(key_pick, (NCX, CZ, 2), 0, 4)
    along_x = jnp.where(picks < 3, 1, values[:, :, 0:2])
    values = jnp.concatenate([along_x, values[:, :, 2:4]], axis=2)
    row_at = jax.random.randint(key_row, (), 0, NCX)
    col_at = jax.random.randint(key_col, (), 0, CZ)
    values = values.at[row_at, col_at].set(BS)
    return values.astype(jnp.int32)


def shard_levels(rng, shape, cuts, smallest, top_value):
    loudness, own = 1.0, jax.random.fold_in(rng, 6)
    for axis_at, shards_of in cuts:
        draws = jnp.exp(jax.random.uniform(jax.random.fold_in(own, axis_at), (shards_of,), jnp.float32, smallest / len(cuts), top_value / len(cuts)))
        loudness = loudness * jnp.repeat(draws, shape[axis_at] // shards_of).reshape([-1 if axis == axis_at else 1 for axis in range(len(shape))])
    return loudness


def setup_inputs(seed: int = 0, part: int = 0) -> dict:
    streams_of = jax.random.split(jax.random.key(seed), 6)
    part_splits = jax.random.split(jax.random.fold_in(streams_of[5], part), 6)
    return {
        "trans_east": jnp.clip(jnp.exp(math.log(20.0) - 2.3025851 * jax.random.uniform(part_splits[0], (NX, NY, NZ), jnp.float32) ** shard_levels(part_splits[0], (NX, NY, NZ), ((0, 16),), -0.2, 0.2)), 2.0, 20.0),
        "trans_north": jnp.clip(jnp.exp(math.log(3.0) - 4.0943445 * jax.random.uniform(part_splits[1], (NX, NY, NZ), jnp.float32) ** shard_levels(part_splits[1], (NX, NY, NZ), ((0, 16),), -0.2, 0.2)), 0.05, 3.0),
        "trans_up": jnp.clip(jnp.exp(math.log(3.0) - 4.0943445 * jax.random.uniform(part_splits[2], (NX, NY, NZ), jnp.float32) ** shard_levels(part_splits[2], (NX, NY, NZ), ((0, 16),), -0.2, 0.2)), 0.05, 3.0),
        "storage": jnp.clip(jnp.exp(math.log(4.0) - 2.9957323 * jax.random.uniform(part_splits[3], (NX, NY, NZ), jnp.float32) ** shard_levels(part_splits[3], (NX, NY, NZ), ((0, 16),), -0.2, 0.2)), 0.2, 4.0),
        "support_reach": draw_support_reach(jax.random.fold_in(jax.random.fold_in(streams_of[5], part), 71), part),
    }


relaxation = 2.0 / 3.0


def next_along(field, axis):
    size = field.shape[axis]
    rest = lax.slice_in_dim(field, 1, size, axis=axis)
    zeros = jnp.zeros_like(lax.slice_in_dim(field, 0, 1, axis=axis))
    return jnp.concatenate([rest, zeros], axis=axis)


def prev_along(field, axis):
    size = field.shape[axis]
    rest = lax.slice_in_dim(field, 0, size - 1, axis=axis)
    zeros = jnp.zeros_like(lax.slice_in_dim(field, 0, 1, axis=axis))
    return jnp.concatenate([zeros, rest], axis=axis)


def apply_box(values, face_x, face_y, face_z, diagonal):
    applied = diagonal * values
    applied = applied - face_x * prev_along(values, 1) - next_along(face_x, 0) * next_along(values, 1)
    applied = applied - face_y * prev_along(values, 2) - next_along(face_y, 1) * next_along(values, 2)
    applied = applied - face_z * prev_along(values, 3) - next_along(face_z, 2) * next_along(values, 3)
    return applied


def support_masks(layer, reach_rows, cells_x, blocks_z):
    plane_pos = jnp.arange(3 * BS, dtype=jnp.int32)
    global_x = BS * (layer - 1) + plane_pos
    in_domain = (global_x >= 0) & (global_x < cells_x)
    along_x = in_domain[None, :] & (plane_pos[None, :] >= BS - reach_rows[:, 0:1]) & (plane_pos[None, :] < 2 * BS + reach_rows[:, 1:2])
    depth_pos = jnp.arange(BS * blocks_z, dtype=jnp.int32)
    block_ids = jnp.arange(blocks_z, dtype=jnp.int32)[:, None]
    along_z = (depth_pos[None, :] >= BS * block_ids - reach_rows[:, 2:3]) & (depth_pos[None, :] < BS * block_ids + BS + reach_rows[:, 3:4])
    support = along_x[:, :, None, None] & along_z[:, None, None, :]
    own_x = (plane_pos >= BS) & (plane_pos < 2 * BS)
    own_z = (depth_pos[None, :] // BS) == block_ids
    initial = own_x[None, :, None, None] & own_z[:, None, None, :]
    initial = jnp.broadcast_to(initial, (blocks_z, 3 * BS, BS, BS * blocks_z)).astype(jnp.float32)
    return support, in_domain, initial


def reference(trans_east, trans_north, trans_up, storage, support_reach):
    face_x = trans_east.at[0].set(0.0)
    face_y = trans_north.at[:, 0].set(0.0)
    face_z = trans_up.at[:, :, 0].set(0.0)
    diagonal = storage + face_x + next_along(face_x, 0) + face_y + next_along(face_y, 1) + face_z + next_along(face_z, 2)
    widths = ((BS, BS), (0, 0), (0, 0))
    padded_x = jnp.pad(face_x, widths)
    padded_y = jnp.pad(face_y, widths)
    padded_z = jnp.pad(face_z, widths)
    padded_d = jnp.pad(diagonal, widths)
    layers = jnp.arange(NCX, dtype=jnp.int32)

    def masks_of(items):
        layer, reach_rows = items
        support, in_domain, initial = support_masks(layer, reach_rows, NX, CZ)
        return support, initial

    supports, basis_vals = lax.map(masks_of, (layers, support_reach))

    for sweep in range(ITERS):
        def smooth(items):
            layer, values, reach_rows = items
            start = (BS * layer).astype(jnp.int32)
            box_x = lax.dynamic_slice_in_dim(padded_x, start, 3 * BS, 0)
            box_y = lax.dynamic_slice_in_dim(padded_y, start, 3 * BS, 0)
            box_z = lax.dynamic_slice_in_dim(padded_z, start, 3 * BS, 0)
            box_d = lax.dynamic_slice_in_dim(padded_d, start, 3 * BS, 0)
            support, in_domain, initial = support_masks(layer, reach_rows, NX, CZ)
            safe_diag = jnp.where(in_domain[:, None, None], box_d, 1.0)
            applied = apply_box(values, box_x, box_y, box_z, safe_diag)
            return jnp.where(support, values - relaxation * applied / safe_diag, 0.0)

        updates = lax.map(smooth, (layers, basis_vals, support_reach))
        partial_value = jnp.sum(updates, axis=1).reshape(NCX, 3, BS, NY, NZ)
        zeros_pad = ((0, 0), (0, 0), (0, 0), (0, 0))
        blocks = jnp.pad(partial_value[:, 0], ((0, 2),) + zeros_pad[1:])
        blocks = blocks + jnp.pad(partial_value[:, 1], ((1, 1),) + zeros_pad[1:])
        blocks = blocks + jnp.pad(partial_value[:, 2], ((2, 0),) + zeros_pad[1:])
        totals = jnp.concatenate([blocks[:-2], blocks[1:-1], blocks[2:]], axis=1)
        totals = totals[:, None]
        basis_vals = jnp.where(supports, updates / jnp.where(supports, totals, 1.0), 0.0)
    return basis_vals
```

```python
import functools

import jax
import jax.numpy as jnp
from jax import lax
from jax.experimental import pallas as pl
from jax.experimental.pallas import tpu as pltpu
from jax.sharding import PartitionSpec as P


TAIL = 8


class Lanes:
    def __init__(self, shape, width):
        lane = lax.broadcasted_iota(jnp.int32, shape, 1)
        self.width = width
        self.lanes = shape[1]
        self.rows = shape[0]
        self.lane = lane
        self.block = lane // width
        self.local = lane - self.block * width
        self.first = self.local == 0
        self.last = self.local == width - 1
        self.upper = self.local >= width // 2
        self.other = jnp.where(self.upper, self.block + 1, self.block - 1)
        self.row0 = lax.broadcasted_iota(jnp.int32, shape, 0) == 0
        self.lane0 = lane == 0

    def zm(self, v):
        return pltpu.roll(v, 1, 1)

    def zp(self, v):
        return pltpu.roll(v, self.lanes - 1, 1)

    def ym(self, v):
        return pltpu.roll(v, 1, 0)

    def yp(self, v):
        return pltpu.roll(v, self.rows - 1, 0)


class Plane:
    def __init__(self, ln, tx, txn, ty, tz, s, valid=None):
        self.ln = ln
        self.tx, self.txn = tx, txn
        self.ty = jnp.where(ln.row0, 0.0, ty)
        self.tz = jnp.where(ln.lane0, 0.0, tz)
        self.typ = ln.yp(self.ty)
        self.tzp = ln.zp(self.tz)
        e = s * (1.0 / 3.0) + ((tx + txn) + (self.ty + self.typ) + (self.tz + self.tzp))
        if valid is not None:
            e = jnp.where(valid, e, 1.0)
        self.half = 0.5 * e + s * (1.0 / 3.0)
        self.all = 1.5 * e
        self.q = 1.0 / self.all
        self.z1 = self.q * jnp.where(ln.first, self.tz, jnp.where(ln.last, self.tzp, 0.0))
        self.zm = ln.zm(self.z1)
        self.zp = ln.zp(self.z1)

    def toward(self, low):
        return self.tx if low else self.txn

    def inward(self, low):
        return self.txn if low else self.tx

    def edge(self, low):
        self.x1 = self.q * self.toward(low)
        self.o1 = 1.0 - self.z1 - self.x1

    def rim(self):
        return self.tz * self.zm + self.tzp * self.zp

    def along_y(self, v):
        return self.ty * self.ln.ym(v) + self.typ * self.ln.yp(v)


def middle(p, below, above, mz):
    ln = p.ln
    vz = p.half * p.z1 + p.tx * below.z1 + p.txn * above.z1 + p.along_y(p.z1)
    vz = vz + p.tz * jnp.where(ln.first, 1.0 - p.zm, p.zm)
    vz = vz + p.tzp * jnp.where(ln.last, 1.0 - p.zp, p.zp)
    kept = vz * mz
    return p.all - vz, kept, p.all - (vz - kept)


def second(p, edge, inner, low, mz, mx):
    below, above = (edge, inner) if low else (inner, edge)
    ln = p.ln
    first_o = ln.zm(p.z1)
    vz = p.half * p.z1 + p.tx * below.z1 + p.txn * above.z1 + p.along_y(p.z1)
    vz = vz + p.tz * jnp.where(ln.first, 1.0 - first_o, first_o)
    vz = vz + p.tzp * jnp.where(ln.last, 1.0 - p.zp, p.zp)
    vx = p.toward(low) * edge.x1
    kept_z, kept_x = vz * mz, vx * mx
    total = p.all - (vz - kept_z) - (vx - kept_x)
    return p.all - vz - vx, kept_z, kept_x, total


def edge_own(p, inner_o1, inner_z1, outer_x1, low, mz):
    ln = p.ln
    om, op = ln.zm(p.o1), ln.zp(p.o1)
    vo = p.half * p.o1 + p.toward(low) * outer_x1 + p.inward(low) * inner_o1 + p.along_y(p.o1)
    vo = vo + p.tz * jnp.where(ln.first, p.zm, om) + p.tzp * jnp.where(ln.last, p.zp, op)
    vz = p.half * p.z1 + p.inward(low) * inner_z1 + p.along_y(p.z1)
    vz = vz + p.tz * jnp.where(ln.first, om, p.zm) + p.tzp * jnp.where(ln.last, op, p.zp)
    return vo, vz * mz


def edge_total(p, mz):
    rim = p.rim()
    return p.all - (rim - rim * mz)


def edge_spill(p, own, low):
    ln = p.ln
    xm, xp = ln.zm(p.x1), ln.zp(p.x1)
    face = p.toward(low)
    vx = p.half * p.x1 + face * own.o1 + p.along_y(p.x1)
    vx = vx + p.tz * jnp.where(ln.first, 0.0, xm) + p.tzp * jnp.where(ln.last, 0.0, xp)
    vd = face * own.z1 + p.tz * jnp.where(ln.first, xm, 0.0) + p.tzp * jnp.where(ln.last, xp, 0.0)
    return vx, vd


def second_spill(p, edge, low, mz, mx):
    vx = p.toward(low) * edge.x1
    kept = vx * mx
    return kept, edge_total(p, mz) - (vx - kept)


def store(ln, dst, layer, plane, blocks, own, other, total):
    scale = 1.0 / total
    own = own * scale
    other = jnp.zeros_like(own) if other is None else other * scale
    for k in range(blocks):
        dst[layer, k, plane] = jnp.where(ln.block == k, own, jnp.where(ln.other == k, other, 0.0))


def pack_kernel(n, width, tx, ty, tz, s, reach, up, down, masks, own_masks, sems):
    copies = []

    def copy(src, dst):
        c = pltpu.make_async_copy(src, dst, sems.at[len(copies)])
        c.start()
        copies.append(c)

    copy(tx.at[pl.ds(0, 3)], down.at[pl.ds(0, 3)])
    for i, a in enumerate((ty, tz, s)):
        copy(a.at[pl.ds(0, 2)], down.at[pl.ds(3 + 2 * i, 2)])
    for i, a in enumerate((tx, ty, tz, s)):
        copy(a.at[pl.ds(n - 2, 2)], up.at[pl.ds(2 * i, 2)])
    layers, blocks, _ = reach.shape
    lanes = masks.shape[-1]
    shape = (blocks, lanes)
    k = lax.broadcasted_iota(jnp.int32, shape, 0)
    lane = lax.broadcasted_iota(jnp.int32, shape, 1)
    block = lane // width
    local = lane - block * width
    zero = jnp.zeros((1, lanes), jnp.float32)

    def row(cond):
        return jnp.sum(jnp.where(cond, 1.0, 0.0), axis=0, keepdims=True)

    for layer in range(layers):
        r = [jnp.broadcast_to(reach[layer, :, j : j + 1], shape) for j in range(4)]
        from_below = (block - 1 == k) & (local < width // 2) & (r[3] >= local + 1)
        from_above = (block + 1 == k) & (local >= width // 2) & (r[2] >= width - local)
        rows = [
            row(from_below | from_above),
            row((block == k) & (r[0] >= 2)),
            row((block == k) & (r[1] >= 2)),
        ]
        own_masks[layer] = jnp.concatenate(rows + [zero] * (TAIL - len(rows)), axis=0)
    copy(own_masks, masks)
    copy(own_masks.at[0], down.at[9, pl.ds(0, TAIL)])
    copy(own_masks.at[layers - 1], up.at[8, pl.ds(0, TAIL)])
    for c in copies:
        c.wait()


def bulk_kernel(width, blocks, tx, ty, tz, s, masks, out, zeros, buf, faces, sems):
    layers = masks.shape[0]
    n, rows, lanes = faces.shape[1:]
    fetch = [pltpu.make_async_copy(a, faces.at[i], sems.at[i]) for i, a in enumerate((tx, ty, tz, s))]
    for c in fetch:
        c.start()
    zeros[...] = jnp.zeros(zeros.shape, jnp.float32)
    depth = zeros.shape[0]
    clears = []
    for layer in range(layers):
        for k in range(blocks):
            for start in (0, 3 * width - depth):
                sem = sems.at[4 + len(clears)]
                c = pltpu.make_async_copy(zeros, out.at[layer, k, pl.ds(start, depth)], sem)
                c.start()
                clears.append(c)
    ln = Lanes((rows, lanes), width)
    for c in fetch:
        c.wait()

    def plane(p):
        return Plane(ln, faces[0, p], faces[0, p + 1], faces[1, p], faces[2, p], faces[3, p])

    sends = []
    for layer in range(layers):
        base = layer * width
        mz = masks[layer, 0:1]
        low, high = layer == 0, layer == layers - 1
        origin = base - width
        if not low:
            ma = masks[layer - 1, 0:1]
            to_above, to_below = masks[layer - 1, 2:3], masks[layer, 1:2]
            a3, a2, a1 = (plane(base - i) for i in (3, 2, 1))
            b0, b1, b2 = (plane(base + i) for i in (0, 1, 2))
            a1.edge(False)
            b0.edge(True)
            prev = origin - width
            put = functools.partial(store, ln, buf)
            vo, vz, vx, total = second(a2, a1, a3, False, ma, to_below)
            put(layer - 1, base - 2 - prev - (width - 2), blocks, vo, vz, total)
            put(layer, base - 2 - origin - (width - 2), blocks, vx, None, total)
            vo, vz = edge_own(a1, 1.0 - a2.z1, a2.z1, b0.x1, False, ma)
            vx, vd = edge_spill(a1, b0, False)
            total = edge_total(a1, ma)
            put(layer - 1, base - 1 - prev - (width - 2), blocks, vo, vz, total)
            put(layer, base - 1 - origin - (width - 2), blocks, vx, vd, total)
            vo, vz = edge_own(b0, 1.0 - b1.z1, b1.z1, a1.x1, True, mz)
            vx, vd = edge_spill(b0, a1, True)
            total = edge_total(b0, mz)
            put(layer, base - origin - (width - 2), blocks, vo, vz, total)
            put(layer - 1, base - prev - (width - 2), blocks, vx, vd, total)
            vo, vz, vx, total = second(b1, b0, b2, True, mz, to_above)
            put(layer, base + 1 - origin - (width - 2), blocks, vo, vz, total)
            put(layer - 1, base + 1 - prev - (width - 2), blocks, vx, None, total)
            sends.append(send_layer(layer - 1, layers, width, blocks, buf, out, sems))
        planes = [plane(base + a) for a in range(1, width - 1)]
        for a in range(2, width - 2):
            vo, vz, total = middle(planes[a - 1], planes[a - 2], planes[a], mz)
            store(ln, buf, layer, a + 2, blocks, vo, vz, total)
        if high:
            sends.append(send_layer(layer, layers, width, blocks, buf, out, sems))
    for group in sends:
        for c in group:
            c.wait()
    for c in clears:
        c.wait()


def span(layer, layers, width):
    return (4 if layer == 0 else 0), (width if layer == layers - 1 else width + 4)


def send_layer(layer, layers, width, blocks, buf, out, sems):
    low, high = span(layer, layers, width)
    group = []
    for k in range(blocks):
        c = pltpu.make_async_copy(
            buf.at[layer, k, pl.ds(low, high - low)],
            out.at[layer, k, pl.ds(width - 2 + low, high - low)],
            sems.at[4 + 2 * layers * blocks + layer * blocks + k],
        )
        c.start()
        group.append(c)
    return group


def edge_kernel(
    n, width, blocks, axis, count, tx, ty, tz, s, masks, below, above, held, out,
    lo, hi, lob, hib, buf, sems,
):
    del held
    layers = masks.shape[0]
    copies = []

    def copy(src, dst):
        c = pltpu.make_async_copy(src, dst, sems.at[len(copies)])
        c.start()
        copies.append(c)

    copy(below, lob)
    copy(above, hib)
    for i, a in enumerate((tx, ty, tz, s)):
        copy(a.at[pl.ds(0, 4)], lo.at[i])
        copy(a.at[pl.ds(n - 4, 4)], hi.at[i])
    me = lax.axis_index(axis)
    for c in copies:
        c.wait()
    rows, lanes = lo.shape[2:]
    ln = Lanes((rows, lanes), width)
    put = functools.partial(store, ln, buf)
    low_ok, high_ok = me > 0, me < count - 1

    tx0 = jnp.where(low_ok, lo[0, 0], 0.0)
    a2 = Plane(ln, lob[0], lob[1], lob[2], lob[4], lob[6], low_ok)
    a1 = Plane(ln, lob[1], tx0, lob[3], lob[5], lob[7], low_ok)
    ma, to_above = lob[8, 0:1], lob[8, 2:3]
    mz, to_below = masks[0, 0:1], masks[0, 1:2]
    b0 = Plane(ln, tx0, lo[0, 1], lo[1, 0], lo[2, 0], lo[3, 0])
    b1, b2 = (Plane(ln, lo[0, i], lo[0, i + 1], lo[1, i], lo[2, i], lo[3, i]) for i in (1, 2))
    a1.edge(False)
    b0.edge(True)
    vx, total = second_spill(a2, a1, False, ma, to_below)
    put(0, 0, blocks, vx, None, total)
    vx, vd = edge_spill(a1, b0, False)
    put(0, 1, blocks, vx, vd, edge_total(a1, ma))
    vo, vz = edge_own(b0, 1.0 - b1.z1, b1.z1, a1.x1, True, mz)
    put(0, 2, blocks, vo, vz, edge_total(b0, mz))
    vo, vz, _, total = second(b1, b0, b2, True, mz, to_above)
    put(0, 3, blocks, vo, vz, total)
    sends = []

    def send(side, layer, start):
        for k in range(blocks):
            c = pltpu.make_async_copy(
                buf.at[side, k], out.at[layer, k, pl.ds(start, 4)], sems.at[len(copies) + len(sends)]
            )
            c.start()
            sends.append(c)

    send(0, 0, width - 2)

    mz, to_above = masks[layers - 1, 0:1], masks[layers - 1, 2:3]
    mb, to_below = hib[9, 0:1], hib[9, 1:2]
    a3, a2 = (Plane(ln, hi[0, i], hi[0, i + 1], hi[1, i], hi[2, i], hi[3, i]) for i in (1, 2))
    a1 = Plane(ln, hi[0, 3], hib[0], hi[1, 3], hi[2, 3], hi[3, 3])
    b0 = Plane(ln, hib[0], hib[1], hib[3], hib[5], hib[7], high_ok)
    b1 = Plane(ln, hib[1], hib[2], hib[4], hib[6], hib[8], high_ok)
    a1.edge(False)
    b0.edge(True)
    vo, vz, _, total = second(a2, a1, a3, False, mz, to_below)
    put(1, 0, blocks, vo, vz, total)
    vo, vz = edge_own(a1, 1.0 - a2.z1, a2.z1, b0.x1, False, mz)
    put(1, 1, blocks, vo, vz, edge_total(a1, mz))
    vx, vd = edge_spill(b0, a1, True)
    put(1, 2, blocks, vx, vd, edge_total(b0, mb))
    vx, total = second_spill(b1, b0, True, mb, to_above)
    put(1, 3, blocks, vx, None, total)
    send(1, layers - 1, 2 * width - 2)
    for c in sends:
        c.wait()


def on_device(trans_east, trans_north, trans_up, storage, support_reach, *, axis, count):
    layers, blocks, _ = support_reach.shape
    n, rows, lanes = trans_east.shape
    width = n // layers
    f32 = jnp.float32
    anywhere = pl.BlockSpec(memory_space=pl.ANY)
    vmem = pl.BlockSpec(memory_space=pltpu.VMEM)
    params = pltpu.CompilerParams(vmem_limit_bytes=16 * 2**20)
    faces = (trans_east, trans_north, trans_up, storage)

    up, down, masks = pl.pallas_call(
        functools.partial(pack_kernel, n, width),
        out_shape=(
            jax.ShapeDtypeStruct((9, rows, lanes), f32),
            jax.ShapeDtypeStruct((10, rows, lanes), f32),
            jax.ShapeDtypeStruct((layers, TAIL, lanes), f32),
        ),
        in_specs=[anywhere] * 4 + [vmem],
        out_specs=(anywhere,) * 3,
        scratch_shapes=[pltpu.VMEM((layers, TAIL, lanes), f32), pltpu.SemaphoreType.DMA((11,))],
        compiler_params=params,
        name="pack",
    )(*faces, support_reach)
    below = lax.ppermute(up, axis, [(i, i + 1) for i in range(count - 1)])
    above = lax.ppermute(down, axis, [(i + 1, i) for i in range(count - 1)])

    out_shape = jax.ShapeDtypeStruct((layers, blocks, 3 * width, rows, lanes), f32)
    bulk = pl.pallas_call(
        functools.partial(bulk_kernel, width, blocks),
        out_shape=out_shape,
        in_specs=[anywhere] * 4 + [vmem],
        out_specs=anywhere,
        scratch_shapes=[
            pltpu.VMEM((width - 2, rows, lanes), f32),
            pltpu.VMEM((layers, blocks, width + 4, rows, lanes), f32),
            pltpu.VMEM((4, n, rows, lanes), f32),
            pltpu.SemaphoreType.DMA((4 + 3 * layers * blocks,)),
        ],
        compiler_params=params,
        cost_estimate=pl.CostEstimate(flops=10**7, bytes_accessed=7 * 10**6, transcendentals=0),
        name="bulk",
    )(*faces, masks)
    return pl.pallas_call(
        functools.partial(edge_kernel, n, width, blocks, axis, count),
        out_shape=out_shape,
        in_specs=[anywhere] * 4 + [vmem] + [anywhere] * 3,
        out_specs=anywhere,
        scratch_shapes=[
            pltpu.VMEM((4, 4, rows, lanes), f32),
            pltpu.VMEM((4, 4, rows, lanes), f32),
            pltpu.VMEM((9, rows, lanes), f32),
            pltpu.VMEM((10, rows, lanes), f32),
            pltpu.VMEM((2, blocks, 4, rows, lanes), f32),
            pltpu.SemaphoreType.DMA((10 + 2 * blocks,)),
        ],
        input_output_aliases={7: 0},
        compiler_params=params,
        cost_estimate=pl.CostEstimate(flops=10**6, bytes_accessed=10**6, transcendentals=0),
        name="edges",
    )(*faces, masks, below, above, bulk)


def solution(mesh):
    spread = P(("groups", "blk"))
    return jax.shard_map(
        functools.partial(on_device, axis="blk", count=mesh.shape["blk"]),
        mesh=mesh,
        in_specs=(spread,) * 5,
        out_specs=spread,
        check_vma=False,
    )
```

```python
import functools

import jax
import jax.numpy as jnp
from jax import lax
from jax.experimental import pallas as pl
from jax.experimental.pallas import tpu as pltpu
from jax.sharding import PartitionSpec as P


TAIL = 8


class Lanes:
    def __init__(self, shape, width):
        lane = lax.broadcasted_iota(jnp.int32, shape, 1)
        self.width = width
        self.lanes = shape[1]
        self.rows = shape[0]
        self.lane = lane
        self.block = lane // width
        self.local = lane - self.block * width
        self.first = self.local == 0
        self.last = self.local == width - 1
        self.upper = self.local >= width // 2
        self.other = jnp.where(self.upper, self.block + 1, self.block - 1)
        self.row0 = lax.broadcasted_iota(jnp.int32, shape, 0) == 0
        self.lane0 = lane == 0

    def zm(self, v):
        return pltpu.roll(v, 1, 1)

    def zp(self, v):
        return pltpu.roll(v, self.lanes - 1, 1)

    def ym(self, v):
        return pltpu.roll(v, 1, 0)

    def yp(self, v):
        return pltpu.roll(v, self.rows - 1, 0)


class Plane:
    def __init__(self, ln, tx, txn, ty, tz, s, valid=None):
        self.ln = ln
        self.tx, self.txn = tx, txn
        self.ty = jnp.where(ln.row0, 0.0, ty)
        self.tz = jnp.where(ln.lane0, 0.0, tz)
        self.typ = ln.yp(self.ty)
        self.tzp = ln.zp(self.tz)
        e = s * (1.0 / 3.0) + ((tx + txn) + (self.ty + self.typ) + (self.tz + self.tzp))
        if valid is not None:
            e = jnp.where(valid, e, 1.0)
        self.half = 0.5 * e + s * (1.0 / 3.0)
        self.all = 1.5 * e
        self.q = 1.0 / self.all
        self.z1 = self.q * jnp.where(ln.first, self.tz, jnp.where(ln.last, self.tzp, 0.0))
        self.zm = ln.zm(self.z1)
        self.zp = ln.zp(self.z1)

    def toward(self, low):
        return self.tx if low else self.txn

    def inward(self, low):
        return self.txn if low else self.tx

    def edge(self, low):
        self.x1 = self.q * self.toward(low)
        self.o1 = 1.0 - self.z1 - self.x1

    def rim(self):
        return self.tz * self.zm + self.tzp * self.zp

    def along_y(self, v):
        return self.ty * self.ln.ym(v) + self.typ * self.ln.yp(v)


def middle(p, below, above, mz):
    ln = p.ln
    vz = p.half * p.z1 + p.tx * below.z1 + p.txn * above.z1 + p.along_y(p.z1)
    vz = vz + p.tz * jnp.where(ln.first, 1.0 - p.zm, p.zm)
    vz = vz + p.tzp * jnp.where(ln.last, 1.0 - p.zp, p.zp)
    kept = vz * mz
    return p.all - vz, kept, p.all - (vz - kept)


def second(p, edge, inner, low, mz, mx):
    below, above = (edge, inner) if low else (inner, edge)
    ln = p.ln
    first_o = ln.zm(p.z1)
    vz = p.half * p.z1 + p.tx * below.z1 + p.txn * above.z1 + p.along_y(p.z1)
    vz = vz + p.tz * jnp.where(ln.first, 1.0 - first_o, first_o)
    vz = vz + p.tzp * jnp.where(ln.last, 1.0 - p.zp, p.zp)
    vx = p.toward(low) * edge.x1
    kept_z, kept_x = vz * mz, vx * mx
    total = p.all - (vz - kept_z) - (vx - kept_x)
    return p.all - vz - vx, kept_z, kept_x, total


def edge_own(p, inner_o1, inner_z1, outer_x1, low, mz):
    ln = p.ln
    om, op = ln.zm(p.o1), ln.zp(p.o1)
    vo = p.half * p.o1 + p.toward(low) * outer_x1 + p.inward(low) * inner_o1 + p.along_y(p.o1)
    vo = vo + p.tz * jnp.where(ln.first, p.zm, om) + p.tzp * jnp.where(ln.last, p.zp, op)
    vz = p.half * p.z1 + p.inward(low) * inner_z1 + p.along_y(p.z1)
    vz = vz + p.tz * jnp.where(ln.first, om, p.zm) + p.tzp * jnp.where(ln.last, op, p.zp)
    return vo, vz * mz


def edge_total(p, mz):
    rim = p.rim()
    return p.all - (rim - rim * mz)


def edge_spill(p, own, low):
    ln = p.ln
    xm, xp = ln.zm(p.x1), ln.zp(p.x1)
    face = p.toward(low)
    vx = p.half * p.x1 + face * own.o1 + p.along_y(p.x1)
    vx = vx + p.tz * jnp.where(ln.first, 0.0, xm) + p.tzp * jnp.where(ln.last, 0.0, xp)
    vd = face * own.z1 + p.tz * jnp.where(ln.first, xm, 0.0) + p.tzp * jnp.where(ln.last, xp, 0.0)
    return vx, vd


def second_spill(p, edge, low, mz, mx):
    vx = p.toward(low) * edge.x1
    kept = vx * mx
    return kept, edge_total(p, mz) - (vx - kept)


def store(ln, dst, layer, plane, blocks, own, other, total):
    scale = 1.0 / total
    own = own * scale
    other = jnp.zeros_like(own) if other is None else other * scale
    for k in range(blocks):
        dst[layer, k, plane] = jnp.where(ln.block == k, own, jnp.where(ln.other == k, other, 0.0))


def pack_kernel(
    n, width, axis, tx, ty, tz, s, reach, msg_a, msg_b, masks, mine, own_masks, held_reach, sems
):
    layers, _, blocks = held_reach.shape
    lanes = masks.shape[-1]
    even = lax.rem(lax.axis_index(axis), 2) == 0

    def planes(down, up):
        pairs = [(tx.at[pl.ds(0, 3)], down.at[pl.ds(0, 3)])]
        for i, a in enumerate((ty, tz, s)):
            pairs.append((a.at[pl.ds(0, 2)], down.at[pl.ds(3 + 2 * i, 2)]))
        for i, a in enumerate((tx, ty, tz, s)):
            pairs.append((a.at[pl.ds(n - 2, 2)], up.at[pl.ds(2 * i, 2)]))
        return [pltpu.make_async_copy(src, dst, sems.at[i]) for i, (src, dst) in enumerate(pairs)]

    def tails(down, up):
        pairs = [
            (own_masks.at[0], down.at[9, pl.ds(0, TAIL)]),
            (own_masks.at[layers - 1], up.at[8, pl.ds(0, TAIL)]),
        ]
        return [pltpu.make_async_copy(src, dst, sems.at[8 + i]) for i, (src, dst) in enumerate(pairs)]

    fetch = pltpu.make_async_copy(reach, held_reach, sems.at[10])
    fetch.start()

    @pl.when(even)
    def _():
        for c in planes(msg_b, msg_a):
            c.start()

    @pl.when(jnp.logical_not(even))
    def _():
        for c in planes(msg_a, msg_b):
            c.start()

    keeps = []
    for i, a in enumerate((tx, ty, tz, s)):
        keeps.append((a.at[pl.ds(0, 4)], mine.at[0, i]))
        keeps.append((a.at[pl.ds(n - 4, 4)], mine.at[1, i]))
    keeps = [pltpu.make_async_copy(src, dst, sems.at[12 + i]) for i, (src, dst) in enumerate(keeps)]
    for c in keeps:
        c.start()
    own_masks[...] = jnp.zeros(own_masks.shape, jnp.float32)
    lane = lax.broadcasted_iota(jnp.int32, (4, lanes), 1)
    block = lane // width
    local = lane - block * width
    fetch.wait()
    for layer in range(layers):
        r = jnp.zeros((4, lanes), jnp.int32)
        for k in range(blocks):
            r = jnp.where(block == k, held_reach[layer, :, k : k + 1], r)
        low = pltpu.roll(r, width, 1)
        high = pltpu.roll(r, lanes - width, 1)
        near = jnp.where(
            local[0:1] < width // 2,
            jnp.where(low[3:4] >= local[0:1] + 1, 1.0, 0.0),
            jnp.where(high[2:3] >= width - local[0:1], 1.0, 0.0),
        )
        own_masks[layer, 0:1] = near
        own_masks[layer, 1:3] = jnp.where(r[0:2] >= 2, 1.0, 0.0)
    keeps.append(pltpu.make_async_copy(own_masks, masks, sems.at[11]))
    keeps[-1].start()

    @pl.when(even)
    def _():
        last = tails(msg_b, msg_a)
        for c in last:
            c.start()
        for c in planes(msg_b, msg_a) + last:
            c.wait()

    @pl.when(jnp.logical_not(even))
    def _():
        last = tails(msg_a, msg_b)
        for c in last:
            c.start()
        for c in planes(msg_a, msg_b) + last:
            c.wait()

    for c in keeps:
        c.wait()


def bulk_kernel(width, blocks, tx, ty, tz, s, masks, out, zeros, buf, faces, sems):
    layers = masks.shape[0]
    n, rows, lanes = faces.shape[1:]
    fetch = [pltpu.make_async_copy(a, faces.at[i], sems.at[i]) for i, a in enumerate((tx, ty, tz, s))]
    for c in fetch:
        c.start()
    zeros[...] = jnp.zeros(zeros.shape, jnp.float32)
    depth = zeros.shape[0]
    clears = []
    for layer in range(layers):
        for k in range(blocks):
            for start in (0, 3 * width - depth):
                sem = sems.at[4 + len(clears)]
                c = pltpu.make_async_copy(zeros, out.at[layer, k, pl.ds(start, depth)], sem)
                c.start()
                clears.append(c)
    ln = Lanes((rows, lanes), width)
    for c in fetch:
        c.wait()

    def plane(p):
        return Plane(ln, faces[0, p], faces[0, p + 1], faces[1, p], faces[2, p], faces[3, p])

    sends = []
    for layer in range(layers):
        base = layer * width
        mz = masks[layer, 0:1]
        low, high = layer == 0, layer == layers - 1
        origin = base - width
        if not low:
            ma = masks[layer - 1, 0:1]
            to_above, to_below = masks[layer - 1, 2:3], masks[layer, 1:2]
            a3, a2, a1 = (plane(base - i) for i in (3, 2, 1))
            b0, b1, b2 = (plane(base + i) for i in (0, 1, 2))
            a1.edge(False)
            b0.edge(True)
            prev = origin - width
            put = functools.partial(store, ln, buf)
            vo, vz, vx, total = second(a2, a1, a3, False, ma, to_below)
            put(layer - 1, base - 2 - prev - (width - 2), blocks, vo, vz, total)
            put(layer, base - 2 - origin - (width - 2), blocks, vx, None, total)
            vo, vz = edge_own(a1, 1.0 - a2.z1, a2.z1, b0.x1, False, ma)
            vx, vd = edge_spill(a1, b0, False)
            total = edge_total(a1, ma)
            put(layer - 1, base - 1 - prev - (width - 2), blocks, vo, vz, total)
            put(layer, base - 1 - origin - (width - 2), blocks, vx, vd, total)
            vo, vz = edge_own(b0, 1.0 - b1.z1, b1.z1, a1.x1, True, mz)
            vx, vd = edge_spill(b0, a1, True)
            total = edge_total(b0, mz)
            put(layer, base - origin - (width - 2), blocks, vo, vz, total)
            put(layer - 1, base - prev - (width - 2), blocks, vx, vd, total)
            vo, vz, vx, total = second(b1, b0, b2, True, mz, to_above)
            put(layer, base + 1 - origin - (width - 2), blocks, vo, vz, total)
            put(layer - 1, base + 1 - prev - (width - 2), blocks, vx, None, total)
            sends.append(send_layer(layer - 1, layers, width, blocks, buf, out, sems))
        planes = [plane(base + a) for a in range(1, width - 1)]
        for a in range(2, width - 2):
            vo, vz, total = middle(planes[a - 1], planes[a - 2], planes[a], mz)
            store(ln, buf, layer, a + 2, blocks, vo, vz, total)
        if high:
            sends.append(send_layer(layer, layers, width, blocks, buf, out, sems))
    for group in sends:
        for c in group:
            c.wait()
    for c in clears:
        c.wait()


def span(layer, layers, width):
    return (4 if layer == 0 else 0), (width if layer == layers - 1 else width + 4)


def send_layer(layer, layers, width, blocks, buf, out, sems):
    low, high = span(layer, layers, width)
    group = []
    for k in range(blocks):
        c = pltpu.make_async_copy(
            buf.at[layer, k, pl.ds(low, high - low)],
            out.at[layer, k, pl.ds(width - 2 + low, high - low)],
            sems.at[4 + 2 * layers * blocks + layer * blocks + k],
        )
        c.start()
        group.append(c)
    return group


def edge_kernel(
    width, blocks, axis, count, masks, mine, got_a, got_b, held, out, buf, sems
):
    del held
    layers = masks.shape[0]
    me = lax.axis_index(axis)
    even = lax.rem(me, 2) == 0
    lo, hi = mine.at[0], mine.at[1]

    class Got:
        def __init__(self, at_even, at_odd):
            self.at_even, self.at_odd = at_even, at_odd

        def __getitem__(self, where):
            return jnp.where(even, self.at_even[where], self.at_odd[where])

    lob, hib = Got(got_b, got_a), Got(got_a, got_b)
    rows, lanes = lo.shape[2:]
    ln = Lanes((rows, lanes), width)
    put = functools.partial(store, ln, buf)
    low_ok, high_ok = me > 0, me < count - 1

    tx0 = jnp.where(low_ok, lo[0, 0], 0.0)
    a2 = Plane(ln, lob[0], lob[1], lob[2], lob[4], lob[6], low_ok)
    a1 = Plane(ln, lob[1], tx0, lob[3], lob[5], lob[7], low_ok)
    ma, to_above = lob[8, 0:1], lob[8, 2:3]
    mz, to_below = masks[0, 0:1], masks[0, 1:2]
    b0 = Plane(ln, tx0, lo[0, 1], lo[1, 0], lo[2, 0], lo[3, 0])
    b1, b2 = (Plane(ln, lo[0, i], lo[0, i + 1], lo[1, i], lo[2, i], lo[3, i]) for i in (1, 2))
    a1.edge(False)
    b0.edge(True)
    vx, total = second_spill(a2, a1, False, ma, to_below)
    put(0, 0, blocks, vx, None, total)
    vx, vd = edge_spill(a1, b0, False)
    put(0, 1, blocks, vx, vd, edge_total(a1, ma))
    vo, vz = edge_own(b0, 1.0 - b1.z1, b1.z1, a1.x1, True, mz)
    put(0, 2, blocks, vo, vz, edge_total(b0, mz))
    vo, vz, _, total = second(b1, b0, b2, True, mz, to_above)
    put(0, 3, blocks, vo, vz, total)
    sends = []

    def send(side, layer, start):
        for k in range(blocks):
            c = pltpu.make_async_copy(
                buf.at[side, k], out.at[layer, k, pl.ds(start, 4)], sems.at[len(sends)]
            )
            c.start()
            sends.append(c)

    send(0, 0, width - 2)

    mz, to_above = masks[layers - 1, 0:1], masks[layers - 1, 2:3]
    mb, to_below = hib[9, 0:1], hib[9, 1:2]
    a3, a2 = (Plane(ln, hi[0, i], hi[0, i + 1], hi[1, i], hi[2, i], hi[3, i]) for i in (1, 2))
    a1 = Plane(ln, hi[0, 3], hib[0], hi[1, 3], hi[2, 3], hi[3, 3])
    b0 = Plane(ln, hib[0], hib[1], hib[3], hib[5], hib[7], high_ok)
    b1 = Plane(ln, hib[1], hib[2], hib[4], hib[6], hib[8], high_ok)
    a1.edge(False)
    b0.edge(True)
    vo, vz, _, total = second(a2, a1, a3, False, mz, to_below)
    put(1, 0, blocks, vo, vz, total)
    vo, vz = edge_own(a1, 1.0 - a2.z1, a2.z1, b0.x1, False, mz)
    put(1, 1, blocks, vo, vz, edge_total(a1, mz))
    vx, vd = edge_spill(b0, a1, True)
    put(1, 2, blocks, vx, vd, edge_total(b0, mb))
    vx, total = second_spill(b1, b0, True, mb, to_above)
    put(1, 3, blocks, vx, None, total)
    send(1, layers - 1, 2 * width - 2)
    for c in sends:
        c.wait()


def swaps(firsts):
    return [pair for i in firsts for pair in ((i, i + 1), (i + 1, i))]


def on_device(trans_east, trans_north, trans_up, storage, support_reach, *, axis, count):
    layers, blocks, _ = support_reach.shape
    n, rows, lanes = trans_east.shape
    width = n // layers
    f32 = jnp.float32
    anywhere = pl.BlockSpec(memory_space=pl.ANY)
    vmem = pl.BlockSpec(memory_space=pltpu.VMEM)
    params = pltpu.CompilerParams(vmem_limit_bytes=16 * 2**20)
    faces = tuple(
        pltpu.with_memory_space_constraint(x, pltpu.HBM)
        for x in (trans_east, trans_north, trans_up, storage)
    )
    reach = jnp.transpose(support_reach, (0, 2, 1))
    reach = pltpu.with_memory_space_constraint(reach, pltpu.HBM)
    message = jax.ShapeDtypeStruct((10, rows, lanes), f32)
    msg_a, msg_b, masks, mine = pl.pallas_call(
        functools.partial(pack_kernel, n, width, axis),
        out_shape=(
            message,
            message,
            jax.ShapeDtypeStruct((layers, TAIL, lanes), f32),
            jax.ShapeDtypeStruct((2, 4, 4, rows, lanes), f32),
        ),
        in_specs=[anywhere] * 5,
        out_specs=(anywhere,) * 4,
        scratch_shapes=[
            pltpu.VMEM((layers, TAIL, lanes), f32),
            pltpu.VMEM((layers, 4, blocks), jnp.int32),
            pltpu.SemaphoreType.DMA((20,)),
        ],
        compiler_params=params,
        name="pack",
    )(*faces, reach)
    got_b = lax.ppermute(msg_b, axis, swaps(range(1, count - 1, 2)))
    got_a = lax.ppermute(msg_a, axis, swaps(range(0, count - 1, 2)))

    out_shape = jax.ShapeDtypeStruct((layers, blocks, 3 * width, rows, lanes), f32)
    bulk = pl.pallas_call(
        functools.partial(bulk_kernel, width, blocks),
        out_shape=out_shape,
        in_specs=[anywhere] * 4 + [vmem],
        out_specs=anywhere,
        scratch_shapes=[
            pltpu.VMEM((width - 2, rows, lanes), f32),
            pltpu.VMEM((layers, blocks, width + 4, rows, lanes), f32),
            pltpu.VMEM((4, n, rows, lanes), f32),
            pltpu.SemaphoreType.DMA((4 + 3 * layers * blocks,)),
        ],
        compiler_params=params,
        cost_estimate=pl.CostEstimate(flops=10**7, bytes_accessed=7 * 10**6, transcendentals=0),
        name="bulk",
    )(*faces, masks)
    return pl.pallas_call(
        functools.partial(edge_kernel, width, blocks, axis, count),
        out_shape=out_shape,
        in_specs=[vmem] * 4 + [anywhere],
        out_specs=anywhere,
        scratch_shapes=[
            pltpu.VMEM((2, blocks, 4, rows, lanes), f32),
            pltpu.SemaphoreType.DMA((2 * blocks,)),
        ],
        input_output_aliases={4: 0},
        compiler_params=params,
        cost_estimate=pl.CostEstimate(flops=10**6, bytes_accessed=10**6, transcendentals=0),
        name="edges",
    )(masks, mine, got_a, got_b, bulk)


def solution(mesh):
    spread = P(("groups", "blk"))
    return jax.shard_map(
        functools.partial(on_device, axis="blk", count=mesh.shape["blk"]),
        mesh=mesh,
        in_specs=(spread,) * 5,
        out_specs=spread,
        check_vma=False,
    )
```

```python
import functools

import jax
import jax.numpy as jnp
from jax import lax
from jax.experimental import pallas as pl
from jax.experimental.pallas import tpu as pltpu
from jax.sharding import PartitionSpec as P


TAIL = 8


class Lanes:
    def __init__(self, shape, width):
        lane = lax.broadcasted_iota(jnp.int32, shape, 1)
        self.width = width
        self.lanes = shape[1]
        self.rows = shape[0]
        self.lane = lane
        self.block = lane // width
        self.local = lane - self.block * width
        self.first = self.local == 0
        self.last = self.local == width - 1
        self.upper = self.local >= width // 2
        self.other = jnp.where(self.upper, self.block + 1, self.block - 1)
        self.row0 = lax.broadcasted_iota(jnp.int32, shape, 0) == 0
        self.lane0 = lane == 0

    def zm(self, v):
        return pltpu.roll(v, 1, 1)

    def zp(self, v):
        return pltpu.roll(v, self.lanes - 1, 1)

    def ym(self, v):
        return pltpu.roll(v, 1, 0)

    def yp(self, v):
        return pltpu.roll(v, self.rows - 1, 0)


class Plane:
    def __init__(self, ln, tx, txn, ty, tz, s, valid=None):
        self.ln = ln
        self.tx, self.txn = tx, txn
        self.ty = jnp.where(ln.row0, 0.0, ty)
        self.tz = jnp.where(ln.lane0, 0.0, tz)
        self.typ = ln.yp(self.ty)
        self.tzp = ln.zp(self.tz)
        e = s * (1.0 / 3.0) + ((tx + txn) + (self.ty + self.typ) + (self.tz + self.tzp))
        if valid is not None:
            e = jnp.where(valid, e, 1.0)
        self.half = 0.5 * e + s * (1.0 / 3.0)
        self.all = 1.5 * e
        self.q = 1.0 / self.all
        self.z1 = self.q * jnp.where(ln.first, self.tz, jnp.where(ln.last, self.tzp, 0.0))
        self.zm = ln.zm(self.z1)
        self.zp = ln.zp(self.z1)

    def toward(self, low):
        return self.tx if low else self.txn

    def inward(self, low):
        return self.txn if low else self.tx

    def edge(self, low):
        self.x1 = self.q * self.toward(low)
        self.o1 = 1.0 - self.z1 - self.x1

    def rim(self):
        return self.tz * self.zm + self.tzp * self.zp

    def along_y(self, v):
        return self.ty * self.ln.ym(v) + self.typ * self.ln.yp(v)


def middle(p, below, above, mz):
    ln = p.ln
    vz = p.half * p.z1 + p.tx * below.z1 + p.txn * above.z1 + p.along_y(p.z1)
    vz = vz + p.tz * jnp.where(ln.first, 1.0 - p.zm, p.zm)
    vz = vz + p.tzp * jnp.where(ln.last, 1.0 - p.zp, p.zp)
    kept = vz * mz
    return p.all - vz, kept, p.all - (vz - kept)


def second(p, edge, inner, low, mz, mx):
    below, above = (edge, inner) if low else (inner, edge)
    ln = p.ln
    first_o = ln.zm(p.z1)
    vz = p.half * p.z1 + p.tx * below.z1 + p.txn * above.z1 + p.along_y(p.z1)
    vz = vz + p.tz * jnp.where(ln.first, 1.0 - first_o, first_o)
    vz = vz + p.tzp * jnp.where(ln.last, 1.0 - p.zp, p.zp)
    vx = p.toward(low) * edge.x1
    kept_z, kept_x = vz * mz, vx * mx
    total = p.all - (vz - kept_z) - (vx - kept_x)
    return p.all - vz - vx, kept_z, kept_x, total


def edge_own(p, inner_o1, inner_z1, outer_x1, low, mz):
    ln = p.ln
    om, op = ln.zm(p.o1), ln.zp(p.o1)
    vo = p.half * p.o1 + p.toward(low) * outer_x1 + p.inward(low) * inner_o1 + p.along_y(p.o1)
    vo = vo + p.tz * jnp.where(ln.first, p.zm, om) + p.tzp * jnp.where(ln.last, p.zp, op)
    vz = p.half * p.z1 + p.inward(low) * inner_z1 + p.along_y(p.z1)
    vz = vz + p.tz * jnp.where(ln.first, om, p.zm) + p.tzp * jnp.where(ln.last, op, p.zp)
    return vo, vz * mz


def edge_total(p, mz):
    rim = p.rim()
    return p.all - (rim - rim * mz)


def edge_spill(p, own, low):
    ln = p.ln
    xm, xp = ln.zm(p.x1), ln.zp(p.x1)
    face = p.toward(low)
    vx = p.half * p.x1 + face * own.o1 + p.along_y(p.x1)
    vx = vx + p.tz * jnp.where(ln.first, 0.0, xm) + p.tzp * jnp.where(ln.last, 0.0, xp)
    vd = face * own.z1 + p.tz * jnp.where(ln.first, xm, 0.0) + p.tzp * jnp.where(ln.last, xp, 0.0)
    return vx, vd


def second_spill(p, edge, low, mz, mx):
    vx = p.toward(low) * edge.x1
    kept = vx * mx
    return kept, edge_total(p, mz) - (vx - kept)


def store(ln, dst, layer, plane, blocks, own, other, total):
    scale = 1.0 / total
    own = own * scale
    other = jnp.zeros_like(own) if other is None else other * scale
    for k in range(blocks):
        dst[layer, k, plane] = jnp.where(ln.block == k, own, jnp.where(ln.other == k, other, 0.0))


def pack_kernel(
    n, width, axis, tx, ty, tz, s, reach, msg_a, msg_b, masks, faces, held_reach, sems
):
    layers, _, blocks = held_reach.shape
    lanes = masks.shape[-1]
    even = lax.rem(lax.axis_index(axis), 2) == 0

    def planes(down, up):
        pairs = [(tx.at[pl.ds(0, 3)], down.at[pl.ds(0, 3)])]
        for i, a in enumerate((ty, tz, s)):
            pairs.append((a.at[pl.ds(0, 2)], down.at[pl.ds(3 + 2 * i, 2)]))
        for i, a in enumerate((tx, ty, tz, s)):
            pairs.append((a.at[pl.ds(n - 2, 2)], up.at[pl.ds(2 * i, 2)]))
        return [pltpu.make_async_copy(src, dst, sems.at[i]) for i, (src, dst) in enumerate(pairs)]

    fetch = pltpu.make_async_copy(reach, held_reach, sems.at[8])
    fetch.start()

    @pl.when(even)
    def _():
        for c in planes(msg_b, msg_a):
            c.start()

    @pl.when(jnp.logical_not(even))
    def _():
        for c in planes(msg_a, msg_b):
            c.start()

    keeps = [
        pltpu.make_async_copy(a, faces.at[i], sems.at[9 + i]) for i, a in enumerate((tx, ty, tz, s))
    ]
    for c in keeps:
        c.start()
    masks[...] = jnp.zeros(masks.shape, jnp.float32)
    lane = lax.broadcasted_iota(jnp.int32, (4, lanes), 1)
    block = lane // width
    local = lane - block * width
    fetch.wait()
    for layer in range(layers):
        r = jnp.zeros((4, lanes), jnp.int32)
        for k in range(blocks):
            r = jnp.where(block == k, held_reach[layer, :, k : k + 1], r)
        low = pltpu.roll(r, width, 1)
        high = pltpu.roll(r, lanes - width, 1)
        near = jnp.where(
            local[0:1] < width // 2,
            jnp.where(low[3:4] >= local[0:1] + 1, 1.0, 0.0),
            jnp.where(high[2:3] >= width - local[0:1], 1.0, 0.0),
        )
        masks[layer, 0:1] = near
        masks[layer, 1:3] = jnp.where(r[0:2] >= 2, 1.0, 0.0)

    def finish(down, up):
        down[9, 0:TAIL] = masks[0]
        up[8, 0:TAIL] = masks[layers - 1]
        for c in planes(down, up):
            c.wait()

    @pl.when(even)
    def _():
        finish(msg_b, msg_a)

    @pl.when(jnp.logical_not(even))
    def _():
        finish(msg_a, msg_b)

    for c in keeps:
        c.wait()


def bulk_kernel(width, blocks, faces, masks, out, zeros, buf, sems):
    layers = masks.shape[0]
    rows, lanes = faces.shape[2:]
    zeros[...] = jnp.zeros(zeros.shape, jnp.float32)
    depth = zeros.shape[0]
    clears = []
    for layer in range(layers):
        for k in range(blocks):
            for start in (0, 3 * width - depth):
                sem = sems.at[len(clears)]
                c = pltpu.make_async_copy(zeros, out.at[layer, k, pl.ds(start, depth)], sem)
                c.start()
                clears.append(c)
    ln = Lanes((rows, lanes), width)

    def plane(p):
        return Plane(ln, faces[0, p], faces[0, p + 1], faces[1, p], faces[2, p], faces[3, p])

    sends = []
    for layer in range(layers):
        base = layer * width
        mz = masks[layer, 0:1]
        low, high = layer == 0, layer == layers - 1
        origin = base - width
        if not low:
            ma = masks[layer - 1, 0:1]
            to_above, to_below = masks[layer - 1, 2:3], masks[layer, 1:2]
            a3, a2, a1 = (plane(base - i) for i in (3, 2, 1))
            b0, b1, b2 = (plane(base + i) for i in (0, 1, 2))
            a1.edge(False)
            b0.edge(True)
            prev = origin - width
            put = functools.partial(store, ln, buf)
            vo, vz, vx, total = second(a2, a1, a3, False, ma, to_below)
            put(layer - 1, base - 2 - prev - (width - 2), blocks, vo, vz, total)
            put(layer, base - 2 - origin - (width - 2), blocks, vx, None, total)
            vo, vz = edge_own(a1, 1.0 - a2.z1, a2.z1, b0.x1, False, ma)
            vx, vd = edge_spill(a1, b0, False)
            total = edge_total(a1, ma)
            put(layer - 1, base - 1 - prev - (width - 2), blocks, vo, vz, total)
            put(layer, base - 1 - origin - (width - 2), blocks, vx, vd, total)
            vo, vz = edge_own(b0, 1.0 - b1.z1, b1.z1, a1.x1, True, mz)
            vx, vd = edge_spill(b0, a1, True)
            total = edge_total(b0, mz)
            put(layer, base - origin - (width - 2), blocks, vo, vz, total)
            put(layer - 1, base - prev - (width - 2), blocks, vx, vd, total)
            vo, vz, vx, total = second(b1, b0, b2, True, mz, to_above)
            put(layer, base + 1 - origin - (width - 2), blocks, vo, vz, total)
            put(layer - 1, base + 1 - prev - (width - 2), blocks, vx, None, total)
            sends.append(send_layer(layer - 1, layers, width, blocks, buf, out, sems))
        planes = [plane(base + a) for a in range(1, width - 1)]
        for a in range(2, width - 2):
            vo, vz, total = middle(planes[a - 1], planes[a - 2], planes[a], mz)
            store(ln, buf, layer, a + 2, blocks, vo, vz, total)
        if high:
            sends.append(send_layer(layer, layers, width, blocks, buf, out, sems))
    for group in sends:
        for c in group:
            c.wait()
    for c in clears:
        c.wait()


def span(layer, layers, width):
    return (4 if layer == 0 else 0), (width if layer == layers - 1 else width + 4)


def send_layer(layer, layers, width, blocks, buf, out, sems):
    low, high = span(layer, layers, width)
    group = []
    for k in range(blocks):
        c = pltpu.make_async_copy(
            buf.at[layer, k, pl.ds(low, high - low)],
            out.at[layer, k, pl.ds(width - 2 + low, high - low)],
            sems.at[(2 * layers + layer) * blocks + k],
        )
        c.start()
        group.append(c)
    return group


def edge_kernel(
    width, blocks, axis, count, faces, masks, got_a, got_b, held, out, buf, sems
):
    del held
    layers = masks.shape[0]
    me = lax.axis_index(axis)
    even = lax.rem(me, 2) == 0
    n = faces.shape[1]
    lo, hi = faces, faces.at[:, pl.ds(n - 4, 4)]

    class Got:
        def __init__(self, at_even, at_odd):
            self.at_even, self.at_odd = at_even, at_odd

        def __getitem__(self, where):
            return jnp.where(even, self.at_even[where], self.at_odd[where])

    lob, hib = Got(got_b, got_a), Got(got_a, got_b)
    rows, lanes = lo.shape[2:]
    ln = Lanes((rows, lanes), width)
    put = functools.partial(store, ln, buf)
    low_ok, high_ok = me > 0, me < count - 1

    tx0 = jnp.where(low_ok, lo[0, 0], 0.0)
    a2 = Plane(ln, lob[0], lob[1], lob[2], lob[4], lob[6], low_ok)
    a1 = Plane(ln, lob[1], tx0, lob[3], lob[5], lob[7], low_ok)
    ma, to_above = lob[8, 0:1], lob[8, 2:3]
    mz, to_below = masks[0, 0:1], masks[0, 1:2]
    b0 = Plane(ln, tx0, lo[0, 1], lo[1, 0], lo[2, 0], lo[3, 0])
    b1, b2 = (Plane(ln, lo[0, i], lo[0, i + 1], lo[1, i], lo[2, i], lo[3, i]) for i in (1, 2))
    a1.edge(False)
    b0.edge(True)
    vx, total = second_spill(a2, a1, False, ma, to_below)
    put(0, 0, blocks, vx, None, total)
    vx, vd = edge_spill(a1, b0, False)
    put(0, 1, blocks, vx, vd, edge_total(a1, ma))
    vo, vz = edge_own(b0, 1.0 - b1.z1, b1.z1, a1.x1, True, mz)
    put(0, 2, blocks, vo, vz, edge_total(b0, mz))
    vo, vz, _, total = second(b1, b0, b2, True, mz, to_above)
    put(0, 3, blocks, vo, vz, total)
    sends = []

    def send(side, layer, start):
        for k in range(blocks):
            c = pltpu.make_async_copy(
                buf.at[side, k], out.at[layer, k, pl.ds(start, 4)], sems.at[len(sends)]
            )
            c.start()
            sends.append(c)

    send(0, 0, width - 2)

    mz, to_above = masks[layers - 1, 0:1], masks[layers - 1, 2:3]
    mb, to_below = hib[9, 0:1], hib[9, 1:2]
    a3, a2 = (Plane(ln, hi[0, i], hi[0, i + 1], hi[1, i], hi[2, i], hi[3, i]) for i in (1, 2))
    a1 = Plane(ln, hi[0, 3], hib[0], hi[1, 3], hi[2, 3], hi[3, 3])
    b0 = Plane(ln, hib[0], hib[1], hib[3], hib[5], hib[7], high_ok)
    b1 = Plane(ln, hib[1], hib[2], hib[4], hib[6], hib[8], high_ok)
    a1.edge(False)
    b0.edge(True)
    vo, vz, _, total = second(a2, a1, a3, False, mz, to_below)
    put(1, 0, blocks, vo, vz, total)
    vo, vz = edge_own(a1, 1.0 - a2.z1, a2.z1, b0.x1, False, mz)
    put(1, 1, blocks, vo, vz, edge_total(a1, mz))
    vx, vd = edge_spill(b0, a1, True)
    put(1, 2, blocks, vx, vd, edge_total(b0, mb))
    vx, total = second_spill(b1, b0, True, mb, to_above)
    put(1, 3, blocks, vx, None, total)
    send(1, layers - 1, 2 * width - 2)
    for c in sends:
        c.wait()


def swaps(firsts):
    return [pair for i in firsts for pair in ((i, i + 1), (i + 1, i))]


def on_device(trans_east, trans_north, trans_up, storage, support_reach, *, axis, count):
    layers, blocks, _ = support_reach.shape
    n, rows, lanes = trans_east.shape
    width = n // layers
    f32 = jnp.float32
    anywhere = pl.BlockSpec(memory_space=pl.ANY)
    vmem = pl.BlockSpec(memory_space=pltpu.VMEM)
    params = pltpu.CompilerParams(vmem_limit_bytes=16 * 2**20)
    outside = tuple(
        pltpu.with_memory_space_constraint(x, pltpu.HBM)
        for x in (trans_east, trans_north, trans_up, storage)
    )
    reach = jnp.transpose(support_reach, (0, 2, 1))
    reach = pltpu.with_memory_space_constraint(reach, pltpu.HBM)
    message = pltpu.VMEM((10, rows, lanes), f32)
    msg_a, msg_b, masks, faces = pl.pallas_call(
        functools.partial(pack_kernel, n, width, axis),
        out_shape=(
            message,
            message,
            pltpu.VMEM((layers, TAIL, lanes), f32),
            pltpu.VMEM((4, n, rows, lanes), f32),
        ),
        in_specs=[anywhere] * 5,
        out_specs=(vmem,) * 4,
        scratch_shapes=[
            pltpu.VMEM((layers, 4, blocks), jnp.int32),
            pltpu.SemaphoreType.DMA((13,)),
        ],
        compiler_params=params,
        name="pack",
    )(*outside, reach)
    got_b = lax.ppermute(msg_b, axis, swaps(range(1, count - 1, 2)))
    got_a = lax.ppermute(msg_a, axis, swaps(range(0, count - 1, 2)))

    out_shape = jax.ShapeDtypeStruct((layers, blocks, 3 * width, rows, lanes), f32)
    bulk = pl.pallas_call(
        functools.partial(bulk_kernel, width, blocks),
        out_shape=out_shape,
        in_specs=[vmem] * 2,
        out_specs=anywhere,
        scratch_shapes=[
            pltpu.VMEM((width - 2, rows, lanes), f32),
            pltpu.VMEM((layers, blocks, width + 4, rows, lanes), f32),
            pltpu.SemaphoreType.DMA((3 * layers * blocks,)),
        ],
        compiler_params=params,
        cost_estimate=pl.CostEstimate(flops=10**7, bytes_accessed=7 * 10**6, transcendentals=0),
        name="bulk",
    )(faces, masks)
    return pl.pallas_call(
        functools.partial(edge_kernel, width, blocks, axis, count),
        out_shape=out_shape,
        in_specs=[vmem] * 4 + [anywhere],
        out_specs=anywhere,
        scratch_shapes=[
            pltpu.VMEM((2, blocks, 4, rows, lanes), f32),
            pltpu.SemaphoreType.DMA((2 * blocks,)),
        ],
        input_output_aliases={4: 0},
        compiler_params=params,
        cost_estimate=pl.CostEstimate(flops=10**6, bytes_accessed=10**6, transcendentals=0),
        name="edges",
    )(faces, masks, got_a, got_b, bulk)


def solution(mesh):
    spread = P(("groups", "blk"))
    return jax.shard_map(
        functools.partial(on_device, axis="blk", count=mesh.shape["blk"]),
        mesh=mesh,
        in_specs=(spread,) * 5,
        out_specs=spread,
        check_vma=False,
    )
```

```python
import functools

import jax
import jax.numpy as jnp
from jax import lax
from jax.experimental import pallas as pl
from jax.experimental.pallas import tpu as pltpu
from jax.sharding import PartitionSpec as P


TAIL = 8


class Lanes:
    def __init__(self, shape, width):
        lane = lax.broadcasted_iota(jnp.int32, shape, 1)
        self.width = width
        self.lanes = shape[1]
        self.rows = shape[0]
        self.lane = lane
        self.block = lane // width
        self.local = lane - self.block * width
        self.first = self.local == 0
        self.last = self.local == width - 1
        self.upper = self.local >= width // 2
        self.other = jnp.where(self.upper, self.block + 1, self.block - 1)
        self.row0 = lax.broadcasted_iota(jnp.int32, shape, 0) == 0
        self.lane0 = lane == 0

    def zm(self, v):
        return pltpu.roll(v, 1, 1)

    def zp(self, v):
        return pltpu.roll(v, self.lanes - 1, 1)

    def ym(self, v):
        return pltpu.roll(v, 1, 0)

    def yp(self, v):
        return pltpu.roll(v, self.rows - 1, 0)


class Plane:
    def __init__(self, ln, tx, txn, ty, tz, s, valid=None):
        self.ln = ln
        self.tx, self.txn = tx, txn
        self.ty = jnp.where(ln.row0, 0.0, ty)
        self.tz = jnp.where(ln.lane0, 0.0, tz)
        self.typ = ln.yp(self.ty)
        self.tzp = ln.zp(self.tz)
        e = s * (1.0 / 3.0) + ((tx + txn) + (self.ty + self.typ) + (self.tz + self.tzp))
        if valid is not None:
            e = jnp.where(valid, e, 1.0)
        self.half = 0.5 * e + s * (1.0 / 3.0)
        self.all = 1.5 * e
        self.q = 1.0 / self.all
        self.z1 = self.q * jnp.where(ln.first, self.tz, jnp.where(ln.last, self.tzp, 0.0))
        self.zm = ln.zm(self.z1)
        self.zp = ln.zp(self.z1)

    def toward(self, low):
        return self.tx if low else self.txn

    def inward(self, low):
        return self.txn if low else self.tx

    def edge(self, low):
        self.x1 = self.q * self.toward(low)
        self.o1 = 1.0 - self.z1 - self.x1

    def rim(self):
        return self.tz * self.zm + self.tzp * self.zp

    def along_y(self, v):
        return self.ty * self.ln.ym(v) + self.typ * self.ln.yp(v)


def middle(p, below, above, mz):
    ln = p.ln
    vz = p.half * p.z1 + p.tx * below.z1 + p.txn * above.z1 + p.along_y(p.z1)
    vz = vz + p.tz * jnp.where(ln.first, 1.0 - p.zm, p.zm)
    vz = vz + p.tzp * jnp.where(ln.last, 1.0 - p.zp, p.zp)
    kept = vz * mz
    return p.all - vz, kept, p.all - (vz - kept)


def second(p, edge, inner, low, mz, mx):
    below, above = (edge, inner) if low else (inner, edge)
    ln = p.ln
    first_o = ln.zm(p.z1)
    vz = p.half * p.z1 + p.tx * below.z1 + p.txn * above.z1 + p.along_y(p.z1)
    vz = vz + p.tz * jnp.where(ln.first, 1.0 - first_o, first_o)
    vz = vz + p.tzp * jnp.where(ln.last, 1.0 - p.zp, p.zp)
    vx = p.toward(low) * edge.x1
    kept_z, kept_x = vz * mz, vx * mx
    total = p.all - (vz - kept_z) - (vx - kept_x)
    return p.all - vz - vx, kept_z, kept_x, total


def edge_own(p, inner_o1, inner_z1, outer_x1, low, mz):
    ln = p.ln
    om, op = ln.zm(p.o1), ln.zp(p.o1)
    vo = p.half * p.o1 + p.toward(low) * outer_x1 + p.inward(low) * inner_o1 + p.along_y(p.o1)
    vo = vo + p.tz * jnp.where(ln.first, p.zm, om) + p.tzp * jnp.where(ln.last, p.zp, op)
    vz = p.half * p.z1 + p.inward(low) * inner_z1 + p.along_y(p.z1)
    vz = vz + p.tz * jnp.where(ln.first, om, p.zm) + p.tzp * jnp.where(ln.last, op, p.zp)
    return vo, vz * mz


def edge_total(p, mz):
    rim = p.rim()
    return p.all - (rim - rim * mz)


def edge_spill(p, own, low):
    ln = p.ln
    xm, xp = ln.zm(p.x1), ln.zp(p.x1)
    face = p.toward(low)
    vx = p.half * p.x1 + face * own.o1 + p.along_y(p.x1)
    vx = vx + p.tz * jnp.where(ln.first, 0.0, xm) + p.tzp * jnp.where(ln.last, 0.0, xp)
    vd = face * own.z1 + p.tz * jnp.where(ln.first, xm, 0.0) + p.tzp * jnp.where(ln.last, xp, 0.0)
    return vx, vd


def second_spill(p, edge, low, mz, mx):
    vx = p.toward(low) * edge.x1
    kept = vx * mx
    return kept, edge_total(p, mz) - (vx - kept)


def store(ln, dst, layer, plane, blocks, own, other, total):
    scale = 1.0 / total
    own = own * scale
    other = jnp.zeros_like(own) if other is None else other * scale
    for k in range(blocks):
        dst[layer, k, plane] = jnp.where(ln.block == k, own, jnp.where(ln.other == k, other, 0.0))


def pack_kernel(
    n, width, axis, tx, ty, tz, s, reach, msg_a, msg_b, masks, faces, held_reach, sems
):
    layers, _, blocks = held_reach.shape
    lanes = masks.shape[-1]
    even = lax.rem(lax.axis_index(axis), 2) == 0

    def planes(down, up):
        pairs = [(tx.at[pl.ds(0, 3)], down.at[pl.ds(0, 3)])]
        for i, a in enumerate((ty, tz, s)):
            pairs.append((a.at[pl.ds(0, 2)], down.at[pl.ds(3 + 2 * i, 2)]))
        for i, a in enumerate((tx, ty, tz, s)):
            pairs.append((a.at[pl.ds(n - 2, 2)], up.at[pl.ds(2 * i, 2)]))
        return [pltpu.make_async_copy(src, dst, sems.at[i]) for i, (src, dst) in enumerate(pairs)]

    fetch = pltpu.make_async_copy(reach, held_reach, sems.at[8])
    fetch.start()

    @pl.when(even)
    def _():
        for c in planes(msg_b, msg_a):
            c.start()

    @pl.when(jnp.logical_not(even))
    def _():
        for c in planes(msg_a, msg_b):
            c.start()

    keeps = [
        pltpu.make_async_copy(a, faces.at[i], sems.at[9 + i]) for i, a in enumerate((tx, ty, tz, s))
    ]
    for c in keeps:
        c.start()
    masks[...] = jnp.zeros(masks.shape, jnp.float32)
    lane = lax.broadcasted_iota(jnp.int32, (4, lanes), 1)
    block = lane // width
    local = lane - block * width
    fetch.wait()
    for layer in range(layers):
        r = jnp.zeros((4, lanes), jnp.int32)
        for k in range(blocks):
            r = jnp.where(block == k, held_reach[layer, :, k : k + 1], r)
        low = pltpu.roll(r, width, 1)
        high = pltpu.roll(r, lanes - width, 1)
        near = jnp.where(
            local[0:1] < width // 2,
            jnp.where(low[3:4] >= local[0:1] + 1, 1.0, 0.0),
            jnp.where(high[2:3] >= width - local[0:1], 1.0, 0.0),
        )
        masks[layer, 0:1] = near
        masks[layer, 1:3] = jnp.where(r[0:2] >= 2, 1.0, 0.0)

    def finish(down, up):
        down[9, 0:TAIL] = masks[0]
        up[8, 0:TAIL] = masks[layers - 1]
        for c in planes(down, up):
            c.wait()

    @pl.when(even)
    def _():
        finish(msg_b, msg_a)

    @pl.when(jnp.logical_not(even))
    def _():
        finish(msg_a, msg_b)

    for c in keeps:
        c.wait()


def bulk_kernel(width, blocks, faces, masks, out, zeros, buf, sems):
    layers = masks.shape[0]
    rows, lanes = faces.shape[2:]
    zeros[...] = jnp.zeros(zeros.shape, jnp.float32)
    depth = zeros.shape[0]
    clears = []
    for layer in range(layers):
        for k in range(blocks):
            for start in (0, 3 * width - depth):
                sem = sems.at[len(clears)]
                c = pltpu.make_async_copy(zeros, out.at[layer, k, pl.ds(start, depth)], sem)
                c.start()
                clears.append(c)
    ln = Lanes((rows, lanes), width)

    def plane(p):
        return Plane(ln, faces[0, p], faces[0, p + 1], faces[1, p], faces[2, p], faces[3, p])

    sends = []
    for layer in range(layers):
        base = layer * width
        mz = masks[layer, 0:1]
        low, high = layer == 0, layer == layers - 1
        origin = base - width
        if not low:
            ma = masks[layer - 1, 0:1]
            to_above, to_below = masks[layer - 1, 2:3], masks[layer, 1:2]
            a3, a2, a1 = (plane(base - i) for i in (3, 2, 1))
            b0, b1, b2 = (plane(base + i) for i in (0, 1, 2))
            a1.edge(False)
            b0.edge(True)
            prev = origin - width
            put = functools.partial(store, ln, buf)
            vo, vz, vx, total = second(a2, a1, a3, False, ma, to_below)
            put(layer - 1, base - 2 - prev - (width - 2), blocks, vo, vz, total)
            put(layer, base - 2 - origin - (width - 2), blocks, vx, None, total)
            vo, vz = edge_own(a1, 1.0 - a2.z1, a2.z1, b0.x1, False, ma)
            vx, vd = edge_spill(a1, b0, False)
            total = edge_total(a1, ma)
            put(layer - 1, base - 1 - prev - (width - 2), blocks, vo, vz, total)
            put(layer, base - 1 - origin - (width - 2), blocks, vx, vd, total)
            vo, vz = edge_own(b0, 1.0 - b1.z1, b1.z1, a1.x1, True, mz)
            vx, vd = edge_spill(b0, a1, True)
            total = edge_total(b0, mz)
            put(layer, base - origin - (width - 2), blocks, vo, vz, total)
            put(layer - 1, base - prev - (width - 2), blocks, vx, vd, total)
            vo, vz, vx, total = second(b1, b0, b2, True, mz, to_above)
            put(layer, base + 1 - origin - (width - 2), blocks, vo, vz, total)
            put(layer - 1, base + 1 - prev - (width - 2), blocks, vx, None, total)
            sends.append(send_layer(layer - 1, layers, width, blocks, buf, out, sems))
        planes = [plane(base + a) for a in range(1, width - 1)]
        for a in range(2, width - 2):
            vo, vz, total = middle(planes[a - 1], planes[a - 2], planes[a], mz)
            store(ln, buf, layer, a + 2, blocks, vo, vz, total)
        if high:
            sends.append(send_layer(layer, layers, width, blocks, buf, out, sems))
    for group in sends:
        for c in group:
            c.wait()
    for c in clears:
        c.wait()


def span(layer, layers, width):
    return (4 if layer == 0 else 0), (width if layer == layers - 1 else width + 4)


def send_layer(layer, layers, width, blocks, buf, out, sems):
    low, high = span(layer, layers, width)
    group = []
    for k in range(blocks):
        c = pltpu.make_async_copy(
            buf.at[layer, k, pl.ds(low, high - low)],
            out.at[layer, k, pl.ds(width - 2 + low, high - low)],
            sems.at[(2 * layers + layer) * blocks + k],
        )
        c.start()
        group.append(c)
    return group


def edge_kernel(
    width, blocks, axis, count, faces, masks, got_a, pair_b, held, out, buf, got_b, sems
):
    del held
    layers = masks.shape[0]
    me = lax.axis_index(axis)
    even = lax.rem(me, 2) == 0
    fetch = pltpu.make_async_copy(pair_b.at[lax.rem(me, 2)], got_b, sems.at[2 * blocks])
    fetch.start()
    n = faces.shape[1]
    lo, hi = faces, faces.at[:, pl.ds(n - 4, 4)]

    class Got:
        def __init__(self, at_even, at_odd):
            self.at_even, self.at_odd = at_even, at_odd

        def __getitem__(self, where):
            return jnp.where(even, self.at_even[where], self.at_odd[where])

    lob, hib = Got(got_b, got_a), Got(got_a, got_b)
    fetch.wait()
    rows, lanes = lo.shape[2:]
    ln = Lanes((rows, lanes), width)
    put = functools.partial(store, ln, buf)
    low_ok, high_ok = me > 0, me < count - 1

    tx0 = jnp.where(low_ok, lo[0, 0], 0.0)
    a2 = Plane(ln, lob[0], lob[1], lob[2], lob[4], lob[6], low_ok)
    a1 = Plane(ln, lob[1], tx0, lob[3], lob[5], lob[7], low_ok)
    ma, to_above = lob[8, 0:1], lob[8, 2:3]
    mz, to_below = masks[0, 0:1], masks[0, 1:2]
    b0 = Plane(ln, tx0, lo[0, 1], lo[1, 0], lo[2, 0], lo[3, 0])
    b1, b2 = (Plane(ln, lo[0, i], lo[0, i + 1], lo[1, i], lo[2, i], lo[3, i]) for i in (1, 2))
    a1.edge(False)
    b0.edge(True)
    vx, total = second_spill(a2, a1, False, ma, to_below)
    put(0, 0, blocks, vx, None, total)
    vx, vd = edge_spill(a1, b0, False)
    put(0, 1, blocks, vx, vd, edge_total(a1, ma))
    vo, vz = edge_own(b0, 1.0 - b1.z1, b1.z1, a1.x1, True, mz)
    put(0, 2, blocks, vo, vz, edge_total(b0, mz))
    vo, vz, _, total = second(b1, b0, b2, True, mz, to_above)
    put(0, 3, blocks, vo, vz, total)
    sends = []

    def send(side, layer, start):
        for k in range(blocks):
            c = pltpu.make_async_copy(
                buf.at[side, k], out.at[layer, k, pl.ds(start, 4)], sems.at[len(sends)]
            )
            c.start()
            sends.append(c)

    send(0, 0, width - 2)

    mz, to_above = masks[layers - 1, 0:1], masks[layers - 1, 2:3]
    mb, to_below = hib[9, 0:1], hib[9, 1:2]
    a3, a2 = (Plane(ln, hi[0, i], hi[0, i + 1], hi[1, i], hi[2, i], hi[3, i]) for i in (1, 2))
    txn = jnp.where(high_ok, hib[0], 0.0)
    a1 = Plane(ln, hi[0, 3], txn, hi[1, 3], hi[2, 3], hi[3, 3])
    b0 = Plane(ln, txn, hib[1], hib[3], hib[5], hib[7], high_ok)
    b1 = Plane(ln, hib[1], hib[2], hib[4], hib[6], hib[8], high_ok)
    a1.edge(False)
    b0.edge(True)
    vo, vz, _, total = second(a2, a1, a3, False, mz, to_below)
    put(1, 0, blocks, vo, vz, total)
    vo, vz = edge_own(a1, 1.0 - a2.z1, a2.z1, b0.x1, False, mz)
    put(1, 1, blocks, vo, vz, edge_total(a1, mz))
    vx, vd = edge_spill(b0, a1, True)
    put(1, 2, blocks, vx, vd, edge_total(b0, mb))
    vx, total = second_spill(b1, b0, True, mb, to_above)
    put(1, 3, blocks, vx, None, total)
    send(1, layers - 1, 2 * width - 2)
    for c in sends:
        c.wait()


def swaps(firsts):
    return [pair for i in firsts for pair in ((i, i + 1), (i + 1, i))]


def pairs(first, count):
    return [[i % count, (i + 1) % count] for i in range(first, first + count, 2)]


def on_device(trans_east, trans_north, trans_up, storage, support_reach, *, axis, count):
    layers, blocks, _ = support_reach.shape
    n, rows, lanes = trans_east.shape
    width = n // layers
    f32 = jnp.float32
    anywhere = pl.BlockSpec(memory_space=pl.ANY)
    vmem = pl.BlockSpec(memory_space=pltpu.VMEM)
    params = pltpu.CompilerParams(vmem_limit_bytes=16 * 2**20)
    outside = tuple(
        pltpu.with_memory_space_constraint(x, pltpu.HBM)
        for x in (trans_east, trans_north, trans_up, storage)
    )
    reach = jnp.transpose(support_reach, (0, 2, 1))
    reach = pltpu.with_memory_space_constraint(reach, pltpu.HBM)
    message = pltpu.VMEM((10, rows, lanes), f32)
    msg_a, msg_b, masks, faces = pl.pallas_call(
        functools.partial(pack_kernel, n, width, axis),
        out_shape=(
            message,
            message,
            pltpu.VMEM((layers, TAIL, lanes), f32),
            pltpu.VMEM((4, n, rows, lanes), f32),
        ),
        in_specs=[anywhere] * 5,
        out_specs=(vmem,) * 4,
        scratch_shapes=[
            pltpu.VMEM((layers, 4, blocks), jnp.int32),
            pltpu.SemaphoreType.DMA((13,)),
        ],
        compiler_params=params,
        name="pack",
    )(*outside, reach)
    got_b = lax.all_gather(msg_b, axis, axis_index_groups=pairs(1, count))
    got_a = lax.ppermute(msg_a, axis, swaps(range(0, count - 1, 2)))

    out_shape = jax.ShapeDtypeStruct((layers, blocks, 3 * width, rows, lanes), f32)
    bulk = pl.pallas_call(
        functools.partial(bulk_kernel, width, blocks),
        out_shape=out_shape,
        in_specs=[vmem] * 2,
        out_specs=anywhere,
        scratch_shapes=[
            pltpu.VMEM((width - 2, rows, lanes), f32),
            pltpu.VMEM((layers, blocks, width + 4, rows, lanes), f32),
            pltpu.SemaphoreType.DMA((3 * layers * blocks,)),
        ],
        compiler_params=params,
        cost_estimate=pl.CostEstimate(flops=10**7, bytes_accessed=7 * 10**6, transcendentals=0),
        name="bulk",
    )(faces, masks)
    return pl.pallas_call(
        functools.partial(edge_kernel, width, blocks, axis, count),
        out_shape=out_shape,
        in_specs=[vmem] * 3 + [anywhere] * 2,
        out_specs=anywhere,
        scratch_shapes=[
            pltpu.VMEM((2, blocks, 4, rows, lanes), f32),
            pltpu.VMEM((10, rows, lanes), f32),
            pltpu.SemaphoreType.DMA((2 * blocks + 1,)),
        ],
        input_output_aliases={4: 0},
        compiler_params=params,
        cost_estimate=pl.CostEstimate(flops=10**6, bytes_accessed=10**6, transcendentals=0),
        name="edges",
    )(faces, masks, got_a, pltpu.with_memory_space_constraint(got_b, pltpu.HBM), bulk)


def solution(mesh):
    spread = P(("groups", "blk"))
    return jax.shard_map(
        functools.partial(on_device, axis="blk", count=mesh.shape["blk"]),
        mesh=mesh,
        in_specs=(spread,) * 5,
        out_specs=spread,
        check_vma=False,
    )
```

```python
import functools

import jax
import jax.numpy as jnp
from jax import lax
from jax.experimental import pallas as pl
from jax.experimental.pallas import tpu as pltpu
from jax.sharding import PartitionSpec as P


TAIL = 8
CHUNK = 4
SPLIT = 2


class Lanes:
    def __init__(self, shape, width):
        lane = lax.broadcasted_iota(jnp.int32, shape, 1)
        self.width = width
        self.lanes = shape[1]
        self.rows = shape[0]
        self.lane = lane
        self.block = lane // width
        self.local = lane - self.block * width
        self.first = self.local == 0
        self.last = self.local == width - 1
        self.upper = self.local >= width // 2
        self.other = jnp.where(self.upper, self.block + 1, self.block - 1)
        self.row0 = lax.broadcasted_iota(jnp.int32, shape, 0) == 0
        self.lane0 = lane == 0

    def zm(self, v):
        return pltpu.roll(v, 1, 1)

    def zp(self, v):
        return pltpu.roll(v, self.lanes - 1, 1)

    def ym(self, v):
        return pltpu.roll(v, 1, 0)

    def yp(self, v):
        return pltpu.roll(v, self.rows - 1, 0)


class Plane:
    def __init__(self, ln, tx, txn, ty, tz, s, valid=None):
        self.ln = ln
        self.tx, self.txn = tx, txn
        self.ty = jnp.where(ln.row0, 0.0, ty)
        self.tz = jnp.where(ln.lane0, 0.0, tz)
        self.typ = ln.yp(self.ty)
        self.tzp = ln.zp(self.tz)
        e = s * (1.0 / 3.0) + ((tx + txn) + (self.ty + self.typ) + (self.tz + self.tzp))
        if valid is not None:
            e = jnp.where(valid, e, 1.0)
        self.half = 0.5 * e + s * (1.0 / 3.0)
        self.all = 1.5 * e
        self.q = 1.0 / self.all
        self.z1 = self.q * jnp.where(ln.first, self.tz, jnp.where(ln.last, self.tzp, 0.0))
        self.zm = ln.zm(self.z1)
        self.zp = ln.zp(self.z1)

    def toward(self, low):
        return self.tx if low else self.txn

    def inward(self, low):
        return self.txn if low else self.tx

    def edge(self, low):
        self.x1 = self.q * self.toward(low)
        self.o1 = 1.0 - self.z1 - self.x1

    def rim(self):
        return self.tz * self.zm + self.tzp * self.zp

    def along_y(self, v):
        return self.ty * self.ln.ym(v) + self.typ * self.ln.yp(v)


def middle(p, below, above, mz):
    ln = p.ln
    vz = p.half * p.z1 + p.tx * below.z1 + p.txn * above.z1 + p.along_y(p.z1)
    vz = vz + p.tz * jnp.where(ln.first, 1.0 - p.zm, p.zm)
    vz = vz + p.tzp * jnp.where(ln.last, 1.0 - p.zp, p.zp)
    kept = vz * mz
    return p.all - vz, kept, p.all - (vz - kept)


def second(p, edge, inner, low, mz, mx):
    below, above = (edge, inner) if low else (inner, edge)
    ln = p.ln
    first_o = ln.zm(p.z1)
    vz = p.half * p.z1 + p.tx * below.z1 + p.txn * above.z1 + p.along_y(p.z1)
    vz = vz + p.tz * jnp.where(ln.first, 1.0 - first_o, first_o)
    vz = vz + p.tzp * jnp.where(ln.last, 1.0 - p.zp, p.zp)
    vx = p.toward(low) * edge.x1
    kept_z, kept_x = vz * mz, vx * mx
    total = p.all - (vz - kept_z) - (vx - kept_x)
    return p.all - vz - vx, kept_z, kept_x, total


def edge_own(p, inner_o1, inner_z1, outer_x1, low, mz):
    ln = p.ln
    om, op = ln.zm(p.o1), ln.zp(p.o1)
    vo = p.half * p.o1 + p.toward(low) * outer_x1 + p.inward(low) * inner_o1 + p.along_y(p.o1)
    vo = vo + p.tz * jnp.where(ln.first, p.zm, om) + p.tzp * jnp.where(ln.last, p.zp, op)
    vz = p.half * p.z1 + p.inward(low) * inner_z1 + p.along_y(p.z1)
    vz = vz + p.tz * jnp.where(ln.first, om, p.zm) + p.tzp * jnp.where(ln.last, op, p.zp)
    return vo, vz * mz


def edge_total(p, mz):
    rim = p.rim()
    return p.all - (rim - rim * mz)


def edge_spill(p, own, low):
    ln = p.ln
    xm, xp = ln.zm(p.x1), ln.zp(p.x1)
    face = p.toward(low)
    vx = p.half * p.x1 + face * own.o1 + p.along_y(p.x1)
    vx = vx + p.tz * jnp.where(ln.first, 0.0, xm) + p.tzp * jnp.where(ln.last, 0.0, xp)
    vd = face * own.z1 + p.tz * jnp.where(ln.first, xm, 0.0) + p.tzp * jnp.where(ln.last, xp, 0.0)
    return vx, vd


def second_spill(p, edge, low, mz, mx):
    vx = p.toward(low) * edge.x1
    kept = vx * mx
    return kept, edge_total(p, mz) - (vx - kept)


def store(ln, dst, layer, plane, blocks, own, other, total):
    scale = 1.0 / total
    own = own * scale
    other = jnp.zeros_like(own) if other is None else other * scale
    for k in range(blocks):
        dst[layer, k, plane] = jnp.where(ln.block == k, own, jnp.where(ln.other == k, other, 0.0))


def pack_kernel(
    n, width, axis, tx, ty, tz, s, reach, msg_a, msg_b, masks, faces, held_reach, sems
):
    layers, _, blocks = held_reach.shape
    lanes = masks.shape[-1]
    fetch = pltpu.make_async_copy(reach, held_reach, sems.at[4])
    copies = [
        pltpu.make_async_copy(a, faces.at[i], sems.at[i]) for i, a in enumerate((tx, ty, tz, s))
    ]
    for c in [fetch] + copies:
        c.start()
    masks[...] = jnp.zeros(masks.shape, jnp.float32)
    lane = lax.broadcasted_iota(jnp.int32, (4, lanes), 1)
    block = lane // width
    local = lane - block * width
    fetch.wait()
    for layer in range(layers):
        r = jnp.zeros((4, lanes), jnp.int32)
        for k in range(blocks):
            r = jnp.where(block == k, held_reach[layer, :, k : k + 1], r)
        low = pltpu.roll(r, width, 1)
        high = pltpu.roll(r, lanes - width, 1)
        near = jnp.where(
            local[0:1] < width // 2,
            jnp.where(low[3:4] >= local[0:1] + 1, 1.0, 0.0),
            jnp.where(high[2:3] >= width - local[0:1], 1.0, 0.0),
        )
        masks[layer, 0:1] = near
        masks[layer, 1:3] = jnp.where(r[0:2] >= 2, 1.0, 0.0)
    even = lax.rem(lax.axis_index(axis), 2) == 0

    def put(tile, up, down):
        up, down = (v.reshape(-1, TAIL, lanes) for v in (up, down))
        where = pl.ds(tile, up.shape[0])
        msg_a[where] = jnp.where(even, up, down)
        msg_b[where] = jnp.where(even, down, up)

    put(0, masks[layers - 1], masks[0])
    for c in copies:
        c.wait()
    for i in range(4):
        for j in range(2):
            put(1 + 2 * (2 * i + j), faces[i, n - 2 + j], faces[i, j])
    put(17, faces[0, n - 1], faces[0, 2])


def bulk_kernel(width, blocks, faces, masks, out, zeros, buf, sems):
    layers = masks.shape[0]
    rows, lanes = faces.shape[2:]
    depth = zeros.shape[0]
    zeros[...] = jnp.zeros(zeros.shape, jnp.float32)

    def clears(k):
        for layer in range(layers):
            for side, start in enumerate((0, 3 * width - depth)):
                sem = sems.at[(layer * 2 + side) * blocks + k]
                yield pltpu.make_async_copy(zeros, out.at[layer, k, pl.ds(start, depth)], sem)

    def send(layer, start, planes, index):
        for i in range(SPLIT):
            few = pl.ds(i * (blocks // SPLIT), blocks // SPLIT)
            yield pltpu.make_async_copy(
                buf.at[layer, few, pl.ds(start, planes)],
                out.at[layer, few, pl.ds(width - 2 + start, planes)],
                sems.at[2 * layers * blocks + index * SPLIT + i],
            )

    @pl.loop(0, blocks)
    def _(k):
        for c in clears(k):
            c.start()

    ln = Lanes((rows, lanes), width)

    def plane(p):
        return Plane(ln, faces[0, p], faces[0, p + 1], faces[1, p], faces[2, p], faces[3, p])

    chunks = (width - 4) // CHUNK

    @pl.loop(0, layers * chunks)
    def _(i):
        layer = i // chunks
        first = 2 + (i - layer * chunks) * CHUNK
        planes = [plane(layer * width + first + j) for j in range(-1, CHUNK + 1)]
        mz = masks[layer, 0:1]
        for j in range(CHUNK):
            vo, vz, total = middle(planes[j + 1], planes[j], planes[j + 2], mz)
            store(ln, buf, layer, first + j + 2, blocks, vo, vz, total)
        for c in send(layer, first + 2, CHUNK, i):
            c.start()

    @pl.loop(1, layers)
    def _(layer):
        base = layer * width
        ma, mb = masks[layer - 1, 0:1], masks[layer, 0:1]
        to_above, to_below = masks[layer - 1, 2:3], masks[layer, 1:2]
        a3, a2, a1 = (plane(base - i) for i in (3, 2, 1))
        b0, b1, b2 = (plane(base + i) for i in (0, 1, 2))
        a1.edge(False)
        b0.edge(True)
        low = functools.partial(store, ln, buf, layer - 1)
        high = functools.partial(store, ln, buf, layer)
        vo, vz, vx, total = second(a2, a1, a3, False, ma, to_below)
        low(width, blocks, vo, vz, total)
        high(0, blocks, vx, None, total)
        vo, vz = edge_own(a1, 1.0 - a2.z1, a2.z1, b0.x1, False, ma)
        vx, vd = edge_spill(a1, b0, False)
        total = edge_total(a1, ma)
        low(width + 1, blocks, vo, vz, total)
        high(1, blocks, vx, vd, total)
        vo, vz = edge_own(b0, 1.0 - b1.z1, b1.z1, a1.x1, True, mb)
        vx, vd = edge_spill(b0, a1, True)
        total = edge_total(b0, mb)
        high(2, blocks, vo, vz, total)
        low(width + 2, blocks, vx, vd, total)
        vo, vz, vx, total = second(b1, b0, b2, True, mb, to_above)
        high(3, blocks, vo, vz, total)
        low(width + 3, blocks, vx, None, total)
        index = layers * chunks + 2 * (layer - 1)
        for c in send(layer - 1, width, 4, index):
            c.start()
        for c in send(layer, 0, 4, index + 1):
            c.start()

    for layer in range(layers):
        for i in range(chunks):
            for c in send(layer, 4 + i * CHUNK, CHUNK, layer * chunks + i):
                c.wait()
    for layer in range(1, layers):
        index = layers * chunks + 2 * (layer - 1)
        for c in send(layer - 1, width, 4, index):
            c.wait()
        for c in send(layer, 0, 4, index + 1):
            c.wait()

    @pl.loop(0, blocks)
    def _(k):
        for c in clears(k):
            c.wait()


def edge_kernel(
    width, blocks, axis, count, faces, masks, got_a, got_b, held, out, buf, sems
):
    del held
    layers = masks.shape[0]
    me = lax.axis_index(axis)
    even = lax.rem(me, 2) == 0
    n, rows, lanes = faces.shape[1:]
    lo, hi = faces, faces.at[:, pl.ds(n - 4, 4)]

    class Got:
        def __init__(self, at_even, at_odd):
            self.at_even, self.at_odd = at_even, at_odd

        def mask(self, row):
            return jnp.where(even, self.at_even[0, row : row + 1], self.at_odd[0, row : row + 1])

        def __getitem__(self, place):
            i, j = place
            tiles = pl.ds(1 + (rows // TAIL) * (2 * i + j), rows // TAIL)
            return jnp.where(even, self.at_even[tiles], self.at_odd[tiles]).reshape(rows, lanes)

    lob, hib = Got(got_b, got_a), Got(got_a, got_b)
    ln = Lanes((rows, lanes), width)
    put = functools.partial(store, ln, buf)
    low_ok, high_ok = me > 0, me < count - 1

    tx0 = jnp.where(low_ok, lo[0, 0], 0.0)
    a2 = Plane(ln, lob[0, 0], lob[0, 1], lob[1, 0], lob[2, 0], lob[3, 0], low_ok)
    a1 = Plane(ln, lob[0, 1], tx0, lob[1, 1], lob[2, 1], lob[3, 1], low_ok)
    ma, to_above = lob.mask(0), lob.mask(2)
    mz, to_below = masks[0, 0:1], masks[0, 1:2]
    b0 = Plane(ln, tx0, lo[0, 1], lo[1, 0], lo[2, 0], lo[3, 0])
    b1, b2 = (Plane(ln, lo[0, i], lo[0, i + 1], lo[1, i], lo[2, i], lo[3, i]) for i in (1, 2))
    a1.edge(False)
    b0.edge(True)
    vx, total = second_spill(a2, a1, False, ma, to_below)
    put(0, 0, blocks, vx, None, total)
    vx, vd = edge_spill(a1, b0, False)
    put(0, 1, blocks, vx, vd, edge_total(a1, ma))
    vo, vz = edge_own(b0, 1.0 - b1.z1, b1.z1, a1.x1, True, mz)
    put(0, 2, blocks, vo, vz, edge_total(b0, mz))
    vo, vz, _, total = second(b1, b0, b2, True, mz, to_above)
    put(0, 3, blocks, vo, vz, total)
    sends = []

    def send(side, layer, start):
        for k in range(blocks):
            c = pltpu.make_async_copy(
                buf.at[side, k], out.at[layer, k, pl.ds(start, 4)], sems.at[len(sends)]
            )
            c.start()
            sends.append(c)


    mz, to_above = masks[layers - 1, 0:1], masks[layers - 1, 2:3]
    mb, to_below = hib.mask(0), hib.mask(1)
    a3, a2 = (Plane(ln, hi[0, i], hi[0, i + 1], hi[1, i], hi[2, i], hi[3, i]) for i in (1, 2))
    a1 = Plane(ln, hi[0, 3], hib[0, 0], hi[1, 3], hi[2, 3], hi[3, 3])
    b0 = Plane(ln, hib[0, 0], hib[0, 1], hib[1, 0], hib[2, 0], hib[3, 0], high_ok)
    b1 = Plane(ln, hib[0, 1], hib[4, 0], hib[1, 1], hib[2, 1], hib[3, 1], high_ok)
    a1.edge(False)
    b0.edge(True)
    vo, vz, _, total = second(a2, a1, a3, False, mz, to_below)
    put(1, 0, blocks, vo, vz, total)
    vo, vz = edge_own(a1, 1.0 - a2.z1, a2.z1, b0.x1, False, mz)
    put(1, 1, blocks, vo, vz, edge_total(a1, mz))
    vx, vd = edge_spill(b0, a1, True)
    put(1, 2, blocks, vx, vd, edge_total(b0, mb))
    vx, total = second_spill(b1, b0, True, mb, to_above)
    put(1, 3, blocks, vx, None, total)
    send(0, 0, width - 2)
    send(1, layers - 1, 2 * width - 2)
    for c in sends:
        c.wait()


def swaps(firsts):
    return [pair for i in firsts for pair in ((i, i + 1), (i + 1, i))]


def on_device(trans_east, trans_north, trans_up, storage, support_reach, *, axis, count):
    layers, blocks, _ = support_reach.shape
    n, rows, lanes = trans_east.shape
    width = n // layers
    f32 = jnp.float32
    anywhere = pl.BlockSpec(memory_space=pl.ANY)
    vmem = pl.BlockSpec(memory_space=pltpu.VMEM)
    params = pltpu.CompilerParams(vmem_limit_bytes=16 * 2**20)
    outside = tuple(
        pltpu.with_memory_space_constraint(x, pltpu.HBM)
        for x in (trans_east, trans_north, trans_up, storage)
    )
    reach = jnp.transpose(support_reach, (0, 2, 1))
    reach = pltpu.with_memory_space_constraint(reach, pltpu.HBM)
    tiles = 1 + 9 * rows // TAIL
    msg_a, msg_b, masks, faces = pl.pallas_call(
        functools.partial(pack_kernel, n, width, axis),
        out_shape=(
            pltpu.VMEM((tiles, TAIL, lanes), f32),
            pltpu.VMEM((tiles + 1, TAIL, lanes), f32),
            pltpu.VMEM((layers, TAIL, lanes), f32),
            pltpu.VMEM((4, n, rows, lanes), f32),
        ),
        in_specs=[anywhere] * 5,
        out_specs=(vmem,) * 4,
        scratch_shapes=[
            pltpu.VMEM((layers, 4, blocks), jnp.int32),
            pltpu.SemaphoreType.DMA((5,)),
        ],
        compiler_params=params,
        name="pack",
    )(*outside, reach)
    got_a = lax.ppermute(msg_a, axis, swaps(range(0, count - 1, 2)))
    got_b = lax.ppermute(msg_b, axis, swaps(range(1, count - 1, 2)))

    out_shape = jax.ShapeDtypeStruct((layers, blocks, 3 * width, rows, lanes), f32)
    sends = layers * ((width - 4) // CHUNK) + 2 * (layers - 1)
    bulk = pl.pallas_call(
        functools.partial(bulk_kernel, width, blocks),
        out_shape=out_shape,
        in_specs=[vmem] * 2,
        out_specs=anywhere,
        scratch_shapes=[
            pltpu.VMEM((width - 2, rows, lanes), f32),
            pltpu.VMEM((layers, blocks, width + 4, rows, lanes), f32),
            pltpu.SemaphoreType.DMA((2 * layers * blocks + sends * SPLIT,)),
        ],
        compiler_params=params,
        cost_estimate=pl.CostEstimate(flops=10**7, bytes_accessed=7 * 10**6, transcendentals=0),
        name="bulk",
    )(faces, masks)
    return pl.pallas_call(
        functools.partial(edge_kernel, width, blocks, axis, count),
        out_shape=out_shape,
        in_specs=[vmem] * 4 + [anywhere],
        out_specs=anywhere,
        scratch_shapes=[
            pltpu.VMEM((2, blocks, 4, rows, lanes), f32),
            pltpu.SemaphoreType.DMA((2 * blocks,)),
        ],
        input_output_aliases={4: 0},
        compiler_params=params,
        cost_estimate=pl.CostEstimate(flops=10**6, bytes_accessed=10**6, transcendentals=0),
        name="edges",
    )(faces, masks, got_a, got_b, bulk)


def solution(mesh):
    spread = P(("groups", "blk"))
    return jax.shard_map(
        functools.partial(on_device, axis="blk", count=mesh.shape["blk"]),
        mesh=mesh,
        in_specs=(spread,) * 5,
        out_specs=spread,
        check_vma=False,
    )
```

```python
import functools

import jax
import jax.numpy as jnp
from jax import lax
from jax.experimental import pallas as pl
from jax.experimental.pallas import tpu as pltpu
from jax.sharding import PartitionSpec as P


TAIL = 8
CHUNK = 12
SPLIT = 2


class Lanes:
    def __init__(self, shape, width):
        lane = lax.broadcasted_iota(jnp.int32, shape, 1)
        self.width = width
        self.lanes = shape[1]
        self.rows = shape[0]
        self.lane = lane
        self.block = lane // width
        self.local = lane - self.block * width
        self.first = self.local == 0
        self.last = self.local == width - 1
        self.upper = self.local >= width // 2
        self.other = jnp.where(self.upper, self.block + 1, self.block - 1)
        self.row0 = lax.broadcasted_iota(jnp.int32, shape, 0) == 0
        self.lane0 = lane == 0

    def zm(self, v):
        return pltpu.roll(v, 1, 1)

    def zp(self, v):
        return pltpu.roll(v, self.lanes - 1, 1)

    def ym(self, v):
        return pltpu.roll(v, 1, 0)

    def yp(self, v):
        return pltpu.roll(v, self.rows - 1, 0)


class Plane:
    def __init__(self, ln, tx, txn, ty, tz, s, valid=None):
        self.ln = ln
        self.tx, self.txn = tx, txn
        self.ty = jnp.where(ln.row0, 0.0, ty)
        self.tz = jnp.where(ln.lane0, 0.0, tz)
        self.typ = ln.yp(self.ty)
        self.tzp = ln.zp(self.tz)
        e = s * (1.0 / 3.0) + ((tx + txn) + (self.ty + self.typ) + (self.tz + self.tzp))
        if valid is not None:
            e = jnp.where(valid, e, 1.0)
        self.half = 0.5 * e + s * (1.0 / 3.0)
        self.all = 1.5 * e
        self.q = 1.0 / self.all
        self.z1 = self.q * jnp.where(ln.first, self.tz, jnp.where(ln.last, self.tzp, 0.0))
        self.zm = ln.zm(self.z1)
        self.zp = ln.zp(self.z1)

    def toward(self, low):
        return self.tx if low else self.txn

    def inward(self, low):
        return self.txn if low else self.tx

    def edge(self, low):
        self.x1 = self.q * self.toward(low)
        self.o1 = 1.0 - self.z1 - self.x1

    def rim(self):
        return self.tz * self.zm + self.tzp * self.zp

    def along_y(self, v):
        return self.ty * self.ln.ym(v) + self.typ * self.ln.yp(v)


def plane_at(ln, faces, p):
    return Plane(ln, faces[0, p], faces[0, p + 1], faces[1, p], faces[2, p], faces[3, p])


def middle(p, below, above, mz):
    ln = p.ln
    vz = p.half * p.z1 + p.tx * below.z1 + p.txn * above.z1 + p.along_y(p.z1)
    vz = vz + p.tz * jnp.where(ln.first, 1.0 - p.zm, p.zm)
    vz = vz + p.tzp * jnp.where(ln.last, 1.0 - p.zp, p.zp)
    kept = vz * mz
    return p.all - vz, kept, p.all - (vz - kept)


def second(p, edge, inner, low, mz, mx):
    below, above = (edge, inner) if low else (inner, edge)
    ln = p.ln
    first_o = ln.zm(p.z1)
    vz = p.half * p.z1 + p.tx * below.z1 + p.txn * above.z1 + p.along_y(p.z1)
    vz = vz + p.tz * jnp.where(ln.first, 1.0 - first_o, first_o)
    vz = vz + p.tzp * jnp.where(ln.last, 1.0 - p.zp, p.zp)
    vx = p.toward(low) * edge.x1
    kept_z, kept_x = vz * mz, vx * mx
    total = p.all - (vz - kept_z) - (vx - kept_x)
    return p.all - vz - vx, kept_z, kept_x, total


def edge_own(p, inner_o1, inner_z1, outer_x1, low, mz):
    ln = p.ln
    om, op = ln.zm(p.o1), ln.zp(p.o1)
    vo = p.half * p.o1 + p.toward(low) * outer_x1 + p.inward(low) * inner_o1 + p.along_y(p.o1)
    vo = vo + p.tz * jnp.where(ln.first, p.zm, om) + p.tzp * jnp.where(ln.last, p.zp, op)
    vz = p.half * p.z1 + p.inward(low) * inner_z1 + p.along_y(p.z1)
    vz = vz + p.tz * jnp.where(ln.first, om, p.zm) + p.tzp * jnp.where(ln.last, op, p.zp)
    return vo, vz * mz


def edge_total(p, mz):
    rim = p.rim()
    return p.all - (rim - rim * mz)


def edge_spill(p, own, low):
    ln = p.ln
    xm, xp = ln.zm(p.x1), ln.zp(p.x1)
    face = p.toward(low)
    vx = p.half * p.x1 + face * own.o1 + p.along_y(p.x1)
    vx = vx + p.tz * jnp.where(ln.first, 0.0, xm) + p.tzp * jnp.where(ln.last, 0.0, xp)
    vd = face * own.z1 + p.tz * jnp.where(ln.first, xm, 0.0) + p.tzp * jnp.where(ln.last, xp, 0.0)
    return vx, vd


def second_spill(face, edge, total, mx):
    vx = face * edge.x1
    kept = vx * mx
    return kept, total - (vx - kept)


def store(ln, dst, layer, plane, blocks, own, other, total):
    scale = 1.0 / total
    own = own * scale
    other = jnp.zeros_like(own) if other is None else other * scale
    for k in range(blocks):
        dst[layer, k, plane] = jnp.where(ln.block == k, own, jnp.where(ln.other == k, other, 0.0))


def pack_kernel(
    n, width, axis, tx, ty, tz, s, reach, msg_a, msg_b, masks, faces, held_reach, sems
):
    layers, _, blocks = held_reach.shape
    lanes = masks.shape[-1]
    fetch = pltpu.make_async_copy(reach, held_reach, sems.at[12])
    fetch.start()
    copies = []
    for j, (start, count) in enumerate(((0, 4), (n - 4, 4), (4, n - 8))):
        for i, a in enumerate((tx, ty, tz, s)):
            part = pl.ds(start, count)
            copies.append(pltpu.make_async_copy(a.at[part], faces.at[i, part], sems.at[4 * j + i]))
            copies[-1].start()
    masks[...] = jnp.zeros(masks.shape, jnp.float32)
    lane = lax.broadcasted_iota(jnp.int32, (4, lanes), 1)
    block = lane // width
    local = lane - block * width
    fetch.wait()
    for layer in range(layers):
        r = jnp.zeros((4, lanes), jnp.int32)
        for k in range(blocks):
            r = jnp.where(block == k, held_reach[layer, :, k : k + 1], r)
        low = pltpu.roll(r, width, 1)
        high = pltpu.roll(r, lanes - width, 1)
        near = jnp.where(
            local[0:1] < width // 2,
            jnp.where(low[3:4] >= local[0:1] + 1, 1.0, 0.0),
            jnp.where(high[2:3] >= width - local[0:1], 1.0, 0.0),
        )
        masks[layer, 0:1] = near
        masks[layer, 1:3] = jnp.where(r[0:2] >= 2, 1.0, 0.0)
    even = lax.rem(lax.axis_index(axis), 2) == 0

    def put(tile, up, down):
        up, down = (v.reshape(-1, TAIL, lanes) for v in (up, down))
        where = pl.ds(tile, up.shape[0])
        msg_a[where] = jnp.where(even, up, down)
        msg_b[where] = jnp.where(even, down, up)

    put(0, masks[layers - 1], masks[0])
    for c in copies[:8]:
        c.wait()
    for i in range(4):
        put(1 + 2 * i, faces[i, n - 1], faces[i, 0])
    put(11, faces[0, n - 1], faces[0, 1])
    ln = Lanes(faces.shape[2:], width)
    top, low = plane_at(ln, faces, n - 2), plane_at(ln, faces, 1)
    put(9, edge_total(top, masks[layers - 1, 0:1]), edge_total(low, masks[0, 0:1]))
    for c in copies[8:]:
        c.wait()


def bulk_kernel(width, blocks, faces, masks, out, zeros, buf, sems):
    layers = masks.shape[0]
    rows, lanes = faces.shape[2:]
    depth = zeros.shape[0]
    zeros[...] = jnp.zeros(zeros.shape, jnp.float32)

    def clears(k):
        for layer in range(layers):
            for side, start in enumerate((0, 3 * width - depth)):
                sem = sems.at[(layer * 2 + side) * blocks + k]
                yield pltpu.make_async_copy(zeros, out.at[layer, k, pl.ds(start, depth)], sem)

    def send(layer, start, planes, index):
        for i in range(SPLIT):
            few = pl.ds(i * (blocks // SPLIT), blocks // SPLIT)
            yield pltpu.make_async_copy(
                buf.at[layer, few, pl.ds(start, planes)],
                out.at[layer, few, pl.ds(width - 2 + start, planes)],
                sems.at[2 * layers * blocks + index * SPLIT + i],
            )

    @pl.loop(0, blocks)
    def _(k):
        for c in clears(k):
            c.start()

    ln = Lanes((rows, lanes), width)

    plane = functools.partial(plane_at, ln, faces)
    chunks = (width - 4) // CHUNK

    @pl.loop(0, layers * chunks)
    def _(i):
        layer = i // chunks
        first = 2 + (i - layer * chunks) * CHUNK
        planes = [plane(layer * width + first + j) for j in range(-1, CHUNK + 1)]
        mz = masks[layer, 0:1]
        for j in range(CHUNK):
            vo, vz, total = middle(planes[j + 1], planes[j], planes[j + 2], mz)
            store(ln, buf, layer, first + j + 2, blocks, vo, vz, total)
        for c in send(layer, first + 2, CHUNK, i):
            c.start()

    @pl.loop(1, layers)
    def _(layer):
        base = layer * width
        ma, mb = masks[layer - 1, 0:1], masks[layer, 0:1]
        to_above, to_below = masks[layer - 1, 2:3], masks[layer, 1:2]
        a3, a2, a1 = (plane(base - i) for i in (3, 2, 1))
        b0, b1, b2 = (plane(base + i) for i in (0, 1, 2))
        a1.edge(False)
        b0.edge(True)
        low = functools.partial(store, ln, buf, layer - 1)
        high = functools.partial(store, ln, buf, layer)
        vo, vz, vx, total = second(a2, a1, a3, False, ma, to_below)
        low(width, blocks, vo, vz, total)
        high(0, blocks, vx, None, total)
        vo, vz = edge_own(a1, 1.0 - a2.z1, a2.z1, b0.x1, False, ma)
        vx, vd = edge_spill(a1, b0, False)
        total = edge_total(a1, ma)
        low(width + 1, blocks, vo, vz, total)
        high(1, blocks, vx, vd, total)
        vo, vz = edge_own(b0, 1.0 - b1.z1, b1.z1, a1.x1, True, mb)
        vx, vd = edge_spill(b0, a1, True)
        total = edge_total(b0, mb)
        high(2, blocks, vo, vz, total)
        low(width + 2, blocks, vx, vd, total)
        vo, vz, vx, total = second(b1, b0, b2, True, mb, to_above)
        high(3, blocks, vo, vz, total)
        low(width + 3, blocks, vx, None, total)
        index = layers * chunks + 2 * (layer - 1)
        for c in send(layer - 1, width, 4, index):
            c.start()
        for c in send(layer, 0, 4, index + 1):
            c.start()

    for layer in range(layers):
        for i in range(chunks):
            for c in send(layer, 4 + i * CHUNK, CHUNK, layer * chunks + i):
                c.wait()
    for layer in range(1, layers):
        index = layers * chunks + 2 * (layer - 1)
        for c in send(layer - 1, width, 4, index):
            c.wait()
        for c in send(layer, 0, 4, index + 1):
            c.wait()

    @pl.loop(0, blocks)
    def _(k):
        for c in clears(k):
            c.wait()


def edge_kernel(
    width, blocks, axis, count, faces, masks, got_a, got_b, held, out, buf, sems
):
    del held
    layers = masks.shape[0]
    me = lax.axis_index(axis)
    even = lax.rem(me, 2) == 0
    n, rows, lanes = faces.shape[1:]
    lo, hi = faces, faces.at[:, pl.ds(n - 4, 4)]

    class Got:
        def __init__(self, at_even, at_odd):
            self.at_even, self.at_odd = at_even, at_odd

        def mask(self, row):
            return jnp.where(even, self.at_even[0, row : row + 1], self.at_odd[0, row : row + 1])

        def __getitem__(self, i):
            tiles = pl.ds(1 + (rows // TAIL) * i, rows // TAIL)
            return jnp.where(even, self.at_even[tiles], self.at_odd[tiles]).reshape(rows, lanes)

    lob, hib = Got(got_b, got_a), Got(got_a, got_b)
    ln = Lanes((rows, lanes), width)
    put = functools.partial(store, ln, buf)
    low_ok, high_ok = me > 0, me < count - 1

    tx0 = jnp.where(low_ok, lo[0, 0], 0.0)
    a1 = Plane(ln, lob[0], tx0, lob[1], lob[2], lob[3], low_ok)
    ma, to_above = lob.mask(0), lob.mask(2)
    mz, to_below = masks[0, 0:1], masks[0, 1:2]
    b0 = Plane(ln, tx0, lo[0, 1], lo[1, 0], lo[2, 0], lo[3, 0])
    b1, b2 = (Plane(ln, lo[0, i], lo[0, i + 1], lo[1, i], lo[2, i], lo[3, i]) for i in (1, 2))
    a1.edge(False)
    b0.edge(True)
    outer = jnp.where(low_ok, lob[4], 1.0)
    vx, total = second_spill(lob[0], a1, outer, to_below)
    put(0, 0, blocks, vx, None, total)
    vx, vd = edge_spill(a1, b0, False)
    put(0, 1, blocks, vx, vd, edge_total(a1, ma))
    vo, vz = edge_own(b0, 1.0 - b1.z1, b1.z1, a1.x1, True, mz)
    put(0, 2, blocks, vo, vz, edge_total(b0, mz))
    vo, vz, _, total = second(b1, b0, b2, True, mz, to_above)
    put(0, 3, blocks, vo, vz, total)
    sends = []

    def send(side, layer, start):
        for k in range(blocks):
            c = pltpu.make_async_copy(
                buf.at[side, k], out.at[layer, k, pl.ds(start, 4)], sems.at[len(sends)]
            )
            c.start()
            sends.append(c)


    mz, to_above = masks[layers - 1, 0:1], masks[layers - 1, 2:3]
    mb, to_below = hib.mask(0), hib.mask(1)
    a3, a2 = (Plane(ln, hi[0, i], hi[0, i + 1], hi[1, i], hi[2, i], hi[3, i]) for i in (1, 2))
    a1 = Plane(ln, hi[0, 3], hib[0], hi[1, 3], hi[2, 3], hi[3, 3])
    b0 = Plane(ln, hib[0], hib[5], hib[1], hib[2], hib[3], high_ok)
    a1.edge(False)
    b0.edge(True)
    vo, vz, _, total = second(a2, a1, a3, False, mz, to_below)
    put(1, 0, blocks, vo, vz, total)
    vo, vz = edge_own(a1, 1.0 - a2.z1, a2.z1, b0.x1, False, mz)
    put(1, 1, blocks, vo, vz, edge_total(a1, mz))
    vx, vd = edge_spill(b0, a1, True)
    put(1, 2, blocks, vx, vd, edge_total(b0, mb))
    outer = jnp.where(high_ok, hib[4], 1.0)
    vx, total = second_spill(hib[5], b0, outer, to_above)
    put(1, 3, blocks, vx, None, total)
    send(0, 0, width - 2)
    send(1, layers - 1, 2 * width - 2)
    for c in sends:
        c.wait()


def swaps(firsts):
    return [pair for i in firsts for pair in ((i, i + 1), (i + 1, i))]


def on_device(trans_east, trans_north, trans_up, storage, support_reach, *, axis, count):
    layers, blocks, _ = support_reach.shape
    n, rows, lanes = trans_east.shape
    width = n // layers
    f32 = jnp.float32
    anywhere = pl.BlockSpec(memory_space=pl.ANY)
    vmem = pl.BlockSpec(memory_space=pltpu.VMEM)
    params = pltpu.CompilerParams(vmem_limit_bytes=16 * 2**20)
    outside = tuple(
        pltpu.with_memory_space_constraint(x, pltpu.HBM)
        for x in (trans_east, trans_north, trans_up, storage)
    )
    reach = jnp.transpose(support_reach, (0, 2, 1))
    reach = pltpu.with_memory_space_constraint(reach, pltpu.HBM)
    tiles = 1 + 6 * rows // TAIL
    msg_a, msg_b, masks, faces = pl.pallas_call(
        functools.partial(pack_kernel, n, width, axis),
        out_shape=(
            pltpu.VMEM((tiles + 1, TAIL, lanes), f32),
            pltpu.VMEM((tiles, TAIL, lanes), f32),
            pltpu.VMEM((layers, TAIL, lanes), f32),
            pltpu.VMEM((4, n, rows, lanes), f32),
        ),
        in_specs=[anywhere] * 5,
        out_specs=(vmem,) * 4,
        scratch_shapes=[
            pltpu.VMEM((layers, 4, blocks), jnp.int32),
            pltpu.SemaphoreType.DMA((13,)),
        ],
        compiler_params=params,
        name="pack",
    )(*outside, reach)
    got_a = lax.ppermute(msg_a, axis, swaps(range(0, count - 1, 2)))
    got_b = lax.ppermute(msg_b, axis, swaps(range(1, count - 1, 2)))

    out_shape = jax.ShapeDtypeStruct((layers, blocks, 3 * width, rows, lanes), f32)
    sends = layers * ((width - 4) // CHUNK) + 2 * (layers - 1)
    bulk = pl.pallas_call(
        functools.partial(bulk_kernel, width, blocks),
        out_shape=out_shape,
        in_specs=[vmem] * 2,
        out_specs=anywhere,
        scratch_shapes=[
            pltpu.VMEM((width - 2, rows, lanes), f32),
            pltpu.VMEM((layers, blocks, width + 4, rows, lanes), f32),
            pltpu.SemaphoreType.DMA((2 * layers * blocks + sends * SPLIT,)),
        ],
        compiler_params=params,
        cost_estimate=pl.CostEstimate(flops=10**7, bytes_accessed=7 * 10**6, transcendentals=0),
        name="bulk",
    )(faces, masks)
    return pl.pallas_call(
        functools.partial(edge_kernel, width, blocks, axis, count),
        out_shape=out_shape,
        in_specs=[vmem] * 4 + [anywhere],
        out_specs=anywhere,
        scratch_shapes=[
            pltpu.VMEM((2, blocks, 4, rows, lanes), f32),
            pltpu.SemaphoreType.DMA((2 * blocks,)),
        ],
        input_output_aliases={4: 0},
        compiler_params=params,
        cost_estimate=pl.CostEstimate(flops=10**6, bytes_accessed=10**6, transcendentals=0),
        name="edges",
    )(faces, masks, got_a, got_b, bulk)


def solution(mesh):
    spread = P(("groups", "blk"))
    return jax.shard_map(
        functools.partial(on_device, axis="blk", count=mesh.shape["blk"]),
        mesh=mesh,
        in_specs=(spread,) * 5,
        out_specs=spread,
        check_vma=False,
    )
```

```python
import functools

import jax
import jax.numpy as jnp
from jax import lax
from jax.experimental import pallas as pl
from jax.experimental.pallas import tpu as pltpu
from jax.sharding import PartitionSpec as P


TAIL = 8
CHUNK = 12
SPLIT = 2


class Lanes:
    def __init__(self, shape, width):
        lane = lax.broadcasted_iota(jnp.int32, shape, 1)
        self.width = width
        self.lanes = shape[1]
        self.rows = shape[0]
        self.lane = lane
        self.block = lane // width
        self.local = lane - self.block * width
        self.first = self.local == 0
        self.last = self.local == width - 1
        self.upper = self.local >= width // 2
        self.other = jnp.where(self.upper, self.block + 1, self.block - 1)
        self.row0 = lax.broadcasted_iota(jnp.int32, shape, 0) == 0
        self.lane0 = lane == 0

    def zm(self, v):
        return pltpu.roll(v, 1, 1)

    def zp(self, v):
        return pltpu.roll(v, self.lanes - 1, 1)

    def ym(self, v):
        return pltpu.roll(v, 1, 0)

    def yp(self, v):
        return pltpu.roll(v, self.rows - 1, 0)


class Plane:
    def __init__(self, ln, tx, txn, ty, tz, s, valid=None):
        self.ln = ln
        self.tx, self.txn = tx, txn
        self.ty = jnp.where(ln.row0, 0.0, ty)
        self.tz = jnp.where(ln.lane0, 0.0, tz)
        self.typ = ln.yp(self.ty)
        self.tzp = ln.zp(self.tz)
        e = s * (1.0 / 3.0) + ((tx + txn) + (self.ty + self.typ) + (self.tz + self.tzp))
        if valid is not None:
            e = jnp.where(valid, e, 1.0)
        self.half = 0.5 * e + s * (1.0 / 3.0)
        self.all = 1.5 * e
        self.q = 1.0 / self.all
        self.z1 = self.q * jnp.where(ln.first, self.tz, jnp.where(ln.last, self.tzp, 0.0))
        self.zm = ln.zm(self.z1)
        self.zp = ln.zp(self.z1)

    def toward(self, low):
        return self.tx if low else self.txn

    def inward(self, low):
        return self.txn if low else self.tx

    def edge(self, low):
        self.x1 = self.q * self.toward(low)
        self.o1 = 1.0 - self.z1 - self.x1

    def rim(self):
        return self.tz * self.zm + self.tzp * self.zp

    def along_y(self, v):
        return self.ty * self.ln.ym(v) + self.typ * self.ln.yp(v)


def plane_at(ln, faces, p):
    return Plane(ln, faces[0, p], faces[0, p + 1], faces[1, p], faces[2, p], faces[3, p])


def middle(p, below, above, mz):
    ln = p.ln
    vz = p.half * p.z1 + p.tx * below.z1 + p.txn * above.z1 + p.along_y(p.z1)
    vz = vz + p.tz * jnp.where(ln.first, 1.0 - p.zm, p.zm)
    vz = vz + p.tzp * jnp.where(ln.last, 1.0 - p.zp, p.zp)
    kept = vz * mz
    return p.all - vz, kept, p.all - (vz - kept)


def second(p, edge, inner, low, mz, mx):
    below, above = (edge, inner) if low else (inner, edge)
    ln = p.ln
    first_o = ln.zm(p.z1)
    vz = p.half * p.z1 + p.tx * below.z1 + p.txn * above.z1 + p.along_y(p.z1)
    vz = vz + p.tz * jnp.where(ln.first, 1.0 - first_o, first_o)
    vz = vz + p.tzp * jnp.where(ln.last, 1.0 - p.zp, p.zp)
    vx = p.toward(low) * edge.x1
    kept_z, kept_x = vz * mz, vx * mx
    total = p.all - (vz - kept_z) - (vx - kept_x)
    return p.all - vz - vx, kept_z, kept_x, total


def edge_own(p, inner_o1, inner_z1, outer_x1, low, mz):
    ln = p.ln
    om, op = ln.zm(p.o1), ln.zp(p.o1)
    vo = p.half * p.o1 + p.toward(low) * outer_x1 + p.inward(low) * inner_o1 + p.along_y(p.o1)
    vo = vo + p.tz * jnp.where(ln.first, p.zm, om) + p.tzp * jnp.where(ln.last, p.zp, op)
    vz = p.half * p.z1 + p.inward(low) * inner_z1 + p.along_y(p.z1)
    vz = vz + p.tz * jnp.where(ln.first, om, p.zm) + p.tzp * jnp.where(ln.last, op, p.zp)
    return vo, vz * mz


def edge_total(p, mz):
    rim = p.rim()
    return p.all - (rim - rim * mz)


def edge_spill(p, own, low):
    ln = p.ln
    xm, xp = ln.zm(p.x1), ln.zp(p.x1)
    face = p.toward(low)
    vx = p.half * p.x1 + face * own.o1 + p.along_y(p.x1)
    vx = vx + p.tz * jnp.where(ln.first, 0.0, xm) + p.tzp * jnp.where(ln.last, 0.0, xp)
    vd = face * own.z1 + p.tz * jnp.where(ln.first, xm, 0.0) + p.tzp * jnp.where(ln.last, xp, 0.0)
    return vx, vd


def work_side(ln, low, valid, faces, masks, msg, put):
    n, rows, lanes = faces.shape[1:]
    layers = masks.shape[0]

    def own(i, j):
        return faces[i, jnp.where(low, j, n - 1 - j)]

    def got(i, j):
        tiles = rows // TAIL
        return msg[pl.ds(1 + tiles * (2 * i + j), tiles)].reshape(rows, lanes)

    f1, f2, f3 = (faces[0, jnp.where(low, j, n - j)] for j in (1, 2, 3))
    f0 = jnp.where(valid, jnp.where(low, faces[0, 0], got(0, 0)), 0.0)
    g1 = jnp.where(low, got(0, 0), got(0, 1))
    g2 = jnp.where(low, got(0, 1), got(4, 0))
    a0 = Plane(ln, f0, f1, own(1, 0), own(2, 0), own(3, 0))
    a1 = Plane(ln, f1, f2, own(1, 1), own(2, 1), own(3, 1))
    a2 = Plane(ln, f2, f3, own(1, 2), own(2, 2), own(3, 2))
    b0 = Plane(ln, g1, f0, got(1, 0), got(2, 0), got(3, 0), valid)
    b1 = Plane(ln, g2, g1, got(1, 1), got(2, 1), got(3, 1), valid)
    mine = masks[jnp.where(low, 0, layers - 1)]
    mz, my_reach = mine[0:1], jnp.where(low, mine[1:2], mine[2:3])
    theirs = msg[0]
    mo, their_reach = theirs[0:1], jnp.where(low, theirs[2:3], theirs[1:2])
    a0.edge(True)
    b0.edge(False)
    vx = g1 * b0.x1
    kept = vx * my_reach
    put(0, kept, None, edge_total(b1, mo) - (vx - kept))
    vx, vd = edge_spill(b0, a0, False)
    put(1, vx, vd, edge_total(b0, mo))
    vo, vz = edge_own(a0, 1.0 - a1.z1, a1.z1, b0.x1, True, mz)
    put(2, vo, vz, edge_total(a0, mz))
    vo, vz, _, total = second(a1, a0, a2, True, mz, their_reach)
    put(3, vo, vz, total)


def store_side(ln, buf, low, blocks):
    def put(i, own, other, total):
        store(ln, buf, jnp.where(low, i, 3 - i), blocks, own, other, total)

    return put


def send_side(buf, out, low, width, sems):
    layers, blocks = out.shape[:2]
    layer = jnp.where(low, 0, layers - 1)
    start = jnp.where(low, width - 2, 2 * width - 2)
    for k in range(blocks):
        yield pltpu.make_async_copy(buf.at[k], out.at[layer, k, pl.ds(start, 4)], sems.at[k])


def store(ln, dst, plane, blocks, own, other, total):
    scale = 1.0 / total
    own = own * scale
    other = jnp.zeros_like(own) if other is None else other * scale
    for k in range(blocks):
        dst[k, plane] = jnp.where(ln.block == k, own, jnp.where(ln.other == k, other, 0.0))


def pack_kernel(
    n, width, axis, tx, ty, tz, s, reach, msg_a, msg_b, masks, faces, held_reach, sems
):
    layers, _, blocks = held_reach.shape
    lanes = masks.shape[-1]
    fetch = pltpu.make_async_copy(reach, held_reach, sems.at[4])
    fetch.start()
    copies = [
        pltpu.make_async_copy(a, faces.at[i], sems.at[i]) for i, a in enumerate((tx, ty, tz, s))
    ]
    for c in copies:
        c.start()
    masks[...] = jnp.zeros(masks.shape, jnp.float32)
    lane = lax.broadcasted_iota(jnp.int32, (4, lanes), 1)
    block = lane // width
    local = lane - block * width
    fetch.wait()
    for layer in range(layers):
        r = jnp.zeros((4, lanes), jnp.int32)
        for k in range(blocks):
            r = jnp.where(block == k, held_reach[layer, :, k : k + 1], r)
        low = pltpu.roll(r, width, 1)
        high = pltpu.roll(r, lanes - width, 1)
        near = jnp.where(
            local[0:1] < width // 2,
            jnp.where(low[3:4] >= local[0:1] + 1, 1.0, 0.0),
            jnp.where(high[2:3] >= width - local[0:1], 1.0, 0.0),
        )
        masks[layer, 0:1] = near
        masks[layer, 1:3] = jnp.where(r[0:2] >= 2, 1.0, 0.0)
    even = lax.rem(lax.axis_index(axis), 2) == 0

    def put(tile, up, down):
        up, down = (v.reshape(-1, TAIL, lanes) for v in (up, down))
        where = pl.ds(tile, up.shape[0])
        msg_a[where] = jnp.where(even, up, down)
        msg_b[where] = jnp.where(even, down, up)

    put(0, masks[layers - 1], masks[0])
    for c in copies:
        c.wait()
    for i in range(4):
        put(1 + 4 * i, faces[i, n - 1], faces[i, 0])
        put(3 + 4 * i, faces[i, n - 2], faces[i, 1])
    put(17, faces[0, n - 1], faces[0, 2])


def bulk_kernel(width, blocks, axis, count, faces, masks, msg, out, zeros, buf, side, sems, side_sems):
    layers = masks.shape[0]
    rows, lanes = faces.shape[2:]
    depth = zeros.shape[0]
    zeros[...] = jnp.zeros(zeros.shape, jnp.float32)

    def clears(k):
        for layer in range(layers):
            for side, start in enumerate((0, 3 * width - depth)):
                sem = sems.at[(layer * 2 + side) * blocks + k]
                yield pltpu.make_async_copy(zeros, out.at[layer, k, pl.ds(start, depth)], sem)

    def send(layer, start, planes, index):
        for i in range(SPLIT):
            few = pl.ds(i * (blocks // SPLIT), blocks // SPLIT)
            yield pltpu.make_async_copy(
                buf.at[layer, few, pl.ds(start, planes)],
                out.at[layer, few, pl.ds(width - 2 + start, planes)],
                sems.at[2 * layers * blocks + index * SPLIT + i],
            )

    @pl.loop(0, blocks)
    def _(k):
        for c in clears(k):
            c.start()

    ln = Lanes((rows, lanes), width)

    plane = functools.partial(plane_at, ln, faces)
    chunks = (width - 4) // CHUNK

    @pl.loop(0, layers * chunks)
    def _(i):
        layer = i // chunks
        first = 2 + (i - layer * chunks) * CHUNK
        planes = [plane(layer * width + first + j) for j in range(-1, CHUNK + 1)]
        mz = masks[layer, 0:1]
        for j in range(CHUNK):
            vo, vz, total = middle(planes[j + 1], planes[j], planes[j + 2], mz)
            store(ln, buf.at[layer], first + j + 2, blocks, vo, vz, total)
        for c in send(layer, first + 2, CHUNK, i):
            c.start()

    @pl.loop(1, layers)
    def _(layer):
        base = layer * width
        ma, mb = masks[layer - 1, 0:1], masks[layer, 0:1]
        to_above, to_below = masks[layer - 1, 2:3], masks[layer, 1:2]
        a3, a2, a1 = (plane(base - i) for i in (3, 2, 1))
        b0, b1, b2 = (plane(base + i) for i in (0, 1, 2))
        a1.edge(False)
        b0.edge(True)
        low = functools.partial(store, ln, buf.at[layer - 1])
        high = functools.partial(store, ln, buf.at[layer])
        vo, vz, vx, total = second(a2, a1, a3, False, ma, to_below)
        low(width, blocks, vo, vz, total)
        high(0, blocks, vx, None, total)
        vo, vz = edge_own(a1, 1.0 - a2.z1, a2.z1, b0.x1, False, ma)
        vx, vd = edge_spill(a1, b0, False)
        total = edge_total(a1, ma)
        low(width + 1, blocks, vo, vz, total)
        high(1, blocks, vx, vd, total)
        vo, vz = edge_own(b0, 1.0 - b1.z1, b1.z1, a1.x1, True, mb)
        vx, vd = edge_spill(b0, a1, True)
        total = edge_total(b0, mb)
        high(2, blocks, vo, vz, total)
        low(width + 2, blocks, vx, vd, total)
        vo, vz, vx, total = second(b1, b0, b2, True, mb, to_above)
        high(3, blocks, vo, vz, total)
        low(width + 3, blocks, vx, None, total)
        index = layers * chunks + 2 * (layer - 1)
        for c in send(layer - 1, width, 4, index):
            c.start()
        for c in send(layer, 0, 4, index + 1):
            c.start()

    me = lax.axis_index(axis)
    lower = lax.rem(me, 2) == 1
    work_side(ln, lower, lower | (me < count - 1), faces, masks, msg, store_side(ln, side, lower, blocks))
    for c in send_side(side, out, lower, width, side_sems):
        c.start()

    for layer in range(layers):
        for i in range(chunks):
            for c in send(layer, 4 + i * CHUNK, CHUNK, layer * chunks + i):
                c.wait()
    for layer in range(1, layers):
        index = layers * chunks + 2 * (layer - 1)
        for c in send(layer - 1, width, 4, index):
            c.wait()
        for c in send(layer, 0, 4, index + 1):
            c.wait()

    for c in send_side(side, out, lower, width, side_sems):
        c.wait()

    @pl.loop(0, blocks)
    def _(k):
        for c in clears(k):
            c.wait()


def edge_kernel(width, blocks, axis, count, faces, masks, msg, held, out, side, sems):
    del held
    me = lax.axis_index(axis)
    lower = lax.rem(me, 2) == 0
    valid = jnp.where(lower, me > 0, me < count - 1)
    ln = Lanes(faces.shape[2:], width)
    work_side(ln, lower, valid, faces, masks, msg, store_side(ln, side, lower, blocks))
    for c in send_side(side, out, lower, width, sems):
        c.start()
    for c in send_side(side, out, lower, width, sems):
        c.wait()


def swaps(firsts):
    return [pair for i in firsts for pair in ((i, i + 1), (i + 1, i))]


def on_device(trans_east, trans_north, trans_up, storage, support_reach, *, axis, count):
    layers, blocks, _ = support_reach.shape
    n, rows, lanes = trans_east.shape
    width = n // layers
    f32 = jnp.float32
    anywhere = pl.BlockSpec(memory_space=pl.ANY)
    vmem = pl.BlockSpec(memory_space=pltpu.VMEM)
    params = pltpu.CompilerParams(vmem_limit_bytes=16 * 2**20)
    outside = tuple(
        pltpu.with_memory_space_constraint(x, pltpu.HBM)
        for x in (trans_east, trans_north, trans_up, storage)
    )
    reach = jnp.transpose(support_reach, (0, 2, 1))
    reach = pltpu.with_memory_space_constraint(reach, pltpu.HBM)
    tiles = 1 + 9 * rows // TAIL
    msg_a, msg_b, masks, faces = pl.pallas_call(
        functools.partial(pack_kernel, n, width, axis),
        out_shape=(
            pltpu.VMEM((tiles + 1, TAIL, lanes), f32),
            pltpu.VMEM((tiles, TAIL, lanes), f32),
            pltpu.VMEM((layers, TAIL, lanes), f32),
            pltpu.VMEM((4, n, rows, lanes), f32),
        ),
        in_specs=[anywhere] * 5,
        out_specs=(vmem,) * 4,
        scratch_shapes=[
            pltpu.VMEM((layers, 4, blocks), jnp.int32),
            pltpu.SemaphoreType.DMA((5,)),
        ],
        compiler_params=params,
        name="pack",
    )(*outside, reach)
    got_a = lax.ppermute(msg_a, axis, swaps(range(0, count - 1, 2)))
    got_b = lax.ppermute(msg_b, axis, swaps(range(1, count - 1, 2)))

    out_shape = jax.ShapeDtypeStruct((layers, blocks, 3 * width, rows, lanes), f32)
    sends = layers * ((width - 4) // CHUNK) + 2 * (layers - 1)
    side = pltpu.VMEM((blocks, 4, rows, lanes), f32)
    bulk = pl.pallas_call(
        functools.partial(bulk_kernel, width, blocks, axis, count),
        out_shape=out_shape,
        in_specs=[vmem] * 3,
        out_specs=anywhere,
        scratch_shapes=[
            pltpu.VMEM((width - 2, rows, lanes), f32),
            pltpu.VMEM((layers, blocks, width + 4, rows, lanes), f32),
            side,
            pltpu.SemaphoreType.DMA((2 * layers * blocks + sends * SPLIT,)),
            pltpu.SemaphoreType.DMA((blocks,)),
        ],
        compiler_params=params,
        cost_estimate=pl.CostEstimate(flops=10**7, bytes_accessed=7 * 10**6, transcendentals=0),
        name="bulk",
    )(faces, masks, got_a)
    return pl.pallas_call(
        functools.partial(edge_kernel, width, blocks, axis, count),
        out_shape=out_shape,
        in_specs=[vmem] * 3 + [anywhere],
        out_specs=anywhere,
        scratch_shapes=[side, pltpu.SemaphoreType.DMA((blocks,))],
        input_output_aliases={3: 0},
        compiler_params=params,
        cost_estimate=pl.CostEstimate(flops=10**6, bytes_accessed=10**6, transcendentals=0),
        name="edges",
    )(faces, masks, got_b, bulk)


def solution(mesh):
    spread = P(("groups", "blk"))
    return jax.shard_map(
        functools.partial(on_device, axis="blk", count=mesh.shape["blk"]),
        mesh=mesh,
        in_specs=(spread,) * 5,
        out_specs=spread,
        check_vma=False,
    )
```

```python
import functools

import jax
import jax.numpy as jnp
from jax import lax
from jax.experimental import pallas as pl
from jax.experimental.pallas import tpu as pltpu
from jax.sharding import PartitionSpec as P


TAIL = 8
CHUNK = 12
EARLY = 1
SPLIT = 2


class Lanes:
    def __init__(self, shape, width):
        lane = lax.broadcasted_iota(jnp.int32, shape, 1)
        self.width = width
        self.lanes = shape[1]
        self.rows = shape[0]
        self.lane = lane
        self.block = lane // width
        self.local = lane - self.block * width
        self.first = self.local == 0
        self.last = self.local == width - 1
        self.upper = self.local >= width // 2
        self.other = jnp.where(self.upper, self.block + 1, self.block - 1)
        self.row0 = lax.broadcasted_iota(jnp.int32, shape, 0) == 0
        self.lane0 = lane == 0

    def zm(self, v):
        return pltpu.roll(v, 1, 1)

    def zp(self, v):
        return pltpu.roll(v, self.lanes - 1, 1)

    def ym(self, v):
        return pltpu.roll(v, 1, 0)

    def yp(self, v):
        return pltpu.roll(v, self.rows - 1, 0)


class Plane:
    def __init__(self, ln, tx, txn, ty, tz, s, valid=None):
        self.ln = ln
        self.tx, self.txn = tx, txn
        self.ty = jnp.where(ln.row0, 0.0, ty)
        self.tz = jnp.where(ln.lane0, 0.0, tz)
        self.typ = ln.yp(self.ty)
        self.tzp = ln.zp(self.tz)
        e = s * (1.0 / 3.0) + ((tx + txn) + (self.ty + self.typ) + (self.tz + self.tzp))
        if valid is not None:
            e = jnp.where(valid, e, 1.0)
        self.half = 0.5 * e + s * (1.0 / 3.0)
        self.all = 1.5 * e
        self.q = 1.0 / self.all
        self.z1 = self.q * jnp.where(ln.first, self.tz, jnp.where(ln.last, self.tzp, 0.0))
        self.zm = ln.zm(self.z1)
        self.zp = ln.zp(self.z1)

    def toward(self, low):
        return self.tx if low else self.txn

    def inward(self, low):
        return self.txn if low else self.tx

    def edge(self, low):
        self.x1 = self.q * self.toward(low)
        self.o1 = 1.0 - self.z1 - self.x1

    def rim(self):
        return self.tz * self.zm + self.tzp * self.zp

    def along_y(self, v):
        return self.ty * self.ln.ym(v) + self.typ * self.ln.yp(v)


def plane_at(ln, faces, p):
    return Plane(ln, faces[0, p], faces[0, p + 1], faces[1, p], faces[2, p], faces[3, p])


def middle(p, below, above, mz):
    ln = p.ln
    vz = p.half * p.z1 + p.tx * below.z1 + p.txn * above.z1 + p.along_y(p.z1)
    vz = vz + p.tz * jnp.where(ln.first, 1.0 - p.zm, p.zm)
    vz = vz + p.tzp * jnp.where(ln.last, 1.0 - p.zp, p.zp)
    kept = vz * mz
    return p.all - vz, kept, p.all - (vz - kept)


def second(p, edge, inner, low, mz, mx):
    below, above = (edge, inner) if low else (inner, edge)
    ln = p.ln
    first_o = ln.zm(p.z1)
    vz = p.half * p.z1 + p.tx * below.z1 + p.txn * above.z1 + p.along_y(p.z1)
    vz = vz + p.tz * jnp.where(ln.first, 1.0 - first_o, first_o)
    vz = vz + p.tzp * jnp.where(ln.last, 1.0 - p.zp, p.zp)
    vx = p.toward(low) * edge.x1
    kept_z, kept_x = vz * mz, vx * mx
    total = p.all - (vz - kept_z) - (vx - kept_x)
    return p.all - vz - vx, kept_z, kept_x, total


def edge_own(p, inner_o1, inner_z1, outer_x1, low, mz):
    ln = p.ln
    om, op = ln.zm(p.o1), ln.zp(p.o1)
    vo = p.half * p.o1 + p.toward(low) * outer_x1 + p.inward(low) * inner_o1 + p.along_y(p.o1)
    vo = vo + p.tz * jnp.where(ln.first, p.zm, om) + p.tzp * jnp.where(ln.last, p.zp, op)
    vz = p.half * p.z1 + p.inward(low) * inner_z1 + p.along_y(p.z1)
    vz = vz + p.tz * jnp.where(ln.first, om, p.zm) + p.tzp * jnp.where(ln.last, op, p.zp)
    return vo, vz * mz


def edge_total(p, mz):
    rim = p.rim()
    return p.all - (rim - rim * mz)


def edge_spill(p, own, low):
    ln = p.ln
    xm, xp = ln.zm(p.x1), ln.zp(p.x1)
    face = p.toward(low)
    vx = p.half * p.x1 + face * own.o1 + p.along_y(p.x1)
    vx = vx + p.tz * jnp.where(ln.first, 0.0, xm) + p.tzp * jnp.where(ln.last, 0.0, xp)
    vd = face * own.z1 + p.tz * jnp.where(ln.first, xm, 0.0) + p.tzp * jnp.where(ln.last, xp, 0.0)
    return vx, vd


def work_side(ln, low, valid, faces, masks, msg, put):
    n, rows, lanes = faces.shape[1:]
    layers = masks.shape[0]

    def own(i, j):
        return faces[i, jnp.where(low, j, n - 1 - j)]

    def got(i, j):
        tiles = rows // TAIL
        return msg[pl.ds(1 + tiles * (2 * i + j), tiles)].reshape(rows, lanes)

    f1, f2, f3 = (faces[0, jnp.where(low, j, n - j)] for j in (1, 2, 3))
    f0 = jnp.where(valid, jnp.where(low, faces[0, 0], got(0, 0)), 0.0)
    g1 = jnp.where(low, got(0, 0), got(0, 1))
    g2 = jnp.where(low, got(0, 1), got(4, 0))
    a0 = Plane(ln, f0, f1, own(1, 0), own(2, 0), own(3, 0))
    a1 = Plane(ln, f1, f2, own(1, 1), own(2, 1), own(3, 1))
    a2 = Plane(ln, f2, f3, own(1, 2), own(2, 2), own(3, 2))
    b0 = Plane(ln, g1, f0, got(1, 0), got(2, 0), got(3, 0), valid)
    b1 = Plane(ln, g2, g1, got(1, 1), got(2, 1), got(3, 1), valid)
    mine = masks[jnp.where(low, 0, layers - 1)]
    mz, my_reach = mine[0:1], jnp.where(low, mine[1:2], mine[2:3])
    theirs = msg[0]
    mo, their_reach = theirs[0:1], jnp.where(low, theirs[2:3], theirs[1:2])
    a0.edge(True)
    b0.edge(False)
    vx = g1 * b0.x1
    kept = vx * my_reach
    put(0, kept, None, edge_total(b1, mo) - (vx - kept))
    vx, vd = edge_spill(b0, a0, False)
    put(1, vx, vd, edge_total(b0, mo))
    vo, vz = edge_own(a0, 1.0 - a1.z1, a1.z1, b0.x1, True, mz)
    put(2, vo, vz, edge_total(a0, mz))
    vo, vz, _, total = second(a1, a0, a2, True, mz, their_reach)
    put(3, vo, vz, total)


def store_side(ln, buf, low, blocks):
    def put(i, own, other, total):
        store(ln, buf, jnp.where(low, i, 3 - i), blocks, own, other, total)

    return put


def send_side(buf, out, low, width, sems):
    layers, blocks = out.shape[:2]
    layer = jnp.where(low, 0, layers - 1)
    start = jnp.where(low, width - 2, 2 * width - 2)
    for k in range(blocks):
        yield pltpu.make_async_copy(buf.at[k], out.at[layer, k, pl.ds(start, 4)], sems.at[k])


def store(ln, dst, plane, blocks, own, other, total):
    scale = 1.0 / total
    own = own * scale
    other = jnp.zeros_like(own) if other is None else other * scale
    for k in range(blocks):
        dst[k, plane] = jnp.where(ln.block == k, own, jnp.where(ln.other == k, other, 0.0))


def clear_copies(zeros, out, k, parts, sems):
    depth = zeros.shape[0]
    for i, part in enumerate(parts):
        layer, side = part // 2, part % 2
        start = side * (out.shape[2] - depth)
        sem = sems.at[i * out.shape[1] + k]
        yield pltpu.make_async_copy(zeros, out.at[layer, k, pl.ds(start, depth)], sem)


def pack_kernel(
    n, width, axis, tx, ty, tz, s, reach, msg_a, msg_b, masks, faces, out,
    held_reach, zeros, sems, clear_sems,
):
    layers, _, blocks = held_reach.shape
    lanes = masks.shape[-1]
    fetch = pltpu.make_async_copy(reach, held_reach, sems.at[4])
    fetch.start()
    copies = [
        pltpu.make_async_copy(a, faces.at[i], sems.at[i]) for i, a in enumerate((tx, ty, tz, s))
    ]
    for c in copies:
        c.start()
    zeros[...] = jnp.zeros(zeros.shape, jnp.float32)

    @pl.loop(0, blocks)
    def _(k):
        for c in clear_copies(zeros, out, k, range(EARLY), clear_sems):
            c.start()

    masks[...] = jnp.zeros(masks.shape, jnp.float32)
    lane = lax.broadcasted_iota(jnp.int32, (4, lanes), 1)
    block = lane // width
    local = lane - block * width
    fetch.wait()
    for layer in range(layers):
        r = jnp.zeros((4, lanes), jnp.int32)
        for k in range(blocks):
            r = jnp.where(block == k, held_reach[layer, :, k : k + 1], r)
        low = pltpu.roll(r, width, 1)
        high = pltpu.roll(r, lanes - width, 1)
        near = jnp.where(
            local[0:1] < width // 2,
            jnp.where(low[3:4] >= local[0:1] + 1, 1.0, 0.0),
            jnp.where(high[2:3] >= width - local[0:1], 1.0, 0.0),
        )
        masks[layer, 0:1] = near
        masks[layer, 1:3] = jnp.where(r[0:2] >= 2, 1.0, 0.0)
    even = lax.rem(lax.axis_index(axis), 2) == 0

    def put(tile, up, down):
        up, down = (v.reshape(-1, TAIL, lanes) for v in (up, down))
        where = pl.ds(tile, up.shape[0])
        msg_a[where] = jnp.where(even, up, down)
        msg_b[where] = jnp.where(even, down, up)

    put(0, masks[layers - 1], masks[0])
    for c in copies:
        c.wait()
    for i in range(4):
        put(1 + 4 * i, faces[i, n - 1], faces[i, 0])
        put(3 + 4 * i, faces[i, n - 2], faces[i, 1])
    put(17, faces[0, n - 1], faces[0, 2])

    @pl.loop(0, blocks)
    def _(k):
        for c in clear_copies(zeros, out, k, range(EARLY), clear_sems):
            c.wait()


def bulk_kernel(width, blocks, axis, count, faces, masks, msg, held, out, zeros, buf, side, sems, side_sems, clear_sems):
    layers = masks.shape[0]
    rows, lanes = faces.shape[2:]
    del held
    late = range(EARLY, 2 * layers)
    zeros[...] = jnp.zeros(zeros.shape, jnp.float32)

    def send(layer, start, planes, index):
        for i in range(SPLIT):
            few = pl.ds(i * (blocks // SPLIT), blocks // SPLIT)
            yield pltpu.make_async_copy(
                buf.at[layer, few, pl.ds(start, planes)],
                out.at[layer, few, pl.ds(width - 2 + start, planes)],
                sems.at[index * SPLIT + i],
            )

    @pl.loop(0, blocks)
    def _(k):
        for c in clear_copies(zeros, out, k, late, clear_sems):
            c.start()

    ln = Lanes((rows, lanes), width)

    plane = functools.partial(plane_at, ln, faces)
    chunks = (width - 4) // CHUNK

    @pl.loop(0, layers * chunks)
    def _(i):
        layer = i // chunks
        first = 2 + (i - layer * chunks) * CHUNK
        planes = [plane(layer * width + first + j) for j in range(-1, CHUNK + 1)]
        mz = masks[layer, 0:1]
        for j in range(CHUNK):
            vo, vz, total = middle(planes[j + 1], planes[j], planes[j + 2], mz)
            store(ln, buf.at[layer], first + j + 2, blocks, vo, vz, total)
        for c in send(layer, first + 2, CHUNK, i):
            c.start()

    @pl.loop(1, layers)
    def _(layer):
        base = layer * width
        ma, mb = masks[layer - 1, 0:1], masks[layer, 0:1]
        to_above, to_below = masks[layer - 1, 2:3], masks[layer, 1:2]
        a3, a2, a1 = (plane(base - i) for i in (3, 2, 1))
        b0, b1, b2 = (plane(base + i) for i in (0, 1, 2))
        a1.edge(False)
        b0.edge(True)
        low = functools.partial(store, ln, buf.at[layer - 1])
        high = functools.partial(store, ln, buf.at[layer])
        vo, vz, vx, total = second(a2, a1, a3, False, ma, to_below)
        low(width, blocks, vo, vz, total)
        high(0, blocks, vx, None, total)
        vo, vz = edge_own(a1, 1.0 - a2.z1, a2.z1, b0.x1, False, ma)
        vx, vd = edge_spill(a1, b0, False)
        total = edge_total(a1, ma)
        low(width + 1, blocks, vo, vz, total)
        high(1, blocks, vx, vd, total)
        vo, vz = edge_own(b0, 1.0 - b1.z1, b1.z1, a1.x1, True, mb)
        vx, vd = edge_spill(b0, a1, True)
        total = edge_total(b0, mb)
        high(2, blocks, vo, vz, total)
        low(width + 2, blocks, vx, vd, total)
        vo, vz, vx, total = second(b1, b0, b2, True, mb, to_above)
        high(3, blocks, vo, vz, total)
        low(width + 3, blocks, vx, None, total)
        index = layers * chunks + 2 * (layer - 1)
        for c in send(layer - 1, width, 4, index):
            c.start()
        for c in send(layer, 0, 4, index + 1):
            c.start()

    me = lax.axis_index(axis)
    lower = lax.rem(me, 2) == 1
    work_side(ln, lower, lower | (me < count - 1), faces, masks, msg, store_side(ln, side, lower, blocks))
    for c in send_side(side, out, lower, width, side_sems):
        c.start()

    for layer in range(layers):
        for i in range(chunks):
            for c in send(layer, 4 + i * CHUNK, CHUNK, layer * chunks + i):
                c.wait()
    for layer in range(1, layers):
        index = layers * chunks + 2 * (layer - 1)
        for c in send(layer - 1, width, 4, index):
            c.wait()
        for c in send(layer, 0, 4, index + 1):
            c.wait()

    for c in send_side(side, out, lower, width, side_sems):
        c.wait()

    @pl.loop(0, blocks)
    def _(k):
        for c in clear_copies(zeros, out, k, late, clear_sems):
            c.wait()


def edge_kernel(width, blocks, axis, count, faces, masks, msg, held, out, side, sems):
    del held
    me = lax.axis_index(axis)
    lower = lax.rem(me, 2) == 0
    valid = jnp.where(lower, me > 0, me < count - 1)
    ln = Lanes(faces.shape[2:], width)
    work_side(ln, lower, valid, faces, masks, msg, store_side(ln, side, lower, blocks))
    for c in send_side(side, out, lower, width, sems):
        c.start()
    for c in send_side(side, out, lower, width, sems):
        c.wait()


def swaps(firsts):
    return [pair for i in firsts for pair in ((i, i + 1), (i + 1, i))]


def on_device(trans_east, trans_north, trans_up, storage, support_reach, *, axis, count):
    layers, blocks, _ = support_reach.shape
    n, rows, lanes = trans_east.shape
    width = n // layers
    f32 = jnp.float32
    anywhere = pl.BlockSpec(memory_space=pl.ANY)
    vmem = pl.BlockSpec(memory_space=pltpu.VMEM)
    params = pltpu.CompilerParams(vmem_limit_bytes=16 * 2**20)
    outside = tuple(
        pltpu.with_memory_space_constraint(x, pltpu.HBM)
        for x in (trans_east, trans_north, trans_up, storage)
    )
    reach = jnp.transpose(support_reach, (0, 2, 1))
    reach = pltpu.with_memory_space_constraint(reach, pltpu.HBM)
    tiles = 1 + 9 * rows // TAIL
    out_shape = jax.ShapeDtypeStruct((layers, blocks, 3 * width, rows, lanes), f32)
    zeros = pltpu.VMEM((width - 2, rows, lanes), f32)
    msg_a, msg_b, masks, faces, cleared = pl.pallas_call(
        functools.partial(pack_kernel, n, width, axis),
        out_shape=(
            pltpu.VMEM((tiles + 1, TAIL, lanes), f32),
            pltpu.VMEM((tiles, TAIL, lanes), f32),
            pltpu.VMEM((layers, TAIL, lanes), f32),
            pltpu.VMEM((4, n, rows, lanes), f32),
            out_shape,
        ),
        in_specs=[anywhere] * 5,
        out_specs=(vmem,) * 4 + (anywhere,),
        scratch_shapes=[
            pltpu.VMEM((layers, 4, blocks), jnp.int32),
            zeros,
            pltpu.SemaphoreType.DMA((5,)),
            pltpu.SemaphoreType.DMA((EARLY * blocks,)),
        ],
        compiler_params=params,
        name="pack",
    )(*outside, reach)
    got_a = lax.ppermute(msg_a, axis, swaps(range(0, count - 1, 2)))
    got_b = lax.ppermute(msg_b, axis, swaps(range(1, count - 1, 2)))

    sends = layers * ((width - 4) // CHUNK) + 2 * (layers - 1)
    side = pltpu.VMEM((blocks, 4, rows, lanes), f32)
    bulk = pl.pallas_call(
        functools.partial(bulk_kernel, width, blocks, axis, count),
        out_shape=out_shape,
        in_specs=[vmem] * 3 + [anywhere],
        out_specs=anywhere,
        scratch_shapes=[
            zeros,
            pltpu.VMEM((layers, blocks, width + 4, rows, lanes), f32),
            side,
            pltpu.SemaphoreType.DMA((sends * SPLIT,)),
            pltpu.SemaphoreType.DMA((blocks,)),
            pltpu.SemaphoreType.DMA(((2 * layers - EARLY) * blocks,)),
        ],
        input_output_aliases={3: 0},
        compiler_params=params,
        cost_estimate=pl.CostEstimate(flops=10**7, bytes_accessed=7 * 10**6, transcendentals=0),
        name="bulk",
    )(faces, masks, got_a, cleared)
    return pl.pallas_call(
        functools.partial(edge_kernel, width, blocks, axis, count),
        out_shape=out_shape,
        in_specs=[vmem] * 3 + [anywhere],
        out_specs=anywhere,
        scratch_shapes=[side, pltpu.SemaphoreType.DMA((blocks,))],
        input_output_aliases={3: 0},
        compiler_params=params,
        cost_estimate=pl.CostEstimate(flops=10**6, bytes_accessed=10**6, transcendentals=0),
        name="edges",
    )(faces, masks, got_b, bulk)


def solution(mesh):
    spread = P(("groups", "blk"))
    return jax.shard_map(
        functools.partial(on_device, axis="blk", count=mesh.shape["blk"]),
        mesh=mesh,
        in_specs=(spread,) * 5,
        out_specs=spread,
        check_vma=False,
    )
```

```python
import functools

import jax
import jax.numpy as jnp
from jax import lax
from jax.experimental import pallas as pl
from jax.experimental.pallas import tpu as pltpu
from jax.sharding import PartitionSpec as P


TAIL = 8
CHUNK = 12
SPLIT = 2


class Lanes:
    def __init__(self, shape, width):
        lane = lax.broadcasted_iota(jnp.int32, shape, 1)
        self.width = width
        self.lanes = shape[1]
        self.rows = shape[0]
        self.lane = lane
        self.block = lane // width
        self.local = lane - self.block * width
        self.first = self.local == 0
        self.last = self.local == width - 1
        self.upper = self.local >= width // 2
        self.other = jnp.where(self.upper, self.block + 1, self.block - 1)
        self.row0 = lax.broadcasted_iota(jnp.int32, shape, 0) == 0
        self.lane0 = lane == 0

    def zm(self, v):
        return pltpu.roll(v, 1, 1)

    def zp(self, v):
        return pltpu.roll(v, self.lanes - 1, 1)

    def ym(self, v):
        return pltpu.roll(v, 1, 0)

    def yp(self, v):
        return pltpu.roll(v, self.rows - 1, 0)


class Plane:
    def __init__(self, ln, tx, txn, ty, tz, s, valid=None):
        self.ln = ln
        self.tx, self.txn = tx, txn
        self.ty = jnp.where(ln.row0, 0.0, ty)
        self.tz = jnp.where(ln.lane0, 0.0, tz)
        self.typ = ln.yp(self.ty)
        self.tzp = ln.zp(self.tz)
        e = s * (1.0 / 3.0) + ((tx + txn) + (self.ty + self.typ) + (self.tz + self.tzp))
        if valid is not None:
            e = jnp.where(valid, e, 1.0)
        self.half = 0.5 * e + s * (1.0 / 3.0)
        self.all = 1.5 * e
        self.q = 1.0 / self.all
        self.z1 = self.q * jnp.where(ln.first, self.tz, jnp.where(ln.last, self.tzp, 0.0))
        self.zm = ln.zm(self.z1)
        self.zp = ln.zp(self.z1)

    def toward(self, low):
        return self.tx if low else self.txn

    def inward(self, low):
        return self.txn if low else self.tx

    def edge(self, low):
        self.x1 = self.q * self.toward(low)
        self.o1 = 1.0 - self.z1 - self.x1

    def rim(self):
        return self.tz * self.zm + self.tzp * self.zp

    def along_y(self, v):
        return self.ty * self.ln.ym(v) + self.typ * self.ln.yp(v)


def plane_at(ln, faces, p):
    return Plane(ln, faces[0, p], faces[0, p + 1], faces[1, p], faces[2, p], faces[3, p])


def middle(p, below, above, mz):
    ln = p.ln
    vz = p.half * p.z1 + p.tx * below.z1 + p.txn * above.z1 + p.along_y(p.z1)
    vz = vz + p.tz * jnp.where(ln.first, 1.0 - p.zm, p.zm)
    vz = vz + p.tzp * jnp.where(ln.last, 1.0 - p.zp, p.zp)
    kept = vz * mz
    return p.all - vz, kept, p.all - (vz - kept)


def second(p, edge, inner, low, mz, mx):
    below, above = (edge, inner) if low else (inner, edge)
    ln = p.ln
    first_o = ln.zm(p.z1)
    vz = p.half * p.z1 + p.tx * below.z1 + p.txn * above.z1 + p.along_y(p.z1)
    vz = vz + p.tz * jnp.where(ln.first, 1.0 - first_o, first_o)
    vz = vz + p.tzp * jnp.where(ln.last, 1.0 - p.zp, p.zp)
    vx = p.toward(low) * edge.x1
    kept_z, kept_x = vz * mz, vx * mx
    total = p.all - (vz - kept_z) - (vx - kept_x)
    return p.all - vz - vx, kept_z, kept_x, total


def edge_own(p, inner_o1, inner_z1, outer_x1, low, mz):
    ln = p.ln
    om, op = ln.zm(p.o1), ln.zp(p.o1)
    vo = p.half * p.o1 + p.toward(low) * outer_x1 + p.inward(low) * inner_o1 + p.along_y(p.o1)
    vo = vo + p.tz * jnp.where(ln.first, p.zm, om) + p.tzp * jnp.where(ln.last, p.zp, op)
    vz = p.half * p.z1 + p.inward(low) * inner_z1 + p.along_y(p.z1)
    vz = vz + p.tz * jnp.where(ln.first, om, p.zm) + p.tzp * jnp.where(ln.last, op, p.zp)
    return vo, vz * mz


def edge_total(p, mz):
    rim = p.rim()
    return p.all - (rim - rim * mz)


def edge_spill(p, own, low):
    ln = p.ln
    xm, xp = ln.zm(p.x1), ln.zp(p.x1)
    face = p.toward(low)
    vx = p.half * p.x1 + face * own.o1 + p.along_y(p.x1)
    vx = vx + p.tz * jnp.where(ln.first, 0.0, xm) + p.tzp * jnp.where(ln.last, 0.0, xp)
    vd = face * own.z1 + p.tz * jnp.where(ln.first, xm, 0.0) + p.tzp * jnp.where(ln.last, xp, 0.0)
    return vx, vd


def work_side(ln, low, valid, faces, masks, msg, put):
    n, rows, lanes = faces.shape[1:]
    layers = masks.shape[0]

    def own(i, j):
        return faces[i, jnp.where(low, j, n - 1 - j)]

    def got(i, j):
        tiles = rows // TAIL
        return msg[pl.ds(1 + tiles * (2 * i + j), tiles)].reshape(rows, lanes)

    f1, f2, f3 = (faces[0, jnp.where(low, j, n - j)] for j in (1, 2, 3))
    f0 = jnp.where(valid, jnp.where(low, faces[0, 0], got(0, 0)), 0.0)
    g1 = jnp.where(low, got(0, 0), got(0, 1))
    g2 = jnp.where(low, got(0, 1), got(4, 0))
    a0 = Plane(ln, f0, f1, own(1, 0), own(2, 0), own(3, 0))
    a1 = Plane(ln, f1, f2, own(1, 1), own(2, 1), own(3, 1))
    a2 = Plane(ln, f2, f3, own(1, 2), own(2, 2), own(3, 2))
    b0 = Plane(ln, g1, f0, got(1, 0), got(2, 0), got(3, 0), valid)
    b1 = Plane(ln, g2, g1, got(1, 1), got(2, 1), got(3, 1), valid)
    mine = masks[jnp.where(low, 0, layers - 1)]
    mz, my_reach = mine[0:1], jnp.where(low, mine[1:2], mine[2:3])
    theirs = msg[0]
    mo, their_reach = theirs[0:1], jnp.where(low, theirs[2:3], theirs[1:2])
    a0.edge(True)
    b0.edge(False)
    vx = g1 * b0.x1
    kept = vx * my_reach
    put(0, kept, None, edge_total(b1, mo) - (vx - kept))
    vx, vd = edge_spill(b0, a0, False)
    put(1, vx, vd, edge_total(b0, mo))
    vo, vz = edge_own(a0, 1.0 - a1.z1, a1.z1, b0.x1, True, mz)
    put(2, vo, vz, edge_total(a0, mz))
    vo, vz, _, total = second(a1, a0, a2, True, mz, their_reach)
    put(3, vo, vz, total)


def store_side(ln, buf, low, blocks):
    def put(i, own, other, total):
        store(ln, buf, jnp.where(low, i, 3 - i), blocks, own, other, total)

    return put


def send_side(buf, out, low, width, sems):
    layers, blocks = out.shape[:2]
    layer = jnp.where(low, 0, layers - 1)
    start = jnp.where(low, width - 2, 2 * width - 2)
    for k in range(blocks):
        yield pltpu.make_async_copy(buf.at[k], out.at[layer, k, pl.ds(start, 4)], sems.at[k])


def store(ln, dst, plane, blocks, own, other, total):
    scale = 1.0 / total
    own = own * scale
    other = jnp.zeros_like(own) if other is None else other * scale
    for k in range(blocks):
        dst[k, plane] = jnp.where(ln.block == k, own, jnp.where(ln.other == k, other, 0.0))


def pack_kernel(
    n, width, axis, tx, ty, tz, s, reach, msg_a, msg_b, masks, faces, held_reach, sems
):
    layers, _, blocks = held_reach.shape
    lanes = masks.shape[-1]
    fetch = pltpu.make_async_copy(reach, held_reach, sems.at[4])
    fetch.start()
    copies = [
        pltpu.make_async_copy(a, faces.at[i], sems.at[i]) for i, a in enumerate((tx, ty, tz, s))
    ]
    for c in copies:
        c.start()
    masks[...] = jnp.zeros(masks.shape, jnp.float32)
    lane = lax.broadcasted_iota(jnp.int32, (4, lanes), 1)
    block = lane // width
    local = lane - block * width
    fetch.wait()
    for layer in range(layers):
        r = jnp.zeros((4, lanes), jnp.int32)
        for k in range(blocks):
            r = jnp.where(block == k, held_reach[layer, :, k : k + 1], r)
        low = pltpu.roll(r, width, 1)
        high = pltpu.roll(r, lanes - width, 1)
        near = jnp.where(
            local[0:1] < width // 2,
            jnp.where(low[3:4] >= local[0:1] + 1, 1.0, 0.0),
            jnp.where(high[2:3] >= width - local[0:1], 1.0, 0.0),
        )
        masks[layer, 0:1] = near
        masks[layer, 1:3] = jnp.where(r[0:2] >= 2, 1.0, 0.0)
    even = lax.rem(lax.axis_index(axis), 2) == 0

    def put(tile, up, down):
        up, down = (v.reshape(-1, TAIL, lanes) for v in (up, down))
        where = pl.ds(tile, up.shape[0])
        msg_a[where] = jnp.where(even, up, down)
        msg_b[0, where] = msg_b[1, where] = jnp.where(even, down, up)

    put(0, masks[layers - 1], masks[0])
    for c in copies:
        c.wait()
    for i in range(4):
        put(1 + 4 * i, faces[i, n - 1], faces[i, 0])
        put(3 + 4 * i, faces[i, n - 2], faces[i, 1])
    put(17, faces[0, n - 1], faces[0, 2])


def bulk_kernel(width, blocks, axis, count, faces, masks, msg, out, zeros, buf, side, sems, side_sems):
    layers = masks.shape[0]
    rows, lanes = faces.shape[2:]
    depth = zeros.shape[0]
    zeros[...] = jnp.zeros(zeros.shape, jnp.float32)

    def clears(k):
        for layer in range(layers):
            for side, start in enumerate((0, 3 * width - depth)):
                sem = sems.at[(layer * 2 + side) * blocks + k]
                yield pltpu.make_async_copy(zeros, out.at[layer, k, pl.ds(start, depth)], sem)

    def send(layer, start, planes, index):
        for i in range(SPLIT):
            few = pl.ds(i * (blocks // SPLIT), blocks // SPLIT)
            yield pltpu.make_async_copy(
                buf.at[layer, few, pl.ds(start, planes)],
                out.at[layer, few, pl.ds(width - 2 + start, planes)],
                sems.at[2 * layers * blocks + index * SPLIT + i],
            )

    @pl.loop(0, blocks)
    def _(k):
        for c in clears(k):
            c.start()

    ln = Lanes((rows, lanes), width)

    plane = functools.partial(plane_at, ln, faces)
    chunks = (width - 4) // CHUNK

    @pl.loop(0, layers * chunks)
    def _(i):
        layer = i // chunks
        first = 2 + (i - layer * chunks) * CHUNK
        planes = [plane(layer * width + first + j) for j in range(-1, CHUNK + 1)]
        mz = masks[layer, 0:1]
        for j in range(CHUNK):
            vo, vz, total = middle(planes[j + 1], planes[j], planes[j + 2], mz)
            store(ln, buf.at[layer], first + j + 2, blocks, vo, vz, total)
        for c in send(layer, first + 2, CHUNK, i):
            c.start()

    @pl.loop(1, layers)
    def _(layer):
        base = layer * width
        ma, mb = masks[layer - 1, 0:1], masks[layer, 0:1]
        to_above, to_below = masks[layer - 1, 2:3], masks[layer, 1:2]
        a3, a2, a1 = (plane(base - i) for i in (3, 2, 1))
        b0, b1, b2 = (plane(base + i) for i in (0, 1, 2))
        a1.edge(False)
        b0.edge(True)
        low = functools.partial(store, ln, buf.at[layer - 1])
        high = functools.partial(store, ln, buf.at[layer])
        vo, vz, vx, total = second(a2, a1, a3, False, ma, to_below)
        low(width, blocks, vo, vz, total)
        high(0, blocks, vx, None, total)
        vo, vz = edge_own(a1, 1.0 - a2.z1, a2.z1, b0.x1, False, ma)
        vx, vd = edge_spill(a1, b0, False)
        total = edge_total(a1, ma)
        low(width + 1, blocks, vo, vz, total)
        high(1, blocks, vx, vd, total)
        vo, vz = edge_own(b0, 1.0 - b1.z1, b1.z1, a1.x1, True, mb)
        vx, vd = edge_spill(b0, a1, True)
        total = edge_total(b0, mb)
        high(2, blocks, vo, vz, total)
        low(width + 2, blocks, vx, vd, total)
        vo, vz, vx, total = second(b1, b0, b2, True, mb, to_above)
        high(3, blocks, vo, vz, total)
        low(width + 3, blocks, vx, None, total)
        index = layers * chunks + 2 * (layer - 1)
        for c in send(layer - 1, width, 4, index):
            c.start()
        for c in send(layer, 0, 4, index + 1):
            c.start()

    me = lax.axis_index(axis)
    lower = lax.rem(me, 2) == 1
    work_side(ln, lower, lower | (me < count - 1), faces, masks, msg, store_side(ln, side, lower, blocks))
    for c in send_side(side, out, lower, width, side_sems):
        c.start()

    for layer in range(layers):
        for i in range(chunks):
            for c in send(layer, 4 + i * CHUNK, CHUNK, layer * chunks + i):
                c.wait()
    for layer in range(1, layers):
        index = layers * chunks + 2 * (layer - 1)
        for c in send(layer - 1, width, 4, index):
            c.wait()
        for c in send(layer, 0, 4, index + 1):
            c.wait()

    for c in send_side(side, out, lower, width, side_sems):
        c.wait()

    @pl.loop(0, blocks)
    def _(k):
        for c in clears(k):
            c.wait()


def edge_kernel(width, blocks, axis, count, faces, masks, msg, held, out, side, sems):
    del held
    me = lax.axis_index(axis)
    lower = lax.rem(me, 2) == 0
    valid = jnp.where(lower, me > 0, me < count - 1)
    ln = Lanes(faces.shape[2:], width)
    work_side(ln, lower, valid, faces, masks, msg.at[jnp.where(lower, 0, 1)], store_side(ln, side, lower, blocks))
    for c in send_side(side, out, lower, width, sems):
        c.start()
    for c in send_side(side, out, lower, width, sems):
        c.wait()


def swaps(firsts):
    return [pair for i in firsts for pair in ((i, i + 1), (i + 1, i))]


def outside_pairs(parts, count):
    inner = [[p * count + i, p * count + i + 1] for p in range(parts) for i in range(1, count - 1, 2)]
    ends = [[p * count + i, (p + 1) * count + i] for p in range(0, parts, 2) for i in (0, count - 1)]
    return inner + ends


def on_device(trans_east, trans_north, trans_up, storage, support_reach, *, axis, count, parts):
    layers, blocks, _ = support_reach.shape
    n, rows, lanes = trans_east.shape
    width = n // layers
    f32 = jnp.float32
    anywhere = pl.BlockSpec(memory_space=pl.ANY)
    vmem = pl.BlockSpec(memory_space=pltpu.VMEM)
    params = pltpu.CompilerParams(vmem_limit_bytes=16 * 2**20)
    outside = tuple(
        pltpu.with_memory_space_constraint(x, pltpu.HBM)
        for x in (trans_east, trans_north, trans_up, storage)
    )
    reach = jnp.transpose(support_reach, (0, 2, 1))
    reach = pltpu.with_memory_space_constraint(reach, pltpu.HBM)
    tiles = 1 + 9 * rows // TAIL
    msg_a, msg_b, masks, faces = pl.pallas_call(
        functools.partial(pack_kernel, n, width, axis),
        out_shape=(
            pltpu.VMEM((tiles + 1, TAIL, lanes), f32),
            pltpu.VMEM((2, tiles, TAIL, lanes), f32),
            pltpu.VMEM((layers, TAIL, lanes), f32),
            pltpu.VMEM((4, n, rows, lanes), f32),
        ),
        in_specs=[anywhere] * 5,
        out_specs=(vmem,) * 4,
        scratch_shapes=[
            pltpu.VMEM((layers, 4, blocks), jnp.int32),
            pltpu.SemaphoreType.DMA((5,)),
        ],
        compiler_params=params,
        name="pack",
    )(*outside, reach)
    got_a = lax.ppermute(msg_a, axis, swaps(range(0, count - 1, 2)))
    got_b = lax.all_to_all(msg_b, ("groups", axis), 0, 0, axis_index_groups=outside_pairs(parts, count))

    out_shape = jax.ShapeDtypeStruct((layers, blocks, 3 * width, rows, lanes), f32)
    sends = layers * ((width - 4) // CHUNK) + 2 * (layers - 1)
    side = pltpu.VMEM((blocks, 4, rows, lanes), f32)
    bulk = pl.pallas_call(
        functools.partial(bulk_kernel, width, blocks, axis, count),
        out_shape=out_shape,
        in_specs=[vmem] * 3,
        out_specs=anywhere,
        scratch_shapes=[
            pltpu.VMEM((width - 2, rows, lanes), f32),
            pltpu.VMEM((layers, blocks, width + 4, rows, lanes), f32),
            side,
            pltpu.SemaphoreType.DMA((2 * layers * blocks + sends * SPLIT,)),
            pltpu.SemaphoreType.DMA((blocks,)),
        ],
        compiler_params=params,
        cost_estimate=pl.CostEstimate(flops=10**7, bytes_accessed=7 * 10**6, transcendentals=0),
        name="bulk",
    )(faces, masks, got_a)
    return pl.pallas_call(
        functools.partial(edge_kernel, width, blocks, axis, count),
        out_shape=out_shape,
        in_specs=[vmem] * 3 + [anywhere],
        out_specs=anywhere,
        scratch_shapes=[side, pltpu.SemaphoreType.DMA((blocks,))],
        input_output_aliases={3: 0},
        compiler_params=params,
        cost_estimate=pl.CostEstimate(flops=10**6, bytes_accessed=10**6, transcendentals=0),
        name="edges",
    )(faces, masks, got_b, bulk)


def solution(mesh):
    spread = P(("groups", "blk"))
    return jax.shard_map(
        functools.partial(on_device, axis="blk", count=mesh.shape["blk"], parts=mesh.shape["groups"]),
        mesh=mesh,
        in_specs=(spread,) * 5,
        out_specs=spread,
        check_vma=False,
    )
```

```python
import functools

import jax
import jax.numpy as jnp
from jax import lax
from jax.experimental import pallas as pl
from jax.experimental.pallas import tpu as pltpu
from jax.sharding import PartitionSpec as P


TAIL = 8
LAST_RUNS = 4


class Lanes:
    def __init__(self, shape, width):
        lane = lax.broadcasted_iota(jnp.int32, shape, 1)
        self.width = width
        self.lanes = shape[1]
        self.rows = shape[0]
        self.lane = lane
        self.block = lane // width
        self.local = lane - self.block * width
        self.first = self.local == 0
        self.last = self.local == width - 1
        self.upper = self.local >= width // 2
        self.other = jnp.where(self.upper, self.block + 1, self.block - 1)
        self.row0 = lax.broadcasted_iota(jnp.int32, shape, 0) == 0
        self.lane0 = lane == 0

    def zm(self, v):
        return pltpu.roll(v, 1, 1)

    def zp(self, v):
        return pltpu.roll(v, self.lanes - 1, 1)

    def ym(self, v):
        return pltpu.roll(v, 1, 0)

    def yp(self, v):
        return pltpu.roll(v, self.rows - 1, 0)


class Plane:
    def __init__(self, ln, tx, txn, ty, tz, s, valid=None):
        self.ln = ln
        self.tx, self.txn = tx, txn
        self.ty = jnp.where(ln.row0, 0.0, ty)
        self.tz = jnp.where(ln.lane0, 0.0, tz)
        self.typ = ln.yp(self.ty)
        self.tzp = ln.zp(self.tz)
        e = s * (1.0 / 3.0) + ((tx + txn) + (self.ty + self.typ) + (self.tz + self.tzp))
        if valid is not None:
            e = jnp.where(valid, e, 1.0)
        self.half = 0.5 * e + s * (1.0 / 3.0)
        self.all = 1.5 * e
        self.q = 1.0 / self.all
        self.z1 = self.q * jnp.where(ln.first, self.tz, jnp.where(ln.last, self.tzp, 0.0))
        self.zm = ln.zm(self.z1)
        self.zp = ln.zp(self.z1)

    def toward(self, low):
        return self.tx if low else self.txn

    def inward(self, low):
        return self.txn if low else self.tx

    def edge(self, low):
        self.x1 = self.q * self.toward(low)
        self.o1 = 1.0 - self.z1 - self.x1

    def rim(self):
        return self.tz * self.zm + self.tzp * self.zp

    def along_y(self, v):
        return self.ty * self.ln.ym(v) + self.typ * self.ln.yp(v)


def plane_at(ln, faces, p):
    return Plane(ln, faces[0, p], faces[0, p + 1], faces[1, p], faces[2, p], faces[3, p])


def middle(p, below, above, mz):
    ln = p.ln
    vz = p.half * p.z1 + p.tx * below.z1 + p.txn * above.z1 + p.along_y(p.z1)
    vz = vz + p.tz * jnp.where(ln.first, 1.0 - p.zm, p.zm)
    vz = vz + p.tzp * jnp.where(ln.last, 1.0 - p.zp, p.zp)
    kept = vz * mz
    return p.all - vz, kept, p.all - (vz - kept)


def second(p, edge, inner, low, mz, mx):
    below, above = (edge, inner) if low else (inner, edge)
    ln = p.ln
    first_o = ln.zm(p.z1)
    vz = p.half * p.z1 + p.tx * below.z1 + p.txn * above.z1 + p.along_y(p.z1)
    vz = vz + p.tz * jnp.where(ln.first, 1.0 - first_o, first_o)
    vz = vz + p.tzp * jnp.where(ln.last, 1.0 - p.zp, p.zp)
    vx = p.toward(low) * edge.x1
    kept_z, kept_x = vz * mz, vx * mx
    total = p.all - (vz - kept_z) - (vx - kept_x)
    return p.all - vz - vx, kept_z, kept_x, total


def edge_own(p, inner_o1, inner_z1, outer_x1, low, mz):
    ln = p.ln
    om, op = ln.zm(p.o1), ln.zp(p.o1)
    vo = p.half * p.o1 + p.toward(low) * outer_x1 + p.inward(low) * inner_o1 + p.along_y(p.o1)
    vo = vo + p.tz * jnp.where(ln.first, p.zm, om) + p.tzp * jnp.where(ln.last, p.zp, op)
    vz = p.half * p.z1 + p.inward(low) * inner_z1 + p.along_y(p.z1)
    vz = vz + p.tz * jnp.where(ln.first, om, p.zm) + p.tzp * jnp.where(ln.last, op, p.zp)
    return vo, vz * mz


def edge_total(p, mz):
    rim = p.rim()
    return p.all - (rim - rim * mz)


def edge_spill(p, own, low):
    ln = p.ln
    xm, xp = ln.zm(p.x1), ln.zp(p.x1)
    face = p.toward(low)
    vx = p.half * p.x1 + face * own.o1 + p.along_y(p.x1)
    vx = vx + p.tz * jnp.where(ln.first, 0.0, xm) + p.tzp * jnp.where(ln.last, 0.0, xp)
    vd = face * own.z1 + p.tz * jnp.where(ln.first, xm, 0.0) + p.tzp * jnp.where(ln.last, xp, 0.0)
    return vx, vd


def store(ln, dst, plane, blocks, own, other, total):
    scale = 1.0 / total
    own = own * scale
    other = jnp.zeros_like(own) if other is None else other * scale
    for k in range(blocks):
        dst[k, plane] = jnp.where(ln.block == k, own, jnp.where(ln.other == k, other, 0.0))


def work_side(ln, low, valid, faces, masks, msg, put):
    n, rows, lanes = faces.shape[1:]
    layers = masks.shape[0]

    def own(i, j):
        return faces[i, jnp.where(low, j, n - 1 - j)]

    def got(i, j):
        tiles = rows // TAIL
        return msg[pl.ds(1 + tiles * (2 * i + j), tiles)].reshape(rows, lanes)

    f1, f2, f3 = (faces[0, jnp.where(low, j, n - j)] for j in (1, 2, 3))
    f0 = jnp.where(valid, jnp.where(low, faces[0, 0], got(0, 0)), 0.0)
    g1 = jnp.where(low, got(0, 0), got(0, 1))
    g2 = jnp.where(low, got(0, 1), got(4, 0))
    a0 = Plane(ln, f0, f1, own(1, 0), own(2, 0), own(3, 0))
    a1 = Plane(ln, f1, f2, own(1, 1), own(2, 1), own(3, 1))
    a2 = Plane(ln, f2, f3, own(1, 2), own(2, 2), own(3, 2))
    b0 = Plane(ln, g1, f0, got(1, 0), got(2, 0), got(3, 0), valid)
    b1 = Plane(ln, g2, g1, got(1, 1), got(2, 1), got(3, 1), valid)
    mine = masks[jnp.where(low, 0, layers - 1)]
    mz, my_reach = mine[0:1], jnp.where(low, mine[1:2], mine[2:3])
    theirs = msg[0]
    mo, their_reach = theirs[0:1], jnp.where(low, theirs[2:3], theirs[1:2])
    a0.edge(True)
    b0.edge(False)
    vx = g1 * b0.x1
    kept = vx * my_reach
    put(0, kept, None, edge_total(b1, mo) - (vx - kept))
    vx, vd = edge_spill(b0, a0, False)
    put(1, vx, vd, edge_total(b0, mo))
    vo, vz = edge_own(a0, 1.0 - a1.z1, a1.z1, b0.x1, True, mz)
    put(2, vo, vz, edge_total(a0, mz))
    vo, vz, _, total = second(a1, a0, a2, True, mz, their_reach)
    put(3, vo, vz, total)


def store_side(ln, buf, low, blocks):
    def put(i, own, other, total):
        store(ln, buf, jnp.where(low, i, 3 - i), blocks, own, other, total)

    return put


def send_side(buf, out, low, width, layers, sems):
    blocks = buf.shape[0]
    layer = jnp.where(low, 0, layers - 1)
    start = jnp.where(low, width - 2, 2 * width - 2)
    for k in range(blocks):
        there = out.at[pl.ds((layer * blocks + k) * 3 * width + start, 4)]
        yield pltpu.make_async_copy(buf.at[k], there, sems.at[k])


def zero_runs(bases, width):
    box, far = 3 * width, width - 2
    return [(0, far)] + [(b * box + 2 * width + 2, 2 * far if b < bases - 1 else far) for b in range(bases)]


def zero_copies(zeros, out, runs, sems):
    return [
        pltpu.make_async_copy(zeros.at[pl.ds(0, count)], out.at[pl.ds(start, count)], sems.at[i])
        for i, (start, count) in enumerate(runs)
    ]


def pack_kernel(
    n, width, axis, tx, ty, tz, s, reach, msg_a, msg_b, masks, faces, held_reach, sems
):
    layers, _, blocks = held_reach.shape
    lanes = masks.shape[-1]
    fetch = pltpu.make_async_copy(reach, held_reach, sems.at[4])
    fetch.start()
    copies = [
        pltpu.make_async_copy(a, faces.at[i], sems.at[i]) for i, a in enumerate((tx, ty, tz, s))
    ]
    for c in copies:
        c.start()
    masks[...] = jnp.zeros(masks.shape, jnp.float32)
    lane = lax.broadcasted_iota(jnp.int32, (4, lanes), 1)
    block = lane // width
    local = lane - block * width
    fetch.wait()
    for layer in range(layers):
        r = jnp.zeros((4, lanes), jnp.int32)
        for k in range(blocks):
            r = jnp.where(block == k, held_reach[layer, :, k : k + 1], r)
        low = pltpu.roll(r, width, 1)
        high = pltpu.roll(r, lanes - width, 1)
        near = jnp.where(
            local[0:1] < width // 2,
            jnp.where(low[3:4] >= local[0:1] + 1, 1.0, 0.0),
            jnp.where(high[2:3] >= width - local[0:1], 1.0, 0.0),
        )
        masks[layer, 0:1] = near
        masks[layer, 1:3] = jnp.where(r[0:2] >= 2, 1.0, 0.0)
    even = lax.rem(lax.axis_index(axis), 2) == 0

    def put(tile, up, down):
        up, down = (v.reshape(-1, TAIL, lanes) for v in (up, down))
        where = pl.ds(tile, up.shape[0])
        msg_a[where] = jnp.where(even, up, down)
        msg_b[where] = jnp.where(even, down, up)

    put(0, masks[layers - 1], masks[0])
    for c in copies:
        c.wait()
    for i in range(4):
        put(1 + 4 * i, faces[i, n - 1], faces[i, 0])
        put(3 + 4 * i, faces[i, n - 2], faces[i, 1])
    put(17, faces[0, n - 1], faces[0, 2])


def bulk_kernel(
    width, blocks, axis, count, faces, masks, msg, out, zeros, buf, side, sems, side_sems, zero_sems
):
    layers = masks.shape[0]
    rows, lanes = faces.shape[2:]
    runs = zero_runs(layers * blocks, width)
    clears = zero_copies(zeros, out, runs[: len(runs) - LAST_RUNS], zero_sems)
    zeros[...] = jnp.zeros(zeros.shape, jnp.float32)
    for c in clears:
        c.start()
    ln = Lanes((rows, lanes), width)
    plane = functools.partial(plane_at, ln, faces)

    def send(layer, start, planes, slot):
        for k in range(blocks):
            base = (layer * blocks + k) * 3 * width + width - 2
            yield pltpu.make_async_copy(
                buf.at[layer, k, pl.ds(start, planes)],
                out.at[pl.ds(base + start, planes)],
                sems.at[slot * blocks + k],
            )

    @pl.loop(1, layers)
    def _(layer):
        base = layer * width
        ma, mb = masks[layer - 1, 0:1], masks[layer, 0:1]
        to_above, to_below = masks[layer - 1, 2:3], masks[layer, 1:2]
        a3, a2, a1 = (plane(base - i) for i in (3, 2, 1))
        b0, b1, b2 = (plane(base + i) for i in (0, 1, 2))
        a1.edge(False)
        b0.edge(True)
        low = functools.partial(store, ln, buf.at[layer - 1])
        high = functools.partial(store, ln, buf.at[layer])
        vo, vz, vx, total = second(a2, a1, a3, False, ma, to_below)
        low(width, blocks, vo, vz, total)
        high(0, blocks, vx, None, total)
        vo, vz = edge_own(a1, 1.0 - a2.z1, a2.z1, b0.x1, False, ma)
        vx, vd = edge_spill(a1, b0, False)
        total = edge_total(a1, ma)
        low(width + 1, blocks, vo, vz, total)
        high(1, blocks, vx, vd, total)
        vo, vz = edge_own(b0, 1.0 - b1.z1, b1.z1, a1.x1, True, mb)
        vx, vd = edge_spill(b0, a1, True)
        total = edge_total(b0, mb)
        high(2, blocks, vo, vz, total)
        low(width + 2, blocks, vx, vd, total)
        vo, vz, vx, total = second(b1, b0, b2, True, mb, to_above)
        high(3, blocks, vo, vz, total)
        low(width + 3, blocks, vx, None, total)

    def span(layer):
        if layers == 1:
            return 4, width - 4
        return jnp.where(layer == 0, 4, 0), width

    @pl.loop(0, layers)
    def _(layer):
        planes = [plane(layer * width + j) for j in range(1, width - 1)]
        mz = masks[layer, 0:1]
        for j in range(2, width - 2):
            vo, vz, total = middle(planes[j - 1], planes[j - 2], planes[j], mz)
            store(ln, buf.at[layer], j + 2, blocks, vo, vz, total)
        for c in send(layer, *span(layer), layer):
            c.start()

    rest = [c for layer in range(1, layers - 1) for c in send(layer, width, 4, layers + layer)]
    for c in rest:
        c.start()

    me = lax.axis_index(axis)
    lower = lax.rem(me, 2) == 1
    work_side(ln, lower, lower | (me < count - 1), faces, masks, msg, store_side(ln, side, lower, blocks))
    for c in send_side(side, out, lower, width, layers, side_sems):
        c.start()
    for layer in range(layers):
        rest += send(layer, *span(layer), layer)
    rest += send_side(side, out, lower, width, layers, side_sems)
    for c in clears + rest:
        c.wait()


def edge_kernel(
    width, blocks, axis, count, faces, masks, msg, held, out, zeros, side, sems, zero_sems
):
    del held
    layers = masks.shape[0]
    runs = zero_runs(layers * blocks, width)
    clears = zero_copies(zeros, out, runs[len(runs) - LAST_RUNS :], zero_sems)
    zeros[...] = jnp.zeros(zeros.shape, jnp.float32)
    for c in clears:
        c.start()
    me = lax.axis_index(axis)
    lower = lax.rem(me, 2) == 0
    valid = jnp.where(lower, me > 0, me < count - 1)
    ln = Lanes(faces.shape[2:], width)
    work_side(ln, lower, valid, faces, masks, msg, store_side(ln, side, lower, blocks))
    for c in send_side(side, out, lower, width, layers, sems):
        c.start()
    for c in clears + list(send_side(side, out, lower, width, layers, sems)):
        c.wait()


def swaps(firsts):
    return [pair for i in firsts for pair in ((i, i + 1), (i + 1, i))]


def on_device(trans_east, trans_north, trans_up, storage, support_reach, *, axis, count):
    layers, blocks, _ = support_reach.shape
    n, rows, lanes = trans_east.shape
    width = n // layers
    f32 = jnp.float32
    anywhere = pl.BlockSpec(memory_space=pl.ANY)
    vmem = pl.BlockSpec(memory_space=pltpu.VMEM)
    params = pltpu.CompilerParams(vmem_limit_bytes=16 * 2**20)
    outside = tuple(
        pltpu.with_memory_space_constraint(x, pltpu.HBM)
        for x in (trans_east, trans_north, trans_up, storage)
    )
    reach = jnp.transpose(support_reach, (0, 2, 1))
    reach = pltpu.with_memory_space_constraint(reach, pltpu.HBM)
    tiles = 1 + 9 * rows // TAIL
    msg_a, msg_b, masks, faces = pl.pallas_call(
        functools.partial(pack_kernel, n, width, axis),
        out_shape=(
            pltpu.VMEM((tiles + 1, TAIL, lanes), f32),
            pltpu.VMEM((tiles, TAIL, lanes), f32),
            pltpu.VMEM((layers, TAIL, lanes), f32),
            pltpu.VMEM((4, n, rows, lanes), f32),
        ),
        in_specs=[anywhere] * 5,
        out_specs=(vmem,) * 4,
        scratch_shapes=[
            pltpu.VMEM((layers, 4, blocks), jnp.int32),
            pltpu.SemaphoreType.DMA((5,)),
        ],
        compiler_params=params,
        name="pack",
    )(*outside, reach)
    got_a = lax.ppermute(msg_a, axis, swaps(range(0, count - 1, 2)))
    got_b = lax.ppermute(msg_b, axis, swaps(range(1, count - 1, 2)))

    bases = layers * blocks
    out_shape = jax.ShapeDtypeStruct((bases * 3 * width, rows, lanes), f32)
    side = pltpu.VMEM((blocks, 4, rows, lanes), f32)
    zeros = pltpu.VMEM((2 * (width - 2), rows, lanes), f32)
    bulk = pl.pallas_call(
        functools.partial(bulk_kernel, width, blocks, axis, count),
        out_shape=out_shape,
        in_specs=[vmem] * 3,
        out_specs=anywhere,
        scratch_shapes=[
            zeros,
            pltpu.VMEM((layers, blocks, width + 4, rows, lanes), f32),
            side,
            pltpu.SemaphoreType.DMA((2 * layers * blocks,)),
            pltpu.SemaphoreType.DMA((blocks,)),
            pltpu.SemaphoreType.DMA((bases + 1 - LAST_RUNS,)),
        ],
        compiler_params=params,
        cost_estimate=pl.CostEstimate(flops=10**7, bytes_accessed=7 * 10**6, transcendentals=0),
        name="bulk",
    )(faces, masks, got_a)
    out = pl.pallas_call(
        functools.partial(edge_kernel, width, blocks, axis, count),
        out_shape=out_shape,
        in_specs=[vmem] * 3 + [anywhere],
        out_specs=anywhere,
        scratch_shapes=[
            zeros,
            side,
            pltpu.SemaphoreType.DMA((blocks,)),
            pltpu.SemaphoreType.DMA((LAST_RUNS,)),
        ],
        input_output_aliases={3: 0},
        compiler_params=params,
        cost_estimate=pl.CostEstimate(flops=10**6, bytes_accessed=10**6, transcendentals=0),
        name="edges",
    )(faces, masks, got_b, bulk)
    return out.reshape(layers, blocks, 3 * width, rows, lanes)


def solution(mesh):
    spread = P(("groups", "blk"))
    return jax.shard_map(
        functools.partial(on_device, axis="blk", count=mesh.shape["blk"]),
        mesh=mesh,
        in_specs=(spread,) * 5,
        out_specs=spread,
        check_vma=False,
    )
```

```python
import functools

import jax
import jax.numpy as jnp
from jax import lax
from jax.experimental import pallas as pl
from jax.experimental.pallas import tpu as pltpu
from jax.sharding import PartitionSpec as P


TAIL = 8


class Lanes:
    def __init__(self, shape, width):
        tile = lax.broadcasted_iota(jnp.int32, (TAIL, shape[1]), 1)

        def rows(v):
            return jnp.concatenate([v] * (shape[0] // TAIL), axis=0)

        self.rows, self.lanes = shape
        self.width = width
        self.lane = rows(tile)
        self.local = rows(lax.rem(tile, width))
        self.first = self.local == 0
        self.last = self.local == width - 1
        self.odd = rows(lax.rem(tile // width, 2)) == 1
        self.row0 = lax.broadcasted_iota(jnp.int32, shape, 0) == 0
        self.lane0 = self.lane == 0

    def around(self, k):
        start = k * self.width - self.width // 2
        return (self.lane >= start) & (self.lane < start + 2 * self.width)

    def zm(self, v):
        return pltpu.roll(v, 1, 1)

    def zp(self, v):
        return pltpu.roll(v, self.lanes - 1, 1)

    def ym(self, v):
        return pltpu.roll(v, 1, 0)

    def yp(self, v):
        return pltpu.roll(v, self.rows - 1, 0)


def reciprocal(x):
    r = pl.reciprocal(x, approx=True)
    return r * (2.0 - x * r)


class Plane:
    def __init__(self, ln, tx, txn, ty, tz, s, valid=None):
        self.ln = ln
        self.tx, self.txn = tx, txn
        self.ty = jnp.where(ln.row0, 0.0, ty)
        self.tz = jnp.where(ln.lane0, 0.0, tz)
        self.typ = ln.yp(self.ty)
        self.tzp = ln.zp(self.tz)
        e = s * (1.0 / 3.0) + ((tx + txn) + (self.ty + self.typ) + (self.tz + self.tzp))
        if valid is not None:
            e = jnp.where(valid, e, 1.0)
        self.half = 0.5 * e + s * (1.0 / 3.0)
        self.all = 1.5 * e
        self.q = reciprocal(self.all)
        self.z1 = self.q * jnp.where(ln.first, self.tz, jnp.where(ln.last, self.tzp, 0.0))
        self.zm = ln.zm(self.z1)
        self.zp = ln.zp(self.z1)

    def toward(self, low):
        return self.tx if low else self.txn

    def inward(self, low):
        return self.txn if low else self.tx

    def edge(self, low):
        self.x1 = self.q * self.toward(low)
        self.o1 = 1.0 - self.z1 - self.x1

    def rim(self):
        return self.tz * self.zm + self.tzp * self.zp

    def along_y(self, v):
        return self.ty * self.ln.ym(v) + self.typ * self.ln.yp(v)


def plane_at(ln, faces, p):
    return Plane(ln, faces[0, p], faces[0, p + 1], faces[1, p], faces[2, p], faces[3, p])


def middle(p, below, above, mz):
    ln = p.ln
    vz = p.half * p.z1 + p.tx * below.z1 + p.txn * above.z1 + p.along_y(p.z1)
    vz = vz + p.tz * jnp.where(ln.first, 1.0 - p.zm, p.zm)
    vz = vz + p.tzp * jnp.where(ln.last, 1.0 - p.zp, p.zp)
    kept = vz * mz
    return p.all - vz, kept, p.all - (vz - kept)


def second(p, edge, inner, low, mz, mx):
    below, above = (edge, inner) if low else (inner, edge)
    ln = p.ln
    first_o = ln.zm(p.z1)
    vz = p.half * p.z1 + p.tx * below.z1 + p.txn * above.z1 + p.along_y(p.z1)
    vz = vz + p.tz * jnp.where(ln.first, 1.0 - first_o, first_o)
    vz = vz + p.tzp * jnp.where(ln.last, 1.0 - p.zp, p.zp)
    vx = p.toward(low) * edge.x1
    kept_z, kept_x = vz * mz, vx * mx
    total = p.all - (vz - kept_z) - (vx - kept_x)
    return p.all - vz - vx, kept_z, kept_x, total


def edge_own(p, inner_o1, inner_z1, outer_x1, low, mz):
    ln = p.ln
    om, op = ln.zm(p.o1), ln.zp(p.o1)
    vo = p.half * p.o1 + p.toward(low) * outer_x1 + p.inward(low) * inner_o1 + p.along_y(p.o1)
    vo = vo + p.tz * jnp.where(ln.first, p.zm, om) + p.tzp * jnp.where(ln.last, p.zp, op)
    vz = p.half * p.z1 + p.inward(low) * inner_z1 + p.along_y(p.z1)
    vz = vz + p.tz * jnp.where(ln.first, om, p.zm) + p.tzp * jnp.where(ln.last, op, p.zp)
    return vo, vz * mz


def edge_total(p, mz):
    rim = p.rim()
    return p.all - (rim - rim * mz)


def edge_spill(p, own, low):
    ln = p.ln
    xm, xp = ln.zm(p.x1), ln.zp(p.x1)
    face = p.toward(low)
    vx = p.half * p.x1 + face * own.o1 + p.along_y(p.x1)
    vx = vx + p.tz * jnp.where(ln.first, 0.0, xm) + p.tzp * jnp.where(ln.last, 0.0, xp)
    vd = face * own.z1 + p.tz * jnp.where(ln.first, xm, 0.0) + p.tzp * jnp.where(ln.last, xp, 0.0)
    return vx, vd


def store(ln, dst, plane, blocks, own, other, total):
    scale = reciprocal(total)
    own = own * scale
    other = jnp.zeros_like(own) if other is None else other * scale
    even, odd = jnp.where(ln.odd, other, own), jnp.where(ln.odd, own, other)
    for k in range(blocks):
        dst[k, plane] = jnp.where(ln.around(k), odd if k % 2 else even, 0.0)


def work_side(ln, low, valid, faces, masks, msg, put):
    n, rows, lanes = faces.shape[1:]
    layers = masks.shape[0]

    def own(i, j):
        return faces[i, jnp.where(low, j, n - 1 - j)]

    def got(i, j):
        tiles = rows // TAIL
        return msg[pl.ds(1 + tiles * (2 * i + j), tiles)].reshape(rows, lanes)

    f1, f2, f3 = (faces[0, jnp.where(low, j, n - j)] for j in (1, 2, 3))
    f0 = jnp.where(valid, jnp.where(low, faces[0, 0], got(0, 0)), 0.0)
    g1 = jnp.where(low, got(0, 0), got(0, 1))
    g2 = jnp.where(low, got(0, 1), got(4, 0))
    a0 = Plane(ln, f0, f1, own(1, 0), own(2, 0), own(3, 0))
    a1 = Plane(ln, f1, f2, own(1, 1), own(2, 1), own(3, 1))
    a2 = Plane(ln, f2, f3, own(1, 2), own(2, 2), own(3, 2))
    b0 = Plane(ln, g1, f0, got(1, 0), got(2, 0), got(3, 0), valid)
    b1 = Plane(ln, g2, g1, got(1, 1), got(2, 1), got(3, 1), valid)
    mine = masks[jnp.where(low, 0, layers - 1)]
    mz, my_reach = mine[0:1], jnp.where(low, mine[1:2], mine[2:3])
    theirs = msg[0]
    mo, their_reach = theirs[0:1], jnp.where(low, theirs[2:3], theirs[1:2])
    a0.edge(True)
    b0.edge(False)
    vx = g1 * b0.x1
    kept = vx * my_reach
    put(0, kept, None, edge_total(b1, mo) - (vx - kept))
    vx, vd = edge_spill(b0, a0, False)
    put(1, vx, vd, edge_total(b0, mo))
    vo, vz = edge_own(a0, 1.0 - a1.z1, a1.z1, b0.x1, True, mz)
    put(2, vo, vz, edge_total(a0, mz))
    vo, vz, _, total = second(a1, a0, a2, True, mz, their_reach)
    put(3, vo, vz, total)


def store_side(ln, buf, low, blocks):
    def put(i, own, other, total):
        store(ln, buf, jnp.where(low, i, 3 - i), blocks, own, other, total)

    return put


def send_one_side(buf, out, low, width, layers, sems, k):
    layer = jnp.where(low, 0, layers - 1)
    start = jnp.where(low, width - 2, 2 * width - 2)
    there = out.at[pl.ds((layer * buf.shape[0] + k) * 3 * width + start, 4)]
    return pltpu.make_async_copy(buf.at[k], there, sems.at[k])


def pack_kernel(
    n, width, axis, tx, ty, tz, s, reach, msg_a, msg_b, masks, faces, held_reach, sems
):
    layers, _, blocks = held_reach.shape
    lanes = masks.shape[-1]
    fetch = pltpu.make_async_copy(reach, held_reach, sems.at[4])
    fetch.start()
    copies = [
        pltpu.make_async_copy(a, faces.at[i], sems.at[i]) for i, a in enumerate((tx, ty, tz, s))
    ]
    for c in copies:
        c.start()
    masks[...] = jnp.zeros(masks.shape, jnp.float32)
    lane = lax.broadcasted_iota(jnp.int32, (4, lanes), 1)
    block = lane // width
    local = lane - block * width
    fetch.wait()
    for layer in range(layers):
        r = jnp.zeros((4, lanes), jnp.int32)
        for k in range(blocks):
            r = jnp.where(block == k, held_reach[layer, :, k : k + 1], r)
        low = pltpu.roll(r, width, 1)
        high = pltpu.roll(r, lanes - width, 1)
        near = jnp.where(
            local[0:1] < width // 2,
            jnp.where(low[3:4] >= local[0:1] + 1, 1.0, 0.0),
            jnp.where(high[2:3] >= width - local[0:1], 1.0, 0.0),
        )
        masks[layer, 0:1] = near
        masks[layer, 1:3] = jnp.where(r[0:2] >= 2, 1.0, 0.0)
    even = lax.rem(lax.axis_index(axis), 2) == 0

    def put(tile, up, down):
        up, down = (v.reshape(-1, TAIL, lanes) for v in (up, down))
        where = pl.ds(tile, up.shape[0])
        msg_a[where] = jnp.where(even, up, down)
        msg_b[where] = jnp.where(even, down, up)

    put(0, masks[layers - 1], masks[0])
    for c in copies:
        c.wait()
    for i in range(4):
        put(1 + 4 * i, faces[i, n - 1], faces[i, 0])
        put(3 + 4 * i, faces[i, n - 2], faces[i, 1])
    put(17, faces[0, n - 1], faces[0, 2])


def bulk_kernel(
    width, blocks, axis, count, faces, masks, msg, out, zeros, buf, side, sems, side_sems, zero_sems
):
    layers = masks.shape[0]
    rows, lanes = faces.shape[2:]
    box, depth = 3 * width, width - 2
    bases = layers * blocks
    zeros[...] = jnp.zeros(zeros.shape, jnp.float32)

    def clear(b, count):
        there = out.at[pl.ds(b * box - depth, count)]
        return pltpu.make_async_copy(zeros.at[pl.ds(0, count)], there, zero_sems.at[b])

    first = pltpu.make_async_copy(zeros.at[pl.ds(0, depth)], out.at[pl.ds(0, depth)], zero_sems.at[0])
    first.start()
    clear(bases, depth).start()

    @pl.loop(1, bases)
    def _(b):
        clear(b, 2 * depth).start()

    ln = Lanes((rows, lanes), width)
    plane = functools.partial(plane_at, ln, faces)
    me = lax.axis_index(axis)
    lower = lax.rem(me, 2) == 1

    def send(k, layer):
        start = 4 if layer == 0 else 0
        count = width + 4 - start - (4 if layer == layers - 1 else 0)
        return pltpu.make_async_copy(
            buf.at[layer, k, pl.ds(start, count)],
            out.at[pl.ds((layer * blocks + k) * box + depth + start, count)],
            sems.at[layer * blocks + k],
        )

    def between(layer):
        base = layer * width
        ma, mb = masks[layer - 1, 0:1], masks[layer, 0:1]
        to_above, to_below = masks[layer - 1, 2:3], masks[layer, 1:2]
        a3, a2, a1 = (plane(base - i) for i in (3, 2, 1))
        b0, b1, b2 = (plane(base + i) for i in (0, 1, 2))
        a1.edge(False)
        b0.edge(True)
        low = functools.partial(store, ln, buf.at[layer - 1])
        high = functools.partial(store, ln, buf.at[layer])
        vo, vz, vx, total = second(a2, a1, a3, False, ma, to_below)
        low(width, blocks, vo, vz, total)
        high(0, blocks, vx, None, total)
        vo, vz = edge_own(a1, 1.0 - a2.z1, a2.z1, b0.x1, False, ma)
        vx, vd = edge_spill(a1, b0, False)
        total = edge_total(a1, ma)
        low(width + 1, blocks, vo, vz, total)
        high(1, blocks, vx, vd, total)
        vo, vz = edge_own(b0, 1.0 - b1.z1, b1.z1, a1.x1, True, mb)
        vx, vd = edge_spill(b0, a1, True)
        total = edge_total(b0, mb)
        high(2, blocks, vo, vz, total)
        low(width + 2, blocks, vx, vd, total)
        vo, vz, vx, total = second(b1, b0, b2, True, mb, to_above)
        high(3, blocks, vo, vz, total)
        low(width + 3, blocks, vx, None, total)

    for layer in range(layers):
        planes = [plane(layer * width + j) for j in range(1, width - 1)]
        mz = masks[layer, 0:1]
        for j in range(2, width - 2):
            vo, vz, total = middle(planes[j - 1], planes[j - 2], planes[j], mz)
            store(ln, buf.at[layer], j + 2, blocks, vo, vz, total)
        if layer < layers - 1:
            between(layer + 1)
        else:
            valid = lower | (me < count - 1)
            work_side(ln, lower, valid, faces, masks, msg, store_side(ln, side, lower, blocks))

        @pl.loop(0, blocks)
        def _(k):
            send(k, layer).start()
            if layer == layers - 1:
                send_one_side(side, out, lower, width, layers, side_sems, k).start()

    first.wait()
    clear(bases, depth).wait()

    @pl.loop(1, bases)
    def _(b):
        clear(b, 2 * depth).wait()

    @pl.loop(0, blocks)
    def _(k):
        for layer in range(layers):
            send(k, layer).wait()
        send_one_side(side, out, lower, width, layers, side_sems, k).wait()


def edge_kernel(width, blocks, axis, count, faces, masks, msg, held, out, side, sems):
    del held
    layers = masks.shape[0]
    me = lax.axis_index(axis)
    lower = lax.rem(me, 2) == 0
    valid = jnp.where(lower, me > 0, me < count - 1)
    ln = Lanes(faces.shape[2:], width)
    work_side(ln, lower, valid, faces, masks, msg, store_side(ln, side, lower, blocks))
    copies = [send_one_side(side, out, lower, width, layers, sems, k) for k in range(blocks)]
    for c in copies:
        c.start()
    for c in copies:
        c.wait()


def swaps(firsts):
    return [pair for i in firsts for pair in ((i, i + 1), (i + 1, i))]


def on_device(trans_east, trans_north, trans_up, storage, support_reach, *, axis, count):
    layers, blocks, _ = support_reach.shape
    n, rows, lanes = trans_east.shape
    width = n // layers
    f32 = jnp.float32
    anywhere = pl.BlockSpec(memory_space=pl.ANY)
    vmem = pl.BlockSpec(memory_space=pltpu.VMEM)
    params = pltpu.CompilerParams(vmem_limit_bytes=16 * 2**20)
    outside = tuple(
        pltpu.with_memory_space_constraint(x, pltpu.HBM)
        for x in (trans_east, trans_north, trans_up, storage)
    )
    reach = jnp.transpose(support_reach, (0, 2, 1))
    reach = pltpu.with_memory_space_constraint(reach, pltpu.HBM)
    tiles = 1 + 9 * rows // TAIL
    msg_a, msg_b, masks, faces = pl.pallas_call(
        functools.partial(pack_kernel, n, width, axis),
        out_shape=(
            pltpu.VMEM((tiles + 1, TAIL, lanes), f32),
            pltpu.VMEM((tiles, TAIL, lanes), f32),
            pltpu.VMEM((layers, TAIL, lanes), f32),
            pltpu.VMEM((4, n, rows, lanes), f32),
        ),
        in_specs=[anywhere] * 5,
        out_specs=(vmem,) * 4,
        scratch_shapes=[
            pltpu.VMEM((layers, 4, blocks), jnp.int32),
            pltpu.SemaphoreType.DMA((5,)),
        ],
        compiler_params=params,
        name="pack",
    )(*outside, reach)
    got_a = lax.ppermute(msg_a, axis, swaps(range(0, count - 1, 2)))
    got_b = lax.ppermute(msg_b, axis, swaps(range(1, count - 1, 2)))

    bases = layers * blocks
    out_shape = jax.ShapeDtypeStruct((bases * 3 * width, rows, lanes), f32)
    side = pltpu.VMEM((blocks, 4, rows, lanes), f32)
    zeros = pltpu.VMEM((2 * (width - 2), rows, lanes), f32)
    bulk = pl.pallas_call(
        functools.partial(bulk_kernel, width, blocks, axis, count),
        out_shape=out_shape,
        in_specs=[vmem] * 3,
        out_specs=anywhere,
        scratch_shapes=[
            zeros,
            pltpu.VMEM((layers, blocks, width + 4, rows, lanes), f32),
            side,
            pltpu.SemaphoreType.DMA((bases,)),
            pltpu.SemaphoreType.DMA((blocks,)),
            pltpu.SemaphoreType.DMA((bases + 1,)),
        ],
        compiler_params=params,
        cost_estimate=pl.CostEstimate(flops=10**7, bytes_accessed=7 * 10**6, transcendentals=0),
        name="bulk",
    )(faces, masks, got_a)
    out = pl.pallas_call(
        functools.partial(edge_kernel, width, blocks, axis, count),
        out_shape=out_shape,
        in_specs=[vmem] * 3 + [anywhere],
        out_specs=anywhere,
        scratch_shapes=[
            side,
            pltpu.SemaphoreType.DMA((blocks,)),
        ],
        input_output_aliases={3: 0},
        compiler_params=params,
        cost_estimate=pl.CostEstimate(flops=10**6, bytes_accessed=10**6, transcendentals=0),
        name="edges",
    )(faces, masks, got_b, bulk)
    return out.reshape(layers, blocks, 3 * width, rows, lanes)


def solution(mesh):
    spread = P(("groups", "blk"))
    return jax.shard_map(
        functools.partial(on_device, axis="blk", count=mesh.shape["blk"]),
        mesh=mesh,
        in_specs=(spread,) * 5,
        out_specs=spread,
        check_vma=False,
    )
```

```python
import functools

import jax
import jax.numpy as jnp
from jax import lax
from jax.experimental import pallas as pl
from jax.experimental.pallas import tpu as pltpu
from jax.sharding import PartitionSpec as P


TAIL = 8
EARLY = 4


class Lanes:
    def __init__(self, shape, width):
        tile = lax.broadcasted_iota(jnp.int32, (TAIL, shape[1]), 1)

        def rows(v):
            return jnp.concatenate([v] * (shape[0] // TAIL), axis=0)

        self.rows, self.lanes = shape
        self.width = width
        self.lane = rows(tile)
        self.local = rows(lax.rem(tile, width))
        self.first = self.local == 0
        self.last = self.local == width - 1
        self.odd = rows(lax.rem(tile // width, 2)) == 1
        self.row0 = lax.broadcasted_iota(jnp.int32, shape, 0) == 0
        self.lane0 = self.lane == 0

    def around(self, k):
        start = k * self.width - self.width // 2
        return (self.lane >= start) & (self.lane < start + 2 * self.width)

    def zm(self, v):
        return pltpu.roll(v, 1, 1)

    def zp(self, v):
        return pltpu.roll(v, self.lanes - 1, 1)

    def ym(self, v):
        return pltpu.roll(v, 1, 0)

    def yp(self, v):
        return pltpu.roll(v, self.rows - 1, 0)


def reciprocal(x):
    r = pl.reciprocal(x, approx=True)
    return r * (2.0 - x * r)


def cross(ln, ty, tz, s):
    ty = jnp.where(ln.row0, 0.0, ty)
    tz = jnp.where(ln.lane0, 0.0, tz)
    typ, tzp = ln.yp(ty), ln.zp(tz)
    return s * (1.0 / 3.0) + ((ty + typ) + (tz + tzp)), (ty, typ, tz, tzp)


class Plane:
    def __init__(self, ln, tx, txn, ty, tz, s, valid=None):
        self.ln = ln
        self.tx, self.txn = tx, txn
        e, (self.ty, self.typ, self.tz, self.tzp) = cross(ln, ty, tz, s)
        e = e + (tx + txn)
        if valid is not None:
            e = jnp.where(valid, e, 1.0)
        self.half = 0.5 * e + s * (1.0 / 3.0)
        self.spread(e)

    def spread(self, e):
        ln = self.ln
        self.all = 1.5 * e
        self.q = reciprocal(self.all)
        self.z1 = self.q * jnp.where(ln.first, self.tz, jnp.where(ln.last, self.tzp, 0.0))
        self.zm = ln.zm(self.z1)
        self.zp = ln.zp(self.z1)

    def toward(self, low):
        return self.tx if low else self.txn

    def inward(self, low):
        return self.txn if low else self.tx

    def edge(self, low):
        self.x1 = self.q * self.toward(low)
        self.o1 = 1.0 - self.z1 - self.x1

    def rim(self):
        return self.tz * self.zm + self.tzp * self.zp

    def along_y(self, v):
        return self.ty * self.ln.ym(v) + self.typ * self.ln.yp(v)


class Rim(Plane):
    def __init__(self, ln, e, tz):
        self.ln = ln
        self.tz = jnp.where(ln.lane0, 0.0, tz)
        self.tzp = ln.zp(self.tz)
        self.spread(e)


def plane_at(ln, faces, p):
    return Plane(ln, faces[0, p], faces[0, p + 1], faces[1, p], faces[2, p], faces[3, p])


def middle(p, below, above, mz):
    ln = p.ln
    vz = p.half * p.z1 + p.tx * below.z1 + p.txn * above.z1 + p.along_y(p.z1)
    vz = vz + p.tz * jnp.where(ln.first, 1.0 - p.zm, p.zm)
    vz = vz + p.tzp * jnp.where(ln.last, 1.0 - p.zp, p.zp)
    kept = vz * mz
    return p.all - vz, kept, p.all - (vz - kept)


def second(p, edge, inner, low, mz, mx):
    below, above = (edge, inner) if low else (inner, edge)
    ln = p.ln
    first_o = ln.zm(p.z1)
    vz = p.half * p.z1 + p.tx * below.z1 + p.txn * above.z1 + p.along_y(p.z1)
    vz = vz + p.tz * jnp.where(ln.first, 1.0 - first_o, first_o)
    vz = vz + p.tzp * jnp.where(ln.last, 1.0 - p.zp, p.zp)
    vx = p.toward(low) * edge.x1
    kept_z, kept_x = vz * mz, vx * mx
    total = p.all - (vz - kept_z) - (vx - kept_x)
    return p.all - vz - vx, kept_z, kept_x, total


def edge_own(p, inner_o1, inner_z1, outer_x1, low, mz):
    ln = p.ln
    om, op = ln.zm(p.o1), ln.zp(p.o1)
    vo = p.half * p.o1 + p.toward(low) * outer_x1 + p.inward(low) * inner_o1 + p.along_y(p.o1)
    vo = vo + p.tz * jnp.where(ln.first, p.zm, om) + p.tzp * jnp.where(ln.last, p.zp, op)
    vz = p.half * p.z1 + p.inward(low) * inner_z1 + p.along_y(p.z1)
    vz = vz + p.tz * jnp.where(ln.first, om, p.zm) + p.tzp * jnp.where(ln.last, op, p.zp)
    return vo, vz * mz


def edge_total(p, mz):
    rim = p.rim()
    return p.all - (rim - rim * mz)


def edge_spill(p, own, low):
    ln = p.ln
    xm, xp = ln.zm(p.x1), ln.zp(p.x1)
    face = p.toward(low)
    vx = p.half * p.x1 + face * own.o1 + p.along_y(p.x1)
    vx = vx + p.tz * jnp.where(ln.first, 0.0, xm) + p.tzp * jnp.where(ln.last, 0.0, xp)
    vd = face * own.z1 + p.tz * jnp.where(ln.first, xm, 0.0) + p.tzp * jnp.where(ln.last, xp, 0.0)
    return vx, vd


def store(ln, dst, plane, blocks, own, other, total):
    scale = reciprocal(total)
    own = own * scale
    other = jnp.zeros_like(own) if other is None else other * scale
    even, odd = jnp.where(ln.odd, other, own), jnp.where(ln.odd, own, other)
    for k in range(blocks):
        dst[k, plane] = jnp.where(ln.around(k), odd if k % 2 else even, 0.0)


def work_side(ln, low, valid, faces, masks, msg, put):
    n, rows, lanes = faces.shape[1:]
    layers = masks.shape[0]

    def own(i, j):
        return faces[i, jnp.where(low, j, n - 1 - j)]

    def got(i):
        tiles = rows // TAIL
        return msg[pl.ds(1 + tiles * i, tiles)].reshape(rows, lanes)

    f1, f2, f3 = (faces[0, jnp.where(low, j, n - j)] for j in (1, 2, 3))
    f0 = jnp.where(valid, jnp.where(low, faces[0, 0], got(6)), 0.0)
    g1 = got(0)
    a0 = Plane(ln, f0, f1, own(1, 0), own(2, 0), own(3, 0))
    a1 = Plane(ln, f1, f2, own(1, 1), own(2, 1), own(3, 1))
    a2 = Plane(ln, f2, f3, own(1, 2), own(2, 2), own(3, 2))
    b0 = Plane(ln, g1, f0, got(1), got(2), got(3), valid)
    b1 = Rim(ln, jnp.where(valid, got(4) + g1, 1.0), got(5))
    mine = masks[jnp.where(low, 0, layers - 1)]
    mz, my_reach = mine[0:1], jnp.where(low, mine[1:2], mine[2:3])
    theirs = msg[0]
    mo, their_reach = theirs[0:1], jnp.where(low, theirs[2:3], theirs[1:2])
    a0.edge(True)
    b0.edge(False)
    vx = g1 * b0.x1
    kept = vx * my_reach
    put(0, kept, None, edge_total(b1, mo) - (vx - kept))
    vx, vd = edge_spill(b0, a0, False)
    put(1, vx, vd, edge_total(b0, mo))
    vo, vz = edge_own(a0, 1.0 - a1.z1, a1.z1, b0.x1, True, mz)
    put(2, vo, vz, edge_total(a0, mz))
    vo, vz, _, total = second(a1, a0, a2, True, mz, their_reach)
    put(3, vo, vz, total)


def store_side(ln, buf, low, blocks):
    def put(i, own, other, total):
        store(ln, buf, jnp.where(low, i, 3 - i), blocks, own, other, total)

    return put


def send_one_side(buf, out, low, width, layers, sems, k):
    layer = jnp.where(low, 0, layers - 1)
    start = jnp.where(low, width - 2, 2 * width - 2)
    there = out.at[pl.ds((layer * buf.shape[0] + k) * 3 * width + start, 4)]
    return pltpu.make_async_copy(buf.at[k], there, sems.at[k])


def clear_run(zeros, out, b, bases, width, sem):
    depth = width - 2
    ends = isinstance(b, int) and b in (0, bases)
    count = depth if ends else 2 * depth
    start = 0 if ends and b == 0 else b * 3 * width - depth
    return pltpu.make_async_copy(zeros.at[pl.ds(0, count)], out.at[pl.ds(start, count)], sem)


def early_runs(bases):
    return range(bases - EARLY, bases)


def pack_kernel(
    n, width, axis, tx, ty, tz, s, reach, msg_a, msg_b, masks, faces, out,
    held_reach, zeros, sems, zero_sems,
):
    layers, _, blocks = held_reach.shape
    lanes = masks.shape[-1]
    fetch = pltpu.make_async_copy(reach, held_reach, sems.at[4])
    fetch.start()
    copies = [
        pltpu.make_async_copy(a, faces.at[i], sems.at[i]) for i, a in enumerate((tx, ty, tz, s))
    ]
    for c in copies:
        c.start()
    rows = faces.shape[2]
    bases = layers * blocks
    clears = [clear_run(zeros, out, b, bases, width, zero_sems.at[i]) for i, b in enumerate(early_runs(bases))]
    even = lax.rem(lax.axis_index(axis), 2) == 0

    @pl.when(jnp.logical_not(even))
    def _():
        zeros[...] = jnp.zeros(zeros.shape, jnp.float32)
        for c in clears:
            c.start()

    masks[...] = jnp.zeros(masks.shape, jnp.float32)
    lane = lax.broadcasted_iota(jnp.int32, (4, lanes), 1)
    block = lane // width
    local = lane - block * width
    fetch.wait()
    for layer in range(layers):
        r = jnp.zeros((4, lanes), jnp.int32)
        for k in range(blocks):
            r = jnp.where(block == k, held_reach[layer, :, k : k + 1], r)
        low = pltpu.roll(r, width, 1)
        high = pltpu.roll(r, lanes - width, 1)
        near = jnp.where(
            local[0:1] < width // 2,
            jnp.where(low[3:4] >= local[0:1] + 1, 1.0, 0.0),
            jnp.where(high[2:3] >= width - local[0:1], 1.0, 0.0),
        )
        masks[layer, 0:1] = near
        masks[layer, 1:3] = jnp.where(r[0:2] >= 2, 1.0, 0.0)

    def put(tile, up, down):
        up, down = (v.reshape(-1, TAIL, lanes) for v in (up, down))
        where = pl.ds(tile, up.shape[0])
        msg_a[where] = jnp.where(even, up, down)
        msg_b[where] = jnp.where(even, down, up)

    put(0, masks[layers - 1], masks[0])
    for c in copies:
        c.wait()
    ln = Lanes(faces.shape[2:], width)
    top, _ = cross(ln, faces[1, n - 2], faces[2, n - 2], faces[3, n - 2])
    low, _ = cross(ln, faces[1, 1], faces[2, 1], faces[3, 1])
    ups = [faces[0, n - 1]] + [faces[i, n - 1] for i in (1, 2, 3)]
    ups += [top + faces[0, n - 2], faces[2, n - 2], faces[0, n - 1]]
    downs = [faces[0, 1]] + [faces[i, 0] for i in (1, 2, 3)]
    downs += [low + faces[0, 2], faces[2, 1], faces[0, 0]]
    for i, (up, down) in enumerate(zip(ups, downs)):
        put(1 + i * (rows // TAIL), up, down)

    @pl.when(jnp.logical_not(even))
    def _():
        for c in clears:
            c.wait()


def bulk_kernel(
    width, blocks, axis, count, faces, masks, msg, held, out, zeros, buf, side, sems, side_sems, zero_sems
):
    del held
    layers = masks.shape[0]
    rows, lanes = faces.shape[2:]
    box, depth = 3 * width, width - 2
    bases = layers * blocks
    zeros[...] = jnp.zeros(zeros.shape, jnp.float32)

    me = lax.axis_index(axis)
    lower = lax.rem(me, 2) == 1
    early = early_runs(bases)

    def clear(b):
        return clear_run(zeros, out, b, bases, width, zero_sems.at[b])

    def each_run(act):
        act(clear(0))
        act(clear(bases))

        @pl.loop(1, early.start)
        def _(b):
            act(clear(b))

        @pl.when(jnp.logical_not(lower))
        def _():
            for b in early:
                act(clear(b))

    each_run(lambda c: c.start())
    ln = Lanes((rows, lanes), width)
    plane = functools.partial(plane_at, ln, faces)

    def send(k, layer):
        start = 4 if layer == 0 else 0
        count = width + 4 - start - (4 if layer == layers - 1 else 0)
        return pltpu.make_async_copy(
            buf.at[layer, k, pl.ds(start, count)],
            out.at[pl.ds((layer * blocks + k) * box + depth + start, count)],
            sems.at[layer * blocks + k],
        )

    def between(layer):
        base = layer * width
        ma, mb = masks[layer - 1, 0:1], masks[layer, 0:1]
        to_above, to_below = masks[layer - 1, 2:3], masks[layer, 1:2]
        a3, a2, a1 = (plane(base - i) for i in (3, 2, 1))
        b0, b1, b2 = (plane(base + i) for i in (0, 1, 2))
        a1.edge(False)
        b0.edge(True)
        low = functools.partial(store, ln, buf.at[layer - 1])
        high = functools.partial(store, ln, buf.at[layer])
        vo, vz, vx, total = second(a2, a1, a3, False, ma, to_below)
        low(width, blocks, vo, vz, total)
        high(0, blocks, vx, None, total)
        vo, vz = edge_own(a1, 1.0 - a2.z1, a2.z1, b0.x1, False, ma)
        vx, vd = edge_spill(a1, b0, False)
        total = edge_total(a1, ma)
        low(width + 1, blocks, vo, vz, total)
        high(1, blocks, vx, vd, total)
        vo, vz = edge_own(b0, 1.0 - b1.z1, b1.z1, a1.x1, True, mb)
        vx, vd = edge_spill(b0, a1, True)
        total = edge_total(b0, mb)
        high(2, blocks, vo, vz, total)
        low(width + 2, blocks, vx, vd, total)
        vo, vz, vx, total = second(b1, b0, b2, True, mb, to_above)
        high(3, blocks, vo, vz, total)
        low(width + 3, blocks, vx, None, total)

    for layer in range(layers):
        planes = [plane(layer * width + j) for j in range(1, width - 1)]
        mz = masks[layer, 0:1]
        for j in range(2, width - 2):
            vo, vz, total = middle(planes[j - 1], planes[j - 2], planes[j], mz)
            store(ln, buf.at[layer], j + 2, blocks, vo, vz, total)
        if layer < layers - 1:
            between(layer + 1)
        else:
            valid = lower | (me < count - 1)
            work_side(ln, lower, valid, faces, masks, msg, store_side(ln, side, lower, blocks))

        @pl.loop(0, blocks)
        def _(k):
            send(k, layer).start()
            if layer == layers - 1:
                send_one_side(side, out, lower, width, layers, side_sems, k).start()

    each_run(lambda c: c.wait())

    @pl.loop(0, blocks)
    def _(k):
        for layer in range(layers):
            send(k, layer).wait()
        send_one_side(side, out, lower, width, layers, side_sems, k).wait()


def edge_kernel(width, blocks, axis, count, faces, masks, msg, held, out, side, sems):
    del held
    layers = masks.shape[0]
    me = lax.axis_index(axis)
    lower = lax.rem(me, 2) == 0
    valid = jnp.where(lower, me > 0, me < count - 1)
    ln = Lanes(faces.shape[2:], width)
    work_side(ln, lower, valid, faces, masks, msg, store_side(ln, side, lower, blocks))
    copies = [send_one_side(side, out, lower, width, layers, sems, k) for k in range(blocks)]
    for c in copies:
        c.start()
    for c in copies:
        c.wait()


def swaps(firsts):
    return [pair for i in firsts for pair in ((i, i + 1), (i + 1, i))]


def on_device(trans_east, trans_north, trans_up, storage, support_reach, *, axis, count):
    layers, blocks, _ = support_reach.shape
    n, rows, lanes = trans_east.shape
    width = n // layers
    f32 = jnp.float32
    anywhere = pl.BlockSpec(memory_space=pl.ANY)
    vmem = pl.BlockSpec(memory_space=pltpu.VMEM)
    params = pltpu.CompilerParams(vmem_limit_bytes=16 * 2**20)
    outside = tuple(
        pltpu.with_memory_space_constraint(x, pltpu.HBM)
        for x in (trans_east, trans_north, trans_up, storage)
    )
    reach = jnp.transpose(support_reach, (0, 2, 1))
    reach = pltpu.with_memory_space_constraint(reach, pltpu.HBM)
    bases = layers * blocks
    out_shape = jax.ShapeDtypeStruct((bases * 3 * width, rows, lanes), f32)
    side = pltpu.VMEM((blocks, 4, rows, lanes), f32)
    zeros = pltpu.VMEM((2 * (width - 2), rows, lanes), f32)
    tiles = 1 + 7 * rows // TAIL
    msg_a, msg_b, masks, faces, cleared = pl.pallas_call(
        functools.partial(pack_kernel, n, width, axis),
        out_shape=(
            pltpu.VMEM((tiles + 1, TAIL, lanes), f32),
            pltpu.VMEM((tiles, TAIL, lanes), f32),
            pltpu.VMEM((layers, TAIL, lanes), f32),
            pltpu.VMEM((4, n, rows, lanes), f32),
            out_shape,
        ),
        in_specs=[anywhere] * 5,
        out_specs=(vmem,) * 4 + (anywhere,),
        scratch_shapes=[
            pltpu.VMEM((layers, 4, blocks), jnp.int32),
            zeros,
            pltpu.SemaphoreType.DMA((5,)),
            pltpu.SemaphoreType.DMA((EARLY,)),
        ],
        compiler_params=params,
        name="pack",
    )(*outside, reach)
    got_a = lax.ppermute(msg_a, axis, swaps(range(0, count - 1, 2)))
    got_b = lax.ppermute(msg_b, axis, swaps(range(1, count - 1, 2)))

    bulk = pl.pallas_call(
        functools.partial(bulk_kernel, width, blocks, axis, count),
        out_shape=out_shape,
        in_specs=[vmem] * 3 + [anywhere],
        out_specs=anywhere,
        scratch_shapes=[
            zeros,
            pltpu.VMEM((layers, blocks, width + 4, rows, lanes), f32),
            side,
            pltpu.SemaphoreType.DMA((bases,)),
            pltpu.SemaphoreType.DMA((blocks,)),
            pltpu.SemaphoreType.DMA((bases + 1,)),
        ],
        input_output_aliases={3: 0},
        compiler_params=params,
        cost_estimate=pl.CostEstimate(flops=10**7, bytes_accessed=7 * 10**6, transcendentals=0),
        name="bulk",
    )(faces, masks, got_a, cleared)
    out = pl.pallas_call(
        functools.partial(edge_kernel, width, blocks, axis, count),
        out_shape=out_shape,
        in_specs=[vmem] * 3 + [anywhere],
        out_specs=anywhere,
        scratch_shapes=[
            side,
            pltpu.SemaphoreType.DMA((blocks,)),
        ],
        input_output_aliases={3: 0},
        compiler_params=params,
        cost_estimate=pl.CostEstimate(flops=10**6, bytes_accessed=10**6, transcendentals=0),
        name="edges",
    )(faces, masks, got_b, bulk)
    return out.reshape(layers, blocks, 3 * width, rows, lanes)


def solution(mesh):
    spread = P(("groups", "blk"))
    return jax.shard_map(
        functools.partial(on_device, axis="blk", count=mesh.shape["blk"]),
        mesh=mesh,
        in_specs=(spread,) * 5,
        out_specs=spread,
        check_vma=False,
    )
```

```python
import functools

import jax
import jax.numpy as jnp
from jax import lax
from jax.experimental import pallas as pl
from jax.experimental.pallas import tpu as pltpu
from jax.sharding import PartitionSpec as P


TAIL = 8
EARLY = 8


class Lanes:
    def __init__(self, shape, width):
        tile = lax.broadcasted_iota(jnp.int32, (TAIL, shape[1]), 1)

        def rows(v):
            return jnp.concatenate([v] * (shape[0] // TAIL), axis=0)

        self.rows, self.lanes = shape
        self.width = width
        self.lane = rows(tile)
        self.local = rows(lax.rem(tile, width))
        self.first = self.local == 0
        self.last = self.local == width - 1
        self.odd = rows(lax.rem(tile // width, 2)) == 1
        self.row0 = lax.broadcasted_iota(jnp.int32, shape, 0) == 0
        self.lane0 = self.lane == 0

    def around(self, k):
        start = k * self.width - self.width // 2
        return (self.lane >= start) & (self.lane < start + 2 * self.width)

    def zm(self, v):
        return pltpu.roll(v, 1, 1)

    def zp(self, v):
        return pltpu.roll(v, self.lanes - 1, 1)

    def ym(self, v):
        return pltpu.roll(v, 1, 0)

    def yp(self, v):
        return pltpu.roll(v, self.rows - 1, 0)


def reciprocal(x):
    r = pl.reciprocal(x, approx=True)
    return r * (2.0 - x * r)


def cross(ln, ty, tz, s):
    ty = jnp.where(ln.row0, 0.0, ty)
    tz = jnp.where(ln.lane0, 0.0, tz)
    typ, tzp = ln.yp(ty), ln.zp(tz)
    return s * (1.0 / 3.0) + ((ty + typ) + (tz + tzp)), (ty, typ, tz, tzp)


class Plane:
    def __init__(self, ln, tx, txn, ty, tz, s, valid=None):
        self.ln = ln
        self.tx, self.txn = tx, txn
        e, (self.ty, self.typ, self.tz, self.tzp) = cross(ln, ty, tz, s)
        e = e + (tx + txn)
        if valid is not None:
            e = jnp.where(valid, e, 1.0)
        self.half = 0.5 * e + s * (1.0 / 3.0)
        self.all = 1.5 * e
        self.q = reciprocal(self.all)
        self.z1 = self.q * jnp.where(ln.first, self.tz, jnp.where(ln.last, self.tzp, 0.0))
        self.zm = ln.zm(self.z1)
        self.zp = ln.zp(self.z1)

    def toward(self, low):
        return self.tx if low else self.txn

    def inward(self, low):
        return self.txn if low else self.tx

    def edge(self, low):
        self.x1 = self.q * self.toward(low)
        self.o1 = 1.0 - self.z1 - self.x1

    def rim(self):
        return self.tz * self.zm + self.tzp * self.zp

    def along_y(self, v):
        return self.ty * self.ln.ym(v) + self.typ * self.ln.yp(v)


def plane_at(ln, faces, p):
    return Plane(ln, faces[0, p], faces[0, p + 1], faces[1, p], faces[2, p], faces[3, p])


def middle(p, below, above, mz):
    ln = p.ln
    vz = p.half * p.z1 + p.tx * below.z1 + p.txn * above.z1 + p.along_y(p.z1)
    vz = vz + p.tz * jnp.where(ln.first, 1.0 - p.zm, p.zm)
    vz = vz + p.tzp * jnp.where(ln.last, 1.0 - p.zp, p.zp)
    kept = vz * mz
    return p.all - vz, kept, p.all - (vz - kept)


def second(p, edge, inner, low, mz, mx):
    below, above = (edge, inner) if low else (inner, edge)
    ln = p.ln
    first_o = ln.zm(p.z1)
    vz = p.half * p.z1 + p.tx * below.z1 + p.txn * above.z1 + p.along_y(p.z1)
    vz = vz + p.tz * jnp.where(ln.first, 1.0 - first_o, first_o)
    vz = vz + p.tzp * jnp.where(ln.last, 1.0 - p.zp, p.zp)
    vx = p.toward(low) * edge.x1
    kept_z, kept_x = vz * mz, vx * mx
    total = p.all - (vz - kept_z) - (vx - kept_x)
    return p.all - vz - vx, kept_z, kept_x, total


def edge_own(p, inner_o1, inner_z1, outer_x1, low, mz):
    ln = p.ln
    om, op = ln.zm(p.o1), ln.zp(p.o1)
    vo = p.half * p.o1 + p.toward(low) * outer_x1 + p.inward(low) * inner_o1 + p.along_y(p.o1)
    vo = vo + p.tz * jnp.where(ln.first, p.zm, om) + p.tzp * jnp.where(ln.last, p.zp, op)
    vz = p.half * p.z1 + p.inward(low) * inner_z1 + p.along_y(p.z1)
    vz = vz + p.tz * jnp.where(ln.first, om, p.zm) + p.tzp * jnp.where(ln.last, op, p.zp)
    return vo, vz * mz


def edge_total(p, mz):
    rim = p.rim()
    return p.all - (rim - rim * mz)


def edge_spill(p, own, low):
    ln = p.ln
    xm, xp = ln.zm(p.x1), ln.zp(p.x1)
    face = p.toward(low)
    vx = p.half * p.x1 + face * own.o1 + p.along_y(p.x1)
    vx = vx + p.tz * jnp.where(ln.first, 0.0, xm) + p.tzp * jnp.where(ln.last, 0.0, xp)
    vd = face * own.z1 + p.tz * jnp.where(ln.first, xm, 0.0) + p.tzp * jnp.where(ln.last, xp, 0.0)
    return vx, vd


def store(ln, dst, plane, blocks, own, other, total):
    scale = reciprocal(total)
    own = own * scale
    other = jnp.zeros_like(own) if other is None else other * scale
    even, odd = jnp.where(ln.odd, other, own), jnp.where(ln.odd, own, other)
    for k in range(blocks):
        dst[k, plane] = jnp.where(ln.around(k), odd if k % 2 else even, 0.0)


def work_side(ln, low, valid, faces, masks, msg, put):
    n, rows, lanes = faces.shape[1:]
    layers = masks.shape[0]

    def own(i, j):
        return faces[i, jnp.where(low, j, n - 1 - j)]

    def got(i):
        tiles = rows // TAIL
        return msg[pl.ds(1 + tiles * i, tiles)].reshape(rows, lanes)

    f1, f2, f3 = (faces[0, jnp.where(low, j, n - j)] for j in (1, 2, 3))
    f0 = jnp.where(valid, jnp.where(low, faces[0, 0], got(5)), 0.0)
    g1 = got(0)
    a0 = Plane(ln, f0, f1, own(1, 0), own(2, 0), own(3, 0))
    a1 = Plane(ln, f1, f2, own(1, 1), own(2, 1), own(3, 1))
    a2 = Plane(ln, f2, f3, own(1, 2), own(2, 2), own(3, 2))
    b0 = Plane(ln, g1, f0, got(1), got(2), got(3), valid)
    b1_total = jnp.where(valid, got(4), 1.0)
    mine = masks[jnp.where(low, 0, layers - 1)]
    mz, my_reach = mine[0:1], jnp.where(low, mine[1:2], mine[2:3])
    theirs = msg[0]
    mo, their_reach = theirs[0:1], jnp.where(low, theirs[2:3], theirs[1:2])
    a0.edge(True)
    b0.edge(False)
    vx = g1 * b0.x1
    kept = vx * my_reach
    put(0, kept, None, b1_total - (vx - kept))
    vx, vd = edge_spill(b0, a0, False)
    put(1, vx, vd, edge_total(b0, mo))
    vo, vz = edge_own(a0, 1.0 - a1.z1, a1.z1, b0.x1, True, mz)
    put(2, vo, vz, edge_total(a0, mz))
    vo, vz, _, total = second(a1, a0, a2, True, mz, their_reach)
    put(3, vo, vz, total)


def store_side(ln, buf, low, blocks):
    def put(i, own, other, total):
        store(ln, buf, jnp.where(low, i, 3 - i), blocks, own, other, total)

    return put


def send_one_side(buf, out, low, width, layers, sems, k):
    layer = jnp.where(low, 0, layers - 1)
    start = jnp.where(low, width - 2, 2 * width - 2)
    there = out.at[pl.ds((layer * buf.shape[0] + k) * 3 * width + start, 4)]
    return pltpu.make_async_copy(buf.at[k], there, sems.at[k])


def clear_run(zeros, out, b, bases, width, sem):
    depth = width - 2
    ends = isinstance(b, int) and b in (0, bases)
    count = depth if ends else 2 * depth
    start = 0 if ends and b == 0 else b * 3 * width - depth
    return pltpu.make_async_copy(zeros.at[pl.ds(0, count)], out.at[pl.ds(start, count)], sem)


def early_runs(bases):
    return range(bases - EARLY, bases)


def pack_kernel(
    n, width, axis, tx, ty, tz, s, reach, msg_a, msg_b, masks, faces, out,
    held_reach, zeros, sems, zero_sems,
):
    layers, _, blocks = held_reach.shape
    lanes = masks.shape[-1]
    fetch = pltpu.make_async_copy(reach, held_reach, sems.at[12])
    fetch.start()
    copies = []
    for start, size in ((0, 4), (n - 4, 4), (4, n - 8)):
        for i, a in enumerate((tx, ty, tz, s)):
            part = pl.ds(start, size)
            copies.append(pltpu.make_async_copy(a.at[part], faces.at[i, part], sems.at[len(copies)]))
            copies[-1].start()
    rows = faces.shape[2]
    bases = layers * blocks
    clears = [clear_run(zeros, out, b, bases, width, zero_sems.at[i]) for i, b in enumerate(early_runs(bases))]
    even = lax.rem(lax.axis_index(axis), 2) == 0

    eager = lax.axis_index(axis) == 1

    @pl.when(eager)
    def _():
        zeros[...] = jnp.zeros(zeros.shape, jnp.float32)
        for c in clears:
            c.start()

    masks[...] = jnp.zeros(masks.shape, jnp.float32)
    lane = lax.broadcasted_iota(jnp.int32, (4, lanes), 1)
    block = lane // width
    local = lane - block * width
    fetch.wait()
    for layer in range(layers):
        r = jnp.zeros((4, lanes), jnp.int32)
        for k in range(blocks):
            r = jnp.where(block == k, held_reach[layer, :, k : k + 1], r)
        low = pltpu.roll(r, width, 1)
        high = pltpu.roll(r, lanes - width, 1)
        near = jnp.where(
            local[0:1] < width // 2,
            jnp.where(low[3:4] >= local[0:1] + 1, 1.0, 0.0),
            jnp.where(high[2:3] >= width - local[0:1], 1.0, 0.0),
        )
        masks[layer, 0:1] = near
        masks[layer, 1:3] = jnp.where(r[0:2] >= 2, 1.0, 0.0)

    def put(tile, up, down):
        up, down = (v.reshape(-1, TAIL, lanes) for v in (up, down))
        where = pl.ds(tile, up.shape[0])
        msg_a[where] = jnp.where(even, up, down)
        msg_b[where] = jnp.where(even, down, up)

    put(0, masks[layers - 1], masks[0])
    for c in copies[:8]:
        c.wait()
    ln = Lanes(faces.shape[2:], width)
    top = edge_total(plane_at(ln, faces, n - 2), masks[layers - 1, 0:1])
    low = edge_total(plane_at(ln, faces, 1), masks[0, 0:1])
    ups = [faces[i, n - 1] for i in range(4)] + [top, faces[0, n - 1]]
    downs = [faces[0, 1]] + [faces[i, 0] for i in (1, 2, 3)] + [low, faces[0, 0]]
    for i, (up, down) in enumerate(zip(ups, downs)):
        put(1 + i * (rows // TAIL), up, down)

    for c in copies[8:]:
        c.wait()

    @pl.when(eager)
    def _():
        for c in clears:
            c.wait()


def bulk_kernel(
    width, blocks, axis, count, faces, masks, msg, held, out, zeros, buf, side, sems, side_sems, zero_sems
):
    del held
    layers = masks.shape[0]
    rows, lanes = faces.shape[2:]
    box, depth = 3 * width, width - 2
    bases = layers * blocks
    zeros[...] = jnp.zeros(zeros.shape, jnp.float32)

    me = lax.axis_index(axis)
    lower = lax.rem(me, 2) == 1
    early = early_runs(bases)

    def clear(b):
        return clear_run(zeros, out, b, bases, width, zero_sems.at[b])

    def each_run(act):
        act(clear(0))
        act(clear(bases))

        @pl.loop(1, early.start)
        def _(b):
            act(clear(b))

        @pl.when(me != 1)
        def _():
            for b in early:
                act(clear(b))

    each_run(lambda c: c.start())
    ln = Lanes((rows, lanes), width)
    plane = functools.partial(plane_at, ln, faces)

    def send(k, layer):
        start = 4 if layer == 0 else 0
        count = width + 4 - start - (4 if layer == layers - 1 else 0)
        return pltpu.make_async_copy(
            buf.at[layer, k, pl.ds(start, count)],
            out.at[pl.ds((layer * blocks + k) * box + depth + start, count)],
            sems.at[layer * blocks + k],
        )

    def between(layer):
        base = layer * width
        ma, mb = masks[layer - 1, 0:1], masks[layer, 0:1]
        to_above, to_below = masks[layer - 1, 2:3], masks[layer, 1:2]
        a3, a2, a1 = (plane(base - i) for i in (3, 2, 1))
        b0, b1, b2 = (plane(base + i) for i in (0, 1, 2))
        a1.edge(False)
        b0.edge(True)
        low = functools.partial(store, ln, buf.at[layer - 1])
        high = functools.partial(store, ln, buf.at[layer])
        vo, vz, vx, total = second(a2, a1, a3, False, ma, to_below)
        low(width, blocks, vo, vz, total)
        high(0, blocks, vx, None, total)
        vo, vz = edge_own(a1, 1.0 - a2.z1, a2.z1, b0.x1, False, ma)
        vx, vd = edge_spill(a1, b0, False)
        total = edge_total(a1, ma)
        low(width + 1, blocks, vo, vz, total)
        high(1, blocks, vx, vd, total)
        vo, vz = edge_own(b0, 1.0 - b1.z1, b1.z1, a1.x1, True, mb)
        vx, vd = edge_spill(b0, a1, True)
        total = edge_total(b0, mb)
        high(2, blocks, vo, vz, total)
        low(width + 2, blocks, vx, vd, total)
        vo, vz, vx, total = second(b1, b0, b2, True, mb, to_above)
        high(3, blocks, vo, vz, total)
        low(width + 3, blocks, vx, None, total)

    for layer in range(layers):
        planes = [plane(layer * width + j) for j in range(1, width - 1)]
        mz = masks[layer, 0:1]
        for j in range(2, width - 2):
            vo, vz, total = middle(planes[j - 1], planes[j - 2], planes[j], mz)
            store(ln, buf.at[layer], j + 2, blocks, vo, vz, total)
        if layer < layers - 1:
            between(layer + 1)
        else:
            valid = lower | (me < count - 1)
            work_side(ln, lower, valid, faces, masks, msg, store_side(ln, side, lower, blocks))

        @pl.loop(0, blocks)
        def _(k):
            send(k, layer).start()
            if layer == layers - 1:
                send_one_side(side, out, lower, width, layers, side_sems, k).start()

    each_run(lambda c: c.wait())

    @pl.loop(0, blocks)
    def _(k):
        for layer in range(layers):
            send(k, layer).wait()
        send_one_side(side, out, lower, width, layers, side_sems, k).wait()


def edge_kernel(width, blocks, axis, count, faces, masks, msg, held, out, side, sems):
    del held
    layers = masks.shape[0]
    me = lax.axis_index(axis)
    lower = lax.rem(me, 2) == 0
    valid = jnp.where(lower, me > 0, me < count - 1)
    ln = Lanes(faces.shape[2:], width)
    work_side(ln, lower, valid, faces, masks, msg, store_side(ln, side, lower, blocks))
    copies = [send_one_side(side, out, lower, width, layers, sems, k) for k in range(blocks)]
    for c in copies:
        c.start()
    for c in copies:
        c.wait()


def swaps(firsts):
    return [pair for i in firsts for pair in ((i, i + 1), (i + 1, i))]


def on_device(trans_east, trans_north, trans_up, storage, support_reach, *, axis, count):
    layers, blocks, _ = support_reach.shape
    n, rows, lanes = trans_east.shape
    width = n // layers
    f32 = jnp.float32
    anywhere = pl.BlockSpec(memory_space=pl.ANY)
    vmem = pl.BlockSpec(memory_space=pltpu.VMEM)
    params = pltpu.CompilerParams(vmem_limit_bytes=16 * 2**20)
    outside = tuple(
        pltpu.with_memory_space_constraint(x, pltpu.HBM)
        for x in (trans_east, trans_north, trans_up, storage)
    )
    reach = jnp.transpose(support_reach, (0, 2, 1))
    reach = pltpu.with_memory_space_constraint(reach, pltpu.HBM)
    bases = layers * blocks
    out_shape = jax.ShapeDtypeStruct((bases * 3 * width, rows, lanes), f32)
    side = pltpu.VMEM((blocks, 4, rows, lanes), f32)
    zeros = pltpu.VMEM((2 * (width - 2), rows, lanes), f32)
    tiles = 1 + 6 * rows // TAIL
    msg_a, msg_b, masks, faces, cleared = pl.pallas_call(
        functools.partial(pack_kernel, n, width, axis),
        out_shape=(
            pltpu.VMEM((tiles + 1, TAIL, lanes), f32),
            pltpu.VMEM((tiles, TAIL, lanes), f32),
            pltpu.VMEM((layers, TAIL, lanes), f32),
            pltpu.VMEM((4, n, rows, lanes), f32),
            out_shape,
        ),
        in_specs=[anywhere] * 5,
        out_specs=(vmem,) * 4 + (anywhere,),
        scratch_shapes=[
            pltpu.VMEM((layers, 4, blocks), jnp.int32),
            zeros,
            pltpu.SemaphoreType.DMA((13,)),
            pltpu.SemaphoreType.DMA((EARLY,)),
        ],
        compiler_params=params,
        name="pack",
    )(*outside, reach)
    got_a = lax.ppermute(msg_a, axis, swaps(range(0, count - 1, 2)))
    got_b = lax.ppermute(msg_b, axis, swaps(range(1, count - 1, 2)))

    bulk = pl.pallas_call(
        functools.partial(bulk_kernel, width, blocks, axis, count),
        out_shape=out_shape,
        in_specs=[vmem] * 3 + [anywhere],
        out_specs=anywhere,
        scratch_shapes=[
            zeros,
            pltpu.VMEM((layers, blocks, width + 4, rows, lanes), f32),
            side,
            pltpu.SemaphoreType.DMA((bases,)),
            pltpu.SemaphoreType.DMA((blocks,)),
            pltpu.SemaphoreType.DMA((bases + 1,)),
        ],
        input_output_aliases={3: 0},
        compiler_params=params,
        cost_estimate=pl.CostEstimate(flops=10**7, bytes_accessed=7 * 10**6, transcendentals=0),
        name="bulk",
    )(faces, masks, got_a, cleared)
    out = pl.pallas_call(
        functools.partial(edge_kernel, width, blocks, axis, count),
        out_shape=out_shape,
        in_specs=[vmem] * 3 + [anywhere],
        out_specs=anywhere,
        scratch_shapes=[
            side,
            pltpu.SemaphoreType.DMA((blocks,)),
        ],
        input_output_aliases={3: 0},
        compiler_params=params,
        cost_estimate=pl.CostEstimate(flops=10**6, bytes_accessed=10**6, transcendentals=0),
        name="edges",
    )(faces, masks, got_b, bulk)
    return out.reshape(layers, blocks, 3 * width, rows, lanes)


def solution(mesh):
    spread = P(("groups", "blk"))
    return jax.shard_map(
        functools.partial(on_device, axis="blk", count=mesh.shape["blk"]),
        mesh=mesh,
        in_specs=(spread,) * 5,
        out_specs=spread,
        check_vma=False,
    )
```

```python
import functools

import jax
import jax.numpy as jnp
from jax import lax
from jax.experimental import pallas as pl
from jax.experimental.pallas import tpu as pltpu
from jax.sharding import PartitionSpec as P


TAIL = 8
EARLY = 8
END = 4


class Lanes:
    def __init__(self, shape, width):
        tile = lax.broadcasted_iota(jnp.int32, (TAIL, shape[1]), 1)

        def rows(v):
            return jnp.concatenate([v] * (shape[0] // TAIL), axis=0)

        self.rows, self.lanes = shape
        self.width = width
        self.lane = rows(tile)
        self.local = rows(lax.rem(tile, width))
        self.first = self.local == 0
        self.last = self.local == width - 1
        self.odd = rows(lax.rem(tile // width, 2)) == 1
        self.row0 = lax.broadcasted_iota(jnp.int32, shape, 0) == 0
        self.lane0 = self.lane == 0

    def around(self, k):
        start = k * self.width - self.width // 2
        return (self.lane >= start) & (self.lane < start + 2 * self.width)

    def zm(self, v):
        return pltpu.roll(v, 1, 1)

    def zp(self, v):
        return pltpu.roll(v, self.lanes - 1, 1)

    def ym(self, v):
        return pltpu.roll(v, 1, 0)

    def yp(self, v):
        return pltpu.roll(v, self.rows - 1, 0)


def reciprocal(x):
    r = pl.reciprocal(x, approx=True)
    return r * (2.0 - x * r)


def cross(ln, ty, tz, s):
    ty = jnp.where(ln.row0, 0.0, ty)
    tz = jnp.where(ln.lane0, 0.0, tz)
    typ, tzp = ln.yp(ty), ln.zp(tz)
    return s * (1.0 / 3.0) + ((ty + typ) + (tz + tzp)), (ty, typ, tz, tzp)


class Plane:
    def __init__(self, ln, tx, txn, ty, tz, s, valid=None):
        self.ln = ln
        self.tx, self.txn = tx, txn
        e, (self.ty, self.typ, self.tz, self.tzp) = cross(ln, ty, tz, s)
        e = e + (tx + txn)
        if valid is not None:
            e = jnp.where(valid, e, 1.0)
        self.half = 0.5 * e + s * (1.0 / 3.0)
        self.spread(e)

    def spread(self, e):
        ln = self.ln
        self.all = 1.5 * e
        self.q = reciprocal(self.all)
        self.z1 = self.q * jnp.where(ln.first, self.tz, jnp.where(ln.last, self.tzp, 0.0))
        self.zm = ln.zm(self.z1)
        self.zp = ln.zp(self.z1)

    def toward(self, low):
        return self.tx if low else self.txn

    def inward(self, low):
        return self.txn if low else self.tx

    def edge(self, low):
        self.x1 = self.q * self.toward(low)
        self.o1 = 1.0 - self.z1 - self.x1

    def rim(self):
        return self.tz * self.zm + self.tzp * self.zp

    def along_y(self, v):
        return self.ty * self.ln.ym(v) + self.typ * self.ln.yp(v)


class Rim(Plane):
    def __init__(self, ln, e, tz):
        self.ln = ln
        self.tz = jnp.where(ln.lane0, 0.0, tz)
        self.tzp = ln.zp(self.tz)
        self.spread(e)


def middle(p, below, above, mz):
    ln = p.ln
    vz = p.half * p.z1 + p.tx * below.z1 + p.txn * above.z1 + p.along_y(p.z1)
    vz = vz + p.tz * jnp.where(ln.first, 1.0 - p.zm, p.zm)
    vz = vz + p.tzp * jnp.where(ln.last, 1.0 - p.zp, p.zp)
    kept = vz * mz
    return p.all - vz, kept, p.all - (vz - kept)


def second(p, edge, inner, low, mz, mx):
    below, above = (edge, inner) if low else (inner, edge)
    ln = p.ln
    first_o = ln.zm(p.z1)
    vz = p.half * p.z1 + p.tx * below.z1 + p.txn * above.z1 + p.along_y(p.z1)
    vz = vz + p.tz * jnp.where(ln.first, 1.0 - first_o, first_o)
    vz = vz + p.tzp * jnp.where(ln.last, 1.0 - p.zp, p.zp)
    vx = p.toward(low) * edge.x1
    kept_z, kept_x = vz * mz, vx * mx
    total = p.all - (vz - kept_z) - (vx - kept_x)
    return p.all - vz - vx, kept_z, kept_x, total


def edge_own(p, inner_o1, inner_z1, outer_x1, low, mz):
    ln = p.ln
    om, op = ln.zm(p.o1), ln.zp(p.o1)
    vo = p.half * p.o1 + p.toward(low) * outer_x1 + p.inward(low) * inner_o1 + p.along_y(p.o1)
    vo = vo + p.tz * jnp.where(ln.first, p.zm, om) + p.tzp * jnp.where(ln.last, p.zp, op)
    vz = p.half * p.z1 + p.inward(low) * inner_z1 + p.along_y(p.z1)
    vz = vz + p.tz * jnp.where(ln.first, om, p.zm) + p.tzp * jnp.where(ln.last, op, p.zp)
    return vo, vz * mz


def edge_total(p, mz):
    rim = p.rim()
    return p.all - (rim - rim * mz)


def edge_spill(p, own, low):
    ln = p.ln
    xm, xp = ln.zm(p.x1), ln.zp(p.x1)
    face = p.toward(low)
    vx = p.half * p.x1 + face * own.o1 + p.along_y(p.x1)
    vx = vx + p.tz * jnp.where(ln.first, 0.0, xm) + p.tzp * jnp.where(ln.last, 0.0, xp)
    vd = face * own.z1 + p.tz * jnp.where(ln.first, xm, 0.0) + p.tzp * jnp.where(ln.last, xp, 0.0)
    return vx, vd


def store(ln, dst, plane, blocks, own, other, total):
    scale = reciprocal(total)
    own = own * scale
    other = jnp.zeros_like(own) if other is None else other * scale
    even, odd = jnp.where(ln.odd, other, own), jnp.where(ln.odd, own, other)
    for k in range(blocks):
        dst[k, plane] = jnp.where(ln.around(k), odd if k % 2 else even, 0.0)


def work_side(ln, low, valid, ends, masks, msg, put):
    rows, lanes = ends.shape[2:]
    layers = masks.shape[0]

    def own(i, j):
        return ends[i, jnp.where(low, j, 2 * END - 1 - j)]

    def got(i):
        tiles = rows // TAIL
        return msg[pl.ds(1 + tiles * i, tiles)].reshape(rows, lanes)

    f1, f2, f3 = (ends[0, jnp.where(low, j, 2 * END - j)] for j in (1, 2, 3))
    f0 = jnp.where(valid, jnp.where(low, ends[0, 0], got(6)), 0.0)
    g1 = got(0)
    a0 = Plane(ln, f0, f1, own(1, 0), own(2, 0), own(3, 0))
    a1 = Plane(ln, f1, f2, own(1, 1), own(2, 1), own(3, 1))
    a2 = Plane(ln, f2, f3, own(1, 2), own(2, 2), own(3, 2))
    b0 = Plane(ln, g1, f0, got(1), got(2), got(3), valid)
    b1 = Rim(ln, jnp.where(valid, got(4) + g1, 1.0), got(5))
    mine = masks[jnp.where(low, 0, layers - 1)]
    mz, my_reach = mine[0:1], jnp.where(low, mine[1:2], mine[2:3])
    theirs = msg[0]
    mo, their_reach = theirs[0:1], jnp.where(low, theirs[2:3], theirs[1:2])
    a0.edge(True)
    b0.edge(False)
    vx = g1 * b0.x1
    kept = vx * my_reach
    put(0, kept, None, edge_total(b1, mo) - (vx - kept))
    vx, vd = edge_spill(b0, a0, False)
    put(1, vx, vd, edge_total(b0, mo))
    vo, vz = edge_own(a0, 1.0 - a1.z1, a1.z1, b0.x1, True, mz)
    put(2, vo, vz, edge_total(a0, mz))
    vo, vz, _, total = second(a1, a0, a2, True, mz, their_reach)
    put(3, vo, vz, total)


def store_side(ln, buf, low, blocks):
    def put(i, own, other, total):
        store(ln, buf, jnp.where(low, i, 3 - i), blocks, own, other, total)

    return put


def send_one_side(buf, out, low, width, layers, sems, k):
    layer = jnp.where(low, 0, layers - 1)
    start = jnp.where(low, width - 2, 2 * width - 2)
    there = out.at[pl.ds((layer * buf.shape[0] + k) * 3 * width + start, 4)]
    return pltpu.make_async_copy(buf.at[k], there, sems.at[k])


def clear_run(zeros, out, b, bases, width, sem):
    depth = width - 2
    ends = isinstance(b, int) and b in (0, bases)
    count = depth if ends else 2 * depth
    start = 0 if ends and b == 0 else b * 3 * width - depth
    return pltpu.make_async_copy(zeros.at[pl.ds(0, count)], out.at[pl.ds(start, count)], sem)


def early_runs(bases):
    return range(bases - EARLY, bases)


def pack_kernel(
    n, width, axis, tx, ty, tz, s, reach, msg_a, msg_b, masks, ends, out,
    held_reach, zeros, sems, zero_sems,
):
    layers, _, blocks = held_reach.shape
    lanes = masks.shape[-1]
    fetch = pltpu.make_async_copy(reach, held_reach, sems.at[8])
    fetch.start()
    copies = []
    for i, a in enumerate((tx, ty, tz, s)):
        for there, here in ((0, 0), (n - END, END)):
            src, dst = a.at[pl.ds(there, END)], ends.at[i, pl.ds(here, END)]
            copies.append(pltpu.make_async_copy(src, dst, sems.at[len(copies)]))
            copies[-1].start()
    rows = ends.shape[2]
    bases = layers * blocks
    clears = [clear_run(zeros, out, b, bases, width, zero_sems.at[i]) for i, b in enumerate(early_runs(bases))]
    even = lax.rem(lax.axis_index(axis), 2) == 0

    eager = lax.axis_index(axis) == 1

    @pl.when(eager)
    def _():
        zeros[...] = jnp.zeros(zeros.shape, jnp.float32)
        for c in clears:
            c.start()

    masks[...] = jnp.zeros(masks.shape, jnp.float32)
    lane = lax.broadcasted_iota(jnp.int32, (4, lanes), 1)
    block = lane // width
    local = lane - block * width
    fetch.wait()
    for layer in range(layers):
        r = jnp.zeros((4, lanes), jnp.int32)
        for k in range(blocks):
            r = jnp.where(block == k, held_reach[layer, :, k : k + 1], r)
        low = pltpu.roll(r, width, 1)
        high = pltpu.roll(r, lanes - width, 1)
        near = jnp.where(
            local[0:1] < width // 2,
            jnp.where(low[3:4] >= local[0:1] + 1, 1.0, 0.0),
            jnp.where(high[2:3] >= width - local[0:1], 1.0, 0.0),
        )
        masks[layer, 0:1] = near
        masks[layer, 1:3] = jnp.where(r[0:2] >= 2, 1.0, 0.0)

    def put(tile, up, down):
        up, down = (v.reshape(-1, TAIL, lanes) for v in (up, down))
        where = pl.ds(tile, up.shape[0])
        msg_a[where] = jnp.where(even, up, down)
        msg_b[where] = jnp.where(even, down, up)

    put(0, masks[layers - 1], masks[0])
    for c in copies:
        c.wait()
    ln = Lanes(ends.shape[2:], width)
    e = 2 * END - 1
    top, _ = cross(ln, ends[1, e - 1], ends[2, e - 1], ends[3, e - 1])
    low, _ = cross(ln, ends[1, 1], ends[2, 1], ends[3, 1])
    ups = [ends[i, e] for i in range(4)] + [top + ends[0, e - 1], ends[2, e - 1], ends[0, e]]
    downs = [ends[0, 1]] + [ends[i, 0] for i in (1, 2, 3)] + [low + ends[0, 2], ends[2, 1], ends[0, 0]]
    for i, (up, down) in enumerate(zip(ups, downs)):
        put(1 + i * (rows // TAIL), up, down)

    @pl.when(eager)
    def _():
        for c in clears:
            c.wait()


def bulk_kernel(
    n, width, blocks, axis, count, tx, ty, tz, s, ends, masks, msg, held, out,
    mid, zeros, buf, side, read_sems, sems, side_sems, zero_sems,
):
    del held
    layers = masks.shape[0]
    rows, lanes = ends.shape[2:]
    box, depth = 3 * width, width - 2
    bases = layers * blocks
    reads = []
    for layer in range(layers):
        start = layer * width + END
        part = pl.ds(start, min(width, n - END - start))
        reads.append([
            pltpu.make_async_copy(a.at[part], mid.at[i, part], read_sems.at[layer * 4 + i])
            for i, a in enumerate((tx, ty, tz, s))
        ])
    for c in sum(reads, []):
        c.start()
    zeros[...] = jnp.zeros(zeros.shape, jnp.float32)

    me = lax.axis_index(axis)
    lower = lax.rem(me, 2) == 1
    early = early_runs(bases)

    def clear(b):
        return clear_run(zeros, out, b, bases, width, zero_sems.at[b])

    def each_run(act):
        act(clear(0))
        act(clear(bases))

        @pl.loop(1, early.start)
        def _(b):
            act(clear(b))

        @pl.when(me != 1)
        def _():
            for b in early:
                act(clear(b))

    each_run(lambda c: c.start())
    ln = Lanes((rows, lanes), width)

    def field(i, p):
        if p < END:
            return ends[i, p]
        return mid[i, p] if p < n - END else ends[i, p - n + 2 * END]

    def plane(p):
        return Plane(ln, field(0, p), field(0, p + 1), field(1, p), field(2, p), field(3, p))

    def send(k, layer):
        start = 4 if layer == 0 else 0
        count = width + 4 - start - (4 if layer == layers - 1 else 0)
        return pltpu.make_async_copy(
            buf.at[layer, k, pl.ds(start, count)],
            out.at[pl.ds((layer * blocks + k) * box + depth + start, count)],
            sems.at[layer * blocks + k],
        )

    def between(layer):
        base = layer * width
        ma, mb = masks[layer - 1, 0:1], masks[layer, 0:1]
        to_above, to_below = masks[layer - 1, 2:3], masks[layer, 1:2]
        a3, a2, a1 = (plane(base - i) for i in (3, 2, 1))
        b0, b1, b2 = (plane(base + i) for i in (0, 1, 2))
        a1.edge(False)
        b0.edge(True)
        low = functools.partial(store, ln, buf.at[layer - 1])
        high = functools.partial(store, ln, buf.at[layer])
        vo, vz, vx, total = second(a2, a1, a3, False, ma, to_below)
        low(width, blocks, vo, vz, total)
        high(0, blocks, vx, None, total)
        vo, vz = edge_own(a1, 1.0 - a2.z1, a2.z1, b0.x1, False, ma)
        vx, vd = edge_spill(a1, b0, False)
        total = edge_total(a1, ma)
        low(width + 1, blocks, vo, vz, total)
        high(1, blocks, vx, vd, total)
        vo, vz = edge_own(b0, 1.0 - b1.z1, b1.z1, a1.x1, True, mb)
        vx, vd = edge_spill(b0, a1, True)
        total = edge_total(b0, mb)
        high(2, blocks, vo, vz, total)
        low(width + 2, blocks, vx, vd, total)
        vo, vz, vx, total = second(b1, b0, b2, True, mb, to_above)
        high(3, blocks, vo, vz, total)
        low(width + 3, blocks, vx, None, total)

    for layer in range(layers):
        for c in reads[layer]:
            c.wait()
        planes = [plane(layer * width + j) for j in range(1, width - 1)]
        mz = masks[layer, 0:1]
        for j in range(2, width - 2):
            vo, vz, total = middle(planes[j - 1], planes[j - 2], planes[j], mz)
            store(ln, buf.at[layer], j + 2, blocks, vo, vz, total)
        if layer < layers - 1:
            between(layer + 1)
        else:
            valid = lower | (me < count - 1)
            work_side(ln, lower, valid, ends, masks, msg, store_side(ln, side, lower, blocks))

        @pl.loop(0, blocks)
        def _(k):
            send(k, layer).start()
            if layer == layers - 1:
                send_one_side(side, out, lower, width, layers, side_sems, k).start()

    each_run(lambda c: c.wait())

    @pl.loop(0, blocks)
    def _(k):
        for layer in range(layers):
            send(k, layer).wait()
        send_one_side(side, out, lower, width, layers, side_sems, k).wait()


def edge_kernel(width, blocks, axis, count, ends, masks, msg, held, out, side, sems):
    del held
    layers = masks.shape[0]
    me = lax.axis_index(axis)
    lower = lax.rem(me, 2) == 0
    valid = jnp.where(lower, me > 0, me < count - 1)
    ln = Lanes(ends.shape[2:], width)
    work_side(ln, lower, valid, ends, masks, msg, store_side(ln, side, lower, blocks))
    copies = [send_one_side(side, out, lower, width, layers, sems, k) for k in range(blocks)]
    for c in copies:
        c.start()
    for c in copies:
        c.wait()


def swaps(firsts):
    return [pair for i in firsts for pair in ((i, i + 1), (i + 1, i))]


def on_device(trans_east, trans_north, trans_up, storage, support_reach, *, axis, count):
    layers, blocks, _ = support_reach.shape
    n, rows, lanes = trans_east.shape
    width = n // layers
    f32 = jnp.float32
    anywhere = pl.BlockSpec(memory_space=pl.ANY)
    vmem = pl.BlockSpec(memory_space=pltpu.VMEM)
    params = pltpu.CompilerParams(vmem_limit_bytes=16 * 2**20)
    outside = tuple(
        pltpu.with_memory_space_constraint(x, pltpu.HBM)
        for x in (trans_east, trans_north, trans_up, storage)
    )
    reach = jnp.transpose(support_reach, (0, 2, 1))
    reach = pltpu.with_memory_space_constraint(reach, pltpu.HBM)
    bases = layers * blocks
    out_shape = jax.ShapeDtypeStruct((bases * 3 * width, rows, lanes), f32)
    side = pltpu.VMEM((blocks, 4, rows, lanes), f32)
    zeros = pltpu.VMEM((2 * (width - 2), rows, lanes), f32)
    tiles = 1 + 7 * rows // TAIL
    msg_a, msg_b, masks, ends, cleared = pl.pallas_call(
        functools.partial(pack_kernel, n, width, axis),
        out_shape=(
            pltpu.VMEM((tiles + 1, TAIL, lanes), f32),
            pltpu.VMEM((tiles, TAIL, lanes), f32),
            pltpu.VMEM((layers, TAIL, lanes), f32),
            pltpu.VMEM((4, 2 * END, rows, lanes), f32),
            out_shape,
        ),
        in_specs=[anywhere] * 5,
        out_specs=(vmem,) * 4 + (anywhere,),
        scratch_shapes=[
            pltpu.VMEM((layers, 4, blocks), jnp.int32),
            zeros,
            pltpu.SemaphoreType.DMA((9,)),
            pltpu.SemaphoreType.DMA((EARLY,)),
        ],
        compiler_params=params,
        name="pack",
    )(*outside, reach)
    got_a = lax.ppermute(msg_a, axis, swaps(range(0, count - 1, 2)))
    got_b = lax.ppermute(msg_b, axis, swaps(range(1, count - 1, 2)))

    bulk = pl.pallas_call(
        functools.partial(bulk_kernel, n, width, blocks, axis, count),
        out_shape=out_shape,
        in_specs=[anywhere] * 4 + [vmem] * 3 + [anywhere],
        out_specs=anywhere,
        scratch_shapes=[
            pltpu.VMEM((4, n, rows, lanes), f32),
            zeros,
            pltpu.VMEM((layers, blocks, width + 4, rows, lanes), f32),
            side,
            pltpu.SemaphoreType.DMA((4 * layers,)),
            pltpu.SemaphoreType.DMA((bases,)),
            pltpu.SemaphoreType.DMA((blocks,)),
            pltpu.SemaphoreType.DMA((bases + 1,)),
        ],
        input_output_aliases={7: 0},
        compiler_params=params,
        cost_estimate=pl.CostEstimate(flops=10**7, bytes_accessed=7 * 10**6, transcendentals=0),
        name="bulk",
    )(*outside, ends, masks, got_a, cleared)
    out = pl.pallas_call(
        functools.partial(edge_kernel, width, blocks, axis, count),
        out_shape=out_shape,
        in_specs=[vmem] * 3 + [anywhere],
        out_specs=anywhere,
        scratch_shapes=[
            side,
            pltpu.SemaphoreType.DMA((blocks,)),
        ],
        input_output_aliases={3: 0},
        compiler_params=params,
        cost_estimate=pl.CostEstimate(flops=10**6, bytes_accessed=10**6, transcendentals=0),
        name="edges",
    )(ends, masks, got_b, bulk)
    return out.reshape(layers, blocks, 3 * width, rows, lanes)


def solution(mesh):
    spread = P(("groups", "blk"))
    return jax.shard_map(
        functools.partial(on_device, axis="blk", count=mesh.shape["blk"]),
        mesh=mesh,
        in_specs=(spread,) * 5,
        out_specs=spread,
        check_vma=False,
    )
```

```python
import functools

import jax
import jax.numpy as jnp
from jax import lax
from jax.experimental import pallas as pl
from jax.experimental.pallas import tpu as pltpu
from jax.sharding import PartitionSpec as P


TAIL = 8
EARLY = 8


class Lanes:
    def __init__(self, shape, width):
        tile = lax.broadcasted_iota(jnp.int32, (TAIL, shape[1]), 1)

        def rows(v):
            return jnp.concatenate([v] * (shape[0] // TAIL), axis=0)

        self.rows, self.lanes = shape
        self.width = width
        self.lane = rows(tile)
        self.local = rows(lax.rem(tile, width))
        self.first = self.local == 0
        self.last = self.local == width - 1
        self.odd = rows(lax.rem(tile // width, 2)) == 1
        self.row0 = lax.broadcasted_iota(jnp.int32, shape, 0) == 0
        self.lane0 = self.lane == 0

    def around(self, k):
        start = k * self.width - self.width // 2
        return (self.lane >= start) & (self.lane < start + 2 * self.width)

    def zm(self, v):
        return pltpu.roll(v, 1, 1)

    def zp(self, v):
        return pltpu.roll(v, self.lanes - 1, 1)

    def ym(self, v):
        return pltpu.roll(v, 1, 0)

    def yp(self, v):
        return pltpu.roll(v, self.rows - 1, 0)


def reciprocal(x):
    r = pl.reciprocal(x, approx=True)
    return r * (2.0 - x * r)


def within_y(ln, ty):
    ty = jnp.where(ln.row0, 0.0, ty)
    return ty, ln.yp(ty)


def within_z(ln, tz):
    tz = jnp.where(ln.lane0, 0.0, tz)
    return tz, ln.zp(tz)


def cross(ln, ty, tz, s):
    ty, typ = within_y(ln, ty)
    tz, tzp = within_z(ln, tz)
    return s * (1.0 / 3.0) + ((ty + typ) + (tz + tzp)), (ty, typ, tz, tzp)


class Plane:
    def __init__(self, ln, tx, txn, ty, tz, s, valid=None):
        self.ln = ln
        self.tx, self.txn = tx, txn
        e, (self.ty, self.typ, self.tz, self.tzp) = cross(ln, ty, tz, s)
        e = e + (tx + txn)
        if valid is not None:
            e = jnp.where(valid, e, 1.0)
        self.half = 0.5 * e + s * (1.0 / 3.0)
        self.spread(e)

    def spread(self, e):
        ln = self.ln
        self.all = 1.5 * e
        self.q = reciprocal(self.all)
        self.z1 = self.q * jnp.where(ln.first, self.tz, jnp.where(ln.last, self.tzp, 0.0))
        self.zm = ln.zm(self.z1)
        self.zp = ln.zp(self.z1)

    def toward(self, low):
        return self.tx if low else self.txn

    def inward(self, low):
        return self.txn if low else self.tx

    def edge(self, low):
        self.x1 = self.q * self.toward(low)
        self.o1 = 1.0 - self.z1 - self.x1

    def rim(self):
        return self.tz * self.zm + self.tzp * self.zp

    def along_y(self, v):
        return self.ty * self.ln.ym(v) + self.typ * self.ln.yp(v)


class Rim(Plane):
    def __init__(self, ln, e, tz):
        self.ln = ln
        self.tz = jnp.where(ln.lane0, 0.0, tz)
        self.tzp = ln.zp(self.tz)
        self.spread(e)


def plane_at(ln, faces, p):
    return Plane(ln, faces[0, p], faces[0, p + 1], faces[1, p], faces[2, p], faces[3, p])


def middle(p, below, above, mz):
    ln = p.ln
    vz = p.half * p.z1 + p.tx * below.z1 + p.txn * above.z1 + p.along_y(p.z1)
    vz = vz + p.tz * jnp.where(ln.first, 1.0 - p.zm, p.zm)
    vz = vz + p.tzp * jnp.where(ln.last, 1.0 - p.zp, p.zp)
    kept = vz * mz
    return p.all - vz, kept, p.all - (vz - kept)


def second(p, edge, inner, low, mz, mx):
    below, above = (edge, inner) if low else (inner, edge)
    ln = p.ln
    first_o = ln.zm(p.z1)
    vz = p.half * p.z1 + p.tx * below.z1 + p.txn * above.z1 + p.along_y(p.z1)
    vz = vz + p.tz * jnp.where(ln.first, 1.0 - first_o, first_o)
    vz = vz + p.tzp * jnp.where(ln.last, 1.0 - p.zp, p.zp)
    vx = p.toward(low) * edge.x1
    kept_z, kept_x = vz * mz, vx * mx
    total = p.all - (vz - kept_z) - (vx - kept_x)
    return p.all - vz - vx, kept_z, kept_x, total


def edge_own(p, inner_o1, inner_z1, outer_x1, low, mz):
    ln = p.ln
    om, op = ln.zm(p.o1), ln.zp(p.o1)
    vo = p.half * p.o1 + p.toward(low) * outer_x1 + p.inward(low) * inner_o1 + p.along_y(p.o1)
    vo = vo + p.tz * jnp.where(ln.first, p.zm, om) + p.tzp * jnp.where(ln.last, p.zp, op)
    vz = p.half * p.z1 + p.inward(low) * inner_z1 + p.along_y(p.z1)
    vz = vz + p.tz * jnp.where(ln.first, om, p.zm) + p.tzp * jnp.where(ln.last, op, p.zp)
    return vo, vz * mz


def edge_total(p, mz):
    rim = p.rim()
    return p.all - (rim - rim * mz)


def edge_spill(p, own, low):
    ln = p.ln
    xm, xp = ln.zm(p.x1), ln.zp(p.x1)
    face = p.toward(low)
    vx = p.half * p.x1 + face * own.o1 + p.along_y(p.x1)
    vx = vx + p.tz * jnp.where(ln.first, 0.0, xm) + p.tzp * jnp.where(ln.last, 0.0, xp)
    vd = face * own.z1 + p.tz * jnp.where(ln.first, xm, 0.0) + p.tzp * jnp.where(ln.last, xp, 0.0)
    return vx, vd


def store(ln, dst, plane, blocks, own, other, total):
    scale = reciprocal(total)
    own = own * scale
    other = jnp.zeros_like(own) if other is None else other * scale
    even, odd = jnp.where(ln.odd, other, own), jnp.where(ln.odd, own, other)
    for k in range(blocks):
        dst[k, plane] = jnp.where(ln.around(k), odd if k % 2 else even, 0.0)


def work_side(ln, low, valid, faces, masks, msg, put):
    n, rows, lanes = faces.shape[1:]
    layers = masks.shape[0]

    def own(i, j):
        return faces[i, jnp.where(low, j, n - 1 - j)]

    def got(i):
        tiles = rows // TAIL
        return msg[pl.ds(1 + tiles * i, tiles)].reshape(rows, lanes)

    f1, f2, f3 = (faces[0, jnp.where(low, j, n - j)] for j in (1, 2, 3))
    f0 = jnp.where(valid, jnp.where(low, faces[0, 0], got(6)), 0.0)
    g1 = got(0)
    a0 = Plane(ln, f0, f1, own(1, 0), own(2, 0), own(3, 0))
    a1 = Plane(ln, f1, f2, own(1, 1), own(2, 1), own(3, 1))
    a2 = Plane(ln, f2, f3, own(1, 2), own(2, 2), own(3, 2))
    b0 = Plane(ln, g1, f0, got(1), got(2), got(3), valid)
    b1 = Rim(ln, jnp.where(valid, got(4) + g1, 1.0), got(5))
    mine = masks[jnp.where(low, 0, layers - 1)]
    mz, my_reach = mine[0:1], jnp.where(low, mine[1:2], mine[2:3])
    theirs = msg[0]
    mo, their_reach = theirs[0:1], jnp.where(low, theirs[2:3], theirs[1:2])
    a0.edge(True)
    b0.edge(False)
    vx = g1 * b0.x1
    kept = vx * my_reach
    put(0, kept, None, edge_total(b1, mo) - (vx - kept))
    vx, vd = edge_spill(b0, a0, False)
    put(1, vx, vd, edge_total(b0, mo))
    vo, vz = edge_own(a0, 1.0 - a1.z1, a1.z1, b0.x1, True, mz)
    put(2, vo, vz, edge_total(a0, mz))
    vo, vz, _, total = second(a1, a0, a2, True, mz, their_reach)
    put(3, vo, vz, total)


def store_side(ln, buf, low, blocks):
    def put(i, own, other, total):
        store(ln, buf, jnp.where(low, i, 3 - i), blocks, own, other, total)

    return put


def send_one_side(buf, out, low, width, layers, sems, k):
    layer = jnp.where(low, 0, layers - 1)
    start = jnp.where(low, width - 2, 2 * width - 2)
    there = out.at[pl.ds((layer * buf.shape[0] + k) * 3 * width + start, 4)]
    return pltpu.make_async_copy(buf.at[k], there, sems.at[k])


def clear_run(zeros, out, b, bases, width, sem):
    depth = width - 2
    ends = isinstance(b, int) and b in (0, bases)
    count = depth if ends else 2 * depth
    start = 0 if ends and b == 0 else b * 3 * width - depth
    return pltpu.make_async_copy(zeros.at[pl.ds(0, count)], out.at[pl.ds(start, count)], sem)


def early_runs(bases):
    return range(bases - EARLY, bases)


def pack_kernel(
    n, width, axis, tx, ty, tz, s, reach, msg_a, msg_b, masks, faces, out,
    held_reach, zeros, sems, zero_sems,
):
    layers, _, blocks = held_reach.shape
    lanes = masks.shape[-1]
    fetch = pltpu.make_async_copy(reach, held_reach, sems.at[4])
    fetch.start()
    copies = [
        pltpu.make_async_copy(a, faces.at[i], sems.at[i]) for i, a in enumerate((tx, ty, tz, s))
    ]
    for i in (1, 2, 0, 3):
        copies[i].start()
    rows = faces.shape[2]
    bases = layers * blocks
    clears = [clear_run(zeros, out, b, bases, width, zero_sems.at[i]) for i, b in enumerate(early_runs(bases))]
    even = lax.rem(lax.axis_index(axis), 2) == 0

    eager = lax.axis_index(axis) == 1

    @pl.when(eager)
    def _():
        zeros[...] = jnp.zeros(zeros.shape, jnp.float32)
        for c in clears:
            c.start()

    masks[...] = jnp.zeros(masks.shape, jnp.float32)
    lane = lax.broadcasted_iota(jnp.int32, (4, lanes), 1)
    block = lane // width
    local = lane - block * width
    fetch.wait()
    for layer in range(layers):
        r = jnp.zeros((4, lanes), jnp.int32)
        for k in range(blocks):
            r = jnp.where(block == k, held_reach[layer, :, k : k + 1], r)
        low = pltpu.roll(r, width, 1)
        high = pltpu.roll(r, lanes - width, 1)
        near = jnp.where(
            local[0:1] < width // 2,
            jnp.where(low[3:4] >= local[0:1] + 1, 1.0, 0.0),
            jnp.where(high[2:3] >= width - local[0:1], 1.0, 0.0),
        )
        masks[layer, 0:1] = near
        masks[layer, 1:3] = jnp.where(r[0:2] >= 2, 1.0, 0.0)

    def put(tile, up, down):
        up, down = (v.reshape(-1, TAIL, lanes) for v in (up, down))
        where = pl.ds(tile, up.shape[0])
        msg_a[where] = jnp.where(even, up, down)
        msg_b[where] = jnp.where(even, down, up)

    put(0, masks[layers - 1], masks[0])
    ln = Lanes(faces.shape[2:], width)
    behind = {}

    def plane(slot, up, down):
        put(1 + slot * (rows // TAIL), up, down)

    for i, across in ((1, lambda v: within_y(ln, v)), (2, lambda v: within_z(ln, v))):
        copies[i].wait()
        plane(i, faces[i, n - 1], faces[i, 0])
        for p in (n - 2, 1):
            v, v_next = across(faces[i, p])
            behind[p] = behind.get(p, 0.0) + (v + v_next)
    plane(5, faces[2, n - 2], faces[2, 1])
    copies[0].wait()
    plane(0, faces[0, n - 1], faces[0, 1])
    plane(6, faces[0, n - 1], faces[0, 0])
    behind = {p: behind[p] + faces[0, q] for p, q in ((n - 2, n - 2), (1, 2))}
    copies[3].wait()
    plane(3, faces[3, n - 1], faces[3, 0])
    plane(4, *(behind[p] + faces[3, p] * (1.0 / 3.0) for p in (n - 2, 1)))

    @pl.when(eager)
    def _():
        for c in clears:
            c.wait()


def bulk_kernel(
    width, blocks, axis, count, faces, masks, msg, held, out, zeros, buf, side, sems, side_sems, zero_sems
):
    del held
    layers = masks.shape[0]
    rows, lanes = faces.shape[2:]
    box, depth = 3 * width, width - 2
    bases = layers * blocks
    zeros[...] = jnp.zeros(zeros.shape, jnp.float32)

    me = lax.axis_index(axis)
    lower = lax.rem(me, 2) == 1
    early = early_runs(bases)

    def clear(b):
        return clear_run(zeros, out, b, bases, width, zero_sems.at[b])

    def each_run(act):
        act(clear(0))
        act(clear(bases))

        @pl.loop(1, early.start)
        def _(b):
            act(clear(b))

        @pl.when(me != 1)
        def _():
            for b in early:
                act(clear(b))

    each_run(lambda c: c.start())
    ln = Lanes((rows, lanes), width)
    plane = functools.partial(plane_at, ln, faces)

    def send(k, layer):
        start = 4 if layer == 0 else 0
        count = width + 4 - start - (4 if layer == layers - 1 else 0)
        return pltpu.make_async_copy(
            buf.at[layer, k, pl.ds(start, count)],
            out.at[pl.ds((layer * blocks + k) * box + depth + start, count)],
            sems.at[layer * blocks + k],
        )

    def between(layer):
        base = layer * width
        ma, mb = masks[layer - 1, 0:1], masks[layer, 0:1]
        to_above, to_below = masks[layer - 1, 2:3], masks[layer, 1:2]
        a3, a2, a1 = (plane(base - i) for i in (3, 2, 1))
        b0, b1, b2 = (plane(base + i) for i in (0, 1, 2))
        a1.edge(False)
        b0.edge(True)
        low = functools.partial(store, ln, buf.at[layer - 1])
        high = functools.partial(store, ln, buf.at[layer])
        vo, vz, vx, total = second(a2, a1, a3, False, ma, to_below)
        low(width, blocks, vo, vz, total)
        high(0, blocks, vx, None, total)
        vo, vz = edge_own(a1, 1.0 - a2.z1, a2.z1, b0.x1, False, ma)
        vx, vd = edge_spill(a1, b0, False)
        total = edge_total(a1, ma)
        low(width + 1, blocks, vo, vz, total)
        high(1, blocks, vx, vd, total)
        vo, vz = edge_own(b0, 1.0 - b1.z1, b1.z1, a1.x1, True, mb)
        vx, vd = edge_spill(b0, a1, True)
        total = edge_total(b0, mb)
        high(2, blocks, vo, vz, total)
        low(width + 2, blocks, vx, vd, total)
        vo, vz, vx, total = second(b1, b0, b2, True, mb, to_above)
        high(3, blocks, vo, vz, total)
        low(width + 3, blocks, vx, None, total)

    for layer in range(layers):
        planes = [plane(layer * width + j) for j in range(1, width - 1)]
        mz = masks[layer, 0:1]
        for j in range(2, width - 2):
            vo, vz, total = middle(planes[j - 1], planes[j - 2], planes[j], mz)
            store(ln, buf.at[layer], j + 2, blocks, vo, vz, total)
        if layer < layers - 1:
            between(layer + 1)
        else:
            valid = lower | (me < count - 1)
            work_side(ln, lower, valid, faces, masks, msg, store_side(ln, side, lower, blocks))

        @pl.loop(0, blocks)
        def _(k):
            send(k, layer).start()
            if layer == layers - 1:
                send_one_side(side, out, lower, width, layers, side_sems, k).start()

    each_run(lambda c: c.wait())

    @pl.loop(0, blocks)
    def _(k):
        for layer in range(layers):
            send(k, layer).wait()
        send_one_side(side, out, lower, width, layers, side_sems, k).wait()


def edge_kernel(width, blocks, axis, count, faces, masks, msg, held, out, side, sems):
    del held
    layers = masks.shape[0]
    me = lax.axis_index(axis)
    lower = lax.rem(me, 2) == 0
    valid = jnp.where(lower, me > 0, me < count - 1)
    ln = Lanes(faces.shape[2:], width)
    work_side(ln, lower, valid, faces, masks, msg, store_side(ln, side, lower, blocks))
    copies = [send_one_side(side, out, lower, width, layers, sems, k) for k in range(blocks)]
    for c in copies:
        c.start()
    for c in copies:
        c.wait()


def swaps(firsts):
    return [pair for i in firsts for pair in ((i, i + 1), (i + 1, i))]


def on_device(trans_east, trans_north, trans_up, storage, support_reach, *, axis, count):
    layers, blocks, _ = support_reach.shape
    n, rows, lanes = trans_east.shape
    width = n // layers
    f32 = jnp.float32
    anywhere = pl.BlockSpec(memory_space=pl.ANY)
    vmem = pl.BlockSpec(memory_space=pltpu.VMEM)
    params = pltpu.CompilerParams(vmem_limit_bytes=16 * 2**20)
    outside = tuple(
        pltpu.with_memory_space_constraint(x, pltpu.HBM)
        for x in (trans_east, trans_north, trans_up, storage)
    )
    reach = jnp.transpose(support_reach, (0, 2, 1))
    reach = pltpu.with_memory_space_constraint(reach, pltpu.HBM)
    bases = layers * blocks
    out_shape = jax.ShapeDtypeStruct((bases * 3 * width, rows, lanes), f32)
    side = pltpu.VMEM((blocks, 4, rows, lanes), f32)
    zeros = pltpu.VMEM((2 * (width - 2), rows, lanes), f32)
    tiles = 1 + 7 * rows // TAIL
    msg_a, msg_b, masks, faces, cleared = pl.pallas_call(
        functools.partial(pack_kernel, n, width, axis),
        out_shape=(
            pltpu.VMEM((tiles + 1, TAIL, lanes), f32),
            pltpu.VMEM((tiles, TAIL, lanes), f32),
            pltpu.VMEM((layers, TAIL, lanes), f32),
            pltpu.VMEM((4, n, rows, lanes), f32),
            out_shape,
        ),
        in_specs=[anywhere] * 5,
        out_specs=(vmem,) * 4 + (anywhere,),
        scratch_shapes=[
            pltpu.VMEM((layers, 4, blocks), jnp.int32),
            zeros,
            pltpu.SemaphoreType.DMA((5,)),
            pltpu.SemaphoreType.DMA((EARLY,)),
        ],
        compiler_params=params,
        name="pack",
    )(*outside, reach)
    got_a = lax.ppermute(msg_a, axis, swaps(range(0, count - 1, 2)))
    got_b = lax.ppermute(msg_b, axis, swaps(range(1, count - 1, 2)))

    bulk = pl.pallas_call(
        functools.partial(bulk_kernel, width, blocks, axis, count),
        out_shape=out_shape,
        in_specs=[vmem] * 3 + [anywhere],
        out_specs=anywhere,
        scratch_shapes=[
            zeros,
            pltpu.VMEM((layers, blocks, width + 4, rows, lanes), f32),
            side,
            pltpu.SemaphoreType.DMA((bases,)),
            pltpu.SemaphoreType.DMA((blocks,)),
            pltpu.SemaphoreType.DMA((bases + 1,)),
        ],
        input_output_aliases={3: 0},
        compiler_params=params,
        cost_estimate=pl.CostEstimate(flops=10**7, bytes_accessed=7 * 10**6, transcendentals=0),
        name="bulk",
    )(faces, masks, got_a, cleared)
    out = pl.pallas_call(
        functools.partial(edge_kernel, width, blocks, axis, count),
        out_shape=out_shape,
        in_specs=[vmem] * 3 + [anywhere],
        out_specs=anywhere,
        scratch_shapes=[
            side,
            pltpu.SemaphoreType.DMA((blocks,)),
        ],
        input_output_aliases={3: 0},
        compiler_params=params,
        cost_estimate=pl.CostEstimate(flops=10**6, bytes_accessed=10**6, transcendentals=0),
        name="edges",
    )(faces, masks, got_b, bulk)
    return out.reshape(layers, blocks, 3 * width, rows, lanes)


def solution(mesh):
    spread = P(("groups", "blk"))
    return jax.shard_map(
        functools.partial(on_device, axis="blk", count=mesh.shape["blk"]),
        mesh=mesh,
        in_specs=(spread,) * 5,
        out_specs=spread,
        check_vma=False,
    )
```

```python
import functools

import jax
import jax.numpy as jnp
from jax import lax
from jax.experimental import pallas as pl
from jax.experimental.pallas import tpu as pltpu
from jax.sharding import PartitionSpec as P


TAIL = 8
EARLY = 12


class Lanes:
    def __init__(self, shape, width):
        tile = lax.broadcasted_iota(jnp.int32, (TAIL, shape[1]), 1)

        def rows(v):
            return jnp.concatenate([v] * (shape[0] // TAIL), axis=0)

        self.rows, self.lanes = shape
        self.width = width
        self.lane = rows(tile)
        self.local = rows(lax.rem(tile, width))
        self.first = self.local == 0
        self.last = self.local == width - 1
        self.odd = rows(lax.rem(tile // width, 2)) == 1
        self.row0 = lax.broadcasted_iota(jnp.int32, shape, 0) == 0
        self.lane0 = self.lane == 0

    def around(self, k):
        start = k * self.width - self.width // 2
        return (self.lane >= start) & (self.lane < start + 2 * self.width)

    def zm(self, v):
        return pltpu.roll(v, 1, 1)

    def zp(self, v):
        return pltpu.roll(v, self.lanes - 1, 1)

    def ym(self, v):
        return pltpu.roll(v, 1, 0)

    def yp(self, v):
        return pltpu.roll(v, self.rows - 1, 0)


def reciprocal(x):
    r = pl.reciprocal(x, approx=True)
    return r * (2.0 - x * r)


class Plane:
    def __init__(self, ln, tx, txn, ty, tz, s, valid=None):
        self.ln = ln
        self.tx, self.txn = tx, txn
        self.ty = jnp.where(ln.row0, 0.0, ty)
        self.tz = jnp.where(ln.lane0, 0.0, tz)
        self.typ = ln.yp(self.ty)
        self.tzp = ln.zp(self.tz)
        e = s * (1.0 / 3.0) + ((tx + txn) + (self.ty + self.typ) + (self.tz + self.tzp))
        if valid is not None:
            e = jnp.where(valid, e, 1.0)
        self.half = 0.5 * e + s * (1.0 / 3.0)
        self.all = 1.5 * e
        self.q = reciprocal(self.all)
        self.z1 = self.q * jnp.where(ln.first, self.tz, jnp.where(ln.last, self.tzp, 0.0))
        self.zm = ln.zm(self.z1)
        self.zp = ln.zp(self.z1)

    def toward(self, low):
        return self.tx if low else self.txn

    def inward(self, low):
        return self.txn if low else self.tx

    def edge(self, low):
        self.x1 = self.q * self.toward(low)
        self.o1 = 1.0 - self.z1 - self.x1

    def rim(self):
        return self.tz * self.zm + self.tzp * self.zp

    def along_y(self, v):
        return self.ty * self.ln.ym(v) + self.typ * self.ln.yp(v)


def plane_at(ln, faces, p):
    return Plane(ln, faces[0, p], faces[0, p + 1], faces[1, p], faces[2, p], faces[3, p])


def middle(p, below, above, mz):
    ln = p.ln
    vz = p.half * p.z1 + p.tx * below.z1 + p.txn * above.z1 + p.along_y(p.z1)
    vz = vz + p.tz * jnp.where(ln.first, 1.0 - p.zm, p.zm)
    vz = vz + p.tzp * jnp.where(ln.last, 1.0 - p.zp, p.zp)
    kept = vz * mz
    return p.all - vz, kept, p.all - (vz - kept)


def second(p, edge, inner, low, mz, mx):
    below, above = (edge, inner) if low else (inner, edge)
    ln = p.ln
    first_o = ln.zm(p.z1)
    vz = p.half * p.z1 + p.tx * below.z1 + p.txn * above.z1 + p.along_y(p.z1)
    vz = vz + p.tz * jnp.where(ln.first, 1.0 - first_o, first_o)
    vz = vz + p.tzp * jnp.where(ln.last, 1.0 - p.zp, p.zp)
    vx = p.toward(low) * edge.x1
    kept_z, kept_x = vz * mz, vx * mx
    total = p.all - (vz - kept_z) - (vx - kept_x)
    return p.all - vz - vx, kept_z, kept_x, total


def edge_own(p, inner_o1, inner_z1, outer_x1, low, mz):
    ln = p.ln
    om, op = ln.zm(p.o1), ln.zp(p.o1)
    vo = p.half * p.o1 + p.toward(low) * outer_x1 + p.inward(low) * inner_o1 + p.along_y(p.o1)
    vo = vo + p.tz * jnp.where(ln.first, p.zm, om) + p.tzp * jnp.where(ln.last, p.zp, op)
    vz = p.half * p.z1 + p.inward(low) * inner_z1 + p.along_y(p.z1)
    vz = vz + p.tz * jnp.where(ln.first, om, p.zm) + p.tzp * jnp.where(ln.last, op, p.zp)
    return vo, vz * mz


def edge_total(p, mz):
    rim = p.rim()
    return p.all - (rim - rim * mz)


def edge_spill(p, own, low):
    ln = p.ln
    xm, xp = ln.zm(p.x1), ln.zp(p.x1)
    face = p.toward(low)
    vx = p.half * p.x1 + face * own.o1 + p.along_y(p.x1)
    vx = vx + p.tz * jnp.where(ln.first, 0.0, xm) + p.tzp * jnp.where(ln.last, 0.0, xp)
    vd = face * own.z1 + p.tz * jnp.where(ln.first, xm, 0.0) + p.tzp * jnp.where(ln.last, xp, 0.0)
    return vx, vd


def store(ln, dst, plane, blocks, own, other, total):
    scale = reciprocal(total)
    own = own * scale
    other = jnp.zeros_like(own) if other is None else other * scale
    even, odd = jnp.where(ln.odd, other, own), jnp.where(ln.odd, own, other)
    for k in range(blocks):
        dst[k, plane] = jnp.where(ln.around(k), odd if k % 2 else even, 0.0)


def work_side(ln, low, valid, faces, masks, msg, put):
    n, rows, lanes = faces.shape[1:]
    layers = masks.shape[0]

    def own(i, j):
        return faces[i, jnp.where(low, j, n - 1 - j)]

    def got(i, j):
        tiles = rows // TAIL
        return msg[pl.ds(1 + tiles * (2 * i + j), tiles)].reshape(rows, lanes)

    f1, f2, f3 = (faces[0, jnp.where(low, j, n - j)] for j in (1, 2, 3))
    f0 = jnp.where(valid, jnp.where(low, faces[0, 0], got(0, 0)), 0.0)
    g1 = jnp.where(low, got(0, 0), got(0, 1))
    g2 = jnp.where(low, got(0, 1), got(4, 0))
    a0 = Plane(ln, f0, f1, own(1, 0), own(2, 0), own(3, 0))
    a1 = Plane(ln, f1, f2, own(1, 1), own(2, 1), own(3, 1))
    a2 = Plane(ln, f2, f3, own(1, 2), own(2, 2), own(3, 2))
    b0 = Plane(ln, g1, f0, got(1, 0), got(2, 0), got(3, 0), valid)
    b1 = Plane(ln, g2, g1, got(1, 1), got(2, 1), got(3, 1), valid)
    mine = masks[jnp.where(low, 0, layers - 1)]
    mz, my_reach = mine[0:1], jnp.where(low, mine[1:2], mine[2:3])
    theirs = msg[0]
    mo, their_reach = theirs[0:1], jnp.where(low, theirs[2:3], theirs[1:2])
    a0.edge(True)
    b0.edge(False)
    vx = g1 * b0.x1
    kept = vx * my_reach
    put(0, kept, None, edge_total(b1, mo) - (vx - kept))
    vx, vd = edge_spill(b0, a0, False)
    put(1, vx, vd, edge_total(b0, mo))
    vo, vz = edge_own(a0, 1.0 - a1.z1, a1.z1, b0.x1, True, mz)
    put(2, vo, vz, edge_total(a0, mz))
    vo, vz, _, total = second(a1, a0, a2, True, mz, their_reach)
    put(3, vo, vz, total)


def store_side(ln, buf, low, blocks):
    def put(i, own, other, total):
        store(ln, buf, jnp.where(low, i, 3 - i), blocks, own, other, total)

    return put


def send_one_side(buf, out, low, width, layers, sems, k):
    layer = jnp.where(low, 0, layers - 1)
    start = jnp.where(low, width - 2, 2 * width - 2)
    there = out.at[pl.ds((layer * buf.shape[0] + k) * 3 * width + start, 4)]
    return pltpu.make_async_copy(buf.at[k], there, sems.at[k])


def clear_run(zeros, out, b, bases, width, sem):
    depth = width - 2
    ends = isinstance(b, int) and b in (0, bases)
    count = depth if ends else 2 * depth
    start = 0 if ends and b == 0 else b * 3 * width - depth
    return pltpu.make_async_copy(zeros.at[pl.ds(0, count)], out.at[pl.ds(start, count)], sem)


def clear_runs(act, zeros, out, first, last, bases, width, sems):
    def body(b, _):
        act(clear_run(zeros, out, b, bases, width, sems.at[b]))

    lax.fori_loop(first, last, body, None)


def pack_kernel(
    n, width, axis, tx, ty, tz, s, reach, msg_a, msg_b, masks, faces, out,
    held_reach, zeros, buf, read_sems, sems, zero_sems,
):
    layers, _, blocks = held_reach.shape
    lanes = masks.shape[-1]
    fetch = pltpu.make_async_copy(reach, held_reach, read_sems.at[4])
    fetch.start()
    copies = [
        pltpu.make_async_copy(a, faces.at[i], read_sems.at[i]) for i, a in enumerate((tx, ty, tz, s))
    ]
    for c in copies:
        c.start()
    bases = layers * blocks
    me = lax.axis_index(axis)
    late = bases - EARLY

    @pl.when(me == 1)
    def _():
        zeros[...] = jnp.zeros(zeros.shape, jnp.float32)
        clear_runs(lambda c: c.start(), zeros, out, late, bases, bases, width, zero_sems)

    masks[...] = jnp.zeros(masks.shape, jnp.float32)
    lane = lax.broadcasted_iota(jnp.int32, (4, lanes), 1)
    block = lane // width
    local = lane - block * width
    fetch.wait()
    for layer in range(layers):
        r = jnp.zeros((4, lanes), jnp.int32)
        for k in range(blocks):
            r = jnp.where(block == k, held_reach[layer, :, k : k + 1], r)
        low = pltpu.roll(r, width, 1)
        high = pltpu.roll(r, lanes - width, 1)
        near = jnp.where(
            local[0:1] < width // 2,
            jnp.where(low[3:4] >= local[0:1] + 1, 1.0, 0.0),
            jnp.where(high[2:3] >= width - local[0:1], 1.0, 0.0),
        )
        masks[layer, 0:1] = near
        masks[layer, 1:3] = jnp.where(r[0:2] >= 2, 1.0, 0.0)
    even = lax.rem(me, 2) == 0

    def put(tile, up, down):
        up, down = (v.reshape(-1, TAIL, lanes) for v in (up, down))
        where = pl.ds(tile, up.shape[0])
        msg_a[where] = jnp.where(even, up, down)
        msg_b[where] = jnp.where(even, down, up)

    put(0, masks[layers - 1], masks[0])
    for c in copies:
        c.wait()
    for i in range(4):
        put(1 + 4 * i, faces[i, n - 1], faces[i, 0])
        put(3 + 4 * i, faces[i, n - 2], faces[i, 1])
    put(17, faces[0, n - 1], faces[0, 2])

    @pl.when(me == 1)
    def _():
        clear_runs(lambda c: c.wait(), zeros, out, late, bases, bases, width, zero_sems)

    @pl.when(me == 0)
    def _():
        inner_planes(width, bases, faces, masks, out, zeros, buf, sems, zero_sems)


def inner_planes(width, last_run, faces, masks, out, zeros, buf, sems, zero_sems):
    layers, blocks = buf.shape[:2]
    rows, lanes = faces.shape[2:]
    box, depth = 3 * width, width - 2
    bases = layers * blocks
    zeros[...] = jnp.zeros(zeros.shape, jnp.float32)

    def each_run(act):
        for b in (0, bases):
            act(clear_run(zeros, out, b, bases, width, zero_sems.at[b]))
        clear_runs(act, zeros, out, 1, last_run, bases, width, zero_sems)

    each_run(lambda c: c.start())
    ln = Lanes((rows, lanes), width)
    plane = functools.partial(plane_at, ln, faces)

    def send(k, layer):
        start = 4 if layer == 0 else 0
        count = width + 4 - start - (4 if layer == layers - 1 else 0)
        return pltpu.make_async_copy(
            buf.at[layer, k, pl.ds(start, count)],
            out.at[pl.ds((layer * blocks + k) * box + depth + start, count)],
            sems.at[layer * blocks + k],
        )

    def between(layer):
        base = layer * width
        ma, mb = masks[layer - 1, 0:1], masks[layer, 0:1]
        to_above, to_below = masks[layer - 1, 2:3], masks[layer, 1:2]
        a3, a2, a1 = (plane(base - i) for i in (3, 2, 1))
        b0, b1, b2 = (plane(base + i) for i in (0, 1, 2))
        a1.edge(False)
        b0.edge(True)
        low = functools.partial(store, ln, buf.at[layer - 1])
        high = functools.partial(store, ln, buf.at[layer])
        vo, vz, vx, total = second(a2, a1, a3, False, ma, to_below)
        low(width, blocks, vo, vz, total)
        high(0, blocks, vx, None, total)
        vo, vz = edge_own(a1, 1.0 - a2.z1, a2.z1, b0.x1, False, ma)
        vx, vd = edge_spill(a1, b0, False)
        total = edge_total(a1, ma)
        low(width + 1, blocks, vo, vz, total)
        high(1, blocks, vx, vd, total)
        vo, vz = edge_own(b0, 1.0 - b1.z1, b1.z1, a1.x1, True, mb)
        vx, vd = edge_spill(b0, a1, True)
        total = edge_total(b0, mb)
        high(2, blocks, vo, vz, total)
        low(width + 2, blocks, vx, vd, total)
        vo, vz, vx, total = second(b1, b0, b2, True, mb, to_above)
        high(3, blocks, vo, vz, total)
        low(width + 3, blocks, vx, None, total)

    for layer in range(layers):
        planes = [plane(layer * width + j) for j in range(1, width - 1)]
        mz = masks[layer, 0:1]
        for j in range(2, width - 2):
            vo, vz, total = middle(planes[j - 1], planes[j - 2], planes[j], mz)
            store(ln, buf.at[layer], j + 2, blocks, vo, vz, total)
        if layer < layers - 1:
            between(layer + 1)

        @pl.loop(0, blocks)
        def _(k):
            send(k, layer).start()

    each_run(lambda c: c.wait())

    @pl.loop(0, blocks)
    def _(k):
        for layer in range(layers):
            send(k, layer).wait()


def bulk_kernel(width, axis, faces, masks, held, out, zeros, buf, sems, zero_sems):
    del held
    me = lax.axis_index(axis)
    bases = sems.shape[0]

    @pl.when(me != 0)
    def _():
        last_run = jnp.where(me == 1, bases - EARLY, bases)
        inner_planes(width, last_run, faces, masks, out, zeros, buf, sems, zero_sems)


def edge_kernel(
    width, blocks, axis, count, faces, masks, got_a, got_b, held, out, side_a, side_b, sems_a, sems_b
):
    del held
    layers = masks.shape[0]
    me = lax.axis_index(axis)
    odd = lax.rem(me, 2) == 1
    ln = Lanes(faces.shape[2:], width)
    copies = []
    for low, msg, side, sems in ((odd, got_a, side_a, sems_a), (jnp.logical_not(odd), got_b, side_b, sems_b)):
        valid = jnp.where(low, me > 0, me < count - 1)
        work_side(ln, low, valid, faces, masks, msg, store_side(ln, side, low, blocks))
        copies += [send_one_side(side, out, low, width, layers, sems, k) for k in range(blocks)]
    for c in copies:
        c.start()
    for c in copies:
        c.wait()


def swaps(firsts):
    return [pair for i in firsts for pair in ((i, i + 1), (i + 1, i))]


def on_device(trans_east, trans_north, trans_up, storage, support_reach, *, axis, count):
    layers, blocks, _ = support_reach.shape
    n, rows, lanes = trans_east.shape
    width = n // layers
    f32 = jnp.float32
    anywhere = pl.BlockSpec(memory_space=pl.ANY)
    vmem = pl.BlockSpec(memory_space=pltpu.VMEM)
    params = pltpu.CompilerParams(vmem_limit_bytes=16 * 2**20)
    outside = tuple(
        pltpu.with_memory_space_constraint(x, pltpu.HBM)
        for x in (trans_east, trans_north, trans_up, storage)
    )
    reach = jnp.transpose(support_reach, (0, 2, 1))
    reach = pltpu.with_memory_space_constraint(reach, pltpu.HBM)
    bases = layers * blocks
    out_shape = jax.ShapeDtypeStruct((bases * 3 * width, rows, lanes), f32)
    inner = [
        pltpu.VMEM((2 * (width - 2), rows, lanes), f32),
        pltpu.VMEM((layers, blocks, width + 4, rows, lanes), f32),
    ]
    inner_sems = [pltpu.SemaphoreType.DMA((bases,)), pltpu.SemaphoreType.DMA((bases + 1,))]
    tiles = 1 + 9 * rows // TAIL
    msg_a, msg_b, masks, faces, started = pl.pallas_call(
        functools.partial(pack_kernel, n, width, axis),
        out_shape=(
            pltpu.VMEM((tiles, TAIL, lanes), f32),
            pltpu.VMEM((tiles + 1, TAIL, lanes), f32),
            pltpu.VMEM((layers, TAIL, lanes), f32),
            pltpu.VMEM((4, n, rows, lanes), f32),
            out_shape,
        ),
        in_specs=[anywhere] * 5,
        out_specs=(vmem,) * 4 + (anywhere,),
        scratch_shapes=[
            pltpu.VMEM((layers, 4, blocks), jnp.int32),
            *inner,
            pltpu.SemaphoreType.DMA((5,)),
            *inner_sems,
        ],
        compiler_params=params,
        name="pack",
    )(*outside, reach)
    got_a = lax.ppermute(msg_a, axis, swaps(range(0, count - 1, 2)))
    got_b = lax.ppermute(msg_b, axis, swaps(range(1, count - 1, 2)))

    bulk = pl.pallas_call(
        functools.partial(bulk_kernel, width, axis),
        out_shape=out_shape,
        in_specs=[vmem] * 2 + [anywhere],
        out_specs=anywhere,
        scratch_shapes=inner + inner_sems,
        input_output_aliases={2: 0},
        compiler_params=params,
        cost_estimate=pl.CostEstimate(flops=10**7, bytes_accessed=7 * 10**6, transcendentals=0),
        name="bulk",
    )(faces, masks, started)
    side = [pltpu.VMEM((blocks, 4, rows, lanes), f32)] * 2
    out = pl.pallas_call(
        functools.partial(edge_kernel, width, blocks, axis, count),
        out_shape=out_shape,
        in_specs=[vmem] * 4 + [anywhere],
        out_specs=anywhere,
        scratch_shapes=side + [pltpu.SemaphoreType.DMA((blocks,))] * 2,
        input_output_aliases={4: 0},
        compiler_params=params,
        cost_estimate=pl.CostEstimate(flops=10**6, bytes_accessed=10**6, transcendentals=0),
        name="edges",
    )(faces, masks, got_a, got_b, bulk)
    return out.reshape(layers, blocks, 3 * width, rows, lanes)


def solution(mesh):
    spread = P(("groups", "blk"))
    return jax.shard_map(
        functools.partial(on_device, axis="blk", count=mesh.shape["blk"]),
        mesh=mesh,
        in_specs=(spread,) * 5,
        out_specs=spread,
        check_vma=False,
    )
```

```python
import functools

import jax
import jax.numpy as jnp
from jax import lax
from jax.experimental import pallas as pl
from jax.experimental.pallas import tpu as pltpu
from jax.sharding import PartitionSpec as P


TAIL = 8
EARLY = 12
STEP = 6


class Lanes:
    def __init__(self, shape, width):
        tile = lax.broadcasted_iota(jnp.int32, (TAIL, shape[1]), 1)

        def rows(v):
            return jnp.concatenate([v] * (shape[0] // TAIL), axis=0)

        self.rows, self.lanes = shape
        self.width = width
        self.lane = rows(tile)
        self.local = rows(lax.rem(tile, width))
        self.first = self.local == 0
        self.last = self.local == width - 1
        self.odd = rows(lax.rem(tile // width, 2)) == 1
        self.row0 = lax.broadcasted_iota(jnp.int32, shape, 0) == 0
        self.lane0 = self.lane == 0

    def around(self, k):
        start = k * self.width - self.width // 2
        return (self.lane >= start) & (self.lane < start + 2 * self.width)

    def zm(self, v):
        return pltpu.roll(v, 1, 1)

    def zp(self, v):
        return pltpu.roll(v, self.lanes - 1, 1)

    def ym(self, v):
        return pltpu.roll(v, 1, 0)

    def yp(self, v):
        return pltpu.roll(v, self.rows - 1, 0)


def reciprocal(x):
    r = pl.reciprocal(x, approx=True)
    return r * (2.0 - x * r)


class Plane:
    def __init__(self, ln, tx, txn, ty, tz, s, valid=None):
        self.ln = ln
        self.tx, self.txn = tx, txn
        self.ty = jnp.where(ln.row0, 0.0, ty)
        self.tz = jnp.where(ln.lane0, 0.0, tz)
        self.typ = ln.yp(self.ty)
        self.tzp = ln.zp(self.tz)
        e = s * (1.0 / 3.0) + ((tx + txn) + (self.ty + self.typ) + (self.tz + self.tzp))
        if valid is not None:
            e = jnp.where(valid, e, 1.0)
        self.half = 0.5 * e + s * (1.0 / 3.0)
        self.all = 1.5 * e
        self.q = reciprocal(self.all)
        self.z1 = self.q * jnp.where(ln.first, self.tz, jnp.where(ln.last, self.tzp, 0.0))
        self.zm = ln.zm(self.z1)
        self.zp = ln.zp(self.z1)

    def toward(self, low):
        return self.tx if low else self.txn

    def inward(self, low):
        return self.txn if low else self.tx

    def edge(self, low):
        self.x1 = self.q * self.toward(low)
        self.o1 = 1.0 - self.z1 - self.x1

    def rim(self):
        return self.tz * self.zm + self.tzp * self.zp

    def along_y(self, v):
        return self.ty * self.ln.ym(v) + self.typ * self.ln.yp(v)


def plane_at(ln, faces, p):
    return Plane(ln, faces[0, p], faces[0, p + 1], faces[1, p], faces[2, p], faces[3, p])


def middle(p, below, above, mz):
    ln = p.ln
    vz = p.half * p.z1 + p.tx * below.z1 + p.txn * above.z1 + p.along_y(p.z1)
    vz = vz + p.tz * jnp.where(ln.first, 1.0 - p.zm, p.zm)
    vz = vz + p.tzp * jnp.where(ln.last, 1.0 - p.zp, p.zp)
    kept = vz * mz
    return p.all - vz, kept, p.all - (vz - kept)


def second(p, edge, inner, low, mz, mx):
    below, above = (edge, inner) if low else (inner, edge)
    ln = p.ln
    first_o = ln.zm(p.z1)
    vz = p.half * p.z1 + p.tx * below.z1 + p.txn * above.z1 + p.along_y(p.z1)
    vz = vz + p.tz * jnp.where(ln.first, 1.0 - first_o, first_o)
    vz = vz + p.tzp * jnp.where(ln.last, 1.0 - p.zp, p.zp)
    vx = p.toward(low) * edge.x1
    kept_z, kept_x = vz * mz, vx * mx
    total = p.all - (vz - kept_z) - (vx - kept_x)
    return p.all - vz - vx, kept_z, kept_x, total


def edge_own(p, inner_o1, inner_z1, outer_x1, low, mz):
    ln = p.ln
    om, op = ln.zm(p.o1), ln.zp(p.o1)
    vo = p.half * p.o1 + p.toward(low) * outer_x1 + p.inward(low) * inner_o1 + p.along_y(p.o1)
    vo = vo + p.tz * jnp.where(ln.first, p.zm, om) + p.tzp * jnp.where(ln.last, p.zp, op)
    vz = p.half * p.z1 + p.inward(low) * inner_z1 + p.along_y(p.z1)
    vz = vz + p.tz * jnp.where(ln.first, om, p.zm) + p.tzp * jnp.where(ln.last, op, p.zp)
    return vo, vz * mz


def edge_total(p, mz):
    rim = p.rim()
    return p.all - (rim - rim * mz)


def edge_spill(p, own, low):
    ln = p.ln
    xm, xp = ln.zm(p.x1), ln.zp(p.x1)
    face = p.toward(low)
    vx = p.half * p.x1 + face * own.o1 + p.along_y(p.x1)
    vx = vx + p.tz * jnp.where(ln.first, 0.0, xm) + p.tzp * jnp.where(ln.last, 0.0, xp)
    vd = face * own.z1 + p.tz * jnp.where(ln.first, xm, 0.0) + p.tzp * jnp.where(ln.last, xp, 0.0)
    return vx, vd


def store(ln, dst, plane, blocks, own, other, total):
    scale = reciprocal(total)
    own = own * scale
    other = jnp.zeros_like(own) if other is None else other * scale
    even, odd = jnp.where(ln.odd, other, own), jnp.where(ln.odd, own, other)
    for k in range(blocks):
        dst[k, plane] = jnp.where(ln.around(k), odd if k % 2 else even, 0.0)


def work_side(ln, low, valid, faces, masks, msg, put):
    n, rows, lanes = faces.shape[1:]
    layers = masks.shape[0]

    def own(i, j):
        return faces[i, jnp.where(low, j, n - 1 - j)]

    def got(i, j):
        tiles = rows // TAIL
        return msg[pl.ds(1 + tiles * (2 * i + j), tiles)].reshape(rows, lanes)

    f1, f2, f3 = (faces[0, jnp.where(low, j, n - j)] for j in (1, 2, 3))
    f0 = jnp.where(valid, jnp.where(low, faces[0, 0], got(0, 0)), 0.0)
    g1 = jnp.where(low, got(0, 0), got(0, 1))
    g2 = jnp.where(low, got(0, 1), got(4, 0))
    a0 = Plane(ln, f0, f1, own(1, 0), own(2, 0), own(3, 0))
    a1 = Plane(ln, f1, f2, own(1, 1), own(2, 1), own(3, 1))
    a2 = Plane(ln, f2, f3, own(1, 2), own(2, 2), own(3, 2))
    b0 = Plane(ln, g1, f0, got(1, 0), got(2, 0), got(3, 0), valid)
    b1 = Plane(ln, g2, g1, got(1, 1), got(2, 1), got(3, 1), valid)
    mine = masks[jnp.where(low, 0, layers - 1)]
    mz, my_reach = mine[0:1], jnp.where(low, mine[1:2], mine[2:3])
    theirs = msg[0]
    mo, their_reach = theirs[0:1], jnp.where(low, theirs[2:3], theirs[1:2])
    a0.edge(True)
    b0.edge(False)
    vx = g1 * b0.x1
    kept = vx * my_reach
    put(0, kept, None, edge_total(b1, mo) - (vx - kept))
    vx, vd = edge_spill(b0, a0, False)
    put(1, vx, vd, edge_total(b0, mo))
    vo, vz = edge_own(a0, 1.0 - a1.z1, a1.z1, b0.x1, True, mz)
    put(2, vo, vz, edge_total(a0, mz))
    vo, vz, _, total = second(a1, a0, a2, True, mz, their_reach)
    put(3, vo, vz, total)


def store_side(ln, buf, low, blocks):
    def put(i, own, other, total):
        store(ln, buf, jnp.where(low, i, 3 - i), blocks, own, other, total)

    return put


def send_one_side(buf, out, low, width, layers, sems, k):
    layer = jnp.where(low, 0, layers - 1)
    start = jnp.where(low, width - 2, 2 * width - 2)
    there = out.at[pl.ds((layer * buf.shape[0] + k) * 3 * width + start, 4)]
    return pltpu.make_async_copy(buf.at[k], there, sems.at[k])


def clear_run(zeros, out, b, bases, width, sem):
    depth = width - 2
    ends = isinstance(b, int) and b in (0, bases)
    count = depth if ends else 2 * depth
    start = 0 if ends and b == 0 else b * 3 * width - depth
    return pltpu.make_async_copy(zeros.at[pl.ds(0, count)], out.at[pl.ds(start, count)], sem)


def clear_runs(act, zeros, out, first, last, bases, width, sems):
    def body(b, _):
        act(clear_run(zeros, out, b, bases, width, sems.at[b]))

    lax.fori_loop(first, last, body, None)


def pack_kernel(
    n, width, axis, tx, ty, tz, s, reach, msg_a, msg_b, masks, faces, out,
    held_reach, zeros, buf, read_sems, sems, zero_sems,
):
    layers, _, blocks = held_reach.shape
    lanes = masks.shape[-1]
    fetch = pltpu.make_async_copy(reach, held_reach, read_sems.at[4])
    fetch.start()
    copies = [
        pltpu.make_async_copy(a, faces.at[i], read_sems.at[i]) for i, a in enumerate((tx, ty, tz, s))
    ]
    for c in copies:
        c.start()
    bases = layers * blocks
    me = lax.axis_index(axis)
    late = bases - EARLY

    @pl.when(me == 1)
    def _():
        zeros[...] = jnp.zeros(zeros.shape, jnp.float32)
        clear_runs(lambda c: c.start(), zeros, out, late, bases, bases, width, zero_sems)

    masks[...] = jnp.zeros(masks.shape, jnp.float32)
    lane = lax.broadcasted_iota(jnp.int32, (4, lanes), 1)
    block = lane // width
    local = lane - block * width
    fetch.wait()
    for layer in range(layers):
        r = jnp.zeros((4, lanes), jnp.int32)
        for k in range(blocks):
            r = jnp.where(block == k, held_reach[layer, :, k : k + 1], r)
        low = pltpu.roll(r, width, 1)
        high = pltpu.roll(r, lanes - width, 1)
        near = jnp.where(
            local[0:1] < width // 2,
            jnp.where(low[3:4] >= local[0:1] + 1, 1.0, 0.0),
            jnp.where(high[2:3] >= width - local[0:1], 1.0, 0.0),
        )
        masks[layer, 0:1] = near
        masks[layer, 1:3] = jnp.where(r[0:2] >= 2, 1.0, 0.0)
    even = lax.rem(me, 2) == 0

    def put(tile, up, down):
        up, down = (v.reshape(-1, TAIL, lanes) for v in (up, down))
        where = pl.ds(tile, up.shape[0])
        msg_a[where] = jnp.where(even, up, down)
        msg_b[where] = jnp.where(even, down, up)

    put(0, masks[layers - 1], masks[0])
    for c in copies:
        c.wait()
    for i in range(4):
        put(1 + 4 * i, faces[i, n - 1], faces[i, 0])
        put(3 + 4 * i, faces[i, n - 2], faces[i, 1])
    put(17, faces[0, n - 1], faces[0, 2])

    @pl.when(me == 1)
    def _():
        clear_runs(lambda c: c.wait(), zeros, out, late, bases, bases, width, zero_sems)

    @pl.when(me == 0)
    def _():
        inner_planes(width, bases, faces, masks, out, zeros, buf, sems, zero_sems)


def inner_planes(width, last_run, faces, masks, out, zeros, buf, sems, zero_sems):
    layers, blocks = buf.shape[:2]
    rows, lanes = faces.shape[2:]
    box, depth = 3 * width, width - 2
    bases = layers * blocks
    zeros[...] = jnp.zeros(zeros.shape, jnp.float32)

    def each_run(act):
        for b in (0, bases):
            act(clear_run(zeros, out, b, bases, width, zero_sems.at[b]))
        clear_runs(act, zeros, out, 1, last_run, bases, width, zero_sems)

    each_run(lambda c: c.start())
    ln = Lanes((rows, lanes), width)
    plane = functools.partial(plane_at, ln, faces)

    def send(k, layer):
        start, size = (4, width - 4) if layers == 1 else (jnp.where(layer == 0, 4, 0), width)
        return pltpu.make_async_copy(
            buf.at[layer, k, pl.ds(start, size)],
            out.at[pl.ds((layer * blocks + k) * box + depth + start, size)],
            sems.at[layer * blocks + k],
        )

    def send_rest(k, layer):
        return pltpu.make_async_copy(
            buf.at[layer, k, pl.ds(width, 4)],
            out.at[pl.ds((layer * blocks + k) * box + depth + width, 4)],
            sems.at[bases + (layer - 1) * blocks + k],
        )

    def between(layer):
        base = layer * width
        ma, mb = masks[layer - 1, 0:1], masks[layer, 0:1]
        to_above, to_below = masks[layer - 1, 2:3], masks[layer, 1:2]
        a3, a2, a1 = (plane(base - i) for i in (3, 2, 1))
        b0, b1, b2 = (plane(base + i) for i in (0, 1, 2))
        a1.edge(False)
        b0.edge(True)
        low = functools.partial(store, ln, buf.at[layer - 1])
        high = functools.partial(store, ln, buf.at[layer])
        vo, vz, vx, total = second(a2, a1, a3, False, ma, to_below)
        low(width, blocks, vo, vz, total)
        high(0, blocks, vx, None, total)
        vo, vz = edge_own(a1, 1.0 - a2.z1, a2.z1, b0.x1, False, ma)
        vx, vd = edge_spill(a1, b0, False)
        total = edge_total(a1, ma)
        low(width + 1, blocks, vo, vz, total)
        high(1, blocks, vx, vd, total)
        vo, vz = edge_own(b0, 1.0 - b1.z1, b1.z1, a1.x1, True, mb)
        vx, vd = edge_spill(b0, a1, True)
        total = edge_total(b0, mb)
        high(2, blocks, vo, vz, total)
        low(width + 2, blocks, vx, vd, total)
        vo, vz, vx, total = second(b1, b0, b2, True, mb, to_above)
        high(3, blocks, vo, vz, total)
        low(width + 3, blocks, vx, None, total)

    pl.loop(1, layers)(between)

    @pl.loop(0, layers)
    def _(layer):
        mz = masks[layer, 0:1]

        @pl.loop(0, (width - 4) // STEP)
        def _(i):
            first = 2 + i * STEP
            planes = [plane(layer * width + first + j) for j in range(-1, STEP + 1)]
            for j in range(STEP):
                vo, vz, total = middle(planes[j + 1], planes[j], planes[j + 2], mz)
                store(ln, buf.at[layer], first + j + 2, blocks, vo, vz, total)

        @pl.loop(0, blocks)
        def _(k):
            send(k, layer).start()

    @pl.loop(1, layers - 1)
    def _(layer):
        for k in range(blocks):
            send_rest(k, layer).start()

    each_run(lambda c: c.wait())

    @pl.loop(0, layers)
    def _(layer):
        for k in range(blocks):
            send(k, layer).wait()

    @pl.loop(1, layers - 1)
    def _(layer):
        for k in range(blocks):
            send_rest(k, layer).wait()


def bulk_kernel(width, axis, faces, masks, held, out, zeros, buf, sems, zero_sems):
    del held
    me = lax.axis_index(axis)
    bases = sems.shape[0] // 2

    @pl.when(me != 0)
    def _():
        last_run = jnp.where(me == 1, bases - EARLY, bases)
        inner_planes(width, last_run, faces, masks, out, zeros, buf, sems, zero_sems)


def edge_kernel(
    width, blocks, axis, count, faces, masks, got_a, got_b, held, out, side_a, side_b, sems_a, sems_b
):
    del held
    layers = masks.shape[0]
    me = lax.axis_index(axis)
    odd = lax.rem(me, 2) == 1
    ln = Lanes(faces.shape[2:], width)
    copies = []
    for low, msg, side, sems in ((odd, got_a, side_a, sems_a), (jnp.logical_not(odd), got_b, side_b, sems_b)):
        valid = jnp.where(low, me > 0, me < count - 1)
        work_side(ln, low, valid, faces, masks, msg, store_side(ln, side, low, blocks))
        copies += [send_one_side(side, out, low, width, layers, sems, k) for k in range(blocks)]
    for c in copies:
        c.start()
    for c in copies:
        c.wait()


def swaps(firsts):
    return [pair for i in firsts for pair in ((i, i + 1), (i + 1, i))]


def on_device(trans_east, trans_north, trans_up, storage, support_reach, *, axis, count):
    layers, blocks, _ = support_reach.shape
    n, rows, lanes = trans_east.shape
    width = n // layers
    f32 = jnp.float32
    anywhere = pl.BlockSpec(memory_space=pl.ANY)
    vmem = pl.BlockSpec(memory_space=pltpu.VMEM)
    params = pltpu.CompilerParams(vmem_limit_bytes=16 * 2**20)
    outside = tuple(
        pltpu.with_memory_space_constraint(x, pltpu.HBM)
        for x in (trans_east, trans_north, trans_up, storage)
    )
    reach = jnp.transpose(support_reach, (0, 2, 1))
    reach = pltpu.with_memory_space_constraint(reach, pltpu.HBM)
    bases = layers * blocks
    out_shape = jax.ShapeDtypeStruct((bases * 3 * width, rows, lanes), f32)
    inner = [
        pltpu.VMEM((2 * (width - 2), rows, lanes), f32),
        pltpu.VMEM((layers, blocks, width + 4, rows, lanes), f32),
    ]
    inner_sems = [pltpu.SemaphoreType.DMA((2 * bases,)), pltpu.SemaphoreType.DMA((bases + 1,))]
    tiles = 1 + 9 * rows // TAIL
    msg_a, msg_b, masks, faces, started = pl.pallas_call(
        functools.partial(pack_kernel, n, width, axis),
        out_shape=(
            pltpu.VMEM((tiles, TAIL, lanes), f32),
            pltpu.VMEM((tiles + 1, TAIL, lanes), f32),
            pltpu.VMEM((layers, TAIL, lanes), f32),
            pltpu.VMEM((4, n, rows, lanes), f32),
            out_shape,
        ),
        in_specs=[anywhere] * 5,
        out_specs=(vmem,) * 4 + (anywhere,),
        scratch_shapes=[
            pltpu.VMEM((layers, 4, blocks), jnp.int32),
            *inner,
            pltpu.SemaphoreType.DMA((5,)),
            *inner_sems,
        ],
        compiler_params=params,
        name="pack",
    )(*outside, reach)
    got_a = lax.ppermute(msg_a, axis, swaps(range(0, count - 1, 2)))
    got_b = lax.ppermute(msg_b, axis, swaps(range(1, count - 1, 2)))

    bulk = pl.pallas_call(
        functools.partial(bulk_kernel, width, axis),
        out_shape=out_shape,
        in_specs=[vmem] * 2 + [anywhere],
        out_specs=anywhere,
        scratch_shapes=inner + inner_sems,
        input_output_aliases={2: 0},
        compiler_params=params,
        cost_estimate=pl.CostEstimate(flops=10**7, bytes_accessed=7 * 10**6, transcendentals=0),
        name="bulk",
    )(faces, masks, started)
    side = [pltpu.VMEM((blocks, 4, rows, lanes), f32)] * 2
    out = pl.pallas_call(
        functools.partial(edge_kernel, width, blocks, axis, count),
        out_shape=out_shape,
        in_specs=[vmem] * 4 + [anywhere],
        out_specs=anywhere,
        scratch_shapes=side + [pltpu.SemaphoreType.DMA((blocks,))] * 2,
        input_output_aliases={4: 0},
        compiler_params=params,
        cost_estimate=pl.CostEstimate(flops=10**6, bytes_accessed=10**6, transcendentals=0),
        name="edges",
    )(faces, masks, got_a, got_b, bulk)
    return out.reshape(layers, blocks, 3 * width, rows, lanes)


def solution(mesh):
    spread = P(("groups", "blk"))
    return jax.shard_map(
        functools.partial(on_device, axis="blk", count=mesh.shape["blk"]),
        mesh=mesh,
        in_specs=(spread,) * 5,
        out_specs=spread,
        check_vma=False,
    )
```

```python
import functools

import jax
import jax.numpy as jnp
from jax import lax
from jax.experimental import pallas as pl
from jax.experimental.pallas import tpu as pltpu
from jax.sharding import PartitionSpec as P


TAIL = 8
EARLY = 12


class Lanes:
    def __init__(self, shape, width):
        tile = lax.broadcasted_iota(jnp.int32, (TAIL, shape[1]), 1)

        def rows(v):
            return jnp.concatenate([v] * (shape[0] // TAIL), axis=0)

        self.rows, self.lanes = shape
        self.width = width
        self.lane = rows(tile)
        self.local = rows(lax.rem(tile, width))
        self.first = self.local == 0
        self.last = self.local == width - 1
        self.odd = rows(lax.rem(tile // width, 2)) == 1
        self.row0 = lax.broadcasted_iota(jnp.int32, shape, 0) == 0
        self.lane0 = self.lane == 0

    def around(self, k):
        start = k * self.width - self.width // 2
        return (self.lane >= start) & (self.lane < start + 2 * self.width)

    def zm(self, v):
        return pltpu.roll(v, 1, 1)

    def zp(self, v):
        return pltpu.roll(v, self.lanes - 1, 1)

    def ym(self, v):
        return pltpu.roll(v, 1, 0)

    def yp(self, v):
        return pltpu.roll(v, self.rows - 1, 0)


def reciprocal(x):
    r = pl.reciprocal(x, approx=True)
    return r * (2.0 - x * r)


def within_y(ln, ty):
    ty = jnp.where(ln.row0, 0.0, ty)
    return ty, ln.yp(ty)


def within_z(ln, tz):
    tz = jnp.where(ln.lane0, 0.0, tz)
    return tz, ln.zp(tz)


def cross(ln, ty, tz, s):
    ty, typ = within_y(ln, ty)
    tz, tzp = within_z(ln, tz)
    return s * (1.0 / 3.0) + ((ty + typ) + (tz + tzp)), (ty, typ, tz, tzp)


class Plane:
    def __init__(self, ln, tx, txn, ty, tz, s, valid=None):
        self.ln = ln
        self.tx, self.txn = tx, txn
        e, (self.ty, self.typ, self.tz, self.tzp) = cross(ln, ty, tz, s)
        e = e + (tx + txn)
        if valid is not None:
            e = jnp.where(valid, e, 1.0)
        self.half = 0.5 * e + s * (1.0 / 3.0)
        self.spread(e)

    def spread(self, e):
        ln = self.ln
        self.all = 1.5 * e
        self.q = reciprocal(self.all)
        self.z1 = self.q * jnp.where(ln.first, self.tz, jnp.where(ln.last, self.tzp, 0.0))
        self.zm = ln.zm(self.z1)
        self.zp = ln.zp(self.z1)

    def toward(self, low):
        return self.tx if low else self.txn

    def inward(self, low):
        return self.txn if low else self.tx

    def edge(self, low):
        self.x1 = self.q * self.toward(low)
        self.o1 = 1.0 - self.z1 - self.x1

    def rim(self):
        return self.tz * self.zm + self.tzp * self.zp

    def along_y(self, v):
        return self.ty * self.ln.ym(v) + self.typ * self.ln.yp(v)


class Rim(Plane):
    def __init__(self, ln, e, tz):
        self.ln = ln
        self.tz = jnp.where(ln.lane0, 0.0, tz)
        self.tzp = ln.zp(self.tz)
        self.spread(e)


def plane_at(ln, faces, p):
    return Plane(ln, faces[0, p], faces[0, p + 1], faces[1, p], faces[2, p], faces[3, p])


def middle(p, below, above, mz):
    ln = p.ln
    vz = p.half * p.z1 + p.tx * below.z1 + p.txn * above.z1 + p.along_y(p.z1)
    vz = vz + p.tz * jnp.where(ln.first, 1.0 - p.zm, p.zm)
    vz = vz + p.tzp * jnp.where(ln.last, 1.0 - p.zp, p.zp)
    kept = vz * mz
    return p.all - vz, kept, p.all - (vz - kept)


def second(p, edge, inner, low, mz, mx):
    below, above = (edge, inner) if low else (inner, edge)
    ln = p.ln
    first_o = ln.zm(p.z1)
    vz = p.half * p.z1 + p.tx * below.z1 + p.txn * above.z1 + p.along_y(p.z1)
    vz = vz + p.tz * jnp.where(ln.first, 1.0 - first_o, first_o)
    vz = vz + p.tzp * jnp.where(ln.last, 1.0 - p.zp, p.zp)
    vx = p.toward(low) * edge.x1
    kept_z, kept_x = vz * mz, vx * mx
    total = p.all - (vz - kept_z) - (vx - kept_x)
    return p.all - vz - vx, kept_z, kept_x, total


def edge_own(p, inner_o1, inner_z1, outer_x1, low, mz):
    ln = p.ln
    om, op = ln.zm(p.o1), ln.zp(p.o1)
    vo = p.half * p.o1 + p.toward(low) * outer_x1 + p.inward(low) * inner_o1 + p.along_y(p.o1)
    vo = vo + p.tz * jnp.where(ln.first, p.zm, om) + p.tzp * jnp.where(ln.last, p.zp, op)
    vz = p.half * p.z1 + p.inward(low) * inner_z1 + p.along_y(p.z1)
    vz = vz + p.tz * jnp.where(ln.first, om, p.zm) + p.tzp * jnp.where(ln.last, op, p.zp)
    return vo, vz * mz


def edge_total(p, mz):
    rim = p.rim()
    return p.all - (rim - rim * mz)


def edge_spill(p, own, low):
    ln = p.ln
    xm, xp = ln.zm(p.x1), ln.zp(p.x1)
    face = p.toward(low)
    vx = p.half * p.x1 + face * own.o1 + p.along_y(p.x1)
    vx = vx + p.tz * jnp.where(ln.first, 0.0, xm) + p.tzp * jnp.where(ln.last, 0.0, xp)
    vd = face * own.z1 + p.tz * jnp.where(ln.first, xm, 0.0) + p.tzp * jnp.where(ln.last, xp, 0.0)
    return vx, vd


def store(ln, dst, plane, blocks, own, other, total):
    scale = reciprocal(total)
    own = own * scale
    other = jnp.zeros_like(own) if other is None else other * scale
    even, odd = jnp.where(ln.odd, other, own), jnp.where(ln.odd, own, other)
    for k in range(blocks):
        dst[k, plane] = jnp.where(ln.around(k), odd if k % 2 else even, 0.0)


def work_side(ln, low, valid, faces, masks, msg, put):
    n, rows, lanes = faces.shape[1:]
    layers = masks.shape[0]

    def own(i, j):
        return faces[i, jnp.where(low, j, n - 1 - j)]

    def got(i):
        tiles = rows // TAIL
        return msg[pl.ds(1 + tiles * i, tiles)].reshape(rows, lanes)

    f1, f2, f3 = (faces[0, jnp.where(low, j, n - j)] for j in (1, 2, 3))
    f0 = jnp.where(valid, jnp.where(low, faces[0, 0], got(6)), 0.0)
    g1 = got(0)
    a0 = Plane(ln, f0, f1, own(1, 0), own(2, 0), own(3, 0))
    a1 = Plane(ln, f1, f2, own(1, 1), own(2, 1), own(3, 1))
    a2 = Plane(ln, f2, f3, own(1, 2), own(2, 2), own(3, 2))
    b0 = Plane(ln, g1, f0, got(1), got(2), got(3), valid)
    b1 = Rim(ln, jnp.where(valid, got(4) + g1, 1.0), got(5))
    mine = masks[jnp.where(low, 0, layers - 1)]
    mz, my_reach = mine[0:1], jnp.where(low, mine[1:2], mine[2:3])
    theirs = msg[0]
    mo, their_reach = theirs[0:1], jnp.where(low, theirs[2:3], theirs[1:2])
    a0.edge(True)
    b0.edge(False)
    vx = g1 * b0.x1
    kept = vx * my_reach
    put(0, kept, None, edge_total(b1, mo) - (vx - kept))
    vx, vd = edge_spill(b0, a0, False)
    put(1, vx, vd, edge_total(b0, mo))
    vo, vz = edge_own(a0, 1.0 - a1.z1, a1.z1, b0.x1, True, mz)
    put(2, vo, vz, edge_total(a0, mz))
    vo, vz, _, total = second(a1, a0, a2, True, mz, their_reach)
    put(3, vo, vz, total)


def store_side(ln, buf, low, blocks):
    def put(i, own, other, total):
        store(ln, buf, jnp.where(low, i, 3 - i), blocks, own, other, total)

    return put


def send_one_side(buf, out, low, width, layers, sem, k):
    layer = jnp.where(low, 0, layers - 1)
    start = jnp.where(low, width - 2, 2 * width - 2)
    there = out.at[pl.ds((layer * buf.shape[0] + k) * 3 * width + start, 4)]
    return pltpu.make_async_copy(buf.at[k], there, sem)


def clear_run(zeros, out, b, bases, width, sem):
    depth = width - 2
    ends = isinstance(b, int) and b in (0, bases)
    count = depth if ends else 2 * depth
    start = 0 if ends and b == 0 else b * 3 * width - depth
    return pltpu.make_async_copy(zeros.at[pl.ds(0, count)], out.at[pl.ds(start, count)], sem)


def clear_runs(zeros, out, first, last, bases, width, sem):
    def body(b, _):
        clear_run(zeros, out, b, bases, width, sem).start()

    lax.fori_loop(first, last, body, None)


def wait_planes(out, count, sem):
    some = out.at[pl.ds(0, count)]
    pltpu.make_async_copy(some, some, sem).wait()


def pack_kernel(
    n, width, axis, tx, ty, tz, s, reach, msg_a, msg_b, masks, faces, out,
    held_reach, zeros, buf, read_sems, sem,
):
    layers, _, blocks = held_reach.shape
    rows, lanes = faces.shape[2:]
    fetch = pltpu.make_async_copy(reach, held_reach, read_sems.at[4])
    fetch.start()
    copies = [
        pltpu.make_async_copy(a, faces.at[i], read_sems.at[i]) for i, a in enumerate((tx, ty, tz, s))
    ]
    for i in (1, 2, 0, 3):
        copies[i].start()
    bases = layers * blocks
    me = lax.axis_index(axis)
    late = bases - EARLY

    @pl.when(me == 1)
    def _():
        zeros[...] = jnp.zeros(zeros.shape, jnp.float32)
        clear_runs(zeros, out, late, bases, bases, width, sem)

    masks[...] = jnp.zeros(masks.shape, jnp.float32)
    lane = lax.broadcasted_iota(jnp.int32, (4, lanes), 1)
    block = lane // width
    local = lane - block * width
    fetch.wait()
    for layer in range(layers):
        r = jnp.zeros((4, lanes), jnp.int32)
        for k in range(blocks):
            r = jnp.where(block == k, held_reach[layer, :, k : k + 1], r)
        low = pltpu.roll(r, width, 1)
        high = pltpu.roll(r, lanes - width, 1)
        near = jnp.where(
            local[0:1] < width // 2,
            jnp.where(low[3:4] >= local[0:1] + 1, 1.0, 0.0),
            jnp.where(high[2:3] >= width - local[0:1], 1.0, 0.0),
        )
        masks[layer, 0:1] = near
        masks[layer, 1:3] = jnp.where(r[0:2] >= 2, 1.0, 0.0)
    even = lax.rem(me, 2) == 0

    def put(tile, up, down):
        up, down = (v.reshape(-1, TAIL, lanes) for v in (up, down))
        where = pl.ds(tile, up.shape[0])
        msg_a[where] = jnp.where(even, up, down)
        msg_b[where] = jnp.where(even, down, up)

    put(0, masks[layers - 1], masks[0])
    ln = Lanes(faces.shape[2:], width)
    behind = {}

    def plane(slot, up, down):
        put(1 + slot * (rows // TAIL), up, down)

    for i, across in ((1, lambda v: within_y(ln, v)), (2, lambda v: within_z(ln, v))):
        copies[i].wait()
        plane(i, faces[i, n - 1], faces[i, 0])
        for p in (n - 2, 1):
            v, v_next = across(faces[i, p])
            behind[p] = behind.get(p, 0.0) + (v + v_next)
    plane(5, faces[2, n - 2], faces[2, 1])
    copies[0].wait()
    plane(0, faces[0, n - 1], faces[0, 1])
    plane(6, faces[0, n - 1], faces[0, 0])
    behind = {p: behind[p] + faces[0, q] for p, q in ((n - 2, n - 2), (1, 2))}
    copies[3].wait()
    plane(3, faces[3, n - 1], faces[3, 0])
    plane(4, *(behind[p] + faces[3, p] * (1.0 / 3.0) for p in (n - 2, 1)))

    @pl.when(me == 1)
    def _():
        wait_planes(out, EARLY * 2 * (width - 2), sem)

    @pl.when(me == 0)
    def _():
        inner_planes(width, bases, faces, masks, out, zeros, buf, sem)
        wait_planes(out, inner_count(layers, blocks, width), sem)


def inner_count(layers, blocks, width):
    return layers * blocks * 3 * width - 8 * blocks


def inner_planes(width, last_run, faces, masks, out, zeros, buf, sem):
    layers, blocks = buf.shape[:2]
    rows, lanes = faces.shape[2:]
    box, depth = 3 * width, width - 2
    bases = layers * blocks
    zeros[...] = jnp.zeros(zeros.shape, jnp.float32)

    for b in (0, bases):
        clear_run(zeros, out, b, bases, width, sem).start()
    clear_runs(zeros, out, 1, last_run, bases, width, sem)
    ln = Lanes((rows, lanes), width)
    plane = functools.partial(plane_at, ln, faces)

    def send(k, layer):
        start = 4 if layer == 0 else 0
        count = width + 4 - start - (4 if layer == layers - 1 else 0)
        return pltpu.make_async_copy(
            buf.at[layer, k, pl.ds(start, count)],
            out.at[pl.ds((layer * blocks + k) * box + depth + start, count)],
            sem,
        )

    def between(layer):
        base = layer * width
        ma, mb = masks[layer - 1, 0:1], masks[layer, 0:1]
        to_above, to_below = masks[layer - 1, 2:3], masks[layer, 1:2]
        a3, a2, a1 = (plane(base - i) for i in (3, 2, 1))
        b0, b1, b2 = (plane(base + i) for i in (0, 1, 2))
        a1.edge(False)
        b0.edge(True)
        low = functools.partial(store, ln, buf.at[layer - 1])
        high = functools.partial(store, ln, buf.at[layer])
        vo, vz, vx, total = second(a2, a1, a3, False, ma, to_below)
        low(width, blocks, vo, vz, total)
        high(0, blocks, vx, None, total)
        vo, vz = edge_own(a1, 1.0 - a2.z1, a2.z1, b0.x1, False, ma)
        vx, vd = edge_spill(a1, b0, False)
        total = edge_total(a1, ma)
        low(width + 1, blocks, vo, vz, total)
        high(1, blocks, vx, vd, total)
        vo, vz = edge_own(b0, 1.0 - b1.z1, b1.z1, a1.x1, True, mb)
        vx, vd = edge_spill(b0, a1, True)
        total = edge_total(b0, mb)
        high(2, blocks, vo, vz, total)
        low(width + 2, blocks, vx, vd, total)
        vo, vz, vx, total = second(b1, b0, b2, True, mb, to_above)
        high(3, blocks, vo, vz, total)
        low(width + 3, blocks, vx, None, total)

    for layer in range(layers):
        planes = [plane(layer * width + j) for j in range(1, width - 1)]
        mz = masks[layer, 0:1]
        for j in range(2, width - 2):
            vo, vz, total = middle(planes[j - 1], planes[j - 2], planes[j], mz)
            store(ln, buf.at[layer], j + 2, blocks, vo, vz, total)
        if layer < layers - 1:
            between(layer + 1)

        @pl.loop(0, blocks)
        def _(k):
            send(k, layer).start()


def bulk_kernel(width, axis, faces, masks, held, out, zeros, buf, sem):
    del held
    me = lax.axis_index(axis)
    layers, blocks = buf.shape[:2]
    bases = layers * blocks
    early = EARLY * 2 * (width - 2)

    @pl.when(me != 0)
    def _():
        last_run = jnp.where(me == 1, bases - EARLY, bases)
        inner_planes(width, last_run, faces, masks, out, zeros, buf, sem)
        wait_planes(out, inner_count(layers, blocks, width) - early, sem)

    @pl.when(me > 1)
    def _():
        wait_planes(out, early, sem)


def edge_kernel(
    width, blocks, axis, count, faces, masks, got_a, got_b, held, out, side_a, side_b, sem
):
    del held
    layers = masks.shape[0]
    me = lax.axis_index(axis)
    odd = lax.rem(me, 2) == 1
    ln = Lanes(faces.shape[2:], width)
    copies = []
    for low, msg, side in ((odd, got_a, side_a), (jnp.logical_not(odd), got_b, side_b)):
        valid = jnp.where(low, me > 0, me < count - 1)
        work_side(ln, low, valid, faces, masks, msg, store_side(ln, side, low, blocks))
        copies += [send_one_side(side, out, low, width, layers, sem, k) for k in range(blocks)]
    for c in copies:
        c.start()
    wait_planes(out, 8 * blocks, sem)


def swaps(firsts):
    return [pair for i in firsts for pair in ((i, i + 1), (i + 1, i))]


def on_device(trans_east, trans_north, trans_up, storage, support_reach, *, axis, count):
    layers, blocks, _ = support_reach.shape
    n, rows, lanes = trans_east.shape
    width = n // layers
    f32 = jnp.float32
    anywhere = pl.BlockSpec(memory_space=pl.ANY)
    vmem = pl.BlockSpec(memory_space=pltpu.VMEM)
    params = pltpu.CompilerParams(vmem_limit_bytes=16 * 2**20)
    outside = tuple(
        pltpu.with_memory_space_constraint(x, pltpu.HBM)
        for x in (trans_east, trans_north, trans_up, storage)
    )
    reach = jnp.transpose(support_reach, (0, 2, 1))
    reach = pltpu.with_memory_space_constraint(reach, pltpu.HBM)
    bases = layers * blocks
    out_shape = jax.ShapeDtypeStruct((bases * 3 * width, rows, lanes), f32)
    inner = [
        pltpu.VMEM((2 * (width - 2), rows, lanes), f32),
        pltpu.VMEM((layers, blocks, width + 4, rows, lanes), f32),
    ]
    tiles = 1 + 7 * rows // TAIL
    msg_a, msg_b, masks, faces, started = pl.pallas_call(
        functools.partial(pack_kernel, n, width, axis),
        out_shape=(
            pltpu.VMEM((tiles, TAIL, lanes), f32),
            pltpu.VMEM((tiles + 1, TAIL, lanes), f32),
            pltpu.VMEM((layers, TAIL, lanes), f32),
            pltpu.VMEM((4, n, rows, lanes), f32),
            out_shape,
        ),
        in_specs=[anywhere] * 5,
        out_specs=(vmem,) * 4 + (anywhere,),
        scratch_shapes=[
            pltpu.VMEM((layers, 4, blocks), jnp.int32),
            *inner,
            pltpu.SemaphoreType.DMA((5,)),
            pltpu.SemaphoreType.DMA,
        ],
        compiler_params=params,
        name="pack",
    )(*outside, reach)
    got_a = lax.ppermute(msg_a, axis, swaps(range(0, count - 1, 2)))
    got_b = lax.ppermute(msg_b, axis, swaps(range(1, count - 1, 2)))

    bulk = pl.pallas_call(
        functools.partial(bulk_kernel, width, axis),
        out_shape=out_shape,
        in_specs=[vmem] * 2 + [anywhere],
        out_specs=anywhere,
        scratch_shapes=inner + [pltpu.SemaphoreType.DMA],
        input_output_aliases={2: 0},
        compiler_params=params,
        cost_estimate=pl.CostEstimate(flops=10**7, bytes_accessed=7 * 10**6, transcendentals=0),
        name="bulk",
    )(faces, masks, started)
    side = [pltpu.VMEM((blocks, 4, rows, lanes), f32)] * 2
    out = pl.pallas_call(
        functools.partial(edge_kernel, width, blocks, axis, count),
        out_shape=out_shape,
        in_specs=[vmem] * 4 + [anywhere],
        out_specs=anywhere,
        scratch_shapes=side + [pltpu.SemaphoreType.DMA],
        input_output_aliases={4: 0},
        compiler_params=params,
        cost_estimate=pl.CostEstimate(flops=10**6, bytes_accessed=10**6, transcendentals=0),
        name="edges",
    )(faces, masks, got_a, got_b, bulk)
    return out.reshape(layers, blocks, 3 * width, rows, lanes)


def solution(mesh):
    spread = P(("groups", "blk"))
    return jax.shard_map(
        functools.partial(on_device, axis="blk", count=mesh.shape["blk"]),
        mesh=mesh,
        in_specs=(spread,) * 5,
        out_specs=spread,
        check_vma=False,
    )
```

```python
import functools

import jax
import jax.numpy as jnp
from jax import lax
from jax.experimental import pallas as pl
from jax.experimental.pallas import tpu as pltpu
from jax.sharding import PartitionSpec as P


TAIL = 8
EARLY = 12
FEW = 4
END = 4


class Lanes:
    def __init__(self, shape, width):
        tile = lax.broadcasted_iota(jnp.int32, (TAIL, shape[1]), 1)

        def rows(v):
            return jnp.concatenate([v] * (shape[0] // TAIL), axis=0)

        self.rows, self.lanes = shape
        self.width = width
        self.lane = rows(tile)
        self.local = rows(lax.rem(tile, width))
        self.first = self.local == 0
        self.last = self.local == width - 1
        self.odd = rows(lax.rem(tile // width, 2)) == 1
        self.row0 = lax.broadcasted_iota(jnp.int32, shape, 0) == 0
        self.lane0 = self.lane == 0

    def around(self, k):
        start = k * self.width - self.width // 2
        return (self.lane >= start) & (self.lane < start + 2 * self.width)

    def zm(self, v):
        return pltpu.roll(v, 1, 1)

    def zp(self, v):
        return pltpu.roll(v, self.lanes - 1, 1)

    def ym(self, v):
        return pltpu.roll(v, 1, 0)

    def yp(self, v):
        return pltpu.roll(v, self.rows - 1, 0)


def reciprocal(x):
    r = pl.reciprocal(x, approx=True)
    return r * (2.0 - x * r)


def within_y(ln, ty):
    ty = jnp.where(ln.row0, 0.0, ty)
    return ty, ln.yp(ty)


def within_z(ln, tz):
    tz = jnp.where(ln.lane0, 0.0, tz)
    return tz, ln.zp(tz)


def cross(ln, ty, tz, s):
    ty, typ = within_y(ln, ty)
    tz, tzp = within_z(ln, tz)
    return s * (1.0 / 3.0) + ((ty + typ) + (tz + tzp)), (ty, typ, tz, tzp)


class Plane:
    def __init__(self, ln, tx, txn, ty, tz, s, valid=None):
        self.ln = ln
        self.tx, self.txn = tx, txn
        e, (self.ty, self.typ, self.tz, self.tzp) = cross(ln, ty, tz, s)
        e = e + (tx + txn)
        if valid is not None:
            e = jnp.where(valid, e, 1.0)
        self.half = 0.5 * e + s * (1.0 / 3.0)
        self.spread(e)

    def spread(self, e):
        ln = self.ln
        self.all = 1.5 * e
        self.q = reciprocal(self.all)
        self.z1 = self.q * jnp.where(ln.first, self.tz, jnp.where(ln.last, self.tzp, 0.0))
        self.zm = ln.zm(self.z1)
        self.zp = ln.zp(self.z1)

    def toward(self, low):
        return self.tx if low else self.txn

    def inward(self, low):
        return self.txn if low else self.tx

    def edge(self, low):
        self.x1 = self.q * self.toward(low)
        self.o1 = 1.0 - self.z1 - self.x1

    def rim(self):
        return self.tz * self.zm + self.tzp * self.zp

    def along_y(self, v):
        return self.ty * self.ln.ym(v) + self.typ * self.ln.yp(v)


class Rim(Plane):
    def __init__(self, ln, e, tz):
        self.ln = ln
        self.tz = jnp.where(ln.lane0, 0.0, tz)
        self.tzp = ln.zp(self.tz)
        self.spread(e)


def middle(p, below, above, mz):
    ln = p.ln
    vz = p.half * p.z1 + p.tx * below.z1 + p.txn * above.z1 + p.along_y(p.z1)
    vz = vz + p.tz * jnp.where(ln.first, 1.0 - p.zm, p.zm)
    vz = vz + p.tzp * jnp.where(ln.last, 1.0 - p.zp, p.zp)
    kept = vz * mz
    return p.all - vz, kept, p.all - (vz - kept)


def second(p, edge, inner, low, mz, mx):
    below, above = (edge, inner) if low else (inner, edge)
    ln = p.ln
    first_o = ln.zm(p.z1)
    vz = p.half * p.z1 + p.tx * below.z1 + p.txn * above.z1 + p.along_y(p.z1)
    vz = vz + p.tz * jnp.where(ln.first, 1.0 - first_o, first_o)
    vz = vz + p.tzp * jnp.where(ln.last, 1.0 - p.zp, p.zp)
    vx = p.toward(low) * edge.x1
    kept_z, kept_x = vz * mz, vx * mx
    total = p.all - (vz - kept_z) - (vx - kept_x)
    return p.all - vz - vx, kept_z, kept_x, total


def edge_own(p, inner_o1, inner_z1, outer_x1, low, mz):
    ln = p.ln
    om, op = ln.zm(p.o1), ln.zp(p.o1)
    vo = p.half * p.o1 + p.toward(low) * outer_x1 + p.inward(low) * inner_o1 + p.along_y(p.o1)
    vo = vo + p.tz * jnp.where(ln.first, p.zm, om) + p.tzp * jnp.where(ln.last, p.zp, op)
    vz = p.half * p.z1 + p.inward(low) * inner_z1 + p.along_y(p.z1)
    vz = vz + p.tz * jnp.where(ln.first, om, p.zm) + p.tzp * jnp.where(ln.last, op, p.zp)
    return vo, vz * mz


def edge_total(p, mz):
    rim = p.rim()
    return p.all - (rim - rim * mz)


def edge_spill(p, own, low):
    ln = p.ln
    xm, xp = ln.zm(p.x1), ln.zp(p.x1)
    face = p.toward(low)
    vx = p.half * p.x1 + face * own.o1 + p.along_y(p.x1)
    vx = vx + p.tz * jnp.where(ln.first, 0.0, xm) + p.tzp * jnp.where(ln.last, 0.0, xp)
    vd = face * own.z1 + p.tz * jnp.where(ln.first, xm, 0.0) + p.tzp * jnp.where(ln.last, xp, 0.0)
    return vx, vd


def store(ln, dst, plane, blocks, own, other, total):
    scale = reciprocal(total)
    own = own * scale
    other = jnp.zeros_like(own) if other is None else other * scale
    even, odd = jnp.where(ln.odd, other, own), jnp.where(ln.odd, own, other)
    for k in range(blocks):
        dst[k, plane] = jnp.where(ln.around(k), odd if k % 2 else even, 0.0)


def work_side(ln, low, valid, faces, masks, msg, put):
    n, rows, lanes = faces.shape[1:]
    layers = masks.shape[0]

    def own(i, j):
        return faces[i, jnp.where(low, j, n - 1 - j)]

    def got(i):
        tiles = rows // TAIL
        return msg[pl.ds(1 + tiles * i, tiles)].reshape(rows, lanes)

    f1, f2, f3 = (faces[0, jnp.where(low, j, n - j)] for j in (1, 2, 3))
    f0 = jnp.where(valid, jnp.where(low, faces[0, 0], got(6)), 0.0)
    g1 = got(0)
    a0 = Plane(ln, f0, f1, own(1, 0), own(2, 0), own(3, 0))
    a1 = Plane(ln, f1, f2, own(1, 1), own(2, 1), own(3, 1))
    a2 = Plane(ln, f2, f3, own(1, 2), own(2, 2), own(3, 2))
    b0 = Plane(ln, g1, f0, got(1), got(2), got(3), valid)
    b1 = Rim(ln, jnp.where(valid, got(4) + g1, 1.0), got(5))
    mine = masks[jnp.where(low, 0, layers - 1)]
    mz, my_reach = mine[0:1], jnp.where(low, mine[1:2], mine[2:3])
    theirs = msg[0]
    mo, their_reach = theirs[0:1], jnp.where(low, theirs[2:3], theirs[1:2])
    a0.edge(True)
    b0.edge(False)
    vx = g1 * b0.x1
    kept = vx * my_reach
    put(0, kept, None, edge_total(b1, mo) - (vx - kept))
    vx, vd = edge_spill(b0, a0, False)
    put(1, vx, vd, edge_total(b0, mo))
    vo, vz = edge_own(a0, 1.0 - a1.z1, a1.z1, b0.x1, True, mz)
    put(2, vo, vz, edge_total(a0, mz))
    vo, vz, _, total = second(a1, a0, a2, True, mz, their_reach)
    put(3, vo, vz, total)


def store_side(ln, buf, low, blocks):
    def put(i, own, other, total):
        store(ln, buf, jnp.where(low, i, 3 - i), blocks, own, other, total)

    return put


def send_side(buf, out, low, layers, sem):
    blocks, width = buf.shape[0], out.shape[1] // 3
    layer = jnp.where(low, 0, layers - 1)
    start = jnp.where(low, width - 2, 2 * width - 2)
    for i in range(0, blocks, FEW):
        there = out.at[pl.ds(layer * blocks + i, FEW), pl.ds(start, 4)]
        yield pltpu.make_async_copy(buf.at[pl.ds(i, FEW)], there, sem)


def clear_run(zeros, out, b, bases, width, sem):
    depth = width - 2
    ends = isinstance(b, int) and b in (0, bases)
    count = depth if ends else 2 * depth
    start = 0 if ends and b == 0 else b * 3 * width - depth
    return pltpu.make_async_copy(zeros.at[pl.ds(0, count)], out.at[pl.ds(start, count)], sem)


def clear_runs(zeros, out, first, last, bases, width, sem):
    def body(b, _):
        clear_run(zeros, out, b, bases, width, sem).start()

    lax.fori_loop(first, last, body, None)


def wait_planes(out, count, sem):
    some = out.at[pl.ds(0, count)]
    pltpu.make_async_copy(some, some, sem).wait()


def pack_kernel(
    n, width, axis, tx, ty, tz, s, reach, msg_a, msg_b, masks, faces, out,
    held_reach, rest, zeros, buf, read_sems, sem,
):
    layers, _, blocks = held_reach.shape
    rows, lanes = faces.shape[2:]
    fetch = pltpu.make_async_copy(reach, held_reach, read_sems.at[4])
    fetch.start()
    class Read:
        def __init__(self, i, a):
            self.parts = [
                pltpu.make_async_copy(a.at[part], faces.at[i, part], read_sems.at[i])
                for part in (pl.ds(n - END, END), pl.ds(0, min(width, n - END)))
            ]

        def start(self):
            for c in self.parts:
                c.start()

        def wait(self):
            both = faces.at[0, pl.ds(0, min(width, n - END) + END)]
            pltpu.make_async_copy(both, both, self.sem).wait()

    copies = [Read(i, a) for i, a in enumerate((tx, ty, tz, s))]
    for i, c in enumerate(copies):
        c.sem = read_sems.at[i]
    for i in (1, 2, 0, 3):
        copies[i].start()
    bases = layers * blocks
    me = lax.axis_index(axis)
    late = bases - EARLY

    @pl.when(me == 1)
    def _():
        zeros[...] = jnp.zeros(zeros.shape, jnp.float32)
        clear_runs(zeros, out, late, bases, bases, width, sem)

    masks[...] = jnp.zeros(masks.shape, jnp.float32)
    lane = lax.broadcasted_iota(jnp.int32, (4, lanes), 1)
    block = lane // width
    local = lane - block * width
    fetch.wait()
    for layer in range(layers):
        r = jnp.zeros((4, lanes), jnp.int32)
        for k in range(blocks):
            r = jnp.where(block == k, held_reach[layer, :, k : k + 1], r)
        low = pltpu.roll(r, width, 1)
        high = pltpu.roll(r, lanes - width, 1)
        near = jnp.where(
            local[0:1] < width // 2,
            jnp.where(low[3:4] >= local[0:1] + 1, 1.0, 0.0),
            jnp.where(high[2:3] >= width - local[0:1], 1.0, 0.0),
        )
        masks[layer, 0:1] = near
        masks[layer, 1:3] = jnp.where(r[0:2] >= 2, 1.0, 0.0)
    even = lax.rem(me, 2) == 0

    def put(tile, up, down):
        up, down = (v.reshape(-1, TAIL, lanes) for v in (up, down))
        where = pl.ds(tile, up.shape[0])
        msg_a[where] = jnp.where(even, up, down)
        msg_b[where] = jnp.where(even, down, up)

    put(0, masks[layers - 1], masks[0])
    ln = Lanes(faces.shape[2:], width)
    behind = {}

    def plane(slot, up, down):
        put(1 + slot * (rows // TAIL), up, down)

    for i, across in ((1, lambda v: within_y(ln, v)), (2, lambda v: within_z(ln, v))):
        copies[i].wait()
        plane(i, faces[i, n - 1], faces[i, 0])
        for p in (n - 2, 1):
            v, v_next = across(faces[i, p])
            behind[p] = behind.get(p, 0.0) + (v + v_next)
    plane(5, faces[2, n - 2], faces[2, 1])
    copies[0].wait()
    plane(0, faces[0, n - 1], faces[0, 1])
    plane(6, faces[0, n - 1], faces[0, 0])
    behind = {p: behind[p] + faces[0, q] for p, q in ((n - 2, n - 2), (1, 2))}
    copies[3].wait()
    plane(3, faces[3, n - 1], faces[3, 0])
    plane(4, *(behind[p] + faces[3, p] * (1.0 / 3.0) for p in (n - 2, 1)))

    @pl.when(me == 1)
    def _():
        wait_planes(out, EARLY * 2 * (width - 2), sem)

    @pl.when(me == 0)
    def _():
        inner_planes(width, bases, (tx, ty, tz, s), faces, rest, masks, out, zeros, buf, sem, read_sems.at[4])
        wait_planes(out, inner_count(layers, blocks, width), sem)


def inner_count(layers, blocks, width):
    return layers * blocks * 3 * width - 8 * blocks


def inner_planes(width, last_run, fields, faces, rest, masks, out, zeros, buf, sem, read_sem):
    layers, blocks = buf.shape[:2]
    rows, lanes = faces.shape[2:]
    box, depth = 3 * width, width - 2
    bases = layers * blocks
    n = faces.shape[1]
    for i, a in enumerate(fields):
        if layers > 1:
            pltpu.make_async_copy(a.at[pl.ds(width, n - END - width)], rest.at[i], read_sem).start()
    zeros[...] = jnp.zeros(zeros.shape, jnp.float32)

    for b in (0, bases):
        clear_run(zeros, out, b, bases, width, sem).start()
    clear_runs(zeros, out, 1, last_run, bases, width, sem)
    ln = Lanes((rows, lanes), width)

    def field(i, p):
        return rest[i, p - width] if width <= p < n - END else faces[i, p]

    def plane(p):
        return Plane(ln, field(0, p), field(0, p + 1), field(1, p), field(2, p), field(3, p))

    def send(k, layer, start, count):
        return pltpu.make_async_copy(
            buf.at[layer, k, pl.ds(start, count)],
            out.at[pl.ds((layer * blocks + k) * box + depth + start, count)],
            sem,
        )

    def between(layer):
        base = layer * width
        ma, mb = masks[layer - 1, 0:1], masks[layer, 0:1]
        to_above, to_below = masks[layer - 1, 2:3], masks[layer, 1:2]
        a3, a2, a1 = (plane(base - i) for i in (3, 2, 1))
        b0, b1, b2 = (plane(base + i) for i in (0, 1, 2))
        a1.edge(False)
        b0.edge(True)
        low = functools.partial(store, ln, buf.at[layer - 1])
        high = functools.partial(store, ln, buf.at[layer])
        vo, vz, vx, total = second(a2, a1, a3, False, ma, to_below)
        low(width, blocks, vo, vz, total)
        high(0, blocks, vx, None, total)
        vo, vz = edge_own(a1, 1.0 - a2.z1, a2.z1, b0.x1, False, ma)
        vx, vd = edge_spill(a1, b0, False)
        total = edge_total(a1, ma)
        low(width + 1, blocks, vo, vz, total)
        high(1, blocks, vx, vd, total)
        vo, vz = edge_own(b0, 1.0 - b1.z1, b1.z1, a1.x1, True, mb)
        vx, vd = edge_spill(b0, a1, True)
        total = edge_total(b0, mb)
        high(2, blocks, vo, vz, total)
        low(width + 2, blocks, vx, vd, total)
        vo, vz, vx, total = second(b1, b0, b2, True, mb, to_above)
        high(3, blocks, vo, vz, total)
        low(width + 3, blocks, vx, None, total)

    for layer in range(layers):
        if layer == 1:
            pltpu.make_async_copy(rest, rest, read_sem).wait()
        planes = [plane(layer * width + j) for j in range(1, width - 1)]
        mz = masks[layer, 0:1]
        for j in range(2, width - 2):
            vo, vz, total = middle(planes[j - 1], planes[j - 2], planes[j], mz)
            store(ln, buf.at[layer], j + 2, blocks, vo, vz, total)
        if layer > 0:
            between(layer)

        @pl.loop(0, blocks)
        def _(k):
            if layer > 0:
                send(k, layer - 1, width, 4).start()
                send(k, layer, 0, width).start()
            else:
                send(k, layer, 4, width - 4).start()


def bulk_kernel(width, axis, tx, ty, tz, s, faces, masks, held, out, rest, zeros, buf, sem, read_sem):
    del held
    me = lax.axis_index(axis)
    layers, blocks = buf.shape[:2]
    bases = layers * blocks
    early = EARLY * 2 * (width - 2)

    @pl.when(me != 0)
    def _():
        last_run = jnp.where(me == 1, bases - EARLY, bases)
        inner_planes(width, last_run, (tx, ty, tz, s), faces, rest, masks, out, zeros, buf, sem, read_sem)
        wait_planes(out, inner_count(layers, blocks, width) - early, sem)

    @pl.when(me > 1)
    def _():
        wait_planes(out, early, sem)


def edge_kernel(
    width, blocks, axis, count, faces, masks, got_a, got_b, held, out, side_a, side_b, sem
):
    del held
    layers = masks.shape[0]
    me = lax.axis_index(axis)
    odd = lax.rem(me, 2) == 1
    ln = Lanes(faces.shape[2:], width)
    copies = []
    for low, msg, side in ((odd, got_a, side_a), (jnp.logical_not(odd), got_b, side_b)):
        valid = jnp.where(low, me > 0, me < count - 1)
        work_side(ln, low, valid, faces, masks, msg, store_side(ln, side, low, blocks))
        copies += list(send_side(side, out, low, layers, sem))
    for c in copies:
        c.start()
    for side in (side_a, side_b):
        pltpu.make_async_copy(side, side, sem).wait()


def swaps(firsts):
    return [pair for i in firsts for pair in ((i, i + 1), (i + 1, i))]


def on_device(trans_east, trans_north, trans_up, storage, support_reach, *, axis, count):
    layers, blocks, _ = support_reach.shape
    n, rows, lanes = trans_east.shape
    width = n // layers
    f32 = jnp.float32
    anywhere = pl.BlockSpec(memory_space=pl.ANY)
    vmem = pl.BlockSpec(memory_space=pltpu.VMEM)
    params = pltpu.CompilerParams(vmem_limit_bytes=16 * 2**20)
    outside = tuple(
        pltpu.with_memory_space_constraint(x, pltpu.HBM)
        for x in (trans_east, trans_north, trans_up, storage)
    )
    reach = jnp.transpose(support_reach, (0, 2, 1))
    reach = pltpu.with_memory_space_constraint(reach, pltpu.HBM)
    bases = layers * blocks
    out_shape = jax.ShapeDtypeStruct((bases * 3 * width, rows, lanes), f32)
    inner = [
        pltpu.VMEM((4, max(n - END - width, 1), rows, lanes), f32),
        pltpu.VMEM((2 * (width - 2), rows, lanes), f32),
        pltpu.VMEM((layers, blocks, width + 4, rows, lanes), f32),
    ]
    tiles = 1 + 7 * rows // TAIL
    msg_a, msg_b, masks, faces, started = pl.pallas_call(
        functools.partial(pack_kernel, n, width, axis),
        out_shape=(
            pltpu.VMEM((tiles, TAIL, lanes), f32),
            pltpu.VMEM((tiles + 1, TAIL, lanes), f32),
            pltpu.VMEM((layers, TAIL, lanes), f32),
            pltpu.VMEM((4, n, rows, lanes), f32),
            out_shape,
        ),
        in_specs=[anywhere] * 5,
        out_specs=(vmem,) * 4 + (anywhere,),
        scratch_shapes=[
            pltpu.VMEM((layers, 4, blocks), jnp.int32),
            *inner,
            pltpu.SemaphoreType.DMA((5,)),
            pltpu.SemaphoreType.DMA,
        ],
        compiler_params=params,
        name="pack",
    )(*outside, reach)
    got_a = lax.ppermute(msg_a, axis, swaps(range(0, count - 1, 2)))
    got_b = lax.ppermute(msg_b, axis, swaps(range(1, count - 1, 2)))

    bulk = pl.pallas_call(
        functools.partial(bulk_kernel, width, axis),
        out_shape=out_shape,
        in_specs=[anywhere] * 4 + [vmem] * 2 + [anywhere],
        out_specs=anywhere,
        scratch_shapes=inner + [pltpu.SemaphoreType.DMA] * 2,
        input_output_aliases={6: 0},
        compiler_params=params,
        cost_estimate=pl.CostEstimate(flops=10**7, bytes_accessed=7 * 10**6, transcendentals=0),
        name="bulk",
    )(*outside, faces, masks, started)
    boxes = jax.ShapeDtypeStruct((bases, 3 * width, rows, lanes), f32)
    side = [pltpu.VMEM((blocks, 4, rows, lanes), f32)] * 2
    out = pl.pallas_call(
        functools.partial(edge_kernel, width, blocks, axis, count),
        out_shape=boxes,
        in_specs=[vmem] * 4 + [anywhere],
        out_specs=anywhere,
        scratch_shapes=side + [pltpu.SemaphoreType.DMA],
        input_output_aliases={4: 0},
        compiler_params=params,
        cost_estimate=pl.CostEstimate(flops=10**6, bytes_accessed=10**6, transcendentals=0),
        name="edges",
    )(faces, masks, got_a, got_b, bulk.reshape(boxes.shape))
    return out.reshape(layers, blocks, 3 * width, rows, lanes)


def solution(mesh):
    spread = P(("groups", "blk"))
    return jax.shard_map(
        functools.partial(on_device, axis="blk", count=mesh.shape["blk"]),
        mesh=mesh,
        in_specs=(spread,) * 5,
        out_specs=spread,
        check_vma=False,
    )
```

```python
import functools

import jax
import jax.numpy as jnp
from jax import lax
from jax.experimental import pallas as pl
from jax.experimental.pallas import tpu as pltpu
from jax.sharding import PartitionSpec as P


TAIL = 8
EARLY = 12
END = 4


class Lanes:
    def __init__(self, shape, width):
        tile = lax.broadcasted_iota(jnp.int32, (TAIL, shape[1]), 1)

        def rows(v):
            return jnp.concatenate([v] * (shape[0] // TAIL), axis=0)

        self.rows, self.lanes = shape
        self.width = width
        self.lane = rows(tile)
        self.local = rows(lax.rem(tile, width))
        self.first = self.local == 0
        self.last = self.local == width - 1
        self.odd = rows(lax.rem(tile // width, 2)) == 1
        self.row0 = lax.broadcasted_iota(jnp.int32, shape, 0) == 0
        self.lane0 = self.lane == 0

    def around(self, k):
        start = k * self.width - self.width // 2
        return (self.lane >= start) & (self.lane < start + 2 * self.width)

    def zm(self, v):
        return pltpu.roll(v, 1, 1)

    def zp(self, v):
        return pltpu.roll(v, self.lanes - 1, 1)

    def ym(self, v):
        return pltpu.roll(v, 1, 0)

    def yp(self, v):
        return pltpu.roll(v, self.rows - 1, 0)


def reciprocal(x):
    r = pl.reciprocal(x, approx=True)
    return r * (2.0 - x * r)


def within_y(ln, ty):
    ty = jnp.where(ln.row0, 0.0, ty)
    return ty, ln.yp(ty)


def within_z(ln, tz):
    tz = jnp.where(ln.lane0, 0.0, tz)
    return tz, ln.zp(tz)


def cross(ln, ty, tz, s):
    ty, typ = within_y(ln, ty)
    tz, tzp = within_z(ln, tz)
    return s * (1.0 / 3.0) + ((ty + typ) + (tz + tzp)), (ty, typ, tz, tzp)


class Plane:
    def __init__(self, ln, tx, txn, ty, tz, s, valid=None):
        self.ln = ln
        self.tx, self.txn = tx, txn
        e, (self.ty, self.typ, self.tz, self.tzp) = cross(ln, ty, tz, s)
        e = e + (tx + txn)
        if valid is not None:
            e = jnp.where(valid, e, 1.0)
        self.half = 0.5 * e + s * (1.0 / 3.0)
        self.spread(e)

    def spread(self, e):
        ln = self.ln
        self.all = 1.5 * e
        self.q = reciprocal(self.all)
        self.z1 = self.q * jnp.where(ln.first, self.tz, jnp.where(ln.last, self.tzp, 0.0))
        self.zm = ln.zm(self.z1)
        self.zp = ln.zp(self.z1)

    def toward(self, low):
        return self.tx if low else self.txn

    def inward(self, low):
        return self.txn if low else self.tx

    def edge(self, low):
        self.x1 = self.q * self.toward(low)
        self.o1 = 1.0 - self.z1 - self.x1

    def rim(self):
        return self.tz * self.zm + self.tzp * self.zp

    def along_y(self, v):
        return self.ty * self.ln.ym(v) + self.typ * self.ln.yp(v)


class Rim(Plane):
    def __init__(self, ln, e, tz):
        self.ln = ln
        self.tz = jnp.where(ln.lane0, 0.0, tz)
        self.tzp = ln.zp(self.tz)
        self.spread(e)


def plane_at(ln, faces, p):
    return Plane(ln, faces[0, p], faces[0, p + 1], faces[1, p], faces[2, p], faces[3, p])


def middle(p, below, above, mz):
    ln = p.ln
    vz = p.half * p.z1 + p.tx * below.z1 + p.txn * above.z1 + p.along_y(p.z1)
    vz = vz + p.tz * jnp.where(ln.first, 1.0 - p.zm, p.zm)
    vz = vz + p.tzp * jnp.where(ln.last, 1.0 - p.zp, p.zp)
    kept = vz * mz
    return p.all - vz, kept, p.all - (vz - kept)


def second(p, edge, inner, low, mz, mx):
    below, above = (edge, inner) if low else (inner, edge)
    ln = p.ln
    first_o = ln.zm(p.z1)
    vz = p.half * p.z1 + p.tx * below.z1 + p.txn * above.z1 + p.along_y(p.z1)
    vz = vz + p.tz * jnp.where(ln.first, 1.0 - first_o, first_o)
    vz = vz + p.tzp * jnp.where(ln.last, 1.0 - p.zp, p.zp)
    vx = p.toward(low) * edge.x1
    kept_z, kept_x = vz * mz, vx * mx
    total = p.all - (vz - kept_z) - (vx - kept_x)
    return p.all - vz - vx, kept_z, kept_x, total


def edge_own(p, inner_o1, inner_z1, outer_x1, low, mz):
    ln = p.ln
    om, op = ln.zm(p.o1), ln.zp(p.o1)
    vo = p.half * p.o1 + p.toward(low) * outer_x1 + p.inward(low) * inner_o1 + p.along_y(p.o1)
    vo = vo + p.tz * jnp.where(ln.first, p.zm, om) + p.tzp * jnp.where(ln.last, p.zp, op)
    vz = p.half * p.z1 + p.inward(low) * inner_z1 + p.along_y(p.z1)
    vz = vz + p.tz * jnp.where(ln.first, om, p.zm) + p.tzp * jnp.where(ln.last, op, p.zp)
    return vo, vz * mz


def edge_total(p, mz):
    rim = p.rim()
    return p.all - (rim - rim * mz)


def edge_spill(p, own, low):
    ln = p.ln
    xm, xp = ln.zm(p.x1), ln.zp(p.x1)
    face = p.toward(low)
    vx = p.half * p.x1 + face * own.o1 + p.along_y(p.x1)
    vx = vx + p.tz * jnp.where(ln.first, 0.0, xm) + p.tzp * jnp.where(ln.last, 0.0, xp)
    vd = face * own.z1 + p.tz * jnp.where(ln.first, xm, 0.0) + p.tzp * jnp.where(ln.last, xp, 0.0)
    return vx, vd


def store(ln, dst, plane, blocks, own, other, total):
    scale = reciprocal(total)
    own = own * scale
    other = jnp.zeros_like(own) if other is None else other * scale
    even, odd = jnp.where(ln.odd, other, own), jnp.where(ln.odd, own, other)
    for k in range(blocks):
        dst[k, plane] = jnp.where(ln.around(k), odd if k % 2 else even, 0.0)


def work_side(ln, low, valid, faces, masks, msg, put):
    n, rows, lanes = faces.shape[1:]
    layers = masks.shape[0]

    def own(i, j):
        return faces[i, jnp.where(low, j, n - 1 - j)]

    def got(i):
        tiles = rows // TAIL
        return msg[pl.ds(1 + tiles * i, tiles)].reshape(rows, lanes)

    f1, f2, f3 = (faces[0, jnp.where(low, j, n - j)] for j in (1, 2, 3))
    f0 = jnp.where(valid, jnp.where(low, faces[0, 0], got(6)), 0.0)
    g1 = got(0)
    a0 = Plane(ln, f0, f1, own(1, 0), own(2, 0), own(3, 0))
    a1 = Plane(ln, f1, f2, own(1, 1), own(2, 1), own(3, 1))
    a2 = Plane(ln, f2, f3, own(1, 2), own(2, 2), own(3, 2))
    b0 = Plane(ln, g1, f0, got(1), got(2), got(3), valid)
    b1 = Rim(ln, jnp.where(valid, got(4) + g1, 1.0), got(5))
    mine = masks[jnp.where(low, 0, layers - 1)]
    mz, my_reach = mine[0:1], jnp.where(low, mine[1:2], mine[2:3])
    theirs = msg[0]
    mo, their_reach = theirs[0:1], jnp.where(low, theirs[2:3], theirs[1:2])
    a0.edge(True)
    b0.edge(False)
    vx = g1 * b0.x1
    kept = vx * my_reach
    put(0, kept, None, edge_total(b1, mo) - (vx - kept))
    vx, vd = edge_spill(b0, a0, False)
    put(1, vx, vd, edge_total(b0, mo))
    vo, vz = edge_own(a0, 1.0 - a1.z1, a1.z1, b0.x1, True, mz)
    put(2, vo, vz, edge_total(a0, mz))
    vo, vz, _, total = second(a1, a0, a2, True, mz, their_reach)
    put(3, vo, vz, total)


def store_side(ln, buf, low, blocks):
    def put(i, own, other, total):
        store(ln, buf, jnp.where(low, i, 3 - i), blocks, own, other, total)

    return put


def send_one_side(buf, out, low, width, layers, sem, k):
    layer = jnp.where(low, 0, layers - 1)
    start = jnp.where(low, width - 2, 2 * width - 2)
    there = out.at[pl.ds((layer * buf.shape[0] + k) * 3 * width + start, 4)]
    return pltpu.make_async_copy(buf.at[k], there, sem)


def clear_run(zeros, out, b, bases, width, sem):
    depth = width - 2
    ends = isinstance(b, int) and b in (0, bases)
    count = depth if ends else 2 * depth
    start = 0 if ends and b == 0 else b * 3 * width - depth
    return pltpu.make_async_copy(zeros.at[pl.ds(0, count)], out.at[pl.ds(start, count)], sem)


def clear_runs(zeros, out, first, last, bases, width, sem):
    def body(b, _):
        clear_run(zeros, out, b, bases, width, sem).start()

    lax.fori_loop(first, last, body, None)


def wait_planes(out, count, sem):
    some = out.at[pl.ds(0, count)]
    pltpu.make_async_copy(some, some, sem).wait()


def reads_later(me):
    return (lax.rem(me, 2) == 0) & (me > 0)


def inner_reads(fields, faces, sem):
    part = pl.ds(END, faces.shape[1] - 2 * END)
    return [pltpu.make_async_copy(a.at[part], faces.at[i, part], sem) for i, a in enumerate(fields)]


def wait_inner(faces, sem):
    inner = faces.at[:, pl.ds(END, faces.shape[1] - 2 * END)]
    pltpu.make_async_copy(inner, inner, sem).wait()


def stage_kernel(axis, tx, ty, tz, s, held_faces, held_msg, faces, msg, sem):
    del held_faces, held_msg, msg

    @pl.when(reads_later(lax.axis_index(axis)))
    def _():
        for c in inner_reads((tx, ty, tz, s), faces, sem):
            c.start()
        wait_inner(faces, sem)


def pack_kernel(
    n, width, axis, tx, ty, tz, s, reach, msg_a, msg_b, masks, faces, out,
    held_reach, zeros, buf, read_sems, sem,
):
    layers, _, blocks = held_reach.shape
    rows, lanes = faces.shape[2:]
    fetch = pltpu.make_async_copy(reach, held_reach, read_sems.at[4])
    fetch.start()
    fields = (tx, ty, tz, s)
    for i in (1, 2, 0, 3):
        for part in (pl.ds(0, END), pl.ds(n - END, END)):
            pltpu.make_async_copy(fields[i].at[part], faces.at[i, part], read_sems.at[i]).start()

    def wait_ends(i):
        both = faces.at[i, pl.ds(0, 2 * END)]
        pltpu.make_async_copy(both, both, read_sems.at[i]).wait()

    bases = layers * blocks
    me = lax.axis_index(axis)
    late = bases - EARLY
    even = lax.rem(me, 2) == 0
    here = jnp.logical_not(reads_later(me))

    @pl.when(here)
    def _():
        for c in inner_reads(fields, faces, read_sems.at[5]):
            c.start()

    @pl.when(me == 1)
    def _():
        zeros[...] = jnp.zeros(zeros.shape, jnp.float32)
        clear_runs(zeros, out, late, bases, bases, width, sem)

    masks[...] = jnp.zeros(masks.shape, jnp.float32)
    lane = lax.broadcasted_iota(jnp.int32, (4, lanes), 1)
    block = lane // width
    local = lane - block * width
    fetch.wait()
    for layer in range(layers):
        r = jnp.zeros((4, lanes), jnp.int32)
        for k in range(blocks):
            r = jnp.where(block == k, held_reach[layer, :, k : k + 1], r)
        low = pltpu.roll(r, width, 1)
        high = pltpu.roll(r, lanes - width, 1)
        near = jnp.where(
            local[0:1] < width // 2,
            jnp.where(low[3:4] >= local[0:1] + 1, 1.0, 0.0),
            jnp.where(high[2:3] >= width - local[0:1], 1.0, 0.0),
        )
        masks[layer, 0:1] = near
        masks[layer, 1:3] = jnp.where(r[0:2] >= 2, 1.0, 0.0)
    def put(tile, up, down):
        up, down = (v.reshape(-1, TAIL, lanes) for v in (up, down))
        where = pl.ds(tile, up.shape[0])
        msg_a[where] = jnp.where(even, up, down)
        msg_b[where] = jnp.where(even, down, up)

    put(0, masks[layers - 1], masks[0])
    ln = Lanes(faces.shape[2:], width)
    behind = {}

    def plane(slot, up, down):
        put(1 + slot * (rows // TAIL), up, down)

    for i, across in ((1, lambda v: within_y(ln, v)), (2, lambda v: within_z(ln, v))):
        wait_ends(i)
        plane(i, faces[i, n - 1], faces[i, 0])
        for p in (n - 2, 1):
            v, v_next = across(faces[i, p])
            behind[p] = behind.get(p, 0.0) + (v + v_next)
    plane(5, faces[2, n - 2], faces[2, 1])
    wait_ends(0)
    plane(0, faces[0, n - 1], faces[0, 1])
    plane(6, faces[0, n - 1], faces[0, 0])
    behind = {p: behind[p] + faces[0, q] for p, q in ((n - 2, n - 2), (1, 2))}
    wait_ends(3)
    plane(3, faces[3, n - 1], faces[3, 0])
    plane(4, *(behind[p] + faces[3, p] * (1.0 / 3.0) for p in (n - 2, 1)))

    @pl.when(here)
    def _():
        wait_inner(faces, read_sems.at[5])

    @pl.when(me == 1)
    def _():
        wait_planes(out, EARLY * 2 * (width - 2), sem)

    @pl.when(me == 0)
    def _():
        inner_planes(width, bases, faces, masks, out, zeros, buf, sem)
        wait_planes(out, inner_count(layers, blocks, width), sem)


def inner_count(layers, blocks, width):
    return layers * blocks * 3 * width - 8 * blocks


def inner_planes(width, last_run, faces, masks, out, zeros, buf, sem):
    layers, blocks = buf.shape[:2]
    rows, lanes = faces.shape[2:]
    box, depth = 3 * width, width - 2
    bases = layers * blocks
    zeros[...] = jnp.zeros(zeros.shape, jnp.float32)

    for b in (0, bases):
        clear_run(zeros, out, b, bases, width, sem).start()
    clear_runs(zeros, out, 1, last_run, bases, width, sem)
    ln = Lanes((rows, lanes), width)
    plane = functools.partial(plane_at, ln, faces)

    def send(k, layer):
        start = 4 if layer == 0 else 0
        count = width + 4 - start - (4 if layer == layers - 1 else 0)
        return pltpu.make_async_copy(
            buf.at[layer, k, pl.ds(start, count)],
            out.at[pl.ds((layer * blocks + k) * box + depth + start, count)],
            sem,
        )

    def between(layer):
        base = layer * width
        ma, mb = masks[layer - 1, 0:1], masks[layer, 0:1]
        to_above, to_below = masks[layer - 1, 2:3], masks[layer, 1:2]
        a3, a2, a1 = (plane(base - i) for i in (3, 2, 1))
        b0, b1, b2 = (plane(base + i) for i in (0, 1, 2))
        a1.edge(False)
        b0.edge(True)
        low = functools.partial(store, ln, buf.at[layer - 1])
        high = functools.partial(store, ln, buf.at[layer])
        vo, vz, vx, total = second(a2, a1, a3, False, ma, to_below)
        low(width, blocks, vo, vz, total)
        high(0, blocks, vx, None, total)
        vo, vz = edge_own(a1, 1.0 - a2.z1, a2.z1, b0.x1, False, ma)
        vx, vd = edge_spill(a1, b0, False)
        total = edge_total(a1, ma)
        low(width + 1, blocks, vo, vz, total)
        high(1, blocks, vx, vd, total)
        vo, vz = edge_own(b0, 1.0 - b1.z1, b1.z1, a1.x1, True, mb)
        vx, vd = edge_spill(b0, a1, True)
        total = edge_total(b0, mb)
        high(2, blocks, vo, vz, total)
        low(width + 2, blocks, vx, vd, total)
        vo, vz, vx, total = second(b1, b0, b2, True, mb, to_above)
        high(3, blocks, vo, vz, total)
        low(width + 3, blocks, vx, None, total)

    for layer in range(layers):
        planes = [plane(layer * width + j) for j in range(1, width - 1)]
        mz = masks[layer, 0:1]
        for j in range(2, width - 2):
            vo, vz, total = middle(planes[j - 1], planes[j - 2], planes[j], mz)
            store(ln, buf.at[layer], j + 2, blocks, vo, vz, total)
        if layer < layers - 1:
            between(layer + 1)

        @pl.loop(0, blocks)
        def _(k):
            send(k, layer).start()


def bulk_kernel(width, axis, faces, masks, held, out, zeros, buf, sem):
    del held
    me = lax.axis_index(axis)
    layers, blocks = buf.shape[:2]
    bases = layers * blocks
    early = EARLY * 2 * (width - 2)

    @pl.when(me != 0)
    def _():
        last_run = jnp.where(me == 1, bases - EARLY, bases)
        inner_planes(width, last_run, faces, masks, out, zeros, buf, sem)
        wait_planes(out, inner_count(layers, blocks, width) - early, sem)

    @pl.when(me > 1)
    def _():
        wait_planes(out, early, sem)


def edge_kernel(
    width, blocks, axis, count, faces, masks, got_a, got_b, held, out, side_a, side_b, sem
):
    del held
    layers = masks.shape[0]
    me = lax.axis_index(axis)
    odd = lax.rem(me, 2) == 1
    ln = Lanes(faces.shape[2:], width)
    copies = []
    for low, msg, side in ((odd, got_a, side_a), (jnp.logical_not(odd), got_b, side_b)):
        valid = jnp.where(low, me > 0, me < count - 1)
        work_side(ln, low, valid, faces, masks, msg, store_side(ln, side, low, blocks))
        copies += [send_one_side(side, out, low, width, layers, sem, k) for k in range(blocks)]
    for c in copies:
        c.start()
    wait_planes(out, 8 * blocks, sem)


def swaps(firsts):
    return [pair for i in firsts for pair in ((i, i + 1), (i + 1, i))]


def on_device(trans_east, trans_north, trans_up, storage, support_reach, *, axis, count):
    layers, blocks, _ = support_reach.shape
    n, rows, lanes = trans_east.shape
    width = n // layers
    f32 = jnp.float32
    anywhere = pl.BlockSpec(memory_space=pl.ANY)
    vmem = pl.BlockSpec(memory_space=pltpu.VMEM)
    params = pltpu.CompilerParams(vmem_limit_bytes=16 * 2**20)
    outside = tuple(
        pltpu.with_memory_space_constraint(x, pltpu.HBM)
        for x in (trans_east, trans_north, trans_up, storage)
    )
    reach = jnp.transpose(support_reach, (0, 2, 1))
    reach = pltpu.with_memory_space_constraint(reach, pltpu.HBM)
    bases = layers * blocks
    out_shape = jax.ShapeDtypeStruct((bases * 3 * width, rows, lanes), f32)
    inner = [
        pltpu.VMEM((2 * (width - 2), rows, lanes), f32),
        pltpu.VMEM((layers, blocks, width + 4, rows, lanes), f32),
    ]
    tiles = 1 + 7 * rows // TAIL
    msg_a, msg_b, masks, faces, started = pl.pallas_call(
        functools.partial(pack_kernel, n, width, axis),
        out_shape=(
            pltpu.VMEM((tiles, TAIL, lanes), f32),
            pltpu.VMEM((tiles + 1, TAIL, lanes), f32),
            pltpu.VMEM((layers, TAIL, lanes), f32),
            pltpu.VMEM((4, n, rows, lanes), f32),
            out_shape,
        ),
        in_specs=[anywhere] * 5,
        out_specs=(vmem,) * 4 + (anywhere,),
        scratch_shapes=[
            pltpu.VMEM((layers, 4, blocks), jnp.int32),
            *inner,
            pltpu.SemaphoreType.DMA((6,)),
            pltpu.SemaphoreType.DMA,
        ],
        compiler_params=params,
        name="pack",
    )(*outside, reach)
    faces, msg_a = pl.pallas_call(
        functools.partial(stage_kernel, axis),
        out_shape=(pltpu.VMEM(faces.shape, f32), pltpu.VMEM(msg_a.shape, f32)),
        in_specs=[anywhere] * 6,
        out_specs=(anywhere,) * 2,
        scratch_shapes=[pltpu.SemaphoreType.DMA],
        input_output_aliases={4: 0, 5: 1},
        compiler_params=params,
        name="stage",
    )(*outside, faces, msg_a)
    got_a = lax.ppermute(msg_a, axis, swaps(range(0, count - 1, 2)))
    got_b = lax.ppermute(msg_b, axis, swaps(range(1, count - 1, 2)))

    bulk = pl.pallas_call(
        functools.partial(bulk_kernel, width, axis),
        out_shape=out_shape,
        in_specs=[vmem] * 2 + [anywhere],
        out_specs=anywhere,
        scratch_shapes=inner + [pltpu.SemaphoreType.DMA],
        input_output_aliases={2: 0},
        compiler_params=params,
        cost_estimate=pl.CostEstimate(flops=10**7, bytes_accessed=7 * 10**6, transcendentals=0),
        name="bulk",
    )(faces, masks, started)
    side = [pltpu.VMEM((blocks, 4, rows, lanes), f32)] * 2
    out = pl.pallas_call(
        functools.partial(edge_kernel, width, blocks, axis, count),
        out_shape=out_shape,
        in_specs=[vmem] * 4 + [anywhere],
        out_specs=anywhere,
        scratch_shapes=side + [pltpu.SemaphoreType.DMA],
        input_output_aliases={4: 0},
        compiler_params=params,
        cost_estimate=pl.CostEstimate(flops=10**6, bytes_accessed=10**6, transcendentals=0),
        name="edges",
    )(faces, masks, got_a, got_b, bulk)
    return out.reshape(layers, blocks, 3 * width, rows, lanes)


def solution(mesh):
    spread = P(("groups", "blk"))
    return jax.shard_map(
        functools.partial(on_device, axis="blk", count=mesh.shape["blk"]),
        mesh=mesh,
        in_specs=(spread,) * 5,
        out_specs=spread,
        check_vma=False,
    )
```

```python
import functools

import jax
import jax.numpy as jnp
from jax import lax
from jax.experimental import pallas as pl
from jax.experimental.pallas import tpu as pltpu
from jax.sharding import PartitionSpec as P


TAIL = 8
EARLY = 15
ODD_EARLY = 4


class Lanes:
    def __init__(self, shape, width):
        tile = lax.broadcasted_iota(jnp.int32, (TAIL, shape[1]), 1)

        def rows(v):
            return jnp.concatenate([v] * (shape[0] // TAIL), axis=0)

        self.rows, self.lanes = shape
        self.width = width
        self.lane = rows(tile)
        self.local = rows(lax.rem(tile, width))
        self.first = self.local == 0
        self.last = self.local == width - 1
        self.odd = rows(lax.rem(tile // width, 2)) == 1
        self.row0 = lax.broadcasted_iota(jnp.int32, shape, 0) == 0
        self.lane0 = self.lane == 0

    def around(self, k):
        start = k * self.width - self.width // 2
        return (self.lane >= start) & (self.lane < start + 2 * self.width)

    def zm(self, v):
        return pltpu.roll(v, 1, 1)

    def zp(self, v):
        return pltpu.roll(v, self.lanes - 1, 1)

    def ym(self, v):
        return pltpu.roll(v, 1, 0)

    def yp(self, v):
        return pltpu.roll(v, self.rows - 1, 0)


def reciprocal(x):
    r = pl.reciprocal(x, approx=True)
    return r * (2.0 - x * r)


def within_y(ln, ty):
    ty = jnp.where(ln.row0, 0.0, ty)
    return ty, ln.yp(ty)


def within_z(ln, tz):
    tz = jnp.where(ln.lane0, 0.0, tz)
    return tz, ln.zp(tz)


def cross(ln, ty, tz, s):
    ty, typ = within_y(ln, ty)
    tz, tzp = within_z(ln, tz)
    return s * (1.0 / 3.0) + ((ty + typ) + (tz + tzp)), (ty, typ, tz, tzp)


class Plane:
    def __init__(self, ln, tx, txn, ty, tz, s, valid=None):
        self.ln = ln
        self.tx, self.txn = tx, txn
        e, (self.ty, self.typ, self.tz, self.tzp) = cross(ln, ty, tz, s)
        e = e + (tx + txn)
        if valid is not None:
            e = jnp.where(valid, e, 1.0)
        self.half = 0.5 * e + s * (1.0 / 3.0)
        self.spread(e)

    def spread(self, e):
        ln = self.ln
        self.all = 1.5 * e
        self.q = reciprocal(self.all)
        self.z1 = self.q * jnp.where(ln.first, self.tz, jnp.where(ln.last, self.tzp, 0.0))
        self.zm = ln.zm(self.z1)
        self.zp = ln.zp(self.z1)

    def toward(self, low):
        return self.tx if low else self.txn

    def inward(self, low):
        return self.txn if low else self.tx

    def edge(self, low):
        self.x1 = self.q * self.toward(low)
        self.o1 = 1.0 - self.z1 - self.x1

    def rim(self):
        return self.tz * self.zm + self.tzp * self.zp

    def along_y(self, v):
        return self.ty * self.ln.ym(v) + self.typ * self.ln.yp(v)


class Rim(Plane):
    def __init__(self, ln, e, tz):
        self.ln = ln
        self.tz = jnp.where(ln.lane0, 0.0, tz)
        self.tzp = ln.zp(self.tz)
        self.spread(e)


def plane_at(ln, faces, p):
    return Plane(ln, faces[0, p], faces[0, p + 1], faces[1, p], faces[2, p], faces[3, p])


def middle(p, below, above, mz):
    ln = p.ln
    vz = p.half * p.z1 + p.tx * below.z1 + p.txn * above.z1 + p.along_y(p.z1)
    vz = vz + p.tz * jnp.where(ln.first, 1.0 - p.zm, p.zm)
    vz = vz + p.tzp * jnp.where(ln.last, 1.0 - p.zp, p.zp)
    kept = vz * mz
    return p.all - vz, kept, p.all - (vz - kept)


def second(p, edge, inner, low, mz, mx):
    below, above = (edge, inner) if low else (inner, edge)
    ln = p.ln
    first_o = ln.zm(p.z1)
    vz = p.half * p.z1 + p.tx * below.z1 + p.txn * above.z1 + p.along_y(p.z1)
    vz = vz + p.tz * jnp.where(ln.first, 1.0 - first_o, first_o)
    vz = vz + p.tzp * jnp.where(ln.last, 1.0 - p.zp, p.zp)
    vx = p.toward(low) * edge.x1
    kept_z, kept_x = vz * mz, vx * mx
    total = p.all - (vz - kept_z) - (vx - kept_x)
    return p.all - vz - vx, kept_z, kept_x, total


def edge_own(p, inner_o1, inner_z1, outer_x1, low, mz):
    ln = p.ln
    om, op = ln.zm(p.o1), ln.zp(p.o1)
    vo = p.half * p.o1 + p.toward(low) * outer_x1 + p.inward(low) * inner_o1 + p.along_y(p.o1)
    vo = vo + p.tz * jnp.where(ln.first, p.zm, om) + p.tzp * jnp.where(ln.last, p.zp, op)
    vz = p.half * p.z1 + p.inward(low) * inner_z1 + p.along_y(p.z1)
    vz = vz + p.tz * jnp.where(ln.first, om, p.zm) + p.tzp * jnp.where(ln.last, op, p.zp)
    return vo, vz * mz


def edge_total(p, mz):
    rim = p.rim()
    return p.all - (rim - rim * mz)


def edge_spill(p, own, low):
    ln = p.ln
    xm, xp = ln.zm(p.x1), ln.zp(p.x1)
    face = p.toward(low)
    vx = p.half * p.x1 + face * own.o1 + p.along_y(p.x1)
    vx = vx + p.tz * jnp.where(ln.first, 0.0, xm) + p.tzp * jnp.where(ln.last, 0.0, xp)
    vd = face * own.z1 + p.tz * jnp.where(ln.first, xm, 0.0) + p.tzp * jnp.where(ln.last, xp, 0.0)
    return vx, vd


def store(ln, dst, plane, blocks, own, other, total):
    scale = reciprocal(total)
    own = own * scale
    other = jnp.zeros_like(own) if other is None else other * scale
    even, odd = jnp.where(ln.odd, other, own), jnp.where(ln.odd, own, other)
    for k in range(blocks):
        dst[k, plane] = jnp.where(ln.around(k), odd if k % 2 else even, 0.0)


def work_side(ln, low, valid, faces, masks, msg, put):
    n, rows, lanes = faces.shape[1:]
    layers = masks.shape[0]

    def own(i, j):
        return faces[i, jnp.where(low, j, n - 1 - j)]

    def got(i):
        tiles = rows // TAIL
        return msg[pl.ds(1 + tiles * i, tiles)].reshape(rows, lanes)

    f1, f2, f3 = (faces[0, jnp.where(low, j, n - j)] for j in (1, 2, 3))
    f0 = jnp.where(valid, jnp.where(low, faces[0, 0], got(6)), 0.0)
    g1 = got(0)
    a0 = Plane(ln, f0, f1, own(1, 0), own(2, 0), own(3, 0))
    a1 = Plane(ln, f1, f2, own(1, 1), own(2, 1), own(3, 1))
    a2 = Plane(ln, f2, f3, own(1, 2), own(2, 2), own(3, 2))
    b0 = Plane(ln, g1, f0, got(1), got(2), got(3), valid)
    b1 = Rim(ln, jnp.where(valid, got(4) + g1, 1.0), got(5))
    mine = masks[jnp.where(low, 0, layers - 1)]
    mz, my_reach = mine[0:1], jnp.where(low, mine[1:2], mine[2:3])
    theirs = msg[0]
    mo, their_reach = theirs[0:1], jnp.where(low, theirs[2:3], theirs[1:2])
    a0.edge(True)
    b0.edge(False)
    vx = g1 * b0.x1
    kept = vx * my_reach
    put(0, kept, None, edge_total(b1, mo) - (vx - kept))
    vx, vd = edge_spill(b0, a0, False)
    put(1, vx, vd, edge_total(b0, mo))
    vo, vz = edge_own(a0, 1.0 - a1.z1, a1.z1, b0.x1, True, mz)
    put(2, vo, vz, edge_total(a0, mz))
    vo, vz, _, total = second(a1, a0, a2, True, mz, their_reach)
    put(3, vo, vz, total)


def store_side(ln, buf, low, blocks):
    def put(i, own, other, total):
        store(ln, buf, jnp.where(low, i, 3 - i), blocks, own, other, total)

    return put


def send_one_side(buf, out, low, width, layers, sem, k):
    layer = jnp.where(low, 0, layers - 1)
    start = jnp.where(low, width - 2, 2 * width - 2)
    there = out.at[pl.ds((layer * buf.shape[0] + k) * 3 * width + start, 4)]
    return pltpu.make_async_copy(buf.at[k], there, sem)


def clear_run(zeros, out, b, bases, width, sem):
    depth = width - 2
    ends = isinstance(b, int) and b in (0, bases)
    count = depth if ends else 2 * depth
    start = 0 if ends and b == 0 else b * 3 * width - depth
    return pltpu.make_async_copy(zeros.at[pl.ds(0, count)], out.at[pl.ds(start, count)], sem)


def clear_runs(zeros, out, first, last, bases, width, sem):
    def body(b, _):
        clear_run(zeros, out, b, bases, width, sem).start()

    lax.fori_loop(first, last, body, None)


def wait_planes(out, count, sem):
    some = out.at[pl.ds(0, count)]
    pltpu.make_async_copy(some, some, sem).wait()


def first_early(me, bases):
    return jnp.where(me == 1, bases - EARLY, jnp.where(lax.rem(me, 2) == 1, bases - ODD_EARLY, bases))


def pack_kernel(
    n, width, axis, tx, ty, tz, s, reach, msg_a, msg_b, masks, faces, out,
    held_reach, zeros, buf, read_sems, sem,
):
    layers, _, blocks = held_reach.shape
    rows, lanes = faces.shape[2:]
    fetch = pltpu.make_async_copy(reach, held_reach, read_sems.at[4])
    fetch.start()
    copies = [
        pltpu.make_async_copy(a, faces.at[i], read_sems.at[i]) for i, a in enumerate((tx, ty, tz, s))
    ]
    for i in (1, 2, 0, 3):
        copies[i].start()
    bases = layers * blocks
    me = lax.axis_index(axis)
    late = first_early(me, bases)

    @pl.when(late < bases)
    def _():
        zeros[...] = jnp.zeros(zeros.shape, jnp.float32)
        clear_runs(zeros, out, late, bases, bases, width, sem)

    masks[...] = jnp.zeros(masks.shape, jnp.float32)
    lane = lax.broadcasted_iota(jnp.int32, (4, lanes), 1)
    block = lane // width
    local = lane - block * width
    fetch.wait()
    for layer in range(layers):
        r = jnp.zeros((4, lanes), jnp.int32)
        for k in range(blocks):
            r = jnp.where(block == k, held_reach[layer, :, k : k + 1], r)
        low = pltpu.roll(r, width, 1)
        high = pltpu.roll(r, lanes - width, 1)
        near = jnp.where(
            local[0:1] < width // 2,
            jnp.where(low[3:4] >= local[0:1] + 1, 1.0, 0.0),
            jnp.where(high[2:3] >= width - local[0:1], 1.0, 0.0),
        )
        masks[layer, 0:1] = near
        masks[layer, 1:3] = jnp.where(r[0:2] >= 2, 1.0, 0.0)
    even = lax.rem(me, 2) == 0

    def put(tile, up, down):
        up, down = (v.reshape(-1, TAIL, lanes) for v in (up, down))
        where = pl.ds(tile, up.shape[0])
        msg_a[where] = jnp.where(even, up, down)
        msg_b[where] = jnp.where(even, down, up)

    put(0, masks[layers - 1], masks[0])
    ln = Lanes(faces.shape[2:], width)
    behind = {}

    def plane(slot, up, down):
        put(1 + slot * (rows // TAIL), up, down)

    for i, across in ((1, lambda v: within_y(ln, v)), (2, lambda v: within_z(ln, v))):
        copies[i].wait()
        plane(i, faces[i, n - 1], faces[i, 0])
        for p in (n - 2, 1):
            v, v_next = across(faces[i, p])
            behind[p] = behind.get(p, 0.0) + (v + v_next)
    plane(5, faces[2, n - 2], faces[2, 1])
    copies[0].wait()
    plane(0, faces[0, n - 1], faces[0, 1])
    plane(6, faces[0, n - 1], faces[0, 0])
    behind = {p: behind[p] + faces[0, q] for p, q in ((n - 2, n - 2), (1, 2))}
    copies[3].wait()
    plane(3, faces[3, n - 1], faces[3, 0])
    plane(4, *(behind[p] + faces[3, p] * (1.0 / 3.0) for p in (n - 2, 1)))

    @pl.when(me == 1)
    def _():
        wait_planes(out, (EARLY - ODD_EARLY) * 2 * (width - 2), sem)

    @pl.when(late < bases)
    def _():
        wait_planes(out, ODD_EARLY * 2 * (width - 2), sem)

    @pl.when(me == 0)
    def _():
        inner_planes(width, bases, faces, masks, out, zeros, buf, sem)
        wait_planes(out, inner_count(layers, blocks, width), sem)


def inner_count(layers, blocks, width):
    return layers * blocks * 3 * width - 8 * blocks


def inner_planes(width, last_run, faces, masks, out, zeros, buf, sem):
    layers, blocks = buf.shape[:2]
    rows, lanes = faces.shape[2:]
    box, depth = 3 * width, width - 2
    bases = layers * blocks
    zeros[...] = jnp.zeros(zeros.shape, jnp.float32)

    for b in (0, bases):
        clear_run(zeros, out, b, bases, width, sem).start()
    clear_runs(zeros, out, 1, last_run, bases, width, sem)
    ln = Lanes((rows, lanes), width)
    plane = functools.partial(plane_at, ln, faces)

    def send(k, layer):
        start = 4 if layer == 0 else 0
        count = width + 4 - start - (4 if layer == layers - 1 else 0)
        return pltpu.make_async_copy(
            buf.at[layer, k, pl.ds(start, count)],
            out.at[pl.ds((layer * blocks + k) * box + depth + start, count)],
            sem,
        )

    def between(layer):
        base = layer * width
        ma, mb = masks[layer - 1, 0:1], masks[layer, 0:1]
        to_above, to_below = masks[layer - 1, 2:3], masks[layer, 1:2]
        a3, a2, a1 = (plane(base - i) for i in (3, 2, 1))
        b0, b1, b2 = (plane(base + i) for i in (0, 1, 2))
        a1.edge(False)
        b0.edge(True)
        low = functools.partial(store, ln, buf.at[layer - 1])
        high = functools.partial(store, ln, buf.at[layer])
        vo, vz, vx, total = second(a2, a1, a3, False, ma, to_below)
        low(width, blocks, vo, vz, total)
        high(0, blocks, vx, None, total)
        vo, vz = edge_own(a1, 1.0 - a2.z1, a2.z1, b0.x1, False, ma)
        vx, vd = edge_spill(a1, b0, False)
        total = edge_total(a1, ma)
        low(width + 1, blocks, vo, vz, total)
        high(1, blocks, vx, vd, total)
        vo, vz = edge_own(b0, 1.0 - b1.z1, b1.z1, a1.x1, True, mb)
        vx, vd = edge_spill(b0, a1, True)
        total = edge_total(b0, mb)
        high(2, blocks, vo, vz, total)
        low(width + 2, blocks, vx, vd, total)
        vo, vz, vx, total = second(b1, b0, b2, True, mb, to_above)
        high(3, blocks, vo, vz, total)
        low(width + 3, blocks, vx, None, total)

    for layer in range(layers):
        planes = [plane(layer * width + j) for j in range(1, width - 1)]
        mz = masks[layer, 0:1]
        for j in range(2, width - 2):
            vo, vz, total = middle(planes[j - 1], planes[j - 2], planes[j], mz)
            store(ln, buf.at[layer], j + 2, blocks, vo, vz, total)
        if layer < layers - 1:
            between(layer + 1)

        @pl.loop(0, blocks)
        def _(k):
            send(k, layer).start()


def bulk_kernel(width, axis, faces, masks, held, out, zeros, buf, sem):
    del held
    me = lax.axis_index(axis)
    layers, blocks = buf.shape[:2]
    bases = layers * blocks
    run = 2 * (width - 2)

    @pl.when(me != 0)
    def _():
        last_run = first_early(me, bases)
        inner_planes(width, last_run, faces, masks, out, zeros, buf, sem)
        wait_planes(out, inner_count(layers, blocks, width) - EARLY * run, sem)

    @pl.when(me > 1)
    def _():
        wait_planes(out, (EARLY - ODD_EARLY) * run, sem)

    @pl.when((me > 1) & (lax.rem(me, 2) == 0))
    def _():
        wait_planes(out, ODD_EARLY * run, sem)


def inside_kernel(blocks, axis, count, faces, masks, msg, held, side):
    del held
    me = lax.axis_index(axis)
    low = lax.rem(me, 2) == 1
    ln = Lanes(faces.shape[2:], masks.shape[2] // blocks)
    work_side(ln, low, low | (me < count - 1), faces, masks, msg, store_side(ln, side, low, blocks))


def edge_kernel(width, blocks, axis, count, faces, masks, msg, inside, held, out, side, sem):
    del held
    layers = masks.shape[0]
    me = lax.axis_index(axis)
    low = lax.rem(me, 2) == 0
    for k in range(blocks):
        send_one_side(inside, out, jnp.logical_not(low), width, layers, sem, k).start()
    ln = Lanes(faces.shape[2:], width)
    valid = jnp.where(low, me > 0, me < count - 1)
    work_side(ln, low, valid, faces, masks, msg, store_side(ln, side, low, blocks))
    for k in range(blocks):
        send_one_side(side, out, low, width, layers, sem, k).start()
    wait_planes(out, 8 * blocks, sem)


def swaps(firsts):
    return [pair for i in firsts for pair in ((i, i + 1), (i + 1, i))]


def on_device(trans_east, trans_north, trans_up, storage, support_reach, *, axis, count):
    layers, blocks, _ = support_reach.shape
    n, rows, lanes = trans_east.shape
    width = n // layers
    f32 = jnp.float32
    anywhere = pl.BlockSpec(memory_space=pl.ANY)
    vmem = pl.BlockSpec(memory_space=pltpu.VMEM)
    params = pltpu.CompilerParams(vmem_limit_bytes=16 * 2**20)
    outside = tuple(
        pltpu.with_memory_space_constraint(x, pltpu.HBM)
        for x in (trans_east, trans_north, trans_up, storage)
    )
    reach = jnp.transpose(support_reach, (0, 2, 1))
    reach = pltpu.with_memory_space_constraint(reach, pltpu.HBM)
    bases = layers * blocks
    out_shape = jax.ShapeDtypeStruct((bases * 3 * width, rows, lanes), f32)
    inner = [
        pltpu.VMEM((2 * (width - 2), rows, lanes), f32),
        pltpu.VMEM((layers, blocks, width + 4, rows, lanes), f32),
    ]
    tiles = 1 + 7 * rows // TAIL
    msg_a, msg_b, masks, faces, started = pl.pallas_call(
        functools.partial(pack_kernel, n, width, axis),
        out_shape=(
            pltpu.VMEM((tiles, TAIL, lanes), f32),
            pltpu.VMEM((tiles + 1, TAIL, lanes), f32),
            pltpu.VMEM((layers, TAIL, lanes), f32),
            pltpu.VMEM((4, n, rows, lanes), f32),
            out_shape,
        ),
        in_specs=[anywhere] * 5,
        out_specs=(vmem,) * 4 + (anywhere,),
        scratch_shapes=[
            pltpu.VMEM((layers, 4, blocks), jnp.int32),
            *inner,
            pltpu.SemaphoreType.DMA((5,)),
            pltpu.SemaphoreType.DMA,
        ],
        compiler_params=params,
        name="pack",
    )(*outside, reach)
    got_a = lax.ppermute(msg_a, axis, swaps(range(0, count - 1, 2)))
    got_b = lax.ppermute(msg_b, axis, swaps(range(1, count - 1, 2)))

    bulk = pl.pallas_call(
        functools.partial(bulk_kernel, width, axis),
        out_shape=out_shape,
        in_specs=[vmem] * 2 + [anywhere],
        out_specs=anywhere,
        scratch_shapes=inner + [pltpu.SemaphoreType.DMA],
        input_output_aliases={2: 0},
        compiler_params=params,
        cost_estimate=pl.CostEstimate(flops=10**7, bytes_accessed=7 * 10**6, transcendentals=0),
        name="bulk",
    )(faces, masks, started)
    side = pltpu.VMEM((blocks, 4, rows, lanes), f32)
    inside = pl.pallas_call(
        functools.partial(inside_kernel, blocks, axis, count),
        out_shape=side,
        in_specs=[vmem] * 3 + [anywhere],
        out_specs=vmem,
        compiler_params=params,
        cost_estimate=pl.CostEstimate(flops=10**6, bytes_accessed=10**6, transcendentals=0),
        name="inside",
    )(faces, masks, got_a, pltpu.with_memory_space_constraint(bulk, pltpu.HBM))
    out = pl.pallas_call(
        functools.partial(edge_kernel, width, blocks, axis, count),
        out_shape=out_shape,
        in_specs=[vmem] * 4 + [anywhere],
        out_specs=anywhere,
        scratch_shapes=[side, pltpu.SemaphoreType.DMA],
        input_output_aliases={4: 0},
        compiler_params=params,
        cost_estimate=pl.CostEstimate(flops=10**6, bytes_accessed=10**6, transcendentals=0),
        name="edges",
    )(faces, masks, got_b, inside, bulk)
    return out.reshape(layers, blocks, 3 * width, rows, lanes)


def solution(mesh):
    spread = P(("groups", "blk"))
    return jax.shard_map(
        functools.partial(on_device, axis="blk", count=mesh.shape["blk"]),
        mesh=mesh,
        in_specs=(spread,) * 5,
        out_specs=spread,
        check_vma=False,
    )
```

```python
import functools

import jax
import jax.numpy as jnp
from jax import lax
from jax.experimental import pallas as pl
from jax.experimental.pallas import tpu as pltpu
from jax.sharding import PartitionSpec as P


TAIL = 8
EARLY = 12


class Lanes:
    def __init__(self, shape, width):
        tile = lax.broadcasted_iota(jnp.int32, (TAIL, shape[1]), 1)

        def rows(v):
            return jnp.concatenate([v] * (shape[0] // TAIL), axis=0)

        self.rows, self.lanes = shape
        self.width = width
        self.lane = rows(tile)
        self.local = rows(lax.rem(tile, width))
        self.first = self.local == 0
        self.last = self.local == width - 1
        self.odd = rows(lax.rem(tile // width, 2)) == 1
        self.row0 = lax.broadcasted_iota(jnp.int32, shape, 0) == 0
        self.lane0 = self.lane == 0

    def around(self, k):
        start = k * self.width - self.width // 2
        return (self.lane >= start) & (self.lane < start + 2 * self.width)

    def zm(self, v):
        return pltpu.roll(v, 1, 1)

    def zp(self, v):
        return pltpu.roll(v, self.lanes - 1, 1)

    def ym(self, v):
        return pltpu.roll(v, 1, 0)

    def yp(self, v):
        return pltpu.roll(v, self.rows - 1, 0)


def reciprocal(x):
    r = pl.reciprocal(x, approx=True)
    return r * (2.0 - x * r)


def within_y(ln, ty):
    ty = jnp.where(ln.row0, 0.0, ty)
    return ty, ln.yp(ty)


def within_z(ln, tz):
    tz = jnp.where(ln.lane0, 0.0, tz)
    return tz, ln.zp(tz)


def cross(ln, ty, tz, s):
    ty, typ = within_y(ln, ty)
    tz, tzp = within_z(ln, tz)
    return s * (1.0 / 3.0) + ((ty + typ) + (tz + tzp)), (ty, typ, tz, tzp)


class Plane:
    def __init__(self, ln, tx, txn, ty, tz, s, valid=None):
        self.ln = ln
        self.tx, self.txn = tx, txn
        e, (self.ty, self.typ, self.tz, self.tzp) = cross(ln, ty, tz, s)
        e = e + (tx + txn)
        if valid is not None:
            e = jnp.where(valid, e, 1.0)
        self.half = 0.5 * e + s * (1.0 / 3.0)
        self.spread(e)

    def spread(self, e):
        ln = self.ln
        self.all = 1.5 * e
        self.q = reciprocal(self.all)
        self.z1 = self.q * jnp.where(ln.first, self.tz, jnp.where(ln.last, self.tzp, 0.0))
        self.zm = ln.zm(self.z1)
        self.zp = ln.zp(self.z1)

    def toward(self, low):
        return self.tx if low else self.txn

    def inward(self, low):
        return self.txn if low else self.tx

    def edge(self, low):
        self.x1 = self.q * self.toward(low)
        self.o1 = 1.0 - self.z1 - self.x1

    def rim(self):
        return self.tz * self.zm + self.tzp * self.zp

    def along_y(self, v):
        return self.ty * self.ln.ym(v) + self.typ * self.ln.yp(v)


class Rim(Plane):
    def __init__(self, ln, e, tz):
        self.ln = ln
        self.tz = jnp.where(ln.lane0, 0.0, tz)
        self.tzp = ln.zp(self.tz)
        self.spread(e)


def plane_at(ln, faces, p):
    return Plane(ln, faces[0, p], faces[0, p + 1], faces[1, p], faces[2, p], faces[3, p])


def middle(p, below, above, mz):
    ln = p.ln
    vz = p.half * p.z1 + p.tx * below.z1 + p.txn * above.z1 + p.along_y(p.z1)
    vz = vz + p.tz * jnp.where(ln.first, 1.0 - p.zm, p.zm)
    vz = vz + p.tzp * jnp.where(ln.last, 1.0 - p.zp, p.zp)
    kept = vz * mz
    return p.all - vz, kept, p.all - (vz - kept)


def second(p, edge, inner, low, mz, mx):
    below, above = (edge, inner) if low else (inner, edge)
    ln = p.ln
    first_o = ln.zm(p.z1)
    vz = p.half * p.z1 + p.tx * below.z1 + p.txn * above.z1 + p.along_y(p.z1)
    vz = vz + p.tz * jnp.where(ln.first, 1.0 - first_o, first_o)
    vz = vz + p.tzp * jnp.where(ln.last, 1.0 - p.zp, p.zp)
    vx = p.toward(low) * edge.x1
    kept_z, kept_x = vz * mz, vx * mx
    total = p.all - (vz - kept_z) - (vx - kept_x)
    return p.all - vz - vx, kept_z, kept_x, total


def edge_own(p, inner_o1, inner_z1, outer_x1, low, mz):
    ln = p.ln
    om, op = ln.zm(p.o1), ln.zp(p.o1)
    vo = p.half * p.o1 + p.toward(low) * outer_x1 + p.inward(low) * inner_o1 + p.along_y(p.o1)
    vo = vo + p.tz * jnp.where(ln.first, p.zm, om) + p.tzp * jnp.where(ln.last, p.zp, op)
    vz = p.half * p.z1 + p.inward(low) * inner_z1 + p.along_y(p.z1)
    vz = vz + p.tz * jnp.where(ln.first, om, p.zm) + p.tzp * jnp.where(ln.last, op, p.zp)
    return vo, vz * mz


def edge_total(p, mz):
    rim = p.rim()
    return p.all - (rim - rim * mz)


def edge_spill(p, own, low):
    ln = p.ln
    xm, xp = ln.zm(p.x1), ln.zp(p.x1)
    face = p.toward(low)
    vx = p.half * p.x1 + face * own.o1 + p.along_y(p.x1)
    vx = vx + p.tz * jnp.where(ln.first, 0.0, xm) + p.tzp * jnp.where(ln.last, 0.0, xp)
    vd = face * own.z1 + p.tz * jnp.where(ln.first, xm, 0.0) + p.tzp * jnp.where(ln.last, xp, 0.0)
    return vx, vd


def store(ln, dst, plane, blocks, own, other, total):
    scale = reciprocal(total)
    own = own * scale
    other = jnp.zeros_like(own) if other is None else other * scale
    even, odd = jnp.where(ln.odd, other, own), jnp.where(ln.odd, own, other)
    for k in range(blocks):
        dst[k, plane] = jnp.where(ln.around(k), odd if k % 2 else even, 0.0)


def work_side(ln, low, valid, faces, masks, msg, put):
    n, rows, lanes = faces.shape[1:]
    layers = masks.shape[0]

    def own(i, j):
        return faces[i, jnp.where(low, j, n - 1 - j)]

    def got(i):
        tiles = rows // TAIL
        return msg[pl.ds(1 + tiles * i, tiles)].reshape(rows, lanes)

    f1, f2, f3 = (faces[0, jnp.where(low, j, n - j)] for j in (1, 2, 3))
    f0 = jnp.where(valid, jnp.where(low, faces[0, 0], got(6)), 0.0)
    g1 = got(0)
    a0 = Plane(ln, f0, f1, own(1, 0), own(2, 0), own(3, 0))
    a1 = Plane(ln, f1, f2, own(1, 1), own(2, 1), own(3, 1))
    a2 = Plane(ln, f2, f3, own(1, 2), own(2, 2), own(3, 2))
    b0 = Plane(ln, g1, f0, got(1), got(2), got(3), valid)
    b1 = Rim(ln, jnp.where(valid, got(4) + g1, 1.0), got(5))
    mine = masks[jnp.where(low, 0, layers - 1)]
    mz, my_reach = mine[0:1], jnp.where(low, mine[1:2], mine[2:3])
    theirs = msg[0]
    mo, their_reach = theirs[0:1], jnp.where(low, theirs[2:3], theirs[1:2])
    a0.edge(True)
    b0.edge(False)
    vx = g1 * b0.x1
    kept = vx * my_reach
    put(0, kept, None, edge_total(b1, mo) - (vx - kept))
    vx, vd = edge_spill(b0, a0, False)
    put(1, vx, vd, edge_total(b0, mo))
    vo, vz = edge_own(a0, 1.0 - a1.z1, a1.z1, b0.x1, True, mz)
    put(2, vo, vz, edge_total(a0, mz))
    vo, vz, _, total = second(a1, a0, a2, True, mz, their_reach)
    put(3, vo, vz, total)


def store_side(ln, buf, low, blocks):
    def put(i, own, other, total):
        store(ln, buf, jnp.where(low, i, 3 - i), blocks, own, other, total)

    return put


def send_one_side(buf, out, low, width, layers, sem, k):
    layer = jnp.where(low, 0, layers - 1)
    start = jnp.where(low, width - 2, 2 * width - 2)
    there = out.at[pl.ds((layer * buf.shape[0] + k) * 3 * width + start, 4)]
    return pltpu.make_async_copy(buf.at[k], there, sem)


def clear_run(zeros, out, b, bases, width, sem):
    depth = width - 2
    ends = isinstance(b, int) and b in (0, bases)
    count = depth if ends else 2 * depth
    start = 0 if ends and b == 0 else b * 3 * width - depth
    return pltpu.make_async_copy(zeros.at[pl.ds(0, count)], out.at[pl.ds(start, count)], sem)


def clear_runs(zeros, out, first, last, bases, width, sem):
    def body(b, _):
        clear_run(zeros, out, b, bases, width, sem).start()

    lax.fori_loop(first, last, body, None)


def wait_planes(out, count, sem):
    some = out.at[pl.ds(0, count)]
    pltpu.make_async_copy(some, some, sem).wait()


def first_early(me, bases):
    return jnp.where(me == 1, bases - EARLY, bases)


def pack_kernel(
    n, width, axis, tx, ty, tz, s, reach, msg_a, msg_b, masks, faces, out,
    held_reach, zeros, buf, read_sems, sem,
):
    layers, _, blocks = held_reach.shape
    rows, lanes = faces.shape[2:]
    fetch = pltpu.make_async_copy(reach, held_reach, read_sems.at[4])
    fetch.start()
    copies = [
        pltpu.make_async_copy(a, faces.at[i], read_sems.at[i]) for i, a in enumerate((tx, ty, tz, s))
    ]
    for i in (1, 2, 0, 3):
        copies[i].start()
    bases = layers * blocks
    me = lax.axis_index(axis)
    late = first_early(me, bases)

    @pl.when(me == 1)
    def _():
        zeros[...] = jnp.zeros(zeros.shape, jnp.float32)
        clear_runs(zeros, out, late, bases, bases, width, sem)

    masks[...] = jnp.zeros(masks.shape, jnp.float32)
    lane = lax.broadcasted_iota(jnp.int32, (4, lanes), 1)
    block = lane // width
    local = lane - block * width
    fetch.wait()
    for layer in range(layers):
        r = jnp.zeros((4, lanes), jnp.int32)
        for k in range(blocks):
            r = jnp.where(block == k, held_reach[layer, :, k : k + 1], r)
        low = pltpu.roll(r, width, 1)
        high = pltpu.roll(r, lanes - width, 1)
        near = jnp.where(
            local[0:1] < width // 2,
            jnp.where(low[3:4] >= local[0:1] + 1, 1.0, 0.0),
            jnp.where(high[2:3] >= width - local[0:1], 1.0, 0.0),
        )
        masks[layer, 0:1] = near
        masks[layer, 1:3] = jnp.where(r[0:2] >= 2, 1.0, 0.0)
    even = lax.rem(me, 2) == 0

    def put(tile, up, down):
        up, down = (v.reshape(-1, TAIL, lanes) for v in (up, down))
        where = pl.ds(tile, up.shape[0])
        msg_a[where] = jnp.where(even, up, down)
        msg_b[where] = jnp.where(even, down, up)

    put(0, masks[layers - 1], masks[0])
    ln = Lanes(faces.shape[2:], width)
    behind = {}

    def plane(slot, up, down):
        put(1 + slot * (rows // TAIL), up, down)

    for i, across in ((1, lambda v: within_y(ln, v)), (2, lambda v: within_z(ln, v))):
        copies[i].wait()
        plane(i, faces[i, n - 1], faces[i, 0])
        for p in (n - 2, 1):
            v, v_next = across(faces[i, p])
            behind[p] = behind.get(p, 0.0) + (v + v_next)
    plane(5, faces[2, n - 2], faces[2, 1])
    copies[0].wait()
    plane(0, faces[0, n - 1], faces[0, 1])
    plane(6, faces[0, n - 1], faces[0, 0])
    behind = {p: behind[p] + faces[0, q] for p, q in ((n - 2, n - 2), (1, 2))}
    copies[3].wait()
    plane(3, faces[3, n - 1], faces[3, 0])
    plane(4, *(behind[p] + faces[3, p] * (1.0 / 3.0) for p in (n - 2, 1)))

    @pl.when(me == 1)
    def _():
        wait_planes(out, EARLY * 2 * (width - 2), sem)

    @pl.when(me == 0)
    def _():
        inner_planes(width, bases, faces, masks, out, zeros, buf, sem)
        wait_planes(out, inner_count(layers, blocks, width), sem)


def inner_count(layers, blocks, width):
    return layers * blocks * 3 * width - 8 * blocks


def inner_planes(width, last_run, faces, masks, out, zeros, buf, sem):
    layers, blocks = buf.shape[:2]
    rows, lanes = faces.shape[2:]
    box, depth = 3 * width, width - 2
    bases = layers * blocks
    zeros[...] = jnp.zeros(zeros.shape, jnp.float32)

    for b in (0, bases):
        clear_run(zeros, out, b, bases, width, sem).start()
    clear_runs(zeros, out, 1, last_run, bases, width, sem)
    ln = Lanes((rows, lanes), width)
    plane = functools.partial(plane_at, ln, faces)

    def send(k, layer):
        start = 4 if layer == 0 else 0
        count = width + 4 - start - (4 if layer == layers - 1 else 0)
        return pltpu.make_async_copy(
            buf.at[layer, k, pl.ds(start, count)],
            out.at[pl.ds((layer * blocks + k) * box + depth + start, count)],
            sem,
        )

    def between(layer):
        base = layer * width
        ma, mb = masks[layer - 1, 0:1], masks[layer, 0:1]
        to_above, to_below = masks[layer - 1, 2:3], masks[layer, 1:2]
        a3, a2, a1 = (plane(base - i) for i in (3, 2, 1))
        b0, b1, b2 = (plane(base + i) for i in (0, 1, 2))
        a1.edge(False)
        b0.edge(True)
        low = functools.partial(store, ln, buf.at[layer - 1])
        high = functools.partial(store, ln, buf.at[layer])
        vo, vz, vx, total = second(a2, a1, a3, False, ma, to_below)
        low(width, blocks, vo, vz, total)
        high(0, blocks, vx, None, total)
        vo, vz = edge_own(a1, 1.0 - a2.z1, a2.z1, b0.x1, False, ma)
        vx, vd = edge_spill(a1, b0, False)
        total = edge_total(a1, ma)
        low(width + 1, blocks, vo, vz, total)
        high(1, blocks, vx, vd, total)
        vo, vz = edge_own(b0, 1.0 - b1.z1, b1.z1, a1.x1, True, mb)
        vx, vd = edge_spill(b0, a1, True)
        total = edge_total(b0, mb)
        high(2, blocks, vo, vz, total)
        low(width + 2, blocks, vx, vd, total)
        vo, vz, vx, total = second(b1, b0, b2, True, mb, to_above)
        high(3, blocks, vo, vz, total)
        low(width + 3, blocks, vx, None, total)

    for layer in range(layers):
        planes = [plane(layer * width + j) for j in range(1, width - 1)]
        mz = masks[layer, 0:1]
        for j in range(2, width - 2):
            vo, vz, total = middle(planes[j - 1], planes[j - 2], planes[j], mz)
            store(ln, buf.at[layer], j + 2, blocks, vo, vz, total)
        if layer < layers - 1:
            between(layer + 1)

        @pl.loop(0, blocks)
        def _(k):
            send(k, layer).start()


def bulk_kernel(width, axis, faces, masks, held, out, zeros, buf, sem):
    del held
    me = lax.axis_index(axis)
    layers, blocks = buf.shape[:2]
    bases = layers * blocks
    run = 2 * (width - 2)

    @pl.when(me != 0)
    def _():
        last_run = first_early(me, bases)
        inner_planes(width, last_run, faces, masks, out, zeros, buf, sem)
        wait_planes(out, inner_count(layers, blocks, width) - EARLY * run, sem)

    @pl.when(me > 1)
    def _():
        wait_planes(out, EARLY * run, sem)


def inside_kernel(blocks, axis, count, faces, masks, msg, held, side):
    del held
    me = lax.axis_index(axis)
    low = lax.rem(me, 2) == 1
    ln = Lanes(faces.shape[2:], masks.shape[2] // blocks)
    work_side(ln, low, low | (me < count - 1), faces, masks, msg, store_side(ln, side, low, blocks))


def edge_kernel(width, blocks, axis, count, faces, masks, msg, inside, held, out, side, sem):
    del held
    layers = masks.shape[0]
    me = lax.axis_index(axis)
    low = lax.rem(me, 2) == 0
    for k in range(blocks):
        send_one_side(inside, out, jnp.logical_not(low), width, layers, sem, k).start()
    ln = Lanes(faces.shape[2:], width)
    valid = jnp.where(low, me > 0, me < count - 1)
    work_side(ln, low, valid, faces, masks, msg, store_side(ln, side, low, blocks))
    for k in range(blocks):
        send_one_side(side, out, low, width, layers, sem, k).start()
    wait_planes(out, 8 * blocks, sem)


def swaps(firsts):
    return [pair for i in firsts for pair in ((i, i + 1), (i + 1, i))]


def on_device(trans_east, trans_north, trans_up, storage, support_reach, *, axis, count):
    layers, blocks, _ = support_reach.shape
    n, rows, lanes = trans_east.shape
    width = n // layers
    f32 = jnp.float32
    anywhere = pl.BlockSpec(memory_space=pl.ANY)
    vmem = pl.BlockSpec(memory_space=pltpu.VMEM)
    params = pltpu.CompilerParams(vmem_limit_bytes=16 * 2**20)
    outside = tuple(
        pltpu.with_memory_space_constraint(x, pltpu.HBM)
        for x in (trans_east, trans_north, trans_up, storage)
    )
    reach = jnp.transpose(support_reach, (0, 2, 1))
    reach = pltpu.with_memory_space_constraint(reach, pltpu.HBM)
    bases = layers * blocks
    out_shape = jax.ShapeDtypeStruct((bases * 3 * width, rows, lanes), f32)
    inner = [
        pltpu.VMEM((2 * (width - 2), rows, lanes), f32),
        pltpu.VMEM((layers, blocks, width + 4, rows, lanes), f32),
    ]
    tiles = 1 + 7 * rows // TAIL
    msg_a, msg_b, masks, faces, started = pl.pallas_call(
        functools.partial(pack_kernel, n, width, axis),
        out_shape=(
            pltpu.VMEM((tiles, TAIL, lanes), f32),
            pltpu.VMEM((tiles + 1, TAIL, lanes), f32),
            pltpu.VMEM((layers, TAIL, lanes), f32),
            pltpu.VMEM((4, n, rows, lanes), f32),
            out_shape,
        ),
        in_specs=[anywhere] * 5,
        out_specs=(vmem,) * 4 + (anywhere,),
        scratch_shapes=[
            pltpu.VMEM((layers, 4, blocks), jnp.int32),
            *inner,
            pltpu.SemaphoreType.DMA((5,)),
            pltpu.SemaphoreType.DMA,
        ],
        compiler_params=params,
        name="pack",
    )(*outside, reach)
    got_a = lax.ppermute(msg_a, axis, swaps(range(0, count - 1, 2)))
    got_b = lax.ppermute(msg_b, axis, swaps(range(1, count - 1, 2)))

    bulk = pl.pallas_call(
        functools.partial(bulk_kernel, width, axis),
        out_shape=out_shape,
        in_specs=[vmem] * 2 + [anywhere],
        out_specs=anywhere,
        scratch_shapes=inner + [pltpu.SemaphoreType.DMA],
        input_output_aliases={2: 0},
        compiler_params=params,
        cost_estimate=pl.CostEstimate(flops=10**7, bytes_accessed=7 * 10**6, transcendentals=0),
        name="bulk",
    )(faces, masks, started)
    side = pltpu.VMEM((blocks, 4, rows, lanes), f32)
    inside = pl.pallas_call(
        functools.partial(inside_kernel, blocks, axis, count),
        out_shape=side,
        in_specs=[vmem] * 3 + [anywhere],
        out_specs=vmem,
        compiler_params=params,
        cost_estimate=pl.CostEstimate(flops=10**6, bytes_accessed=10**6, transcendentals=0),
        name="inside",
    )(faces, masks, got_a, pltpu.with_memory_space_constraint(bulk, pltpu.HBM))
    out = pl.pallas_call(
        functools.partial(edge_kernel, width, blocks, axis, count),
        out_shape=out_shape,
        in_specs=[vmem] * 4 + [anywhere],
        out_specs=anywhere,
        scratch_shapes=[side, pltpu.SemaphoreType.DMA],
        input_output_aliases={4: 0},
        compiler_params=params,
        cost_estimate=pl.CostEstimate(flops=10**6, bytes_accessed=10**6, transcendentals=0),
        name="edges",
    )(faces, masks, got_b, inside, bulk)
    return out.reshape(layers, blocks, 3 * width, rows, lanes)


def solution(mesh):
    spread = P(("groups", "blk"))
    return jax.shard_map(
        functools.partial(on_device, axis="blk", count=mesh.shape["blk"]),
        mesh=mesh,
        in_specs=(spread,) * 5,
        out_specs=spread,
        check_vma=False,
    )
```

```python
import functools

import jax
import jax.numpy as jnp
from jax import lax
from jax.experimental import pallas as pl
from jax.experimental.pallas import tpu as pltpu
from jax.sharding import PartitionSpec as P


TAIL = 8
EARLY = 12


class Lanes:
    def __init__(self, shape, width):
        tile = lax.broadcasted_iota(jnp.int32, (TAIL, shape[1]), 1)

        def rows(v):
            return jnp.concatenate([v] * (shape[0] // TAIL), axis=0)

        self.rows, self.lanes = shape
        self.width = width
        self.lane = rows(tile)
        self.local = rows(lax.rem(tile, width))
        self.first = self.local == 0
        self.last = self.local == width - 1
        self.odd = rows(lax.rem(tile // width, 2)) == 1
        self.row0 = lax.broadcasted_iota(jnp.int32, shape, 0) == 0
        self.lane0 = self.lane == 0

    def around(self, k):
        start = k * self.width - self.width // 2
        return (self.lane >= start) & (self.lane < start + 2 * self.width)

    def zm(self, v):
        return pltpu.roll(v, 1, 1)

    def zp(self, v):
        return pltpu.roll(v, self.lanes - 1, 1)

    def ym(self, v):
        return pltpu.roll(v, 1, 0)

    def yp(self, v):
        return pltpu.roll(v, self.rows - 1, 0)


def reciprocal(x):
    r = pl.reciprocal(x, approx=True)
    return r * (2.0 - x * r)


def within_y(ln, ty):
    ty = jnp.where(ln.row0, 0.0, ty)
    return ty, ln.yp(ty)


def within_z(ln, tz):
    tz = jnp.where(ln.lane0, 0.0, tz)
    return tz, ln.zp(tz)


def cross(ln, ty, tz, s):
    ty, typ = within_y(ln, ty)
    tz, tzp = within_z(ln, tz)
    return s * (1.0 / 3.0) + ((ty + typ) + (tz + tzp)), (ty, typ, tz, tzp)


class Plane:
    def __init__(self, ln, tx, txn, ty, tz, s, valid=None):
        self.ln = ln
        self.tx, self.txn = tx, txn
        e, (self.ty, self.typ, self.tz, self.tzp) = cross(ln, ty, tz, s)
        e = e + (tx + txn)
        if valid is not None:
            e = jnp.where(valid, e, 1.0)
        self.half = 0.5 * e + s * (1.0 / 3.0)
        self.spread(e)

    def spread(self, e):
        ln = self.ln
        self.all = 1.5 * e
        self.q = reciprocal(self.all)
        self.z1 = self.q * jnp.where(ln.first, self.tz, jnp.where(ln.last, self.tzp, 0.0))
        self.zm = ln.zm(self.z1)
        self.zp = ln.zp(self.z1)

    def toward(self, low):
        return self.tx if low else self.txn

    def inward(self, low):
        return self.txn if low else self.tx

    def edge(self, low):
        self.x1 = self.q * self.toward(low)
        self.o1 = 1.0 - self.z1 - self.x1

    def rim(self):
        return self.tz * self.zm + self.tzp * self.zp

    def along_y(self, v):
        return self.ty * self.ln.ym(v) + self.typ * self.ln.yp(v)


class Rim(Plane):
    def __init__(self, ln, e, tz):
        self.ln = ln
        self.tz = jnp.where(ln.lane0, 0.0, tz)
        self.tzp = ln.zp(self.tz)
        self.spread(e)


def plane_at(ln, faces, p):
    return Plane(ln, faces[0, p], faces[0, p + 1], faces[1, p], faces[2, p], faces[3, p])


def middle(p, below, above, mz):
    ln = p.ln
    vz = p.half * p.z1 + p.tx * below.z1 + p.txn * above.z1 + p.along_y(p.z1)
    vz = vz + p.tz * jnp.where(ln.first, 1.0 - p.zm, p.zm)
    vz = vz + p.tzp * jnp.where(ln.last, 1.0 - p.zp, p.zp)
    kept = vz * mz
    return p.all - vz, kept, p.all - (vz - kept)


def second(p, edge, inner, low, mz, mx):
    below, above = (edge, inner) if low else (inner, edge)
    ln = p.ln
    first_o = ln.zm(p.z1)
    vz = p.half * p.z1 + p.tx * below.z1 + p.txn * above.z1 + p.along_y(p.z1)
    vz = vz + p.tz * jnp.where(ln.first, 1.0 - first_o, first_o)
    vz = vz + p.tzp * jnp.where(ln.last, 1.0 - p.zp, p.zp)
    vx = p.toward(low) * edge.x1
    kept_z, kept_x = vz * mz, vx * mx
    total = p.all - (vz - kept_z) - (vx - kept_x)
    return p.all - vz - vx, kept_z, kept_x, total


def edge_own(p, inner_o1, inner_z1, outer_x1, low, mz):
    ln = p.ln
    om, op = ln.zm(p.o1), ln.zp(p.o1)
    vo = p.half * p.o1 + p.toward(low) * outer_x1 + p.inward(low) * inner_o1 + p.along_y(p.o1)
    vo = vo + p.tz * jnp.where(ln.first, p.zm, om) + p.tzp * jnp.where(ln.last, p.zp, op)
    vz = p.half * p.z1 + p.inward(low) * inner_z1 + p.along_y(p.z1)
    vz = vz + p.tz * jnp.where(ln.first, om, p.zm) + p.tzp * jnp.where(ln.last, op, p.zp)
    return vo, vz * mz


def edge_total(p, mz):
    rim = p.rim()
    return p.all - (rim - rim * mz)


def edge_spill(p, own, low):
    ln = p.ln
    xm, xp = ln.zm(p.x1), ln.zp(p.x1)
    face = p.toward(low)
    vx = p.half * p.x1 + face * own.o1 + p.along_y(p.x1)
    vx = vx + p.tz * jnp.where(ln.first, 0.0, xm) + p.tzp * jnp.where(ln.last, 0.0, xp)
    vd = face * own.z1 + p.tz * jnp.where(ln.first, xm, 0.0) + p.tzp * jnp.where(ln.last, xp, 0.0)
    return vx, vd


def store(ln, dst, plane, blocks, own, other, total):
    scale = reciprocal(total)
    own = own * scale
    other = jnp.zeros_like(own) if other is None else other * scale
    even, odd = jnp.where(ln.odd, other, own), jnp.where(ln.odd, own, other)
    for k in range(blocks):
        dst[k, plane] = jnp.where(ln.around(k), odd if k % 2 else even, 0.0)


def work_side(ln, low, valid, faces, masks, msg, put):
    n, rows, lanes = faces.shape[1:]
    layers = masks.shape[0]

    def own(i, j):
        return faces[i, jnp.where(low, j, n - 1 - j)]

    def got(i):
        tiles = rows // TAIL
        return msg[pl.ds(1 + tiles * i, tiles)].reshape(rows, lanes)

    f1, f2, f3 = (faces[0, jnp.where(low, j, n - j)] for j in (1, 2, 3))
    f0 = jnp.where(valid, jnp.where(low, faces[0, 0], got(6)), 0.0)
    g1 = got(0)
    a0 = Plane(ln, f0, f1, own(1, 0), own(2, 0), own(3, 0))
    a1 = Plane(ln, f1, f2, own(1, 1), own(2, 1), own(3, 1))
    a2 = Plane(ln, f2, f3, own(1, 2), own(2, 2), own(3, 2))
    b0 = Plane(ln, g1, f0, got(1), got(2), got(3), valid)
    b1 = Rim(ln, jnp.where(valid, got(4) + g1, 1.0), got(5))
    mine = masks[jnp.where(low, 0, layers - 1)]
    mz, my_reach = mine[0:1], jnp.where(low, mine[1:2], mine[2:3])
    theirs = msg[0]
    mo, their_reach = theirs[0:1], jnp.where(low, theirs[2:3], theirs[1:2])
    a0.edge(True)
    b0.edge(False)
    vx = g1 * b0.x1
    kept = vx * my_reach
    put(0, kept, None, edge_total(b1, mo) - (vx - kept))
    vx, vd = edge_spill(b0, a0, False)
    put(1, vx, vd, edge_total(b0, mo))
    vo, vz = edge_own(a0, 1.0 - a1.z1, a1.z1, b0.x1, True, mz)
    put(2, vo, vz, edge_total(a0, mz))
    vo, vz, _, total = second(a1, a0, a2, True, mz, their_reach)
    put(3, vo, vz, total)


def store_side(ln, buf, low, blocks):
    def put(i, own, other, total):
        store(ln, buf, jnp.where(low, i, 3 - i), blocks, own, other, total)

    return put


def send_one_side(buf, out, low, width, layers, sem, k):
    layer = jnp.where(low, 0, layers - 1)
    start = jnp.where(low, width - 2, 2 * width - 2)
    there = out.at[pl.ds((layer * buf.shape[0] + k) * 3 * width + start, 4)]
    return pltpu.make_async_copy(buf.at[k], there, sem)


def clear_run(zeros, out, b, bases, width, sem):
    depth = width - 2
    ends = isinstance(b, int) and b in (0, bases)
    count = depth if ends else 2 * depth
    start = 0 if ends and b == 0 else b * 3 * width - depth
    return pltpu.make_async_copy(zeros.at[pl.ds(0, count)], out.at[pl.ds(start, count)], sem)


def clear_runs(zeros, out, first, last, bases, width, sem):
    def body(b, _):
        clear_run(zeros, out, b, bases, width, sem).start()

    lax.fori_loop(first, last, body, None)


def wait_planes(out, count, sem):
    some = out.at[pl.ds(0, count)]
    pltpu.make_async_copy(some, some, sem).wait()


def pack_kernel(
    n, width, axis, tx, ty, tz, s, reach, msg_a, msg_b, masks, faces, out,
    held_reach, zeros, buf, read_sems, sem,
):
    layers, _, blocks = held_reach.shape
    rows, lanes = faces.shape[2:]
    fetch = pltpu.make_async_copy(reach, held_reach, read_sems.at[2])
    fetch.start()
    copies = [
        pltpu.make_async_copy(a, faces.at[i], read_sems.at[0 if i in (1, 2) else 1])
        for i, a in enumerate((tx, ty, tz, s))
    ]
    for i in (1, 2, 0, 3):
        copies[i].start()
    bases = layers * blocks
    me = lax.axis_index(axis)
    late = bases - EARLY

    @pl.when(me == 1)
    def _():
        zeros[...] = jnp.zeros(zeros.shape, jnp.float32)
        clear_runs(zeros, out, late, bases, bases, width, sem)

    masks[...] = jnp.zeros(masks.shape, jnp.float32)
    lane = lax.broadcasted_iota(jnp.int32, (4, lanes), 1)
    block = lane // width
    local = lane - block * width
    fetch.wait()
    for layer in range(layers):
        r = jnp.zeros((4, lanes), jnp.int32)
        for k in range(blocks):
            r = jnp.where(block == k, held_reach[layer, :, k : k + 1], r)
        low = pltpu.roll(r, width, 1)
        high = pltpu.roll(r, lanes - width, 1)
        near = jnp.where(
            local[0:1] < width // 2,
            jnp.where(low[3:4] >= local[0:1] + 1, 1.0, 0.0),
            jnp.where(high[2:3] >= width - local[0:1], 1.0, 0.0),
        )
        masks[layer, 0:1] = near
        masks[layer, 1:3] = jnp.where(r[0:2] >= 2, 1.0, 0.0)
    even = lax.rem(me, 2) == 0

    def put(tile, up, down):
        up, down = (v.reshape(-1, TAIL, lanes) for v in (up, down))
        where = pl.ds(tile, up.shape[0])
        msg_a[where] = jnp.where(even, up, down)
        msg_b[where] = jnp.where(even, down, up)

    put(0, masks[layers - 1], masks[0])
    ln = Lanes(faces.shape[2:], width)
    behind = {}

    def plane(slot, up, down):
        put(1 + slot * (rows // TAIL), up, down)

    def wait_two(sem):
        two = faces.at[pl.ds(0, 2)]
        pltpu.make_async_copy(two, two, sem).wait()

    wait_two(read_sems.at[0])
    for i, across in ((1, lambda v: within_y(ln, v)), (2, lambda v: within_z(ln, v))):
        plane(i, faces[i, n - 1], faces[i, 0])
        for p in (n - 2, 1):
            v, v_next = across(faces[i, p])
            behind[p] = behind.get(p, 0.0) + (v + v_next)
    plane(5, faces[2, n - 2], faces[2, 1])
    wait_two(read_sems.at[1])
    plane(0, faces[0, n - 1], faces[0, 1])
    plane(6, faces[0, n - 1], faces[0, 0])
    behind = {p: behind[p] + faces[0, q] for p, q in ((n - 2, n - 2), (1, 2))}
    plane(3, faces[3, n - 1], faces[3, 0])
    plane(4, *(behind[p] + faces[3, p] * (1.0 / 3.0) for p in (n - 2, 1)))

    @pl.when(me == 1)
    def _():
        wait_planes(out, EARLY * 2 * (width - 2), sem)

    @pl.when(me == 0)
    def _():
        inner_planes(width, bases, faces, masks, out, zeros, buf, sem)
        wait_planes(out, inner_count(layers, blocks, width), sem)


def inner_count(layers, blocks, width):
    return layers * blocks * 3 * width - 8 * blocks


def inner_planes(width, last_run, faces, masks, out, zeros, buf, sem):
    layers, blocks = buf.shape[:2]
    rows, lanes = faces.shape[2:]
    box, depth = 3 * width, width - 2
    bases = layers * blocks
    zeros[...] = jnp.zeros(zeros.shape, jnp.float32)

    for b in (0, bases):
        clear_run(zeros, out, b, bases, width, sem).start()
    clear_runs(zeros, out, 1, last_run, bases, width, sem)
    ln = Lanes((rows, lanes), width)
    plane = functools.partial(plane_at, ln, faces)

    def send(k, layer):
        start = 4 if layer == 0 else 0
        count = width + 4 - start - (4 if layer == layers - 1 else 0)
        return pltpu.make_async_copy(
            buf.at[layer, k, pl.ds(start, count)],
            out.at[pl.ds((layer * blocks + k) * box + depth + start, count)],
            sem,
        )

    def between(layer):
        base = layer * width
        ma, mb = masks[layer - 1, 0:1], masks[layer, 0:1]
        to_above, to_below = masks[layer - 1, 2:3], masks[layer, 1:2]
        a3, a2, a1 = (plane(base - i) for i in (3, 2, 1))
        b0, b1, b2 = (plane(base + i) for i in (0, 1, 2))
        a1.edge(False)
        b0.edge(True)
        low = functools.partial(store, ln, buf.at[layer - 1])
        high = functools.partial(store, ln, buf.at[layer])
        vo, vz, vx, total = second(a2, a1, a3, False, ma, to_below)
        low(width, blocks, vo, vz, total)
        high(0, blocks, vx, None, total)
        vo, vz = edge_own(a1, 1.0 - a2.z1, a2.z1, b0.x1, False, ma)
        vx, vd = edge_spill(a1, b0, False)
        total = edge_total(a1, ma)
        low(width + 1, blocks, vo, vz, total)
        high(1, blocks, vx, vd, total)
        vo, vz = edge_own(b0, 1.0 - b1.z1, b1.z1, a1.x1, True, mb)
        vx, vd = edge_spill(b0, a1, True)
        total = edge_total(b0, mb)
        high(2, blocks, vo, vz, total)
        low(width + 2, blocks, vx, vd, total)
        vo, vz, vx, total = second(b1, b0, b2, True, mb, to_above)
        high(3, blocks, vo, vz, total)
        low(width + 3, blocks, vx, None, total)

    for layer in range(layers):
        planes = [plane(layer * width + j) for j in range(1, width - 1)]
        mz = masks[layer, 0:1]
        for j in range(2, width - 2):
            vo, vz, total = middle(planes[j - 1], planes[j - 2], planes[j], mz)
            store(ln, buf.at[layer], j + 2, blocks, vo, vz, total)
        if layer < layers - 1:
            between(layer + 1)

        @pl.loop(0, blocks)
        def _(k):
            send(k, layer).start()


def bulk_kernel(width, axis, faces, masks, held, out, zeros, buf, sem):
    del held
    me = lax.axis_index(axis)
    layers, blocks = buf.shape[:2]
    bases = layers * blocks
    early = EARLY * 2 * (width - 2)

    @pl.when(me != 0)
    def _():
        last_run = jnp.where(me == 1, bases - EARLY, bases)
        inner_planes(width, last_run, faces, masks, out, zeros, buf, sem)
        wait_planes(out, inner_count(layers, blocks, width) - early, sem)

    @pl.when(me > 1)
    def _():
        wait_planes(out, early, sem)


def edge_kernel(
    width, blocks, axis, count, faces, masks, got_a, got_b, held, out, side_a, side_b, sem
):
    del held
    layers = masks.shape[0]
    me = lax.axis_index(axis)
    odd = lax.rem(me, 2) == 1
    ln = Lanes(faces.shape[2:], width)
    for low, msg, side in ((odd, got_a, side_a), (jnp.logical_not(odd), got_b, side_b)):
        valid = jnp.where(low, me > 0, me < count - 1)
        work_side(ln, low, valid, faces, masks, msg, store_side(ln, side, low, blocks))
        for k in range(blocks):
            send_one_side(side, out, low, width, layers, sem, k).start()
    wait_planes(out, 8 * blocks, sem)


def swaps(firsts):
    return [pair for i in firsts for pair in ((i, i + 1), (i + 1, i))]


def on_device(trans_east, trans_north, trans_up, storage, support_reach, *, axis, count):
    layers, blocks, _ = support_reach.shape
    n, rows, lanes = trans_east.shape
    width = n // layers
    f32 = jnp.float32
    anywhere = pl.BlockSpec(memory_space=pl.ANY)
    vmem = pl.BlockSpec(memory_space=pltpu.VMEM)
    params = pltpu.CompilerParams(vmem_limit_bytes=16 * 2**20)
    outside = tuple(
        pltpu.with_memory_space_constraint(x, pltpu.HBM)
        for x in (trans_east, trans_north, trans_up, storage)
    )
    reach = jnp.transpose(support_reach, (0, 2, 1))
    reach = pltpu.with_memory_space_constraint(reach, pltpu.HBM)
    bases = layers * blocks
    out_shape = jax.ShapeDtypeStruct((bases * 3 * width, rows, lanes), f32)
    inner = [
        pltpu.VMEM((2 * (width - 2), rows, lanes), f32),
        pltpu.VMEM((layers, blocks, width + 4, rows, lanes), f32),
    ]
    tiles = 1 + 7 * rows // TAIL
    msg_a, msg_b, masks, faces, started = pl.pallas_call(
        functools.partial(pack_kernel, n, width, axis),
        out_shape=(
            pltpu.VMEM((tiles, TAIL, lanes), f32),
            pltpu.VMEM((tiles + 1, TAIL, lanes), f32),
            pltpu.VMEM((layers, TAIL, lanes), f32),
            pltpu.VMEM((4, n, rows, lanes), f32),
            out_shape,
        ),
        in_specs=[anywhere] * 5,
        out_specs=(vmem,) * 4 + (anywhere,),
        scratch_shapes=[
            pltpu.VMEM((layers, 4, blocks), jnp.int32),
            *inner,
            pltpu.SemaphoreType.DMA((3,)),
            pltpu.SemaphoreType.DMA,
        ],
        compiler_params=params,
        name="pack",
    )(*outside, reach)
    got_a = lax.ppermute(msg_a, axis, swaps(range(0, count - 1, 2)))
    got_b = lax.ppermute(msg_b, axis, swaps(range(1, count - 1, 2)))

    bulk = pl.pallas_call(
        functools.partial(bulk_kernel, width, axis),
        out_shape=out_shape,
        in_specs=[vmem] * 2 + [anywhere],
        out_specs=anywhere,
        scratch_shapes=inner + [pltpu.SemaphoreType.DMA],
        input_output_aliases={2: 0},
        compiler_params=params,
        cost_estimate=pl.CostEstimate(flops=10**7, bytes_accessed=7 * 10**6, transcendentals=0),
        name="bulk",
    )(faces, masks, started)
    side = [pltpu.VMEM((blocks, 4, rows, lanes), f32)] * 2
    out = pl.pallas_call(
        functools.partial(edge_kernel, width, blocks, axis, count),
        out_shape=out_shape,
        in_specs=[vmem] * 4 + [anywhere],
        out_specs=anywhere,
        scratch_shapes=side + [pltpu.SemaphoreType.DMA],
        input_output_aliases={4: 0},
        compiler_params=params,
        cost_estimate=pl.CostEstimate(flops=10**6, bytes_accessed=10**6, transcendentals=0),
        name="edges",
    )(faces, masks, got_a, got_b, bulk)
    return out.reshape(layers, blocks, 3 * width, rows, lanes)


def solution(mesh):
    spread = P(("groups", "blk"))
    return jax.shard_map(
        functools.partial(on_device, axis="blk", count=mesh.shape["blk"]),
        mesh=mesh,
        in_specs=(spread,) * 5,
        out_specs=spread,
        check_vma=False,
    )
```

```python
import functools

import jax
import jax.numpy as jnp
from jax import lax
from jax.experimental import pallas as pl
from jax.experimental.pallas import tpu as pltpu
from jax.sharding import PartitionSpec as P


TAIL = 8
EARLY = 12


class Lanes:
    def __init__(self, shape, width):
        tile = lax.broadcasted_iota(jnp.int32, (TAIL, shape[1]), 1)

        def rows(v):
            return jnp.concatenate([v] * (shape[0] // TAIL), axis=0)

        self.rows, self.lanes = shape
        self.width = width
        self.lane = rows(tile)
        self.local = rows(lax.rem(tile, width))
        self.first = self.local == 0
        self.last = self.local == width - 1
        self.odd = rows(lax.rem(tile // width, 2)) == 1
        self.row0 = lax.broadcasted_iota(jnp.int32, shape, 0) == 0
        self.lane0 = self.lane == 0

    def around(self, k):
        start = k * self.width - self.width // 2
        return (self.lane >= start) & (self.lane < start + 2 * self.width)

    def zm(self, v):
        return pltpu.roll(v, 1, 1)

    def zp(self, v):
        return pltpu.roll(v, self.lanes - 1, 1)

    def ym(self, v):
        return pltpu.roll(v, 1, 0)

    def yp(self, v):
        return pltpu.roll(v, self.rows - 1, 0)


def reciprocal(x):
    r = pl.reciprocal(x, approx=True)
    return r * (2.0 - x * r)


def within_y(ln, ty):
    ty = jnp.where(ln.row0, 0.0, ty)
    return ty, ln.yp(ty)


def within_z(ln, tz):
    tz = jnp.where(ln.lane0, 0.0, tz)
    return tz, ln.zp(tz)


def cross(ln, ty, tz, s):
    ty, typ = within_y(ln, ty)
    tz, tzp = within_z(ln, tz)
    return s * (1.0 / 3.0) + ((ty + typ) + (tz + tzp)), (ty, typ, tz, tzp)


class Plane:
    def __init__(self, ln, tx, txn, ty, tz, s, valid=None):
        self.ln = ln
        self.tx, self.txn = tx, txn
        e, (self.ty, self.typ, self.tz, self.tzp) = cross(ln, ty, tz, s)
        e = e + (tx + txn)
        if valid is not None:
            e = jnp.where(valid, e, 1.0)
        self.half = 0.5 * e + s * (1.0 / 3.0)
        self.spread(e)

    def spread(self, e):
        ln = self.ln
        self.all = 1.5 * e
        self.q = reciprocal(self.all)
        self.z1 = self.q * jnp.where(ln.first, self.tz, jnp.where(ln.last, self.tzp, 0.0))
        self.zm = ln.zm(self.z1)
        self.zp = ln.zp(self.z1)

    def toward(self, low):
        return self.tx if low else self.txn

    def inward(self, low):
        return self.txn if low else self.tx

    def edge(self, low):
        self.x1 = self.q * self.toward(low)
        self.o1 = 1.0 - self.z1 - self.x1

    def rim(self):
        return self.tz * self.zm + self.tzp * self.zp

    def along_y(self, v):
        return self.ty * self.ln.ym(v) + self.typ * self.ln.yp(v)


class Rim(Plane):
    def __init__(self, ln, e, tz):
        self.ln = ln
        self.tz = jnp.where(ln.lane0, 0.0, tz)
        self.tzp = ln.zp(self.tz)
        self.spread(e)


def plane_at(ln, faces, p):
    return Plane(ln, faces[0, p], faces[0, p + 1], faces[1, p], faces[2, p], faces[3, p])


def middle(p, below, above, mz):
    ln = p.ln
    vz = p.half * p.z1 + p.tx * below.z1 + p.txn * above.z1 + p.along_y(p.z1)
    vz = vz + p.tz * jnp.where(ln.first, 1.0 - p.zm, p.zm)
    vz = vz + p.tzp * jnp.where(ln.last, 1.0 - p.zp, p.zp)
    kept = vz * mz
    return p.all - vz, kept, p.all - (vz - kept)


def second(p, edge, inner, low, mz, mx):
    below, above = (edge, inner) if low else (inner, edge)
    ln = p.ln
    first_o = ln.zm(p.z1)
    vz = p.half * p.z1 + p.tx * below.z1 + p.txn * above.z1 + p.along_y(p.z1)
    vz = vz + p.tz * jnp.where(ln.first, 1.0 - first_o, first_o)
    vz = vz + p.tzp * jnp.where(ln.last, 1.0 - p.zp, p.zp)
    vx = p.toward(low) * edge.x1
    kept_z, kept_x = vz * mz, vx * mx
    total = p.all - (vz - kept_z) - (vx - kept_x)
    return p.all - vz - vx, kept_z, kept_x, total


def edge_own(p, inner_o1, inner_z1, outer_x1, low, mz):
    ln = p.ln
    om, op = ln.zm(p.o1), ln.zp(p.o1)
    vo = p.half * p.o1 + p.toward(low) * outer_x1 + p.inward(low) * inner_o1 + p.along_y(p.o1)
    vo = vo + p.tz * jnp.where(ln.first, p.zm, om) + p.tzp * jnp.where(ln.last, p.zp, op)
    vz = p.half * p.z1 + p.inward(low) * inner_z1 + p.along_y(p.z1)
    vz = vz + p.tz * jnp.where(ln.first, om, p.zm) + p.tzp * jnp.where(ln.last, op, p.zp)
    return vo, vz * mz


def edge_total(p, mz):
    rim = p.rim()
    return p.all - (rim - rim * mz)


def edge_spill(p, own, low):
    ln = p.ln
    xm, xp = ln.zm(p.x1), ln.zp(p.x1)
    face = p.toward(low)
    vx = p.half * p.x1 + face * own.o1 + p.along_y(p.x1)
    vx = vx + p.tz * jnp.where(ln.first, 0.0, xm) + p.tzp * jnp.where(ln.last, 0.0, xp)
    vd = face * own.z1 + p.tz * jnp.where(ln.first, xm, 0.0) + p.tzp * jnp.where(ln.last, xp, 0.0)
    return vx, vd


def store(ln, dst, plane, blocks, own, other, total):
    scale = reciprocal(total)
    own = own * scale
    other = jnp.zeros_like(own) if other is None else other * scale
    even, odd = jnp.where(ln.odd, other, own), jnp.where(ln.odd, own, other)
    for k in range(blocks):
        dst[k, plane] = jnp.where(ln.around(k), odd if k % 2 else even, 0.0)


def work_side(ln, low, valid, faces, masks, msg, put):
    n, rows, lanes = faces.shape[1:]
    layers = masks.shape[0]

    def own(i, j):
        return faces[i, jnp.where(low, j, n - 1 - j)]

    def got(i):
        tiles = rows // TAIL
        return msg[pl.ds(1 + tiles * i, tiles)].reshape(rows, lanes)

    f1, f2, f3 = (faces[0, jnp.where(low, j, n - j)] for j in (1, 2, 3))
    f0 = jnp.where(valid, jnp.where(low, faces[0, 0], got(6)), 0.0)
    g1 = got(0)
    a0 = Plane(ln, f0, f1, own(1, 0), own(2, 0), own(3, 0))
    a1 = Plane(ln, f1, f2, own(1, 1), own(2, 1), own(3, 1))
    a2 = Plane(ln, f2, f3, own(1, 2), own(2, 2), own(3, 2))
    b0 = Plane(ln, g1, f0, got(1), got(2), got(3), valid)
    b1 = Rim(ln, jnp.where(valid, got(4) + g1, 1.0), got(5))
    mine = masks[jnp.where(low, 0, layers - 1)]
    mz, my_reach = mine[0:1], jnp.where(low, mine[1:2], mine[2:3])
    theirs = msg[0]
    mo, their_reach = theirs[0:1], jnp.where(low, theirs[2:3], theirs[1:2])
    a0.edge(True)
    b0.edge(False)
    vx = g1 * b0.x1
    kept = vx * my_reach
    put(0, kept, None, edge_total(b1, mo) - (vx - kept))
    vx, vd = edge_spill(b0, a0, False)
    put(1, vx, vd, edge_total(b0, mo))
    vo, vz = edge_own(a0, 1.0 - a1.z1, a1.z1, b0.x1, True, mz)
    put(2, vo, vz, edge_total(a0, mz))
    vo, vz, _, total = second(a1, a0, a2, True, mz, their_reach)
    put(3, vo, vz, total)


def store_side(ln, buf, low, blocks):
    def put(i, own, other, total):
        store(ln, buf, jnp.where(low, i, 3 - i), blocks, own, other, total)

    return put


def send_one_side(buf, out, low, width, layers, sem, k):
    layer = jnp.where(low, 0, layers - 1)
    start = jnp.where(low, width - 2, 2 * width - 2)
    there = out.at[pl.ds((layer * buf.shape[0] + k) * 3 * width + start, 4)]
    return pltpu.make_async_copy(buf.at[k], there, sem)


def clear_run(zeros, out, b, bases, width, sem):
    depth = width - 2
    ends = isinstance(b, int) and b in (0, bases)
    count = depth if ends else 2 * depth
    start = 0 if ends and b == 0 else b * 3 * width - depth
    return pltpu.make_async_copy(zeros.at[pl.ds(0, count)], out.at[pl.ds(start, count)], sem)


def clear_runs(zeros, out, first, last, bases, width, sem):
    def body(b, _):
        clear_run(zeros, out, b, bases, width, sem).start()

    lax.fori_loop(first, last, body, None)


def wait_planes(out, count, sem):
    some = out.at[pl.ds(0, count)]
    pltpu.make_async_copy(some, some, sem).wait()


def first_early(me, bases):
    return jnp.where(me == 1, bases - EARLY, bases)


def pack_kernel(
    n, width, axis, tx, ty, tz, s, reach, msg_a, msg_b, masks, faces, out,
    held_reach, zeros, buf, read_sems, sem,
):
    layers, _, blocks = held_reach.shape
    rows, lanes = faces.shape[2:]
    fetch = pltpu.make_async_copy(reach, held_reach, read_sems.at[4])
    fetch.start()
    copies = [
        pltpu.make_async_copy(a, faces.at[i], read_sems.at[i]) for i, a in enumerate((tx, ty, tz, s))
    ]
    for i in (1, 2, 0, 3):
        copies[i].start()
    bases = layers * blocks
    me = lax.axis_index(axis)
    late = first_early(me, bases)

    @pl.when(me == 1)
    def _():
        zeros[...] = jnp.zeros(zeros.shape, jnp.float32)
        clear_runs(zeros, out, late, bases, bases, width, sem)

    masks[...] = jnp.zeros(masks.shape, jnp.float32)
    lane = lax.broadcasted_iota(jnp.int32, (4, lanes), 1)
    block = lane // width
    local = lane - block * width
    fetch.wait()
    for layer in range(layers):
        r = jnp.zeros((4, lanes), jnp.int32)
        for k in range(blocks):
            r = jnp.where(block == k, held_reach[layer, :, k : k + 1], r)
        low = pltpu.roll(r, width, 1)
        high = pltpu.roll(r, lanes - width, 1)
        near = jnp.where(
            local[0:1] < width // 2,
            jnp.where(low[3:4] >= local[0:1] + 1, 1.0, 0.0),
            jnp.where(high[2:3] >= width - local[0:1], 1.0, 0.0),
        )
        masks[layer, 0:1] = near
        masks[layer, 1:3] = jnp.where(r[0:2] >= 2, 1.0, 0.0)
    even = lax.rem(me, 2) == 0

    def put(tile, up, down):
        up, down = (v.reshape(-1, TAIL, lanes) for v in (up, down))
        where = pl.ds(tile, up.shape[0])
        msg_a[where] = jnp.where(even, up, down)
        msg_b[where] = jnp.where(even, down, up)

    put(0, masks[layers - 1], masks[0])
    ln = Lanes(faces.shape[2:], width)
    behind = {}

    def plane(slot, up, down):
        put(1 + slot * (rows // TAIL), up, down)

    for i, across in ((1, lambda v: within_y(ln, v)), (2, lambda v: within_z(ln, v))):
        copies[i].wait()
        plane(i, faces[i, n - 1], faces[i, 0])
        for p in (n - 2, 1):
            v, v_next = across(faces[i, p])
            behind[p] = behind.get(p, 0.0) + (v + v_next)
    plane(5, faces[2, n - 2], faces[2, 1])
    copies[0].wait()
    plane(0, faces[0, n - 1], faces[0, 1])
    plane(6, faces[0, n - 1], faces[0, 0])
    behind = {p: behind[p] + faces[0, q] for p, q in ((n - 2, n - 2), (1, 2))}
    copies[3].wait()
    plane(3, faces[3, n - 1], faces[3, 0])
    plane(4, *(behind[p] + faces[3, p] * (1.0 / 3.0) for p in (n - 2, 1)))

    @pl.when(me == 1)
    def _():
        wait_planes(out, EARLY * 2 * (width - 2), sem)

    @pl.when(me == 0)
    def _():
        inner_planes(width, bases, faces, masks, out, zeros, buf, sem)
        wait_planes(out, inner_count(layers, blocks, width), sem)


def inner_count(layers, blocks, width):
    return layers * blocks * 3 * width - 8 * blocks


def inner_planes(width, last_run, faces, masks, out, zeros, buf, sem):
    layers, blocks = buf.shape[:2]
    rows, lanes = faces.shape[2:]
    box, depth = 3 * width, width - 2
    bases = layers * blocks
    zeros[...] = jnp.zeros(zeros.shape, jnp.float32)

    for b in (0, bases):
        clear_run(zeros, out, b, bases, width, sem).start()
    clear_runs(zeros, out, 1, last_run, bases, width, sem)
    ln = Lanes((rows, lanes), width)
    plane = functools.partial(plane_at, ln, faces)

    def send(k, layer):
        start = 4 if layer == 0 else 0
        count = width + 4 - start - (4 if layer == layers - 1 else 0)
        return pltpu.make_async_copy(
            buf.at[layer, k, pl.ds(start, count)],
            out.at[pl.ds((layer * blocks + k) * box + depth + start, count)],
            sem,
        )

    def between(layer):
        base = layer * width
        ma, mb = masks[layer - 1, 0:1], masks[layer, 0:1]
        to_above, to_below = masks[layer - 1, 2:3], masks[layer, 1:2]
        a3, a2, a1 = (plane(base - i) for i in (3, 2, 1))
        b0, b1, b2 = (plane(base + i) for i in (0, 1, 2))
        a1.edge(False)
        b0.edge(True)
        low = functools.partial(store, ln, buf.at[layer - 1])
        high = functools.partial(store, ln, buf.at[layer])
        vo, vz, vx, total = second(a2, a1, a3, False, ma, to_below)
        low(width, blocks, vo, vz, total)
        high(0, blocks, vx, None, total)
        vo, vz = edge_own(a1, 1.0 - a2.z1, a2.z1, b0.x1, False, ma)
        vx, vd = edge_spill(a1, b0, False)
        total = edge_total(a1, ma)
        low(width + 1, blocks, vo, vz, total)
        high(1, blocks, vx, vd, total)
        vo, vz = edge_own(b0, 1.0 - b1.z1, b1.z1, a1.x1, True, mb)
        vx, vd = edge_spill(b0, a1, True)
        total = edge_total(b0, mb)
        high(2, blocks, vo, vz, total)
        low(width + 2, blocks, vx, vd, total)
        vo, vz, vx, total = second(b1, b0, b2, True, mb, to_above)
        high(3, blocks, vo, vz, total)
        low(width + 3, blocks, vx, None, total)

    for layer in range(layers):
        planes = [plane(layer * width + j) for j in range(1, width - 1)]
        mz = masks[layer, 0:1]
        for j in range(2, width - 2):
            vo, vz, total = middle(planes[j - 1], planes[j - 2], planes[j], mz)
            store(ln, buf.at[layer], j + 2, blocks, vo, vz, total)
        if layer < layers - 1:
            between(layer + 1)

        @pl.loop(0, blocks, unroll=True)
        def _(k):
            send(k, layer).start()


def bulk_kernel(width, axis, faces, masks, held, out, zeros, buf, sem):
    del held
    me = lax.axis_index(axis)
    layers, blocks = buf.shape[:2]
    bases = layers * blocks
    run = 2 * (width - 2)

    @pl.when(me != 0)
    def _():
        last_run = first_early(me, bases)
        inner_planes(width, last_run, faces, masks, out, zeros, buf, sem)
        wait_planes(out, inner_count(layers, blocks, width) - EARLY * run, sem)

    @pl.when(me > 1)
    def _():
        wait_planes(out, EARLY * run, sem)


def inside_kernel(blocks, axis, count, faces, masks, msg, held, side):
    del held
    me = lax.axis_index(axis)
    low = lax.rem(me, 2) == 1
    ln = Lanes(faces.shape[2:], masks.shape[2] // blocks)
    work_side(ln, low, low | (me < count - 1), faces, masks, msg, store_side(ln, side, low, blocks))


def edge_kernel(width, blocks, axis, count, faces, masks, msg, inside, held, out, side, sem):
    del held
    layers = masks.shape[0]
    me = lax.axis_index(axis)
    low = lax.rem(me, 2) == 0
    for k in range(blocks):
        send_one_side(inside, out, jnp.logical_not(low), width, layers, sem, k).start()
    ln = Lanes(faces.shape[2:], width)
    valid = jnp.where(low, me > 0, me < count - 1)
    work_side(ln, low, valid, faces, masks, msg, store_side(ln, side, low, blocks))
    for k in range(blocks):
        send_one_side(side, out, low, width, layers, sem, k).start()
    wait_planes(out, 8 * blocks, sem)


def swaps(firsts):
    return [pair for i in firsts for pair in ((i, i + 1), (i + 1, i))]


def on_device(trans_east, trans_north, trans_up, storage, support_reach, *, axis, count):
    layers, blocks, _ = support_reach.shape
    n, rows, lanes = trans_east.shape
    width = n // layers
    f32 = jnp.float32
    anywhere = pl.BlockSpec(memory_space=pl.ANY)
    vmem = pl.BlockSpec(memory_space=pltpu.VMEM)
    params = pltpu.CompilerParams(vmem_limit_bytes=16 * 2**20)
    outside = tuple(
        pltpu.with_memory_space_constraint(x, pltpu.HBM)
        for x in (trans_east, trans_north, trans_up, storage)
    )
    reach = jnp.transpose(support_reach, (0, 2, 1))
    reach = pltpu.with_memory_space_constraint(reach, pltpu.HBM)
    bases = layers * blocks
    out_shape = jax.ShapeDtypeStruct((bases * 3 * width, rows, lanes), f32)
    inner = [
        pltpu.VMEM((2 * (width - 2), rows, lanes), f32),
        pltpu.VMEM((layers, blocks, width + 4, rows, lanes), f32),
    ]
    tiles = 1 + 7 * rows // TAIL
    msg_a, msg_b, masks, faces, started = pl.pallas_call(
        functools.partial(pack_kernel, n, width, axis),
        out_shape=(
            pltpu.VMEM((tiles, TAIL, lanes), f32),
            pltpu.VMEM((tiles + 1, TAIL, lanes), f32),
            pltpu.VMEM((layers, TAIL, lanes), f32),
            pltpu.VMEM((4, n, rows, lanes), f32),
            out_shape,
        ),
        in_specs=[anywhere] * 5,
        out_specs=(vmem,) * 4 + (anywhere,),
        scratch_shapes=[
            pltpu.VMEM((layers, 4, blocks), jnp.int32),
            *inner,
            pltpu.SemaphoreType.DMA((5,)),
            pltpu.SemaphoreType.DMA,
        ],
        compiler_params=params,
        name="pack",
    )(*outside, reach)
    got_a = lax.ppermute(msg_a, axis, swaps(range(0, count - 1, 2)))
    got_b = lax.ppermute(msg_b, axis, swaps(range(1, count - 1, 2)))

    bulk = pl.pallas_call(
        functools.partial(bulk_kernel, width, axis),
        out_shape=out_shape,
        in_specs=[vmem] * 2 + [anywhere],
        out_specs=anywhere,
        scratch_shapes=inner + [pltpu.SemaphoreType.DMA],
        input_output_aliases={2: 0},
        compiler_params=params,
        cost_estimate=pl.CostEstimate(flops=10**7, bytes_accessed=7 * 10**6, transcendentals=0),
        name="bulk",
    )(faces, masks, started)
    side = pltpu.VMEM((blocks, 4, rows, lanes), f32)
    inside = pl.pallas_call(
        functools.partial(inside_kernel, blocks, axis, count),
        out_shape=side,
        in_specs=[vmem] * 3 + [anywhere],
        out_specs=vmem,
        compiler_params=params,
        cost_estimate=pl.CostEstimate(flops=10**6, bytes_accessed=10**6, transcendentals=0),
        name="inside",
    )(faces, masks, got_a, pltpu.with_memory_space_constraint(bulk, pltpu.HBM))
    out = pl.pallas_call(
        functools.partial(edge_kernel, width, blocks, axis, count),
        out_shape=out_shape,
        in_specs=[vmem] * 4 + [anywhere],
        out_specs=anywhere,
        scratch_shapes=[side, pltpu.SemaphoreType.DMA],
        input_output_aliases={4: 0},
        compiler_params=params,
        cost_estimate=pl.CostEstimate(flops=10**6, bytes_accessed=10**6, transcendentals=0),
        name="edges",
    )(faces, masks, got_b, inside, bulk)
    return out.reshape(layers, blocks, 3 * width, rows, lanes)


def solution(mesh):
    spread = P(("groups", "blk"))
    return jax.shard_map(
        functools.partial(on_device, axis="blk", count=mesh.shape["blk"]),
        mesh=mesh,
        in_specs=(spread,) * 5,
        out_specs=spread,
        check_vma=False,
    )
```
